32 devices in a mesh: dp: 8 (over y, x, core), tensor: 4 (over z).
Axes of the slice: x: 2, y: 2, z: 4, core: 2. Of those that a mesh axis runs over, the one named last changes fastest.
Arguments:
- pixels: bfloat16 [24576, 768], P('dp'), may hold values from -6 to 6
- coords: int32 [2, 24576], P(None, 'dp'), may hold values from 0 to 63
- lengths: int32 [24, 8], P('dp'), may hold values from 1 to 512, 1024 in all within a row
- labels: int32 [192, 1000], P('dp'), may hold values 0 or 1
- patch_table: float32 [768, 768], P(None, 'dp'), may hold values from -0.21875 to 0.21875
- patch_first: float32 [768, 768], P(None, 'dp'), may hold values from -0.00010681152 to 0.00010681152
- patch_second: float32 [768, 768], P(None, 'dp'), may hold values from 2.928355e-10 to 1.171342e-09
- position_table: float32 [2, 64, 768], P(None, None, 'dp'), may hold values from -3 to 3
- position_first: float32 [2, 64, 768], P(None, None, 'dp'), may hold values from -0.00010681152 to 0.00010681152
- position_second: float32 [2, 64, 768], P(None, None, 'dp'), may hold values from 5.85671e-11 to 2.342684e-10
- attend_in: float32 [768, 3, 768], P('dp', None, 'tensor'), may hold values from -0.21875 to 0.21875
- attend_in_first: float32 [768, 3, 768], P('dp', None, 'tensor'), may hold values from -0.00010681152 to 0.00010681152
- attend_in_second: float32 [768, 3, 768], P('dp', None, 'tensor'), may hold values from 2.928355e-10 to 1.171342e-09
- attend_out: float32 [768, 768], P('tensor', 'dp'), may hold values from -1.75 to 1.75
- attend_out_first: float32 [768, 768], P('tensor', 'dp'), may hold values from -0.00010681152 to 0.00010681152
- attend_out_second: float32 [768, 768], P('tensor', 'dp'), may hold values from 5.85671e-11 to 2.342684e-10
- expand: float32 [768, 3072], P('dp', 'tensor'), may hold values from -0.21875 to 0.21875
- expand_first: float32 [768, 3072], P('dp', 'tensor'), may hold values from -0.00010681152 to 0.00010681152
- expand_second: float32 [768, 3072], P('dp', 'tensor'), may hold values from 2.928355e-10 to 1.171342e-09
- shrink: float32 [3072, 768], P('tensor', 'dp'), may hold values from -0.109375 to 0.109375
- shrink_first: float32 [3072, 768], P('tensor', 'dp'), may hold values from -0.00010681152 to 0.00010681152
- shrink_second: float32 [3072, 768], P('tensor', 'dp'), may hold values from 2.928355e-10 to 1.171342e-09
- classify: float32 [768, 1000], P('dp'), may hold values from -0.875 to 0.875
- classify_first: float32 [768, 1000], P('dp'), may hold values from -0.00010681152 to 0.00010681152
- classify_second: float32 [768, 1000], P('dp'), may hold values from 2.928355e-10 to 1.171342e-09
- vectors: float32 [4, 768], replicated, may hold values from -3 to 3
- vectors_first: float32 [4, 768], replicated, may hold values from -0.0004272461 to 0.0004272461
- vectors_second: float32 [4, 768], replicated, may hold values from 4.685368e-09 to 1.8741472e-08
- head_gains: float32 [2, 64], replicated, may hold values from 0.5 to 1.5
- head_gains_first: float32 [2, 64], replicated, may hold values from -0.0004272461 to 0.0004272461
- head_gains_second: float32 [2, 64], replicated, may hold values from 4.685368e-09 to 1.8741472e-08
Outputs:
- patch_new: float32 [768, 768], P(None, 'dp')
- patch_first_new: float32 [768, 768], P(None, 'dp')
- patch_second_new: float32 [768, 768], P(None, 'dp')
- position_new: float32 [2, 64, 768], P(None, None, 'dp')
- position_first_new: float32 [2, 64, 768], P(None, None, 'dp')
- position_second_new: float32 [2, 64, 768], P(None, None, 'dp')
- attend_in_new: float32 [768, 3, 768], P('dp', None, 'tensor')
- attend_in_first_new: float32 [768, 3, 768], P('dp', None, 'tensor')
- attend_in_second_new: float32 [768, 3, 768], P('dp', None, 'tensor')
- attend_out_new: float32 [768, 768], P('tensor', 'dp')
- attend_out_first_new: float32 [768, 768], P('tensor', 'dp')
- attend_out_second_new: float32 [768, 768], P('tensor', 'dp')
- expand_new: float32 [768, 3072], P('dp', 'tensor')
- expand_first_new: float32 [768, 3072], P('dp', 'tensor')
- expand_second_new: float32 [768, 3072], P('dp', 'tensor')
- shrink_new: float32 [3072, 768], P('tensor', 'dp')
- shrink_first_new: float32 [3072, 768], P('tensor', 'dp')
- shrink_second_new: float32 [3072, 768], P('tensor', 'dp')
- classify_new: float32 [768, 1000], P('dp')
- classify_first_new: float32 [768, 1000], P('dp')
- classify_second_new: float32 [768, 1000], P('dp')
- vectors_new: float32 [4, 768], replicated
- vectors_first_new: float32 [4, 768], replicated
- vectors_second_new: float32 [4, 768], replicated
- head_gains_new: float32 [2, 64], replicated
- head_gains_first_new: float32 [2, 64], replicated
- head_gains_second_new: float32 [2, 64], replicated
- loss_value: float32 [], replicated
- grad_norm: float32 [], replicated
The draws below stay inside these ranges and needn't reach their ends.
Inputs may be any that keep to these rules, and one draw needn't show every extreme that they name: Each pack's 8 image lengths add up to 1024.
All inputs are finite; a program needn't handle non-finite values. No bound on the sum of `labels` on one device may be relied on, other than what follows from the above.
Results may differ from the reference program's by a relative error of at most 0.025.
Values may be sent and summed in bfloat16 or wider, within the bound.
A program may use at most 256 MiB of HBM per device.

```python
import math
import jax
import jax.numpy as jnp
import numpy as np
from jax import lax

D = 768
HEADS = 12
HD = 64
FF = 3072
PIX = 768
CLASSES = 1000
LEN = 1024
PMAX = 64
IMGS_PACK = 8
STEP = 10
PACKS = 24
TOKENS = 24576
IMAGES = 192
PARAMS = 8537216
N_TENSOR = 4


def draw_vectors(key, part):
    key = jax.random.fold_in(key, 7)
    gain_key, query_key = jax.random.split(key)
    place = jnp.arange(D, dtype=jnp.float32)[None, :] / (D - 1)
    rough = jax.random.uniform(gain_key, (3, D), jnp.float32, 0.85, 1.15)
    gains = (0.6 + 1.2 * place) * rough
    query = jnp.clip(jax.random.normal(query_key, (1, D), jnp.float32), -3.0, 3.0)
    return jnp.concatenate([gains, query], axis=0)


def place_ends(array, stream_key, smallest, top_value):
    longest = array.shape.index(max(array.shape))
    spots = []
    for shift in (0, 1):
        where = [jax.random.randint(jax.random.fold_in(stream_key, axis), (), 0, length) for axis, length in enumerate(array.shape)]
        where[longest] = (where[longest] + shift) % array.shape[longest]
        spots.append(tuple(where))
    return array.at[spots[0]].set(smallest).at[spots[1]].set(top_value)


def shard_levels(own_key, shape, pieces, least, top_value):
    factor_of = 1.0
    for axis_at, blocks in pieces:
        draws = jax.random.uniform(jax.random.fold_in(jax.random.fold_in(own_key, 6), axis_at), (blocks,), jnp.float32, least / len(pieces), top_value / len(pieces))
        factor_of = factor_of * jnp.repeat(jnp.exp(draws), shape[axis_at] // blocks).reshape((-1,) + (1,) * (len(shape) - 1 - axis_at))
    return factor_of


def length_profile(number_of, total, most, skew):
    loads = [(1 << 20) // math.isqrt(rank ** skew) + 1 for rank in range(2, number_of + 1)]
    spare, given = total - most - (number_of - 1), [1] * (number_of - 1)
    while spare > 0:
        free = [i for i in range(number_of - 1) if given[i] < most]
        mass, budget = sum([loads[i] for i in free]), spare
        for i in free:
            addition = min(most - given[i], max(1, budget * loads[i] // mass), spare)
            given[i] = given[i] + addition
            spare = spare - addition
    return np.array([most] + given)


def ragged_sizes(key, number_of, total, most, lean):
    if number_of == 2:
        one = jax.random.randint(key, (), max(1, total - most), min(most, total - 1) + 1)
        return jnp.stack([one, total - one])
    sizes = jnp.asarray(length_profile(number_of, total, most, lean), jnp.int32)
    pairs = (number_of - 1) // 2
    giver, receiver = sizes[1:1 + 2 * pairs:2], sizes[2:2 + 2 * pairs:2]
    room = jnp.minimum(giver - 1, most - receiver)
    passed = jax.random.randint(jax.random.fold_in(key, 1), (pairs,), 0, 1 << 20) % (room + 1)
    sizes = sizes.at[1:1 + 2 * pairs:2].set(giver - passed).at[2:2 + 2 * pairs:2].set(receiver + passed)
    return sizes[jax.random.permutation(jax.random.fold_in(key, 2), number_of)]


def scatter_about(key, extent, spread, reach, cuts=(), kind=jnp.bfloat16):
    level = shard_levels(key, extent, cuts, -0.22, 0.18) if cuts else 1.0
    drawn = jax.random.normal(key, extent, jnp.float32) * spread * level
    return jnp.minimum(jnp.maximum(drawn, -reach), reach).astype(kind)


def setup_inputs(seed: int = 0) -> dict:
    splits = jax.random.split(jax.random.key(seed), 32)
    return {
        "pixels": scatter_about(splits[0], (TOKENS, PIX), 1.0, 6.0, ((0, 8),)),
        "coords": place_ends(jax.random.randint(splits[1], (2, TOKENS), 0, PMAX), jax.random.fold_in(splits[1], 1), 0, PMAX - 1).astype(jnp.int32),
        "lengths": jax.vmap(lambda own: ragged_sizes(own, IMGS_PACK, LEN, LEN // 2, 2))(jax.random.split(splits[2], PACKS)).reshape((PACKS, IMGS_PACK)).astype(jnp.int32),
        "labels": place_ends((jax.random.randint(splits[3], (IMAGES, CLASSES), 0, 200) < 1).astype(jnp.int32), jax.random.fold_in(splits[3], 1), 0, 1),
        "patch_table": scatter_about(splits[4], (PIX, D), PIX ** -0.5, 0.21875, ((1, 8),), jnp.float32),
        "patch_first": scatter_about(splits[5], (PIX, D), (0.05 * PARAMS ** -0.5), 0.00010681152, ((1, 8),), jnp.float32),
        "patch_second": jnp.clip(jnp.exp(math.log(1.1713420233760985e-09) - 1.3862944 * jax.random.uniform(splits[6], (PIX, D), jnp.float32) ** shard_levels(splits[6], (PIX, D), ((1, 8),), -0.2, 0.2)), 2.928355058440246e-10, 1.1713420233760985e-09),
        "position_table": scatter_about(splits[7], (2, PMAX, D), 0.5, 3.0, ((2, 8),), jnp.float32),
        "position_first": scatter_about(splits[8], (2, PMAX, D), (0.05 * PARAMS ** -0.5), 0.00010681152, ((2, 8),), jnp.float32),
        "position_second": jnp.clip(jnp.exp(math.log(2.342684102263348e-10) - 1.3862944 * jax.random.uniform(splits[9], (2, PMAX, D), jnp.float32) ** shard_levels(splits[9], (2, PMAX, D), ((2, 8),), -0.2, 0.2)), 5.85671025565837e-11, 2.342684102263348e-10),
        "attend_in": scatter_about(splits[10], (D, 3, D), D ** -0.5, 0.21875, ((0, 8), (2, 4)), jnp.float32),
        "attend_in_first": scatter_about(splits[11], (D, 3, D), (0.05 * PARAMS ** -0.5), 0.00010681152, ((0, 8), (2, 4)), jnp.float32),
        "attend_in_second": jnp.clip(jnp.exp(math.log(1.1713420233760985e-09) - 1.3862944 * jax.random.uniform(splits[12], (D, 3, D), jnp.float32) ** shard_levels(splits[12], (D, 3, D), ((0, 8), (2, 4)), -0.2, 0.2)), 2.928355058440246e-10, 1.1713420233760985e-09),
        "attend_out": scatter_about(splits[13], (D, D), (D // 64) ** -0.5, 1.75, ((0, 4), (1, 8)), jnp.float32),
        "attend_out_first": scatter_about(splits[14], (D, D), (0.05 * PARAMS ** -0.5), 0.00010681152, ((0, 4), (1, 8)), jnp.float32),
        "attend_out_second": jnp.clip(jnp.exp(math.log(2.342684102263348e-10) - 1.3862944 * jax.random.uniform(splits[15], (D, D), jnp.float32) ** shard_levels(splits[15], (D, D), ((0, 4), (1, 8)), -0.2, 0.2)), 5.85671025565837e-11, 2.342684102263348e-10),
        "expand": scatter_about(splits[16], (D, FF), D ** -0.5, 0.21875, ((0, 8), (1, 4)), jnp.float32),
        "expand_first": scatter_about(splits[17], (D, FF), (0.05 * PARAMS ** -0.5), 0.00010681152, ((0, 8), (1, 4)), jnp.float32),
        "expand_second": jnp.clip(jnp.exp(math.log(1.1713420233760985e-09) - 1.3862944 * jax.random.uniform(splits[18], (D, FF), jnp.float32) ** shard_levels(splits[18], (D, FF), ((0, 8), (1, 4)), -0.2, 0.2)), 2.928355058440246e-10, 1.1713420233760985e-09),
        "shrink": scatter_about(splits[19], (FF, D), FF ** -0.5, 0.109375, ((0, 4), (1, 8)), jnp.float32),
        "shrink_first": scatter_about(splits[20], (FF, D), (0.05 * PARAMS ** -0.5), 0.00010681152, ((0, 4), (1, 8)), jnp.float32),
        "shrink_second": jnp.clip(jnp.exp(math.log(1.1713420233760985e-09) - 1.3862944 * jax.random.uniform(splits[21], (FF, D), jnp.float32) ** shard_levels(splits[21], (FF, D), ((0, 4), (1, 8)), -0.2, 0.2)), 2.928355058440246e-10, 1.1713420233760985e-09),
        "classify": scatter_about(splits[22], (D, CLASSES), (D // 16) ** -0.5, 0.875, ((0, 8),), jnp.float32),
        "classify_first": scatter_about(splits[23], (D, CLASSES), (0.05 * PARAMS ** -0.5), 0.00010681152, ((0, 8),), jnp.float32),
        "classify_second": jnp.clip(jnp.exp(math.log(1.1713420233760985e-09) - 1.3862944 * jax.random.uniform(splits[24], (D, CLASSES), jnp.float32) ** shard_levels(splits[24], (D, CLASSES), ((0, 8),), -0.2, 0.2)), 2.928355058440246e-10, 1.1713420233760985e-09),
        "vectors": draw_vectors(jax.random.fold_in(splits[31], 71), 0),
        "vectors_first": scatter_about(splits[26], (4, D), (0.2 * PARAMS ** -0.5), 0.0004272461, (), jnp.float32),
        "vectors_second": jnp.clip(jnp.exp(jax.random.uniform(splits[27], (4, D), jnp.float32, math.log(4.685368093504394e-09), math.log(1.8741472374017576e-08))), 4.685368093504394e-09, 1.8741472374017576e-08),
        "head_gains": jnp.clip(1.0 + 0.1 * jax.random.normal(splits[28], (2, HD), jnp.float32), 0.5, 1.5),
        "head_gains_first": scatter_about(splits[29], (2, HD), (0.2 * PARAMS ** -0.5), 0.0004272461, (), jnp.float32),
        "head_gains_second": jnp.clip(jnp.exp(jax.random.uniform(splits[30], (2, HD), jnp.float32, math.log(4.685368093504394e-09), math.log(1.8741472374017576e-08))), 4.685368093504394e-09, 1.8741472374017576e-08),
    }


NEGATIVE = -1e+30
NORM_EPS = 1e-06
CLIP = 0.05
RATES = (0.03, 0.2, 0.03, 0.1, 0.03, 0.03, 0.1, 1.0, 1.0)
DECAY = 0.05
BETA_ONE = 0.5
BETA_TWO = 0.5
ADAM_EPS = 1e-08
SHIFT = -4.0
HIGH = lax.Precision.HIGHEST

@jax.custom_vjp
def low(v):
    return lax.optimization_barrier(v.astype(jnp.bfloat16)).astype(jnp.float32)

@jax.custom_vjp
def low_back(v):
    return v

def low_keep(v):
    return (low(v), None)

def low_pass(kept, grad):
    return (grad,)

def back_keep(v):
    return (v, None)

def back_low(kept, grad):
    return (low(grad),)
low.defvjp(low_keep, low_pass)
low_back.defvjp(back_keep, back_low)

def matmul_high(left, right):
    return jnp.dot(left, right, precision=HIGH)

def layer_norm(values, gain_row):
    center = values - lax.optimization_barrier(jnp.mean(values, axis=-1, keepdims=True))
    return center * lax.rsqrt(lax.optimization_barrier(jnp.mean(center * center, axis=-1, keepdims=True)) + NORM_EPS) * gain_row

def image_index(lengths, pack_rows):
    image_ends = jnp.cumsum(lengths, axis=-1)
    positions = lax.broadcasted_iota(jnp.int32, (lengths.shape[0], pack_rows, 1), 1)
    image_ids = lax.optimization_barrier(jnp.sum((positions >= image_ends[:, None, :]).astype(jnp.int32), axis=-1))
    slots = lax.broadcasted_iota(jnp.int32, (1, 1, lengths.shape[1]), 2)
    return (image_ids, image_ids[:, :, None] == slots)

def pack_loss(weights, pack_item):
    w_patch, w_pos, w_in, w_out, w_up, w_down, w_head, vectors, head_gains = weights
    pixel_rows, coord_rows, pack_lengths, pack_labels = pack_item
    position_grid = jnp.arange(PMAX, dtype=jnp.int32)[None, :]
    one_x = (coord_rows[0][:, None] == position_grid).astype(jnp.float32)
    one_y = (coord_rows[1][:, None] == position_grid).astype(jnp.float32)
    embedded = low_back(matmul_high(pixel_rows, w_patch) + matmul_high(one_x, w_pos[0]) + matmul_high(one_y, w_pos[1]))
    first_low = low(layer_norm(embedded, vectors[0]))
    per_group = w_in.shape[2] // N_TENSOR
    joined = jnp.concatenate([low_back(jnp.einsum('td,dcf->tcf', low_back(first_low), w_in[:, :, group * per_group:(group + 1) * per_group], precision=HIGH)) for group in range(N_TENSOR)], axis=2)
    heads = joined.reshape(LEN, 3, HEADS, HD)
    query_rows = low(layer_norm(heads[:, 0], head_gains[0]))
    key_rows = low(layer_norm(heads[:, 1], head_gains[1]))
    value_rows = low(heads[:, 2])
    image_ids, members = image_index(pack_lengths[None], LEN)
    image_ids = image_ids[0]
    members = members[0]
    scores = low_back(jnp.einsum('qhd,khd->hqk', query_rows, key_rows, precision=HIGH)) * HD ** (-0.5)
    scores = jnp.where((image_ids[:, None] == image_ids[None, :])[None], scores, NEGATIVE)
    probability = jax.nn.softmax(scores, axis=-1)
    attended = low(low_back(jnp.einsum('hqk,khd->qhd', low(probability), value_rows, precision=HIGH))).reshape(LEN, D)
    attend_total = low_back(sum((low(matmul_high(attended[:, group * per_group:(group + 1) * per_group], w_out[group * per_group:(group + 1) * per_group])) for group in range(N_TENSOR))))
    middle = embedded + attend_total
    second_low = low(layer_norm(middle, vectors[1]))
    hidden_per = w_up.shape[1] // N_TENSOR
    hidden = jnp.concatenate([low_back(matmul_high(low_back(second_low), w_up[:, group * hidden_per:(group + 1) * hidden_per])) for group in range(N_TENSOR)], axis=1)
    active = low(jax.nn.gelu(hidden, approximate=False))
    branch = low_back(sum((low(matmul_high(active[:, group * hidden_per:(group + 1) * hidden_per], w_down[group * hidden_per:(group + 1) * hidden_per])) for group in range(N_TENSOR))))
    output_rows = middle + branch
    last_norm = layer_norm(output_rows, vectors[2])
    pool_logit = lax.optimization_barrier(jnp.sum(last_norm * vectors[3], axis=-1)) / D ** 0.5
    pool_weights = jax.nn.softmax(jnp.where(members, pool_logit[:, None], NEGATIVE), axis=0)
    pooled = jnp.einsum('si,sd->id', pool_weights, last_norm, precision=HIGH)
    logits = low_back(matmul_high(low(pooled), w_head)) + SHIFT
    return jnp.sum(jax.nn.softplus(logits) - pack_labels * logits)

def forward(params, pixels, coords, lengths, labels):
    weights = tuple((low(entry) for entry in params[:7])) + (params[7], params[8])
    pack_items = (pixels.reshape(PACKS, LEN, PIX), jnp.transpose(coords.reshape(2, PACKS, LEN), (1, 0, 2)), lengths, labels.reshape(PACKS, IMGS_PACK, CLASSES).astype(jnp.float32))

    def pack_step(running, pack_item):
        return (running + pack_loss(weights, pack_item), None)
    total, _unused = lax.scan(jax.checkpoint(pack_step), jnp.zeros((), jnp.float32), pack_items)
    return total

def adam(master, first_moment, second_moment, gradient, clip_scale, rate, decay_rate):
    gradient = gradient * clip_scale
    first_new = BETA_ONE * first_moment + (1 - BETA_ONE) * gradient
    second_new = BETA_TWO * second_moment + (1 - BETA_TWO) * gradient * gradient
    update = first_new / (1 - BETA_ONE ** STEP) / (jnp.sqrt(second_new / (1 - BETA_TWO ** STEP)) + ADAM_EPS)
    return (master - rate * (update + decay_rate * master), first_new, second_new)

def reference(pixels, coords, lengths, labels, patch_table, patch_first, patch_second, position_table, position_first, position_second, attend_in, attend_in_first, attend_in_second, attend_out, attend_out_first, attend_out_second, expand, expand_first, expand_second, shrink, shrink_first, shrink_second, classify, classify_first, classify_second, vectors, vectors_first, vectors_second, head_gains, head_gains_first, head_gains_second):
    params = (patch_table, position_table, attend_in, attend_out, expand, shrink, classify, vectors, head_gains)
    pixel_values = pixels.astype(jnp.float32)
    loss_value, pull = jax.vjp(lambda *entries: forward(entries, pixel_values, coords, lengths, labels), *params)
    grads = pull(jnp.ones_like(loss_value) / IMAGES)
    grad_norm = jnp.sqrt(sum((jnp.sum(entry * entry) for entry in grads)))
    clip_scale = CLIP / jnp.maximum(grad_norm, CLIP)
    firsts = (patch_first, position_first, attend_in_first, attend_out_first, expand_first, shrink_first, classify_first, vectors_first, head_gains_first)
    seconds = (patch_second, position_second, attend_in_second, attend_out_second, expand_second, shrink_second, classify_second, vectors_second, head_gains_second)
    results = [adam(params[slot], firsts[slot], seconds[slot], grads[slot], clip_scale, RATES[slot], DECAY if slot < 7 else 0.0) for slot in range(9)]
    return (results[0][0], results[0][1], results[0][2], results[1][0], results[1][1], results[1][2], results[2][0], results[2][1], results[2][2], results[3][0], results[3][1], results[3][2], results[4][0], results[4][1], results[4][2], results[5][0], results[5][1], results[5][2], results[6][0], results[6][1], results[6][2], results[7][0], results[7][1], results[7][2], results[8][0], results[8][1], results[8][2], loss_value, grad_norm)
```

```python
import functools

import jax
import jax.numpy as jnp
from jax import lax
from jax.experimental import pallas as pl
from jax.experimental.pallas import tpu as pltpu
from jax.sharding import PartitionSpec as P

STEP = 10
NORM_EPS = 1e-06
CLIP = 0.05
RATE_BASE = 0.03
RATE_POSITION = 0.2
RATE_MIDDLE = 0.1
RATE_VECTOR = 1.0
DECAY = 0.05
BETA_ONE = 0.5
BETA_TWO = 0.5
ADAM_EPS = 1e-08
SHIFT = -4.0
NEGATIVE = -1e30
APART = 128.0
LOW = jnp.bfloat16
F32 = jnp.float32
VMEM_BYTES = 56 * 1024 * 1024
TAIL_P = 0.3
TAIL = (
    0.1196293,
    0.12075397,
    0.09991341,
    0.12856192,
    -0.05368424,
    0.20635419,
    -0.1572035,
    0.03567488,
)


def mm(left, right):
    return lax.dot_general(left, right, (((1,), (0,)), ((), ())), preferred_element_type=F32)


def mm_nt(left, right):
    return lax.dot_general(left, right, (((1,), (1,)), ((), ())), preferred_element_type=F32)


def split_two(values):
    high = values.astype(LOW)
    return high, (values - high.astype(F32)).astype(LOW)


def split_three(values):
    high = values.astype(LOW)
    rest = values - high.astype(F32)
    middle = rest.astype(LOW)
    return high, middle, (rest - middle.astype(F32)).astype(LOW)


def row_norm(values):
    center = values - jnp.mean(values, axis=-1, keepdims=True)
    inverse = lax.rsqrt(jnp.mean(center * center, axis=-1, keepdims=True) + NORM_EPS)
    return center * inverse, inverse


def row_norm_back(gradient, gain_row, normed, inverse):
    scaled = gradient * gain_row
    return inverse * (
        scaled
        - jnp.mean(scaled, axis=-1, keepdims=True)
        - normed * jnp.mean(scaled * normed, axis=-1, keepdims=True)
    )


def half_mean_matrix(scale):
    row = lax.broadcasted_iota(jnp.int32, (128, 128), 0)
    col = lax.broadcasted_iota(jnp.int32, (128, 128), 1)
    return jnp.where((row >= 64) == (col >= 64), scale, 0.0).astype(LOW)


def half_sum(values, block):
    high, low = split_two(values)
    return mm(high, block) + mm(low, block)


def half_norm(values, block):
    center = values - half_sum(values, block)
    inverse = lax.rsqrt(half_sum(center * center, block) + NORM_EPS)
    return center * inverse, inverse


def half_norm_back(gradient, gain_row, normed, inverse, block):
    scaled = gradient * gain_row
    return inverse * (scaled - half_sum(scaled, block) - normed * half_sum(scaled * normed, block))


def gelu_pair(inner):
    size = jnp.abs(inner)
    near = 1.0 / (1.0 + TAIL_P * size)
    bell = jnp.exp(-0.5 * inner * inner)
    poly = TAIL[-1]
    for factor in TAIL[-2::-1]:
        poly = poly * near + factor
    tail = poly * near * bell
    share = jnp.where(inner >= 0, 1.0 - tail, tail)
    return inner * share, share + inner * bell * 0.3989422804014327


def embed_kernel(pack_ref, pix_ref, coord_ref, wp_ref, win_ref, gain_ref, emb_ref, h1_ref, q_ref, k_ref, v_ref):
    rows = pix_ref.shape[0]
    pixels = pix_ref.shape[1]
    groups = win_ref.shape[0]
    part = win_ref.shape[2] // 3
    spots = (wp_ref.shape[1] - pixels) // 2
    lane = lax.broadcasted_iota(jnp.int32, (rows, 2 * spots), 1)
    hot = ((lane == coord_ref[:, 0:1]) | (lane - spots == coord_ref[:, 1:2])).astype(F32).astype(LOW)
    embedded = mm_nt(pix_ref[...], wp_ref[:, :pixels]) + mm_nt(hot, wp_ref[:, pixels:])
    emb_ref[...] = embedded
    normed, _ = row_norm(embedded)
    first = (normed * gain_ref[0:1]).astype(LOW)
    h1_ref[...] = first
    parts = [mm(first, win_ref[group]) for group in range(groups)]
    q_ref[...] = jnp.concatenate([entry[:, :part] for entry in parts], axis=1)
    k_ref[...] = jnp.concatenate([entry[:, part : 2 * part] for entry in parts], axis=1)
    v_ref[...] = jnp.concatenate([entry[:, 2 * part :].astype(LOW) for entry in parts], axis=1)


def embed_call(pack, pixels, coords, w_pp, w_in, vectors, rows):
    width = vectors.shape[1]
    tile = 256
    steps = rows // tile
    whole2 = lambda i, p: (0, 0)
    tiled = pl.BlockSpec((tile, width), lambda i, p: (i, 0))
    return pl.pallas_call(
        embed_kernel,
        grid_spec=pltpu.PrefetchScalarGridSpec(
            num_scalar_prefetch=1,
            grid=(steps,),
            in_specs=[
                pl.BlockSpec((tile, pixels.shape[1]), lambda i, p: (p[0] * steps + i, 0)),
                pl.BlockSpec((tile, 2), lambda i, p: (p[0] * steps + i, 0)),
                pl.BlockSpec(w_pp.shape, whole2),
                pl.BlockSpec(w_in.shape, lambda i, p: (0, 0, 0)),
                pl.BlockSpec(vectors.shape, whole2),
            ],
            out_specs=[tiled] * 5,
        ),
        out_shape=[
            jax.ShapeDtypeStruct((rows, width), F32),
            jax.ShapeDtypeStruct((rows, width), LOW),
            jax.ShapeDtypeStruct((rows, width), F32),
            jax.ShapeDtypeStruct((rows, width), F32),
            jax.ShapeDtypeStruct((rows, width), LOW),
        ],
        compiler_params=pltpu.CompilerParams(vmem_limit_bytes=VMEM_BYTES),
        name="embed",
    )(pack, pixels, coords, w_pp, w_in, vectors)


def image_marks(bound_ref, rows):
    place = lax.broadcasted_iota(jnp.int32, (rows, 128), 0)
    return (place >= bound_ref[0:1, :]) & (place < bound_ref[1:2, :])


def half_lane(rows):
    lane = lax.broadcasted_iota(jnp.int32, (rows, 128), 1)
    return lane, jnp.where(lane >= 64, lane - 64, lane)


def attend_kernel(q_ref, k_ref, v_ref, gain_ref, bound_ref, o_ref, lse_ref, ka_ref, va_ref, qa_ref):
    rows = q_ref.shape[0]
    tile = 256
    block = half_mean_matrix(1.0 / 64)
    lane, inner = half_lane(rows)
    marks = image_marks(bound_ref, rows)
    one = jnp.where(inner == 8, 1.0, 0.0)
    query_feature = jnp.where(marks, 1.0, one)
    key_feature = jnp.where(marks, APART, -APART * one)
    k_normed, _ = half_norm(k_ref[...], block)
    ka_ref[:, :128] = (k_normed * gain_ref[1:2]).astype(LOW)
    ka_ref[:, 128:] = key_feature.astype(LOW)
    va_ref[:, :128] = v_ref[...]
    va_ref[:, 128:] = jnp.ones((rows, 128), LOW)
    q_normed, _ = half_norm(q_ref[...], block)
    query = (q_normed * gain_ref[0:1]).astype(LOW).astype(F32) * 0.125
    for head in range(2):
        mine = (lane < 64) if head == 0 else (lane >= 64)
        qa_ref[head, :, :128] = jnp.where(mine, query, 0.0).astype(LOW)
        qa_ref[head, :, 128:] = jnp.where(mine, query_feature, 0.0).astype(LOW)
    keys = ka_ref[...]
    values = va_ref[...]
    first = lane[:tile] < 64
    for step in range(rows // tile):
        part = slice(step * tile, (step + 1) * tile)
        outs = []
        for head in range(2):
            score = mm_nt(qa_ref[head, part, :], keys)
            outs.append(mm(jnp.exp(score).astype(LOW), values))
        total = jnp.where(first, outs[0][:, 128:], outs[1][:, 128:])
        o_ref[part, :] = (jnp.where(first, outs[0][:, :128], outs[1][:, :128]) / total).astype(LOW)
        lse_ref[part, :] = jnp.log(total)


def attend_call(q_raw, k_raw, value, gains, bounds):
    rows, width = q_raw.shape
    pair = pl.BlockSpec((rows, 128), lambda j: (0, j))
    small = lambda a: pl.BlockSpec(a.shape, lambda j: (0, 0))
    return pl.pallas_call(
        attend_kernel,
        grid=(width // 128,),
        in_specs=[pair, pair, pair, small(gains), small(bounds)],
        out_specs=[pair, pair],
        out_shape=[
            jax.ShapeDtypeStruct((rows, width), LOW),
            jax.ShapeDtypeStruct((rows, width), F32),
        ],
        scratch_shapes=[
            pltpu.VMEM((rows, 256), LOW),
            pltpu.VMEM((rows, 256), LOW),
            pltpu.VMEM((2, rows, 256), LOW),
        ],
        compiler_params=pltpu.CompilerParams(vmem_limit_bytes=VMEM_BYTES),
        name="attend",
    )(q_raw, k_raw, value, gains, bounds)


def attend_back_kernel(
    q_ref, k_ref, v_ref, o_ref, lse_ref, do_ref, gain_ref, bound_ref,
    dq_ref, dk_ref, dv_ref, dgain_ref,
    ka_ref, va_ref, qa_ref, da_ref, qt_ref, dot_ref, dqs_ref, dkt_ref, dvt_ref,
):
    rows = q_ref.shape[0]
    tile = 256
    block = half_mean_matrix(1.0 / 64)
    block_sum = half_mean_matrix(1.0)
    lane, inner = half_lane(rows)
    marks = image_marks(bound_ref, rows)
    one = jnp.where(inner == 8, 1.0, 0.0)
    three = (inner >= 9) & (inner < 12)
    key_feature = jnp.where(marks, APART, jnp.where(three, 1.0, -APART * one))

    def spread(values):
        high, middle, low = split_three(values)
        return jnp.where(
            inner == 9, high.astype(F32), jnp.where(inner == 10, middle.astype(F32), low.astype(F32))
        )

    query_feature = jnp.where(three, spread(-lse_ref[...]), jnp.where(marks, 1.0, one))
    k_normed, k_inverse = half_norm(k_ref[...], block)
    ka_ref[:, :128] = (k_normed * gain_ref[1:2]).astype(LOW)
    ka_ref[:, 128:] = key_feature.astype(LOW)
    va_ref[:, :128] = v_ref[...]
    va_ref[:, 128:] = jnp.where(three, 1.0, 0.0).astype(LOW)
    q_normed, q_inverse = half_norm(q_ref[...], block)
    query = (q_normed * gain_ref[0:1]).astype(LOW).astype(F32)
    qt_ref[...] = jnp.transpose(query).astype(LOW)
    query = query * 0.125
    above = do_ref[...].astype(F32)
    dot_ref[...] = jnp.transpose(above).astype(LOW)
    inside = half_sum(above * o_ref[...].astype(F32), block_sum)
    above_feature = jnp.where(three, spread(inside * -0.125), 0.0)
    above = above * 0.125
    for head in range(2):
        mine = (lane < 64) if head == 0 else (lane >= 64)
        qa_ref[head, :, :128] = jnp.where(mine, query, 0.0).astype(LOW)
        qa_ref[head, :, 128:] = jnp.where(mine, query_feature, 0.0).astype(LOW)
        da_ref[head, :, :128] = jnp.where(mine, above, 0.0).astype(LOW)
        da_ref[head, :, 128:] = jnp.where(mine, above_feature, 0.0).astype(LOW)
    keys = ka_ref[...]
    values = va_ref[...]
    key_low = ka_ref[:, :128]
    first = lane[:tile] < 64
    for step in range(rows // tile):
        part = slice(step * tile, (step + 1) * tile)
        outs = []
        for head in range(2):
            mine = slice(64 * head, 64 * head + 64)
            prob = jnp.exp(mm_nt(qa_ref[head, part, :], keys))
            d_prob = mm_nt(da_ref[head, part, :], values)
            d_score = (prob * d_prob).astype(LOW)
            outs.append(mm(d_score, key_low))
            d_key = mm(qt_ref[mine, part], d_score)
            d_value = mm(dot_ref[mine, part], prob.astype(LOW))
            if step == 0:
                dkt_ref[mine, :] = d_key
                dvt_ref[mine, :] = d_value
            else:
                dkt_ref[mine, :] += d_key
                dvt_ref[mine, :] += d_value
        dqs_ref[part, :] = jnp.where(first, outs[0], outs[1])
    d_query = dqs_ref[...]
    d_key = jnp.transpose(dkt_ref[...])
    dv_ref[...] = jnp.transpose(dvt_ref[...]).astype(LOW)
    dq_ref[...] = half_norm_back(d_query, gain_ref[0:1], q_normed, q_inverse, block).astype(LOW)
    dk_ref[...] = half_norm_back(d_key, gain_ref[1:2], k_normed, k_inverse, block).astype(LOW)
    dgain_ref[0, 0:1] = jnp.sum(d_query * q_normed, axis=0, keepdims=True)
    dgain_ref[0, 1:2] = jnp.sum(d_key * k_normed, axis=0, keepdims=True)


def attend_back_call(q_raw, k_raw, value, attended, lse, d_attended, gains, bounds):
    rows, width = q_raw.shape
    pairs = width // 128
    pair = pl.BlockSpec((rows, 128), lambda j: (0, j))
    small = lambda a: pl.BlockSpec(a.shape, lambda j: (0, 0))
    low = jax.ShapeDtypeStruct((rows, width), LOW)
    return pl.pallas_call(
        attend_back_kernel,
        grid=(pairs,),
        in_specs=[pair] * 6 + [small(gains), small(bounds)],
        out_specs=[pair, pair, pair, pl.BlockSpec((1, 2, 128), lambda j: (j, 0, 0))],
        out_shape=[low, low, low, jax.ShapeDtypeStruct((pairs, 2, 128), F32)],
        scratch_shapes=[
            pltpu.VMEM((rows, 256), LOW),
            pltpu.VMEM((rows, 256), LOW),
            pltpu.VMEM((2, rows, 256), LOW),
            pltpu.VMEM((2, rows, 256), LOW),
            pltpu.VMEM((128, rows), LOW),
            pltpu.VMEM((128, rows), LOW),
            pltpu.VMEM((rows, 128), F32),
            pltpu.VMEM((128, rows), F32),
            pltpu.VMEM((128, rows), F32),
        ],
        compiler_params=pltpu.CompilerParams(vmem_limit_bytes=VMEM_BYTES),
        name="attend_back",
    )(q_raw, k_raw, value, attended, lse, d_attended, gains, bounds)


def mlp_kernel(o_ref, emb_ref, wout_ref, wup_ref, wdn_ref, vec_ref, x1_ref, h2_ref, act_ref, slope_ref, x2_ref):
    step = pl.program_id(0)
    rows, _ = o_ref.shape
    groups, _, part = wout_ref.shape
    tile = 256

    @pl.when(step == 0)
    def _():
        for at in range(rows // tile):
            span = slice(at * tile, (at + 1) * tile)
            branch = mm_nt(o_ref[span, :part], wout_ref[0])
            for group in range(1, groups):
                branch += mm_nt(o_ref[span, group * part : (group + 1) * part], wout_ref[group])
            middle = emb_ref[span, :] + branch
            x1_ref[span, :] = middle
            x2_ref[span, :] = middle
            normed, _ = row_norm(middle)
            h2_ref[span, :] = (normed * vec_ref[1:2]).astype(LOW)

    for at in range(rows // tile):
        span = slice(at * tile, (at + 1) * tile)
        active, slope = gelu_pair(mm(h2_ref[span, :], wup_ref[0]))
        active = active.astype(LOW)
        act_ref[span, :] = active
        slope_ref[span, :] = slope.astype(LOW)
        x2_ref[span, :] += mm_nt(active, wdn_ref[0])


def mlp_call(attended, embedded, w_out, w_up, w_dn, vectors):
    rows, width = embedded.shape
    groups, _, per = w_up.shape
    chunk = per // 2
    hidden = groups * per
    whole = lambda a: pl.BlockSpec(a.shape, lambda j: (0,) * a.ndim)
    weight = pl.BlockSpec((1, width, chunk), lambda j: (j // 2, 0, j % 2))
    full = pl.BlockSpec((rows, width), lambda j: (0, 0))
    piece = pl.BlockSpec((rows, chunk), lambda j: (0, j))
    return pl.pallas_call(
        mlp_kernel,
        grid=(hidden // chunk,),
        in_specs=[whole(attended), whole(embedded), whole(w_out), weight, weight, whole(vectors)],
        out_specs=[full, full, piece, piece, full],
        out_shape=[
            jax.ShapeDtypeStruct((rows, width), F32),
            jax.ShapeDtypeStruct((rows, width), LOW),
            jax.ShapeDtypeStruct((rows, hidden), LOW),
            jax.ShapeDtypeStruct((rows, hidden), LOW),
            jax.ShapeDtypeStruct((rows, width), F32),
        ],
        compiler_params=pltpu.CompilerParams(vmem_limit_bytes=VMEM_BYTES),
        name="mlp",
    )(attended, embedded, w_out, w_up, w_dn, vectors)


def pool_kernel(
    pack_ref, x2_ref, label_ref, wcls_ref, vec_ref, bound_ref, valid_ref,
    dx2_ref, dcls_ref, loss_ref, dvec_ref,
    norm_ref, inv_ref,
    *, images, image_count,
):
    rows, width = x2_ref.shape
    tile = 256
    root = width**0.5
    gain = vec_ref[2:3]
    query = vec_ref[3:4]
    lane = lax.broadcasted_iota(jnp.int32, (rows, 128), 1)
    marks = image_marks(bound_ref, rows) & (lane < 64)
    logits = []
    for at in range(rows // tile):
        span = slice(at * tile, (at + 1) * tile)
        normed, inverse = row_norm(x2_ref[span, :])
        norm_ref[span, :] = normed
        inv_ref[span, :] = jnp.broadcast_to(inverse, (tile, 128))
        logits.append(jnp.sum(normed * gain * query, axis=-1, keepdims=True) / root)
    logit = jnp.concatenate(logits, axis=0)
    masked = jnp.where(marks, logit, NEGATIVE)
    grown = jnp.exp(masked - jnp.max(masked, axis=0, keepdims=True))
    shares = jnp.where(marks, grown / jnp.sum(grown, axis=0, keepdims=True), 0.0)
    weight = jnp.sum(shares, axis=-1, keepdims=True)
    member = jnp.transpose(marks.astype(F32))[:16].astype(LOW)
    pooled = jnp.zeros((16, width), F32)
    for at in range(rows // tile):
        span = slice(at * tile, (at + 1) * tile)
        for entry in split_three(norm_ref[span, :] * gain * weight[span]):
            pooled += mm(member[:, span], entry)
    pooled_low = pooled.astype(LOW)
    scores = mm(pooled_low, wcls_ref[...])[:images] + SHIFT
    target = label_ref[...].astype(F32)
    valid = valid_ref[0, 0]
    soft = jnp.maximum(scores, 0.0) + jnp.log1p(jnp.exp(-jnp.abs(scores)))
    loss_rows = jnp.sum(soft - target * scores, axis=-1, keepdims=True)
    loss_ref[...] = jnp.broadcast_to(jnp.sum(loss_rows, axis=0, keepdims=True) * valid, loss_ref.shape)
    d_score = (1.0 / (1.0 + jnp.exp(-scores)) - target) / image_count * valid
    d_score = jnp.concatenate([d_score, jnp.zeros((16 - images, d_score.shape[1]), F32)], axis=0).astype(LOW)
    dcls_ref[...] = mm(jnp.transpose(pooled).astype(LOW), d_score).astype(LOW)
    d_pooled = mm_nt(d_score, wcls_ref[...])[:images]
    parts = jnp.concatenate(
        [entry.astype(F32) for entry in split_three(d_pooled)]
        + [jnp.zeros((128 - 3 * images, width), F32)],
        axis=0,
    ).astype(LOW)
    marks_f = marks.astype(F32)
    thrice = (
        marks_f + pltpu.roll(marks_f, images, 1) + pltpu.roll(marks_f, 2 * images, 1)
    ).astype(LOW)
    d_weights = []
    for at in range(rows // tile):
        span = slice(at * tile, (at + 1) * tile)
        spread = mm(thrice[span], parts)
        dx2_ref[span, :] = spread
        d_weights.append(jnp.sum(spread * (norm_ref[span, :] * gain), axis=-1, keepdims=True))
    d_weight = jnp.concatenate(d_weights, axis=0)
    inside = jnp.sum(shares * d_weight, axis=0, keepdims=True)
    d_logit = weight * (d_weight - jnp.sum(marks_f * inside, axis=-1, keepdims=True))
    gain_sum = jnp.zeros((1, width), F32)
    query_sum = jnp.zeros((1, width), F32)
    for at in range(rows // tile):
        span = slice(at * tile, (at + 1) * tile)
        normed = norm_ref[span, :]
        inverse = inv_ref[span, 0:1]
        d_last = dx2_ref[span, :] * weight[span] + d_logit[span] * (query / root)
        gain_sum += jnp.sum(d_last * normed, axis=0, keepdims=True)
        query_sum += jnp.sum(d_logit[span] * normed, axis=0, keepdims=True)
        dx2_ref[span, :] = row_norm_back(d_last, gain, normed, inverse)
    dvec_ref[0:1, :] = gain_sum
    dvec_ref[1:2, :] = query_sum * gain / root


def pool_call(pack, x2, labels, w_cls, vectors, bounds, valid, images, image_count):
    rows, width = x2.shape
    classes = labels.shape[1]
    whole = lambda a: pl.BlockSpec(a.shape, lambda j, p: (0,) * a.ndim)
    full = lambda *shape: pl.BlockSpec(shape, lambda j, p: (0,) * len(shape))
    return pl.pallas_call(
        functools.partial(pool_kernel, images=images, image_count=image_count),
        grid_spec=pltpu.PrefetchScalarGridSpec(
            num_scalar_prefetch=1,
            grid=(1,),
            in_specs=[
                whole(x2),
                pl.BlockSpec((images, classes), lambda j, p: (p[0], 0)),
                whole(w_cls),
                whole(vectors),
                whole(bounds),
                pl.BlockSpec(memory_space=pltpu.SMEM),
            ],
            out_specs=[full(rows, width), full(width, classes), full(8, 128), full(2, width)],
            scratch_shapes=[pltpu.VMEM((rows, width), F32), pltpu.VMEM((rows, 128), F32)],
        ),
        out_shape=[
            jax.ShapeDtypeStruct((rows, width), F32),
            jax.ShapeDtypeStruct((width, classes), LOW),
            jax.ShapeDtypeStruct((8, 128), F32),
            jax.ShapeDtypeStruct((2, width), F32),
        ],
        compiler_params=pltpu.CompilerParams(vmem_limit_bytes=VMEM_BYTES),
        name="pool",
    )(pack, x2, labels, w_cls, vectors, bounds, valid)


def mlp_back_kernel(
    dx2_ref, act_ref, slope_ref, h2_ref, x1_ref, o_ref, wout_ref, wup_ref, wdn_ref, vec_ref,
    ddn_ref, dup_ref, dout_ref, do_ref, dmid_ref, dvec_ref,
    low_ref, lowt_ref, h2t_ref, acc_ref, dh_ref,
):
    step = pl.program_id(0)
    rows, width = dx2_ref.shape
    groups, _, part = wout_ref.shape
    tile = 256

    @pl.when(step == 0)
    def _():
        for at in range(rows // tile):
            span = slice(at * tile, (at + 1) * tile)
            values = dx2_ref[span, :]
            low_ref[span, :] = values.astype(LOW)
            lowt_ref[:, span] = jnp.transpose(values).astype(LOW)
            h2t_ref[:, span] = jnp.transpose(h2_ref[span, :].astype(F32)).astype(LOW)
            acc_ref[span, :] = jnp.zeros((tile, width), F32)

    for at in range(rows // tile):
        span = slice(at * tile, (at + 1) * tile)
        d_hidden = (mm(low_ref[span, :], wdn_ref[0]) * slope_ref[span, :].astype(F32)).astype(LOW)
        dh_ref[span, :] = d_hidden
        acc_ref[span, :] += mm_nt(d_hidden, wup_ref[0])
    for at in range(width // tile):
        span = slice(at * tile, (at + 1) * tile)
        ddn_ref[0, span, :] = mm(lowt_ref[span, :], act_ref[...]).astype(LOW)
        dup_ref[0, span, :] = mm(h2t_ref[span, :], dh_ref[...]).astype(LOW)

    @pl.when(step == pl.num_programs(0) - 1)
    def _():
        gain = vec_ref[1:2]
        gain_sum = jnp.zeros((1, width), F32)
        for at in range(rows // tile):
            span = slice(at * tile, (at + 1) * tile)
            normed, inverse = row_norm(x1_ref[span, :])
            d_second = acc_ref[span, :]
            gain_sum += jnp.sum(d_second * normed, axis=0, keepdims=True)
            d_middle = dx2_ref[span, :] + row_norm_back(d_second, gain, normed, inverse)
            dmid_ref[span, :] = d_middle
            low = d_middle.astype(LOW)
            lowt_ref[:, span] = jnp.transpose(d_middle).astype(LOW)
            do_ref[span, :] = jnp.concatenate(
                [mm(low, wout_ref[group]) for group in range(groups)], axis=1
            ).astype(LOW)
        dvec_ref[...] = gain_sum
        for group in range(groups):
            piece = o_ref[:, group * part : (group + 1) * part]
            for at in range(width // tile):
                span = slice(at * tile, (at + 1) * tile)
                dout_ref[group, span, :] = mm(lowt_ref[span, :], piece).astype(LOW)


def mlp_back_call(dx2, active, slope, h2, x1, attended, w_out, w_up, w_dn, vectors):
    rows, width = dx2.shape
    groups, _, per = w_up.shape
    chunk = per // 2
    hidden = groups * per
    whole = lambda a: pl.BlockSpec(a.shape, lambda j: (0,) * a.ndim, pipeline_mode=pl.Buffered(1))
    weight = pl.BlockSpec((1, width, chunk), lambda j: (j // 2, 0, j % 2))
    piece = pl.BlockSpec((rows, chunk), lambda j: (0, j))
    full = lambda *shape: pl.BlockSpec(shape, lambda j: (0,) * len(shape))
    return pl.pallas_call(
        mlp_back_kernel,
        grid=(hidden // chunk,),
        in_specs=[
            whole(dx2), piece, piece, whole(h2), whole(x1), whole(attended), whole(w_out),
            weight, weight, whole(vectors),
        ],
        out_specs=[weight, weight, full(*w_out.shape), full(rows, width), full(rows, width), full(1, width)],
        out_shape=[
            jax.ShapeDtypeStruct(w_dn.shape, LOW),
            jax.ShapeDtypeStruct(w_up.shape, LOW),
            jax.ShapeDtypeStruct(w_out.shape, LOW),
            jax.ShapeDtypeStruct((rows, width), LOW),
            jax.ShapeDtypeStruct((rows, width), F32),
            jax.ShapeDtypeStruct((1, width), F32),
        ],
        scratch_shapes=[
            pltpu.VMEM((rows, width), LOW),
            pltpu.VMEM((width, rows), LOW),
            pltpu.VMEM((width, rows), LOW),
            pltpu.VMEM((rows, width), F32),
            pltpu.VMEM((rows, chunk), LOW),
        ],
        compiler_params=pltpu.CompilerParams(vmem_limit_bytes=VMEM_BYTES),
        name="mlp_back",
    )(dx2, active, slope, h2, x1, attended, w_out, w_up, w_dn, vectors)


def embed_back_kernel(
    pack_ref, dq_ref, dk_ref, dv_ref, h1_ref, emb_ref, dmid_ref, pix_ref, coord_ref, win_ref, vec_ref,
    din_ref, dpp_ref, dvec_ref,
    h1t_ref, join_ref, acc_ref,
):
    step = pl.program_id(0)
    rows, width = h1_ref.shape
    groups = pl.num_programs(0)
    part = win_ref.shape[2] // 3
    tile = 256

    @pl.when(step == 0)
    def _():
        for at in range(rows // tile):
            span = slice(at * tile, (at + 1) * tile)
            h1t_ref[:, span] = jnp.transpose(h1_ref[span, :].astype(F32)).astype(LOW)
            acc_ref[span, :] = jnp.zeros((tile, width), F32)

    for group in range(width // part):

        @pl.when(step == group)
        def _():
            mine = slice(group * part, (group + 1) * part)
            join_ref[...] = jnp.concatenate([dq_ref[:, mine], dk_ref[:, mine], dv_ref[:, mine]], axis=1)

    for at in range(rows // tile):
        span = slice(at * tile, (at + 1) * tile)
        acc_ref[span, :] += mm_nt(join_ref[span, :], win_ref[0])
    for at in range(width // tile):
        span = slice(at * tile, (at + 1) * tile)
        din_ref[0, span, :] = mm(h1t_ref[span, :], join_ref[...]).astype(LOW)

    @pl.when(step == groups - 1)
    def _():
        gain = vec_ref[0:1]
        pixels = pix_ref.shape[1]
        spots = (dpp_ref.shape[1] - pixels) // 2
        gain_sum = jnp.zeros((1, width), F32)
        for at in range(rows // tile):
            span = slice(at * tile, (at + 1) * tile)
            normed, inverse = row_norm(emb_ref[span, :])
            d_first = acc_ref[span, :]
            gain_sum += jnp.sum(d_first * normed, axis=0, keepdims=True)
            d_embed = dmid_ref[span, :] + row_norm_back(d_first, gain, normed, inverse)
            h1t_ref[:, span] = jnp.transpose(d_embed).astype(LOW)
        dvec_ref[...] = gain_sum
        lane = lax.broadcasted_iota(jnp.int32, (rows, 2 * spots), 1)
        hot = ((lane == coord_ref[:, 0:1]) | (lane - spots == coord_ref[:, 1:2])).astype(F32).astype(LOW)
        for at in range(width // tile):
            span = slice(at * tile, (at + 1) * tile)
            dpp_ref[span, :pixels] = mm(h1t_ref[span, :], pix_ref[...]).astype(LOW)
            dpp_ref[span, pixels:] = mm(h1t_ref[span, :], hot).astype(LOW)


def embed_back_call(pack, dq, dk, dv, h1, embedded, d_middle, pixels, coords, w_in, w_pp_shape, vectors):
    rows, width = h1.shape
    groups = w_in.shape[0]
    whole = lambda a: pl.BlockSpec(a.shape, lambda j, p: (0,) * a.ndim, pipeline_mode=pl.Buffered(1))
    full = lambda *shape: pl.BlockSpec(shape, lambda j, p: (0,) * len(shape))
    weight = pl.BlockSpec((1,) + w_in.shape[1:], lambda j, p: (j, 0, 0))
    return pl.pallas_call(
        embed_back_kernel,
        grid_spec=pltpu.PrefetchScalarGridSpec(
            num_scalar_prefetch=1,
            grid=(groups,),
            in_specs=[
                whole(dq), whole(dk), whole(dv), whole(h1), whole(embedded), whole(d_middle),
                pl.BlockSpec((rows, pixels.shape[1]), lambda j, p: (p[0], 0)),
                pl.BlockSpec((rows, 2), lambda j, p: (p[0], 0)),
                weight,
                whole(vectors),
            ],
            out_specs=[weight, full(*w_pp_shape), full(1, width)],
            scratch_shapes=[
                pltpu.VMEM((width, rows), LOW),
                pltpu.VMEM((rows, w_in.shape[2]), LOW),
                pltpu.VMEM((rows, width), F32),
            ],
        ),
        out_shape=[
            jax.ShapeDtypeStruct(w_in.shape, LOW),
            jax.ShapeDtypeStruct(w_pp_shape, LOW),
            jax.ShapeDtypeStruct((1, width), F32),
        ],
        compiler_params=pltpu.CompilerParams(vmem_limit_bytes=VMEM_BYTES),
        name="embed_back",
    )(pack, dq, dk, dv, h1, embedded, d_middle, pixels, coords, w_in, vectors)


def pack_step(pack, valid, pixels, coords, lengths, labels, weights, vectors, head_gains, image_count):
    w_pp, w_in, w_out, w_up, w_dn, w_cls = weights
    packs, images = lengths.shape
    rows = pixels.shape[0] // packs
    mine = lax.dynamic_index_in_dim(lengths, pack[0], 0, keepdims=False)
    ends = jnp.cumsum(mine)
    fill = jnp.full((64 - images,), 1 << 30, jnp.int32)
    starts = jnp.concatenate([ends - mine, fill])
    ends = jnp.concatenate([ends, fill])
    bounds = jnp.stack([jnp.tile(starts, 2), jnp.tile(ends, 2)])
    gains = jnp.tile(head_gains, (1, 2))
    places = coords.T
    embedded, h1, q_raw, k_raw, value = embed_call(pack, pixels, places, w_pp, w_in, vectors, rows)
    attended, lse = attend_call(q_raw, k_raw, value, gains, bounds)
    x1, h2, active, slope, x2 = mlp_call(attended, embedded, w_out, w_up, w_dn, vectors)
    dx2, d_cls, loss, dvec_pool = pool_call(
        pack, x2, labels, w_cls, vectors, bounds, valid, images, image_count
    )
    d_dn, d_up, d_out, d_attended, d_middle, dvec_two = mlp_back_call(
        dx2, active, slope, h2, x1, attended, w_out, w_up, w_dn, vectors
    )
    dq, dk, dv, d_gain = attend_back_call(q_raw, k_raw, value, attended, lse, d_attended, gains, bounds)
    d_in, d_pp, dvec_one = embed_back_call(
        pack, dq, dk, dv, h1, embedded, d_middle, pixels, places, w_in, w_pp.shape, vectors
    )
    d_vectors = jnp.concatenate([dvec_one, dvec_two, dvec_pool], axis=0)
    d_gains = jnp.sum(d_gain.reshape(-1, 2, 2, 64), axis=(0, 2))
    return (d_pp, d_in, d_out, d_up, d_dn, d_cls), d_vectors, d_gains, loss[0, 0]


def adam(master, first_moment, second_moment, gradient, clip_scale, rate, decay_rate):
    gradient = gradient * clip_scale
    first_new = BETA_ONE * first_moment + (1 - BETA_ONE) * gradient
    second_new = BETA_TWO * second_moment + (1 - BETA_TWO) * gradient * gradient
    update = (
        first_new / (1 - BETA_ONE**STEP) / (jnp.sqrt(second_new / (1 - BETA_TWO**STEP)) + ADAM_EPS)
    )
    return (master - rate * (update + decay_rate * master), first_new, second_new)


def squared(entry):
    return jnp.sum(entry * entry)


def per_device(
    pixels, coords, lengths, labels,
    patch_table, patch_first, patch_second,
    position_table, position_first, position_second,
    attend_in, attend_in_first, attend_in_second,
    attend_out, attend_out_first, attend_out_second,
    expand, expand_first, expand_second,
    shrink, shrink_first, shrink_second,
    classify, classify_first, classify_second,
    vectors, vectors_first, vectors_second,
    head_gains, head_gains_first, head_gains_second,
):
    packs, images = lengths.shape
    members = lax.axis_size("tensor")
    width = vectors.shape[1]
    share = attend_in.shape[0]
    seat = lax.axis_index("tensor")
    pack = jnp.minimum(seat, packs - 1).astype(jnp.int32)[None]
    valid = (seat < packs).astype(F32).reshape(1, 1)
    image_count = images * packs * lax.axis_size("dp")
    shards = (
        jnp.concatenate(
            [patch_table.T, jnp.transpose(position_table, (2, 0, 1)).reshape(share, -1)], axis=1
        ).astype(LOW),
        attend_in.reshape(share, -1).astype(LOW),
        attend_out.T.astype(LOW),
        expand.astype(LOW),
        shrink.T.astype(LOW),
        classify.astype(LOW),
    )
    both = ("tensor", "dp")

    def gather(shard):
        return lax.all_gather(shard, both, axis=0, tiled=True).reshape(members, width, -1)

    weights = (
        lax.all_gather(shards[0], "dp", axis=0, tiled=True),
        gather(shards[1]),
        gather(shards[2]),
        gather(shards[3]),
        gather(shards[4]),
        lax.all_gather(shards[5], "dp", axis=0, tiled=True),
    )
    grads, grad_vectors, grad_gains, loss_local = pack_step(
        pack, valid, pixels, coords, lengths, labels, weights, vectors, head_gains, image_count
    )
    grad_vectors, grad_gains, loss_total = lax.psum((grad_vectors, grad_gains, loss_local), both)

    def scatter(grad):
        return lax.psum_scatter(
            grad.reshape(members * width, -1), both, scatter_dimension=0, tiled=True
        ).astype(F32)

    def scatter_whole(grad):
        return lax.psum(lax.psum_scatter(grad, "dp", scatter_dimension=0, tiled=True), "tensor").astype(F32)

    share_pp = scatter_whole(grads[0])
    share_in, share_out, share_up, share_dn = (scatter(entry) for entry in grads[1:5])
    share_cls = scatter_whole(grads[5])
    leader = (seat == 0).astype(F32)
    split_squares = squared(share_in) + squared(share_out) + squared(share_up) + squared(share_dn)
    whole_squares = squared(share_pp) + squared(share_cls)
    squares = lax.psum(split_squares + leader * whole_squares, both)
    grad_norm = jnp.sqrt(squares + squared(grad_vectors) + squared(grad_gains))
    clip_scale = CLIP / jnp.maximum(grad_norm, CLIP)
    pixel_width = patch_table.shape[0]
    share_patch = share_pp[:, :pixel_width].T
    share_pos = jnp.transpose(
        share_pp[:, pixel_width:].reshape(share, position_table.shape[0], position_table.shape[1]), (1, 2, 0)
    )
    results = (
        adam(patch_table, patch_first, patch_second, share_patch, clip_scale, RATE_BASE, DECAY),
        adam(position_table, position_first, position_second, share_pos, clip_scale, RATE_POSITION, DECAY),
        adam(
            attend_in, attend_in_first, attend_in_second,
            share_in.reshape(attend_in.shape), clip_scale, RATE_BASE, DECAY,
        ),
        adam(attend_out, attend_out_first, attend_out_second, share_out.T, clip_scale, RATE_MIDDLE, DECAY),
        adam(expand, expand_first, expand_second, share_up, clip_scale, RATE_BASE, DECAY),
        adam(shrink, shrink_first, shrink_second, share_dn.T, clip_scale, RATE_BASE, DECAY),
        adam(classify, classify_first, classify_second, share_cls, clip_scale, RATE_MIDDLE, DECAY),
        adam(vectors, vectors_first, vectors_second, grad_vectors, clip_scale, RATE_VECTOR, 0.0),
        adam(head_gains, head_gains_first, head_gains_second, grad_gains, clip_scale, RATE_VECTOR, 0.0),
    )
    return tuple(entry for group in results for entry in group) + (loss_total, grad_norm)


def solution(mesh):
    data = P("dp", None)
    in_specs = (
        (data, P(None, "dp"), data, data)
        + (P(None, "dp"),) * 3
        + (P(None, None, "dp"),) * 3
        + (P("dp", None, "tensor"),) * 3
        + (P("tensor", "dp"),) * 3
        + (P("dp", "tensor"),) * 3
        + (P("tensor", "dp"),) * 3
        + (data,) * 3
        + (P(),) * 6
    )
    out_specs = in_specs[4:] + (P(), P())
    return jax.shard_map(per_device, mesh=mesh, in_specs=in_specs, out_specs=out_specs, check_vma=False)
```

```python
import functools

import jax
import jax.numpy as jnp
from jax import lax
from jax.experimental import pallas as pl
from jax.experimental.pallas import tpu as pltpu
from jax.sharding import PartitionSpec as P

STEP = 10
NORM_EPS = 1e-06
CLIP = 0.05
RATE_BASE = 0.03
RATE_POSITION = 0.2
RATE_MIDDLE = 0.1
RATE_VECTOR = 1.0
DECAY = 0.05
BETA_ONE = 0.5
BETA_TWO = 0.5
ADAM_EPS = 1e-08
SHIFT = -4.0
NEGATIVE = -1e30
APART = 128.0
LOW = jnp.bfloat16
F32 = jnp.float32
VMEM_BYTES = 56 * 1024 * 1024
TAIL_P = 0.3
TAIL = (
    0.1196293,
    0.12075397,
    0.09991341,
    0.12856192,
    -0.05368424,
    0.20635419,
    -0.1572035,
    0.03567488,
)


def mm(left, right):
    return lax.dot_general(left, right, (((1,), (0,)), ((), ())), preferred_element_type=F32)


def mm_nt(left, right):
    return lax.dot_general(left, right, (((1,), (1,)), ((), ())), preferred_element_type=F32)


def split_two(values):
    high = values.astype(LOW)
    return high, (values - high.astype(F32)).astype(LOW)


def split_three(values):
    high = values.astype(LOW)
    rest = values - high.astype(F32)
    middle = rest.astype(LOW)
    return high, middle, (rest - middle.astype(F32)).astype(LOW)


def row_norm(values):
    center = values - jnp.mean(values, axis=-1, keepdims=True)
    inverse = lax.rsqrt(jnp.mean(center * center, axis=-1, keepdims=True) + NORM_EPS)
    return center * inverse, inverse


def row_norm_back(gradient, gain_row, normed, inverse):
    scaled = gradient * gain_row
    return inverse * (
        scaled
        - jnp.mean(scaled, axis=-1, keepdims=True)
        - normed * jnp.mean(scaled * normed, axis=-1, keepdims=True)
    )


def half_mean_matrix(scale):
    row = lax.broadcasted_iota(jnp.int32, (128, 128), 0)
    col = lax.broadcasted_iota(jnp.int32, (128, 128), 1)
    return jnp.where((row >= 64) == (col >= 64), scale, 0.0).astype(LOW)


def half_sum(values, block):
    high, low = split_two(values)
    return mm(high, block) + mm(low, block)


def half_norm(values, block):
    center = values - half_sum(values, block)
    inverse = lax.rsqrt(half_sum(center * center, block) + NORM_EPS)
    return center * inverse, inverse


def half_norm_back(gradient, gain_row, normed, inverse, block):
    scaled = gradient * gain_row
    return inverse * (scaled - half_sum(scaled, block) - normed * half_sum(scaled * normed, block))


def gelu_pair(inner):
    size = jnp.abs(inner)
    near = 1.0 / (1.0 + TAIL_P * size)
    bell = jnp.exp(-0.5 * inner * inner)
    poly = TAIL[-1]
    for factor in TAIL[-2::-1]:
        poly = poly * near + factor
    tail = poly * near * bell
    share = jnp.where(inner >= 0, 1.0 - tail, tail)
    return inner * share, share + inner * bell * 0.3989422804014327


def embed_kernel(pack_ref, pix_ref, coord_ref, wp_ref, win_ref, gain_ref, emb_ref, h1_ref, q_ref, k_ref, v_ref):
    rows = pix_ref.shape[0]
    pixels = pix_ref.shape[1]
    groups = win_ref.shape[0]
    part = win_ref.shape[2] // 3
    spots = (wp_ref.shape[1] - pixels) // 2
    lane = lax.broadcasted_iota(jnp.int32, (rows, 2 * spots), 1)
    hot = ((lane == coord_ref[:, 0:1]) | (lane - spots == coord_ref[:, 1:2])).astype(F32).astype(LOW)
    embedded = mm_nt(pix_ref[...], wp_ref[:, :pixels]) + mm_nt(hot, wp_ref[:, pixels:])
    emb_ref[...] = embedded
    normed, _ = row_norm(embedded)
    first = (normed * gain_ref[0:1]).astype(LOW)
    h1_ref[...] = first
    parts = [mm(first, win_ref[group]) for group in range(groups)]
    q_ref[...] = jnp.concatenate([entry[:, :part] for entry in parts], axis=1)
    k_ref[...] = jnp.concatenate([entry[:, part : 2 * part] for entry in parts], axis=1)
    v_ref[...] = jnp.concatenate([entry[:, 2 * part :].astype(LOW) for entry in parts], axis=1)


def embed_call(pack, pixels, coords, w_pp, w_in, vectors, rows):
    width = vectors.shape[1]
    tile = 256
    steps = rows // tile
    whole2 = lambda i, p: (0, 0)
    tiled = pl.BlockSpec((tile, width), lambda i, p: (i, 0))
    return pl.pallas_call(
        embed_kernel,
        grid_spec=pltpu.PrefetchScalarGridSpec(
            num_scalar_prefetch=1,
            grid=(steps,),
            in_specs=[
                pl.BlockSpec((tile, pixels.shape[1]), lambda i, p: (p[0] * steps + i, 0)),
                pl.BlockSpec((tile, 2), lambda i, p: (p[0] * steps + i, 0)),
                pl.BlockSpec(w_pp.shape, whole2),
                pl.BlockSpec(w_in.shape, lambda i, p: (0, 0, 0)),
                pl.BlockSpec(vectors.shape, whole2),
            ],
            out_specs=[tiled] * 5,
        ),
        out_shape=[
            jax.ShapeDtypeStruct((rows, width), F32),
            jax.ShapeDtypeStruct((rows, width), LOW),
            jax.ShapeDtypeStruct((rows, width), F32),
            jax.ShapeDtypeStruct((rows, width), F32),
            jax.ShapeDtypeStruct((rows, width), LOW),
        ],
        compiler_params=pltpu.CompilerParams(vmem_limit_bytes=VMEM_BYTES),
        name="embed",
    )(pack, pixels, coords, w_pp, w_in, vectors)


def image_marks(bound_ref, rows):
    place = lax.broadcasted_iota(jnp.int32, (rows, 128), 0)
    return (place >= bound_ref[0:1, :]) & (place < bound_ref[1:2, :])


def half_lane(rows):
    lane = lax.broadcasted_iota(jnp.int32, (rows, 128), 1)
    return lane, jnp.where(lane >= 64, lane - 64, lane)


def attend_kernel(q_ref, k_ref, v_ref, gain_ref, bound_ref, o_ref, lse_ref, ka_ref, va_ref, qa_ref):
    rows = q_ref.shape[0]
    tile = 256
    block = half_mean_matrix(1.0 / 64)
    lane, inner = half_lane(rows)
    marks = image_marks(bound_ref, rows)
    one = jnp.where(inner == 8, 1.0, 0.0)
    query_feature = jnp.where(marks, 1.0, one)
    key_feature = jnp.where(marks, APART, -APART * one)
    k_normed, _ = half_norm(k_ref[...], block)
    ka_ref[:, :128] = (k_normed * gain_ref[1:2]).astype(LOW)
    ka_ref[:, 128:] = key_feature.astype(LOW)
    va_ref[:, :128] = v_ref[...]
    va_ref[:, 128:] = jnp.ones((rows, 128), LOW)
    q_normed, _ = half_norm(q_ref[...], block)
    query = (q_normed * gain_ref[0:1]).astype(LOW).astype(F32) * 0.125
    for head in range(2):
        mine = (lane < 64) if head == 0 else (lane >= 64)
        qa_ref[head, :, :128] = jnp.where(mine, query, 0.0).astype(LOW)
        qa_ref[head, :, 128:] = jnp.where(mine, query_feature, 0.0).astype(LOW)
    keys = ka_ref[...]
    values = va_ref[...]
    first = lane[:tile] < 64
    for step in range(rows // tile):
        part = slice(step * tile, (step + 1) * tile)
        outs = []
        for head in range(2):
            score = mm_nt(qa_ref[head, part, :], keys)
            outs.append(mm(jnp.exp(score).astype(LOW), values))
        total = jnp.where(first, outs[0][:, 128:], outs[1][:, 128:])
        o_ref[part, :] = (jnp.where(first, outs[0][:, :128], outs[1][:, :128]) / total).astype(LOW)
        lse_ref[part, :] = jnp.log(total)


def attend_call(q_raw, k_raw, value, gains, bounds):
    rows, width = q_raw.shape
    pair = pl.BlockSpec((rows, 128), lambda j: (0, j))
    small = lambda a: pl.BlockSpec(a.shape, lambda j: (0, 0))
    return pl.pallas_call(
        attend_kernel,
        grid=(width // 128,),
        in_specs=[pair, pair, pair, small(gains), small(bounds)],
        out_specs=[pair, pair],
        out_shape=[
            jax.ShapeDtypeStruct((rows, width), LOW),
            jax.ShapeDtypeStruct((rows, width), F32),
        ],
        scratch_shapes=[
            pltpu.VMEM((rows, 256), LOW),
            pltpu.VMEM((rows, 256), LOW),
            pltpu.VMEM((2, rows, 256), LOW),
        ],
        compiler_params=pltpu.CompilerParams(vmem_limit_bytes=VMEM_BYTES),
        name="attend",
    )(q_raw, k_raw, value, gains, bounds)


def attend_back_kernel(
    q_ref, k_ref, v_ref, o_ref, lse_ref, do_ref, gain_ref, bound_ref,
    dq_ref, dk_ref, dv_ref, dgain_ref,
    ka_ref, va_ref, qa_ref, da_ref, qt_ref, dot_ref, dqs_ref, dkt_ref, dvt_ref,
):
    rows = q_ref.shape[0]
    tile = 256
    block = half_mean_matrix(1.0 / 64)
    block_sum = half_mean_matrix(1.0)
    lane, inner = half_lane(rows)
    marks = image_marks(bound_ref, rows)
    one = jnp.where(inner == 8, 1.0, 0.0)
    three = (inner >= 9) & (inner < 12)
    key_feature = jnp.where(marks, APART, jnp.where(three, 1.0, -APART * one))

    def spread(values):
        high, middle, low = split_three(values)
        return jnp.where(
            inner == 9, high.astype(F32), jnp.where(inner == 10, middle.astype(F32), low.astype(F32))
        )

    query_feature = jnp.where(three, spread(-lse_ref[...]), jnp.where(marks, 1.0, one))
    k_normed, k_inverse = half_norm(k_ref[...], block)
    ka_ref[:, :128] = (k_normed * gain_ref[1:2]).astype(LOW)
    ka_ref[:, 128:] = key_feature.astype(LOW)
    va_ref[:, :128] = v_ref[...]
    va_ref[:, 128:] = jnp.where(three, 1.0, 0.0).astype(LOW)
    q_normed, q_inverse = half_norm(q_ref[...], block)
    query = (q_normed * gain_ref[0:1]).astype(LOW).astype(F32)
    qt_ref[...] = jnp.transpose(query).astype(LOW)
    query = query * 0.125
    above = do_ref[...].astype(F32)
    dot_ref[...] = jnp.transpose(above).astype(LOW)
    inside = half_sum(above * o_ref[...].astype(F32), block_sum)
    above_feature = jnp.where(three, spread(inside * -0.125), 0.0)
    above = above * 0.125
    for head in range(2):
        mine = (lane < 64) if head == 0 else (lane >= 64)
        qa_ref[head, :, :128] = jnp.where(mine, query, 0.0).astype(LOW)
        qa_ref[head, :, 128:] = jnp.where(mine, query_feature, 0.0).astype(LOW)
        da_ref[head, :, :128] = jnp.where(mine, above, 0.0).astype(LOW)
        da_ref[head, :, 128:] = jnp.where(mine, above_feature, 0.0).astype(LOW)
    keys = ka_ref[...]
    values = va_ref[...]
    key_low = ka_ref[:, :128]
    first = lane[:tile] < 64
    for step in range(rows // tile):
        part = slice(step * tile, (step + 1) * tile)
        outs = []
        for head in range(2):
            mine = slice(64 * head, 64 * head + 64)
            prob = jnp.exp(mm_nt(qa_ref[head, part, :], keys))
            d_prob = mm_nt(da_ref[head, part, :], values)
            d_score = (prob * d_prob).astype(LOW)
            outs.append(mm(d_score, key_low))
            d_key = mm(qt_ref[mine, part], d_score)
            d_value = mm(dot_ref[mine, part], prob.astype(LOW))
            if step == 0:
                dkt_ref[mine, :] = d_key
                dvt_ref[mine, :] = d_value
            else:
                dkt_ref[mine, :] += d_key
                dvt_ref[mine, :] += d_value
        dqs_ref[part, :] = jnp.where(first, outs[0], outs[1])
    d_query = dqs_ref[...]
    d_key = jnp.transpose(dkt_ref[...])
    dv_ref[...] = jnp.transpose(dvt_ref[...]).astype(LOW)
    dq_ref[...] = half_norm_back(d_query, gain_ref[0:1], q_normed, q_inverse, block).astype(LOW)
    dk_ref[...] = half_norm_back(d_key, gain_ref[1:2], k_normed, k_inverse, block).astype(LOW)
    dgain_ref[0, 0:1] = jnp.sum(d_query * q_normed, axis=0, keepdims=True)
    dgain_ref[0, 1:2] = jnp.sum(d_key * k_normed, axis=0, keepdims=True)


def attend_back_call(q_raw, k_raw, value, attended, lse, d_attended, gains, bounds):
    rows, width = q_raw.shape
    pairs = width // 128
    pair = pl.BlockSpec((rows, 128), lambda j: (0, j))
    small = lambda a: pl.BlockSpec(a.shape, lambda j: (0, 0))
    low = jax.ShapeDtypeStruct((rows, width), LOW)
    return pl.pallas_call(
        attend_back_kernel,
        grid=(pairs,),
        in_specs=[pair] * 6 + [small(gains), small(bounds)],
        out_specs=[pair, pair, pair, pl.BlockSpec((1, 2, 128), lambda j: (j, 0, 0))],
        out_shape=[low, low, low, jax.ShapeDtypeStruct((pairs, 2, 128), F32)],
        scratch_shapes=[
            pltpu.VMEM((rows, 256), LOW),
            pltpu.VMEM((rows, 256), LOW),
            pltpu.VMEM((2, rows, 256), LOW),
            pltpu.VMEM((2, rows, 256), LOW),
            pltpu.VMEM((128, rows), LOW),
            pltpu.VMEM((128, rows), LOW),
            pltpu.VMEM((rows, 128), F32),
            pltpu.VMEM((128, rows), F32),
            pltpu.VMEM((128, rows), F32),
        ],
        compiler_params=pltpu.CompilerParams(vmem_limit_bytes=VMEM_BYTES),
        name="attend_back",
    )(q_raw, k_raw, value, attended, lse, d_attended, gains, bounds)


def mlp_kernel(o_ref, emb_ref, wout_ref, wup_ref, wdn_ref, vec_ref, x1_ref, h2_ref, act_ref, slope_ref, x2_ref):
    step = pl.program_id(0)
    rows, _ = o_ref.shape
    groups, _, part = wout_ref.shape
    tile = 256

    @pl.when(step == 0)
    def _():
        for at in range(rows // tile):
            span = slice(at * tile, (at + 1) * tile)
            branch = mm_nt(o_ref[span, :part], wout_ref[0])
            for group in range(1, groups):
                branch += mm_nt(o_ref[span, group * part : (group + 1) * part], wout_ref[group])
            middle = emb_ref[span, :] + branch
            x1_ref[span, :] = middle
            x2_ref[span, :] = middle
            normed, _ = row_norm(middle)
            h2_ref[span, :] = (normed * vec_ref[1:2]).astype(LOW)

    for at in range(rows // tile):
        span = slice(at * tile, (at + 1) * tile)
        active, slope = gelu_pair(mm(h2_ref[span, :], wup_ref[0]))
        active = active.astype(LOW)
        act_ref[span, :] = active
        slope_ref[span, :] = slope.astype(LOW)
        x2_ref[span, :] += mm_nt(active, wdn_ref[0])


def mlp_call(attended, embedded, w_out, w_up, w_dn, vectors):
    rows, width = embedded.shape
    groups, _, per = w_up.shape
    chunk = per // 2
    hidden = groups * per
    whole = lambda a: pl.BlockSpec(a.shape, lambda j: (0,) * a.ndim)
    weight = pl.BlockSpec((1, width, chunk), lambda j: (j // 2, 0, j % 2))
    full = pl.BlockSpec((rows, width), lambda j: (0, 0))
    piece = pl.BlockSpec((rows, chunk), lambda j: (0, j))
    return pl.pallas_call(
        mlp_kernel,
        grid=(hidden // chunk,),
        in_specs=[whole(attended), whole(embedded), whole(w_out), weight, weight, whole(vectors)],
        out_specs=[full, full, piece, piece, full],
        out_shape=[
            jax.ShapeDtypeStruct((rows, width), F32),
            jax.ShapeDtypeStruct((rows, width), LOW),
            jax.ShapeDtypeStruct((rows, hidden), LOW),
            jax.ShapeDtypeStruct((rows, hidden), LOW),
            jax.ShapeDtypeStruct((rows, width), F32),
        ],
        compiler_params=pltpu.CompilerParams(vmem_limit_bytes=VMEM_BYTES),
        name="mlp",
    )(attended, embedded, w_out, w_up, w_dn, vectors)


def pool_kernel(
    pack_ref, x2_ref, label_ref, wcls_ref, vec_ref, bound_ref, valid_ref,
    dx2_ref, dcls_ref, loss_ref, dvec_ref,
    norm_ref, inv_ref,
    *, images, image_count,
):
    rows, width = x2_ref.shape
    tile = 256
    root = width**0.5
    gain = vec_ref[2:3]
    query = vec_ref[3:4]
    lane = lax.broadcasted_iota(jnp.int32, (rows, 128), 1)
    marks = image_marks(bound_ref, rows) & (lane < 64)
    logits = []
    for at in range(rows // tile):
        span = slice(at * tile, (at + 1) * tile)
        normed, inverse = row_norm(x2_ref[span, :])
        norm_ref[span, :] = normed
        inv_ref[span, :] = jnp.broadcast_to(inverse, (tile, 128))
        logits.append(jnp.sum(normed * gain * query, axis=-1, keepdims=True) / root)
    logit = jnp.concatenate(logits, axis=0)
    masked = jnp.where(marks, logit, NEGATIVE)
    grown = jnp.exp(masked - jnp.max(masked, axis=0, keepdims=True))
    shares = jnp.where(marks, grown / jnp.sum(grown, axis=0, keepdims=True), 0.0)
    weight = jnp.sum(shares, axis=-1, keepdims=True)
    member = jnp.transpose(marks.astype(F32))[:16].astype(LOW)
    pooled = jnp.zeros((16, width), F32)
    for at in range(rows // tile):
        span = slice(at * tile, (at + 1) * tile)
        for entry in split_three(norm_ref[span, :] * gain * weight[span]):
            pooled += mm(member[:, span], entry)
    pooled_low = pooled.astype(LOW)
    scores = mm(pooled_low, wcls_ref[...])[:images] + SHIFT
    target = label_ref[...].astype(F32)
    valid = valid_ref[0, 0]
    soft = jnp.maximum(scores, 0.0) + jnp.log1p(jnp.exp(-jnp.abs(scores)))
    loss_rows = jnp.sum(soft - target * scores, axis=-1, keepdims=True)
    loss_ref[...] = jnp.broadcast_to(jnp.sum(loss_rows, axis=0, keepdims=True) * valid, loss_ref.shape)
    d_score = (1.0 / (1.0 + jnp.exp(-scores)) - target) / image_count * valid
    d_score = jnp.concatenate([d_score, jnp.zeros((16 - images, d_score.shape[1]), F32)], axis=0).astype(LOW)
    dcls_ref[...] = mm(jnp.transpose(pooled).astype(LOW), d_score).astype(LOW)
    d_pooled = mm_nt(d_score, wcls_ref[...])[:images]
    parts = jnp.concatenate(
        [entry.astype(F32) for entry in split_three(d_pooled)]
        + [jnp.zeros((128 - 3 * images, width), F32)],
        axis=0,
    ).astype(LOW)
    marks_f = marks.astype(F32)
    thrice = (
        marks_f + pltpu.roll(marks_f, images, 1) + pltpu.roll(marks_f, 2 * images, 1)
    ).astype(LOW)
    d_weights = []
    for at in range(rows // tile):
        span = slice(at * tile, (at + 1) * tile)
        spread = mm(thrice[span], parts)
        dx2_ref[span, :] = spread
        d_weights.append(jnp.sum(spread * (norm_ref[span, :] * gain), axis=-1, keepdims=True))
    d_weight = jnp.concatenate(d_weights, axis=0)
    inside = jnp.sum(shares * d_weight, axis=0, keepdims=True)
    d_logit = weight * (d_weight - jnp.sum(marks_f * inside, axis=-1, keepdims=True))
    gain_sum = jnp.zeros((1, width), F32)
    query_sum = jnp.zeros((1, width), F32)
    for at in range(rows // tile):
        span = slice(at * tile, (at + 1) * tile)
        normed = norm_ref[span, :]
        inverse = inv_ref[span, 0:1]
        d_last = dx2_ref[span, :] * weight[span] + d_logit[span] * (query / root)
        gain_sum += jnp.sum(d_last * normed, axis=0, keepdims=True)
        query_sum += jnp.sum(d_logit[span] * normed, axis=0, keepdims=True)
        dx2_ref[span, :] = row_norm_back(d_last, gain, normed, inverse)
    dvec_ref[0:1, :] = gain_sum
    dvec_ref[1:2, :] = query_sum * gain / root


def pool_call(pack, x2, labels, w_cls, vectors, bounds, valid, images, image_count):
    rows, width = x2.shape
    classes = labels.shape[1]
    whole = lambda a: pl.BlockSpec(a.shape, lambda j, p: (0,) * a.ndim)
    full = lambda *shape: pl.BlockSpec(shape, lambda j, p: (0,) * len(shape))
    return pl.pallas_call(
        functools.partial(pool_kernel, images=images, image_count=image_count),
        grid_spec=pltpu.PrefetchScalarGridSpec(
            num_scalar_prefetch=1,
            grid=(1,),
            in_specs=[
                whole(x2),
                pl.BlockSpec((images, classes), lambda j, p: (p[0], 0)),
                whole(w_cls),
                whole(vectors),
                whole(bounds),
                pl.BlockSpec(memory_space=pltpu.SMEM),
            ],
            out_specs=[full(rows, width), full(width, classes), full(8, 128), full(2, width)],
            scratch_shapes=[pltpu.VMEM((rows, width), F32), pltpu.VMEM((rows, 128), F32)],
        ),
        out_shape=[
            jax.ShapeDtypeStruct((rows, width), F32),
            jax.ShapeDtypeStruct((width, classes), LOW),
            jax.ShapeDtypeStruct((8, 128), F32),
            jax.ShapeDtypeStruct((2, width), F32),
        ],
        compiler_params=pltpu.CompilerParams(vmem_limit_bytes=VMEM_BYTES),
        name="pool",
    )(pack, x2, labels, w_cls, vectors, bounds, valid)


def mlp_back_kernel(
    dx2_ref, act_ref, slope_ref, h2_ref, x1_ref, o_ref, wout_ref, wup_ref, wdn_ref, vec_ref,
    ddn_ref, dup_ref, dout_ref, do_ref, dmid_ref, dvec_ref,
    low_ref, lowt_ref, h2t_ref, acc_ref, dh_ref,
):
    step = pl.program_id(0)
    rows, width = dx2_ref.shape
    groups, _, part = wout_ref.shape
    tile = 256

    @pl.when(step == 0)
    def _():
        for at in range(rows // tile):
            span = slice(at * tile, (at + 1) * tile)
            values = dx2_ref[span, :]
            low_ref[span, :] = values.astype(LOW)
            lowt_ref[:, span] = jnp.transpose(values).astype(LOW)
            h2t_ref[:, span] = jnp.transpose(h2_ref[span, :].astype(F32)).astype(LOW)
            acc_ref[span, :] = jnp.zeros((tile, width), F32)

    for at in range(rows // tile):
        span = slice(at * tile, (at + 1) * tile)
        d_hidden = (mm(low_ref[span, :], wdn_ref[0]) * slope_ref[span, :].astype(F32)).astype(LOW)
        dh_ref[span, :] = d_hidden
        acc_ref[span, :] += mm_nt(d_hidden, wup_ref[0])
    for at in range(width // tile):
        span = slice(at * tile, (at + 1) * tile)
        ddn_ref[0, span, :] = mm(lowt_ref[span, :], act_ref[...]).astype(LOW)
        dup_ref[0, span, :] = mm(h2t_ref[span, :], dh_ref[...]).astype(LOW)

    @pl.when(step == pl.num_programs(0) - 1)
    def _():
        gain = vec_ref[1:2]
        gain_sum = jnp.zeros((1, width), F32)
        for at in range(rows // tile):
            span = slice(at * tile, (at + 1) * tile)
            normed, inverse = row_norm(x1_ref[span, :])
            d_second = acc_ref[span, :]
            gain_sum += jnp.sum(d_second * normed, axis=0, keepdims=True)
            d_middle = dx2_ref[span, :] + row_norm_back(d_second, gain, normed, inverse)
            dmid_ref[span, :] = d_middle
            low = d_middle.astype(LOW)
            lowt_ref[:, span] = jnp.transpose(d_middle).astype(LOW)
            do_ref[span, :] = jnp.concatenate(
                [mm(low, wout_ref[group]) for group in range(groups)], axis=1
            ).astype(LOW)
        dvec_ref[...] = gain_sum
        for group in range(groups):
            piece = o_ref[:, group * part : (group + 1) * part]
            for at in range(width // tile):
                span = slice(at * tile, (at + 1) * tile)
                dout_ref[group, span, :] = mm(lowt_ref[span, :], piece).astype(LOW)


def mlp_back_call(dx2, active, slope, h2, x1, attended, w_out, w_up, w_dn, vectors):
    rows, width = dx2.shape
    groups, _, per = w_up.shape
    chunk = per // 2
    hidden = groups * per
    whole = lambda a: pl.BlockSpec(a.shape, lambda j: (0,) * a.ndim, pipeline_mode=pl.Buffered(1))
    weight = pl.BlockSpec((1, width, chunk), lambda j: (j // 2, 0, j % 2))
    piece = pl.BlockSpec((rows, chunk), lambda j: (0, j))
    full = lambda *shape: pl.BlockSpec(shape, lambda j: (0,) * len(shape))
    return pl.pallas_call(
        mlp_back_kernel,
        grid=(hidden // chunk,),
        in_specs=[
            whole(dx2), piece, piece, whole(h2), whole(x1), whole(attended), whole(w_out),
            weight, weight, whole(vectors),
        ],
        out_specs=[weight, weight, full(*w_out.shape), full(rows, width), full(rows, width), full(1, width)],
        out_shape=[
            jax.ShapeDtypeStruct(w_dn.shape, LOW),
            jax.ShapeDtypeStruct(w_up.shape, LOW),
            jax.ShapeDtypeStruct(w_out.shape, LOW),
            jax.ShapeDtypeStruct((rows, width), LOW),
            jax.ShapeDtypeStruct((rows, width), F32),
            jax.ShapeDtypeStruct((1, width), F32),
        ],
        scratch_shapes=[
            pltpu.VMEM((rows, width), LOW),
            pltpu.VMEM((width, rows), LOW),
            pltpu.VMEM((width, rows), LOW),
            pltpu.VMEM((rows, width), F32),
            pltpu.VMEM((rows, chunk), LOW),
        ],
        compiler_params=pltpu.CompilerParams(vmem_limit_bytes=VMEM_BYTES),
        name="mlp_back",
    )(dx2, active, slope, h2, x1, attended, w_out, w_up, w_dn, vectors)


def embed_back_kernel(
    pack_ref, dq_ref, dk_ref, dv_ref, h1_ref, emb_ref, dmid_ref, pix_ref, coord_ref, win_ref, vec_ref,
    din_ref, dpp_ref, dvec_ref,
    h1t_ref, join_ref, acc_ref,
):
    step = pl.program_id(0)
    rows, width = h1_ref.shape
    groups = pl.num_programs(0)
    part = win_ref.shape[2] // 3
    tile = 256

    @pl.when(step == 0)
    def _():
        for at in range(rows // tile):
            span = slice(at * tile, (at + 1) * tile)
            h1t_ref[:, span] = jnp.transpose(h1_ref[span, :].astype(F32)).astype(LOW)
            acc_ref[span, :] = jnp.zeros((tile, width), F32)

    for group in range(width // part):

        @pl.when(step == group)
        def _():
            mine = slice(group * part, (group + 1) * part)
            join_ref[...] = jnp.concatenate([dq_ref[:, mine], dk_ref[:, mine], dv_ref[:, mine]], axis=1)

    for at in range(rows // tile):
        span = slice(at * tile, (at + 1) * tile)
        acc_ref[span, :] += mm_nt(join_ref[span, :], win_ref[0])
    for at in range(width // tile):
        span = slice(at * tile, (at + 1) * tile)
        din_ref[0, span, :] = mm(h1t_ref[span, :], join_ref[...]).astype(LOW)

    @pl.when(step == groups - 1)
    def _():
        gain = vec_ref[0:1]
        pixels = pix_ref.shape[1]
        spots = (dpp_ref.shape[1] - pixels) // 2
        gain_sum = jnp.zeros((1, width), F32)
        for at in range(rows // tile):
            span = slice(at * tile, (at + 1) * tile)
            normed, inverse = row_norm(emb_ref[span, :])
            d_first = acc_ref[span, :]
            gain_sum += jnp.sum(d_first * normed, axis=0, keepdims=True)
            d_embed = dmid_ref[span, :] + row_norm_back(d_first, gain, normed, inverse)
            h1t_ref[:, span] = jnp.transpose(d_embed).astype(LOW)
        dvec_ref[...] = gain_sum
        lane = lax.broadcasted_iota(jnp.int32, (rows, 2 * spots), 1)
        hot = ((lane == coord_ref[:, 0:1]) | (lane - spots == coord_ref[:, 1:2])).astype(F32).astype(LOW)
        for at in range(width // tile):
            span = slice(at * tile, (at + 1) * tile)
            dpp_ref[span, :pixels] = mm(h1t_ref[span, :], pix_ref[...]).astype(LOW)
            dpp_ref[span, pixels:] = mm(h1t_ref[span, :], hot).astype(LOW)


def embed_back_call(pack, dq, dk, dv, h1, embedded, d_middle, pixels, coords, w_in, w_pp_shape, vectors):
    rows, width = h1.shape
    groups = w_in.shape[0]
    whole = lambda a: pl.BlockSpec(a.shape, lambda j, p: (0,) * a.ndim, pipeline_mode=pl.Buffered(1))
    full = lambda *shape: pl.BlockSpec(shape, lambda j, p: (0,) * len(shape))
    weight = pl.BlockSpec((1,) + w_in.shape[1:], lambda j, p: (j, 0, 0))
    return pl.pallas_call(
        embed_back_kernel,
        grid_spec=pltpu.PrefetchScalarGridSpec(
            num_scalar_prefetch=1,
            grid=(groups,),
            in_specs=[
                whole(dq), whole(dk), whole(dv), whole(h1), whole(embedded), whole(d_middle),
                pl.BlockSpec((rows, pixels.shape[1]), lambda j, p: (p[0], 0)),
                pl.BlockSpec((rows, 2), lambda j, p: (p[0], 0)),
                weight,
                whole(vectors),
            ],
            out_specs=[weight, full(*w_pp_shape), full(1, width)],
            scratch_shapes=[
                pltpu.VMEM((width, rows), LOW),
                pltpu.VMEM((rows, w_in.shape[2]), LOW),
                pltpu.VMEM((rows, width), F32),
            ],
        ),
        out_shape=[
            jax.ShapeDtypeStruct(w_in.shape, LOW),
            jax.ShapeDtypeStruct(w_pp_shape, LOW),
            jax.ShapeDtypeStruct((1, width), F32),
        ],
        compiler_params=pltpu.CompilerParams(vmem_limit_bytes=VMEM_BYTES),
        name="embed_back",
    )(pack, dq, dk, dv, h1, embedded, d_middle, pixels, coords, w_in, vectors)


def pack_step(pack, valid, pixels, coords, lengths, labels, weights, vectors, head_gains, image_count):
    w_pp, w_in, w_out, w_up, w_dn, w_cls = weights
    packs, images = lengths.shape
    rows = pixels.shape[0] // packs
    mine = lax.dynamic_index_in_dim(lengths, pack[0], 0, keepdims=False)
    ends = jnp.cumsum(mine)
    fill = jnp.full((64 - images,), 1 << 30, jnp.int32)
    starts = jnp.concatenate([ends - mine, fill])
    ends = jnp.concatenate([ends, fill])
    bounds = jnp.stack([jnp.tile(starts, 2), jnp.tile(ends, 2)])
    gains = jnp.tile(head_gains, (1, 2))
    places = coords.T
    embedded, h1, q_raw, k_raw, value = embed_call(pack, pixels, places, w_pp, w_in, vectors, rows)
    attended, lse = attend_call(q_raw, k_raw, value, gains, bounds)
    x1, h2, active, slope, x2 = mlp_call(attended, embedded, w_out, w_up, w_dn, vectors)
    dx2, d_cls, loss, dvec_pool = pool_call(
        pack, x2, labels, w_cls, vectors, bounds, valid, images, image_count
    )
    d_dn, d_up, d_out, d_attended, d_middle, dvec_two = mlp_back_call(
        dx2, active, slope, h2, x1, attended, w_out, w_up, w_dn, vectors
    )
    dq, dk, dv, d_gain = attend_back_call(q_raw, k_raw, value, attended, lse, d_attended, gains, bounds)
    d_in, d_pp, dvec_one = embed_back_call(
        pack, dq, dk, dv, h1, embedded, d_middle, pixels, places, w_in, w_pp.shape, vectors
    )
    d_vectors = jnp.concatenate([dvec_one, dvec_two, dvec_pool], axis=0)
    d_gains = jnp.sum(d_gain.reshape(-1, 2, 2, 64), axis=(0, 2))
    return (d_pp, d_in, d_out, d_up, d_dn, d_cls), d_vectors, d_gains, loss[0, 0]


MESH = pl.DeviceIdType.MESH


class Seat:
    def __init__(self):
        self.me = lax.axis_index("dp")
        self.z = lax.axis_index("tensor")
        self.c = lax.rem(self.me, 2)
        self.x = lax.rem(lax.div(self.me, 2), 2)
        self.y = lax.div(self.me, 4)
        self.core = self.me + 1 - 2 * self.c
        self.xn = self.me + 2 - 4 * self.x
        self.yn = self.me + 4 - 8 * self.y
        self.diag = self.xn + 4 - 8 * self.y


def link(src, dst, sems, at, device):
    return pltpu.make_async_remote_copy(
        src_ref=src,
        dst_ref=dst,
        send_sem=sems[0].at[at],
        recv_sem=sems[1].at[at],
        device_id=device,
        device_id_type=MESH,
    )


def greet(seat, depth):
    barrier = pltpu.get_barrier_semaphore()
    for near in (seat.core, seat.xn, seat.yn):
        pl.semaphore_signal(barrier, inc=1, device_id={"dp": near}, device_id_type=MESH)
    for ahead in range(1, depth):
        pl.semaphore_signal(
            barrier, inc=1, device_id={"tensor": lax.rem(seat.z + ahead, depth)}, device_id_type=MESH
        )
    pl.semaphore_wait(barrier, 2 + depth)


def gather_kernel(*refs, count, split):
    shards, outs = refs[:count], refs[count : 2 * count]
    own_sem, send_sem, recv_sem = refs[2 * count :]
    sems = (send_sem, recv_sem)
    seat = Seat()
    depth = 4
    share = shards[0].shape[0]
    half = share // 2
    greet(seat, depth)

    def rows(owner):
        return pl.ds(pl.multiple_of(owner * share, share), share)

    def column(k, owner):
        return outs[k].at[:, rows(owner), :] if split[k] else outs[k].at[rows(owner), :]

    def halves(k, owner, which):
        if split[k]:
            return outs[k].at[pl.ds(2 * which, 2), rows(owner), :]
        return outs[k].at[pl.ds(pl.multiple_of(owner * share + which * half, half), half), :]

    def block(k, level):
        return outs[k].at[level, rows(seat.me), :]

    def keep(k):
        mine = block(k, seat.z) if split[k] else column(k, seat.me)
        return pltpu.make_async_copy(shards[k], mine, own_sem.at[k])

    def along(k, hop, way):
        level = seat.z - way * hop
        source = shards[k] if hop == 0 else block(k, level)
        at = (k, hop + (0 if way > 0 else 3))
        return link(source, block(k, level), sems, at, {"tensor": seat.z + way})

    def arrives(k, hop, way):
        level = seat.z - way * (hop + 1)
        at = (k, hop + (0 if way > 0 else 3))
        return link(block(k, level), block(k, level), sems, at, {"tensor": seat.z - way})

    def sends(hop, way):
        level, to = seat.z - way * hop, seat.z + way
        return (level >= 0) & (level < depth) & (to >= 0) & (to < depth)

    def gets(hop, way):
        level = seat.z - way * (hop + 1)
        return (level >= 0) & (level < depth)

    def start_z(k):
        keep(k).start()
        if split[k]:
            for way in (1, -1):

                @pl.when(sends(0, way))
                def _():
                    along(k, 0, way).start()

    def relay_z(k):
        if split[k]:
            for hop in range(depth - 1):
                for way in (1, -1):

                    @pl.when(gets(hop, way))
                    def _():
                        arrives(k, hop, way).wait_recv()

                    if hop + 1 < depth - 1:

                        @pl.when(sends(hop + 1, way))
                        def _():
                            along(k, hop + 1, way).start()

    def own_x(k):
        return link(column(k, seat.me), column(k, seat.me), sems, (k, 6), {"dp": seat.xn})

    def own_y(k):
        return link(column(k, seat.me), column(k, seat.me), sems, (k, 7), {"dp": seat.yn})

    def pass_x(k):
        return link(halves(k, seat.yn, 1), halves(k, seat.yn, 1), sems, (k, 8), {"dp": seat.xn})

    def pass_y(k):
        return link(halves(k, seat.xn, 0), halves(k, seat.xn, 0), sems, (k, 9), {"dp": seat.yn})

    def over(k, which):
        owner = (seat.me, seat.xn, seat.yn, seat.diag)[which]
        return link(column(k, owner), column(k, owner), sems, (k, 10 + which), {"dp": seat.core})

    def wait_column(k, at, region, device):
        link(region, region, sems, (k, at), device).wait_recv()

    def start_plane(k):
        keep(k).wait()
        own_x(k).start()
        own_y(k).start()
        over(k, 0).start()

    def relay_plane(k):
        wait_column(k, 6, column(k, seat.xn), {"dp": seat.xn})
        pass_y(k).start()
        over(k, 1).start()
        wait_column(k, 7, column(k, seat.yn), {"dp": seat.yn})
        pass_x(k).start()
        over(k, 2).start()

    def finish_plane(k):
        wait_column(k, 8, halves(k, seat.diag, 1), {"dp": seat.xn})
        wait_column(k, 9, halves(k, seat.diag, 0), {"dp": seat.yn})
        over(k, 3).start()

    def drain(k):
        for which, shift in ((0, 0), (1, 1), (2, 2), (3, 3)):
            owner = (seat.me, seat.xn, seat.yn, seat.diag)[which] + 1 - 2 * seat.c
            wait_column(k, 10 + which, column(k, owner), {"dp": seat.core})
        if split[k]:
            for hop in range(depth - 1):
                for way in (1, -1):

                    @pl.when(sends(hop, way))
                    def _():
                        along(k, hop, way).wait_send()

        for copy in (own_x(k), own_y(k), pass_x(k), pass_y(k)):
            copy.wait_send()
        for which in range(4):
            over(k, which).wait_send()

    for k in range(count):
        start_z(k)
    for turn in range(count + 2):
        if turn < count:
            relay_z(turn)
            start_plane(turn)
        if 0 <= turn - 1 < count:
            relay_plane(turn - 1)
        if 0 <= turn - 2 < count:
            finish_plane(turn - 2)
    for k in range(count):
        drain(k)


def gather_call(shards, split, depth, width, collective_id):
    count = len(shards)
    shapes = [
        jax.ShapeDtypeStruct(((depth, width) if apart else (width,)) + entry.shape[1:], entry.dtype)
        for entry, apart in zip(shards, split)
    ]
    return pl.pallas_call(
        functools.partial(gather_kernel, count=count, split=split),
        out_shape=shapes,
        in_specs=[pl.BlockSpec(memory_space=pl.ANY)] * count,
        out_specs=[pl.BlockSpec(memory_space=pl.ANY)] * count,
        scratch_shapes=[
            pltpu.SemaphoreType.DMA((count,)),
            pltpu.SemaphoreType.DMA((count, 14)),
            pltpu.SemaphoreType.DMA((count, 14)),
        ],
        compiler_params=pltpu.CompilerParams(
            collective_id=collective_id, has_side_effects=True, vmem_limit_bytes=VMEM_BYTES
        ),
        name="gather_weights",
    )(*shards)


def scatter_kernel(*refs, count, split):
    grads, small_ref = refs[:count], refs[count]
    outs, small_out, square_out = refs[count + 1 : 2 * count + 1], refs[2 * count + 1], refs[2 * count + 2]
    rest = refs[2 * count + 3 :]
    own, core_in, one_x, one_y, two_x, two_y, up_in, down_in, result = (
        rest[k * count : (k + 1) * count] for k in range(9)
    )
    tiny, tiny_in, own_sem, send_sem, recv_sem, tiny_send, tiny_recv, out_sem = rest[9 * count :]
    sems = (send_sem, recv_sem)
    seat = Seat()
    depth = 4
    x, y, z, c = seat.x, seat.y, seat.z, seat.c
    dp = lambda near: {"dp": near}

    def load(k):
        source = grads[k].at[:, :, :, c] if split[k] else grads[k].at[:, :, c]
        return pltpu.make_async_copy(source, own[k], own_sem.at[k])

    def to_core(k):
        source = grads[k].at[:, :, :, 1 - c] if split[k] else grads[k].at[:, :, 1 - c]
        return link(source, core_in[k], sems, (k, 0), dp(seat.core))

    def first_x(k):
        half = own[k].shape[-2] // 2
        source = own[k].at[0:2, :, 1 - x] if split[k] else own[k].at[:, 1 - x, 0:half]
        return link(source, one_x[k], sems, (k, 1), dp(seat.xn))

    def first_y(k):
        half = own[k].shape[-2] // 2
        source = own[k].at[2:4, 1 - y] if split[k] else own[k].at[1 - y, :, half : 2 * half]
        return link(source, one_y[k], sems, (k, 2), dp(seat.yn))

    def second_y(k):
        half = own[k].shape[-2] // 2
        source = own[k].at[0:2, 1 - y, x] if split[k] else own[k].at[1 - y, x, 0:half]
        return link(source, two_y[k], sems, (k, 3), dp(seat.yn))

    def second_x(k):
        half = own[k].shape[-2] // 2
        source = own[k].at[2:4, y, 1 - x] if split[k] else own[k].at[y, 1 - x, half : 2 * half]
        return link(source, two_x[k], sems, (k, 4), dp(seat.xn))

    def along(k, level, way):
        buffer = up_in if way > 0 else down_in
        at = (k, 5 + level if way > 0 else 9 + level)
        return link(own[k].at[level, y, x], buffer[k].at[level], sems, at, {"tensor": z + way})

    def whole_z(k, ahead):
        to = lax.rem(z + ahead, depth)
        return link(own[k].at[y, x], up_in[k].at[z], sems, (k, 5 + ahead), {"tensor": to})

    def whole_from(k, ahead):
        source = lax.rem(z - ahead + depth, depth)
        return link(own[k].at[y, x], up_in[k].at[source], sems, (k, 5 + ahead), {"tensor": source})

    def stage_one(k):
        load(k).wait()
        to_core(k).wait_recv()
        lead = own[k].shape[:-2]
        blocks = 1
        for size in lead:
            blocks *= size

        def add(b, carry):
            at, left = [], b
            for size in lead[::-1]:
                at.append(lax.rem(left, size))
                left = lax.div(left, size)
            at = tuple(at[::-1])
            own[k][at] = own[k][at] + core_in[k][at]
            return carry

        lax.fori_loop(0, blocks, add, 0)
        first_x(k).start()
        first_y(k).start()

    def stage_two(k):
        half = own[k].shape[-2] // 2
        first_x(k).wait_recv()
        for a in range(2):
            for b in range(2 if split[k] else 1):
                if split[k]:
                    own[k][a, b, x] = own[k][a, b, x] + one_x[k][a, b]
                else:
                    own[k][a, x, 0:half] = own[k][a, x, 0:half] + one_x[k][a]
        second_y(k).start()
        first_y(k).wait_recv()
        for a in range(2):
            for b in range(2 if split[k] else 1):
                if split[k]:
                    own[k][2 + a, y, b] = own[k][2 + a, y, b] + one_y[k][a, b]
                else:
                    own[k][y, a, half : 2 * half] = own[k][y, a, half : 2 * half] + one_y[k][a]
        second_x(k).start()

    def stage_three(k):
        half = own[k].shape[-2] // 2
        second_y(k).wait_recv()
        second_x(k).wait_recv()
        if split[k]:
            for a in range(2):
                own[k][a, y, x] = own[k][a, y, x] + two_y[k][a]
                own[k][2 + a, y, x] = own[k][2 + a, y, x] + two_x[k][a]
            for way in (1, -1):

                @pl.when(z == (0 if way > 0 else depth - 1))
                def _():
                    for level in range(depth):
                        far = depth - 1 - level if way > 0 else level
                        if far != (0 if way > 0 else depth - 1):
                            along(k, far, way).start()
        else:
            own[k][y, x, 0:half] = own[k][y, x, 0:half] + two_y[k][...]
            own[k][y, x, half : 2 * half] = own[k][y, x, half : 2 * half] + two_x[k][...]
            for ahead in range(1, depth):
                whole_z(k, ahead).start()

    def stage_four(k):
        if split[k]:
            for level in range(depth):
                far = depth - 1 - level

                @pl.when((z > 0) & (z < far))
                def _():
                    along(k, far, 1).wait_recv()
                    own[k][far, y, x] = own[k][far, y, x] + up_in[k][far]
                    along(k, far, 1).start()

                @pl.when((z < depth - 1) & (z > level))
                def _():
                    along(k, level, -1).wait_recv()
                    own[k][level, y, x] = own[k][level, y, x] + down_in[k][level]
                    along(k, level, -1).start()

            result[k][...] = own[k][z, y, x].astype(F32)

            @pl.when(z > 0)
            def _():
                along(k, z, 1).wait_recv()
                result[k][...] += up_in[k][z].astype(F32)

            @pl.when(z < depth - 1)
            def _():
                along(k, z, -1).wait_recv()
                result[k][...] += down_in[k][z].astype(F32)

            factor = 1.0
        else:
            for ahead in range(1, depth):
                whole_from(k, ahead).wait_recv()
            up_in[k][z] = own[k][y, x]
            total = up_in[k][0].astype(F32)
            for level in range(1, depth):
                total += up_in[k][level].astype(F32)
            result[k][...] = total
            factor = jnp.where(z == 0, 1.0, 0.0)
        pltpu.make_async_copy(result[k], outs[k], out_sem.at[k]).start()
        values = result[k][...]
        return jnp.sum(jnp.sum(values * values, axis=0, keepdims=True), axis=1, keepdims=True) * factor

    def drain(k):
        pltpu.make_async_copy(result[k], outs[k], out_sem.at[k]).wait()
        for copy in (to_core(k), first_x(k), first_y(k), second_x(k), second_y(k)):
            copy.wait_send()
        if split[k]:
            for level in range(depth):

                @pl.when(z < level)
                def _():
                    along(k, level, 1).wait_send()

                @pl.when(z > level)
                def _():
                    along(k, level, -1).wait_send()

        else:
            for ahead in range(1, depth):
                whole_z(k, ahead).wait_send()

    def tiny_sum(which, first):
        view = tiny[which]
        came = tiny_in[which]
        tsems = (tiny_send, tiny_recv)
        for hop, near in enumerate((seat.core, seat.xn, seat.yn)):
            copy = link(view.at[0], came.at[hop], tsems, (which, hop), dp(near))
            copy.start()
            copy.wait_recv()
            copy.wait_send()
            view[0] = view[0] + came[hop]
        copies = []
        for ahead in range(1, depth):
            to = lax.rem(z + ahead, depth)
            copies.append(link(view.at[0], came.at[3 + z], tsems, (which, 2 + ahead), {"tensor": to}))
            copies[-1].start()
        for ahead in range(1, depth):
            source = lax.rem(z - ahead + depth, depth)
            link(view.at[0], came.at[3 + source], tsems, (which, 2 + ahead), {"tensor": source}).wait_recv()
        for copy in copies:
            copy.wait_send()
        came[3 + z] = view[0]
        total = came[3]
        for level in range(1, depth):
            total = total + came[3 + level]
        view[0] = total

    for k in range(count):
        load(k).start()
    greet(seat, depth)
    for k in range(count):
        to_core(k).start()
    squares = jnp.zeros((1, 1), F32)
    for turn in range(count + 3):
        if turn < count:
            stage_one(turn)
        if 0 <= turn - 1 < count:
            stage_two(turn - 1)
        if 0 <= turn - 2 < count:
            stage_three(turn - 2)
        if turn == count:
            tiny[0][0] = small_ref[...]
            tiny_sum(0, True)
            small_out[...] = tiny[0][0]
        if 0 <= turn - 3 < count:
            squares = squares + stage_four(turn - 3)
    tiny[1][0] = jnp.broadcast_to(squares, tiny[1].shape[1:])
    tiny_sum(1, False)
    square_out[...] = tiny[1][0]
    for k in range(count):
        drain(k)


def scatter_call(grads, small, split, collective_id):
    count = len(grads)
    depth = 4
    tails = [entry.shape[-2:] for entry in grads]
    own, core_in, one, two, up = [], [], [], [], []
    for entry, apart, (share, cols) in zip(grads, split, tails):
        lead = (depth, 2, 2) if apart else (2, 2)
        own.append(pltpu.VMEM(lead + (share, cols), LOW))
        core_in.append(pltpu.VMEM(lead + (share, cols), LOW))
        one.append(pltpu.VMEM((2, 2, share, cols) if apart else (2, share // 2, cols), LOW))
        two.append(pltpu.VMEM((2, share, cols) if apart else (share // 2, cols), LOW))
        up.append(pltpu.VMEM((depth, share, cols), LOW))
    results = [pltpu.VMEM(tail, F32) for tail in tails]
    anywhere = pl.BlockSpec(memory_space=pl.ANY)
    inside = pl.BlockSpec(memory_space=pltpu.VMEM)
    return pl.pallas_call(
        functools.partial(scatter_kernel, count=count, split=split),
        out_shape=[jax.ShapeDtypeStruct(tail, F32) for tail in tails]
        + [jax.ShapeDtypeStruct(small.shape, F32), jax.ShapeDtypeStruct((8, 128), F32)],
        in_specs=[anywhere] * count + [inside],
        out_specs=[anywhere] * count + [inside, inside],
        scratch_shapes=own + core_in + one + one + two + two + up + up + results
        + [
            [pltpu.VMEM((1,) + small.shape, F32), pltpu.VMEM((1, 8, 128), F32)],
            [pltpu.VMEM((7,) + small.shape, F32), pltpu.VMEM((7, 8, 128), F32)],
            pltpu.SemaphoreType.DMA((count,)),
            pltpu.SemaphoreType.DMA((count, 13)),
            pltpu.SemaphoreType.DMA((count, 13)),
            pltpu.SemaphoreType.DMA((2, 6)),
            pltpu.SemaphoreType.DMA((2, 6)),
            pltpu.SemaphoreType.DMA((count,)),
        ],
        compiler_params=pltpu.CompilerParams(
            collective_id=collective_id, has_side_effects=True, vmem_limit_bytes=VMEM_BYTES
        ),
        name="scatter_grads",
    )(*grads, small)


def adam(master, first_moment, second_moment, gradient, clip_scale, rate, decay_rate):
    gradient = gradient * clip_scale
    first_new = BETA_ONE * first_moment + (1 - BETA_ONE) * gradient
    second_new = BETA_TWO * second_moment + (1 - BETA_TWO) * gradient * gradient
    update = (
        first_new / (1 - BETA_ONE**STEP) / (jnp.sqrt(second_new / (1 - BETA_TWO**STEP)) + ADAM_EPS)
    )
    return (master - rate * (update + decay_rate * master), first_new, second_new)


def squared(entry):
    return jnp.sum(entry * entry)


def per_device(
    pixels, coords, lengths, labels,
    patch_table, patch_first, patch_second,
    position_table, position_first, position_second,
    attend_in, attend_in_first, attend_in_second,
    attend_out, attend_out_first, attend_out_second,
    expand, expand_first, expand_second,
    shrink, shrink_first, shrink_second,
    classify, classify_first, classify_second,
    vectors, vectors_first, vectors_second,
    head_gains, head_gains_first, head_gains_second,
):
    packs, images = lengths.shape
    members = lax.axis_size("tensor")
    width = vectors.shape[1]
    share = attend_in.shape[0]
    seat = lax.axis_index("tensor")
    pack = jnp.minimum(seat, packs - 1).astype(jnp.int32)[None]
    valid = (seat < packs).astype(F32).reshape(1, 1)
    image_count = images * packs * lax.axis_size("dp")
    shards = (
        jnp.concatenate(
            [patch_table.T, jnp.transpose(position_table, (2, 0, 1)).reshape(share, -1)], axis=1
        ).astype(LOW),
        attend_in.reshape(share, -1).astype(LOW),
        attend_out.T.astype(LOW),
        expand.astype(LOW),
        shrink.T.astype(LOW),
        classify.astype(LOW),
    )
    both = ("tensor", "dp")
    close = lax.axis_size("dp") == 8 and members == 4
    if close:
        weights = gather_call(shards, (False, True, True, True, True, False), members, width, 0)
    else:

        def gather(shard):
            return lax.all_gather(shard, both, axis=0, tiled=True).reshape(members, width, -1)

        weights = (
            lax.all_gather(shards[0], "dp", axis=0, tiled=True),
            gather(shards[1]),
            gather(shards[2]),
            gather(shards[3]),
            gather(shards[4]),
            lax.all_gather(shards[5], "dp", axis=0, tiled=True),
        )
    grads, grad_vectors, grad_gains, loss_local = pack_step(
        pack, valid, pixels, coords, lengths, labels, weights, vectors, head_gains, image_count
    )
    if close:
        d_pp, d_in, d_out, d_up, d_dn, d_cls = grads
        small = jnp.zeros((16, width), F32)
        small = small.at[:4].set(grad_vectors)
        small = small.at[4, : grad_gains.size].set(grad_gains.reshape(-1))
        small = small.at[5].set(loss_local)
        cut = lambda entry: entry.reshape(entry.shape[:-2] + (2, 2, 2, share) + entry.shape[-1:])
        share_dn, share_up, share_out, share_cls, share_in, share_pp, small, squares = scatter_call(
            [cut(entry) for entry in (d_dn, d_up, d_out, d_cls, d_in, d_pp)],
            small,
            (True, True, True, False, True, False),
            1,
        )
        grad_vectors = small[:4]
        grad_gains = small[4, : head_gains.size].reshape(head_gains.shape)
        loss_total = small[5, 0]
        squares = squares[0, 0]
    else:
        grad_vectors, grad_gains, loss_total = lax.psum((grad_vectors, grad_gains, loss_local), both)

        def scatter(grad):
            return lax.psum_scatter(
                grad.reshape(members * width, -1), both, scatter_dimension=0, tiled=True
            ).astype(F32)

        def scatter_whole(grad):
            part = lax.psum_scatter(grad, "dp", scatter_dimension=0, tiled=True)
            return lax.psum(part, "tensor").astype(F32)

        share_pp = scatter_whole(grads[0])
        share_in, share_out, share_up, share_dn = (scatter(entry) for entry in grads[1:5])
        share_cls = scatter_whole(grads[5])
        leader = (seat == 0).astype(F32)
        split_squares = squared(share_in) + squared(share_out) + squared(share_up) + squared(share_dn)
        squares = lax.psum(split_squares + leader * (squared(share_pp) + squared(share_cls)), both)
    grad_norm = jnp.sqrt(squares + squared(grad_vectors) + squared(grad_gains))
    clip_scale = CLIP / jnp.maximum(grad_norm, CLIP)
    pixel_width = patch_table.shape[0]
    share_patch = share_pp[:, :pixel_width].T
    share_pos = jnp.transpose(
        share_pp[:, pixel_width:].reshape(share, position_table.shape[0], position_table.shape[1]), (1, 2, 0)
    )
    results = (
        adam(patch_table, patch_first, patch_second, share_patch, clip_scale, RATE_BASE, DECAY),
        adam(position_table, position_first, position_second, share_pos, clip_scale, RATE_POSITION, DECAY),
        adam(
            attend_in, attend_in_first, attend_in_second,
            share_in.reshape(attend_in.shape), clip_scale, RATE_BASE, DECAY,
        ),
        adam(attend_out, attend_out_first, attend_out_second, share_out.T, clip_scale, RATE_MIDDLE, DECAY),
        adam(expand, expand_first, expand_second, share_up, clip_scale, RATE_BASE, DECAY),
        adam(shrink, shrink_first, shrink_second, share_dn.T, clip_scale, RATE_BASE, DECAY),
        adam(classify, classify_first, classify_second, share_cls, clip_scale, RATE_MIDDLE, DECAY),
        adam(vectors, vectors_first, vectors_second, grad_vectors, clip_scale, RATE_VECTOR, 0.0),
        adam(head_gains, head_gains_first, head_gains_second, grad_gains, clip_scale, RATE_VECTOR, 0.0),
    )
    return tuple(entry for group in results for entry in group) + (loss_total, grad_norm)


def solution(mesh):
    data = P("dp", None)
    in_specs = (
        (data, P(None, "dp"), data, data)
        + (P(None, "dp"),) * 3
        + (P(None, None, "dp"),) * 3
        + (P("dp", None, "tensor"),) * 3
        + (P("tensor", "dp"),) * 3
        + (P("dp", "tensor"),) * 3
        + (P("tensor", "dp"),) * 3
        + (data,) * 3
        + (P(),) * 6
    )
    out_specs = in_specs[4:] + (P(), P())
    return jax.shard_map(per_device, mesh=mesh, in_specs=in_specs, out_specs=out_specs, check_vma=False)
```

```python
import functools

import jax
import jax.numpy as jnp
from jax import lax
from jax.experimental import pallas as pl
from jax.experimental.pallas import tpu as pltpu
from jax.sharding import PartitionSpec as P

STEP = 10
NORM_EPS = 1e-06
CLIP = 0.05
RATE_BASE = 0.03
RATE_POSITION = 0.2
RATE_MIDDLE = 0.1
RATE_VECTOR = 1.0
DECAY = 0.05
BETA_ONE = 0.5
BETA_TWO = 0.5
ADAM_EPS = 1e-08
SHIFT = -4.0
NEGATIVE = -1e30
APART = 128.0
LOW = jnp.bfloat16
F32 = jnp.float32
VMEM_BYTES = 56 * 1024 * 1024
TAIL_P = 0.3
TAIL = (
    0.1196293,
    0.12075397,
    0.09991341,
    0.12856192,
    -0.05368424,
    0.20635419,
    -0.1572035,
    0.03567488,
)


def mm(left, right):
    return lax.dot_general(left, right, (((1,), (0,)), ((), ())), preferred_element_type=F32)


def mm_nt(left, right):
    return lax.dot_general(left, right, (((1,), (1,)), ((), ())), preferred_element_type=F32)


def split_two(values):
    high = values.astype(LOW)
    return high, (values - high.astype(F32)).astype(LOW)


def split_three(values):
    high = values.astype(LOW)
    rest = values - high.astype(F32)
    middle = rest.astype(LOW)
    return high, middle, (rest - middle.astype(F32)).astype(LOW)


def row_norm(values):
    center = values - jnp.mean(values, axis=-1, keepdims=True)
    inverse = lax.rsqrt(jnp.mean(center * center, axis=-1, keepdims=True) + NORM_EPS)
    return center * inverse, inverse


def row_norm_back(gradient, gain_row, normed, inverse):
    scaled = gradient * gain_row
    return inverse * (
        scaled
        - jnp.mean(scaled, axis=-1, keepdims=True)
        - normed * jnp.mean(scaled * normed, axis=-1, keepdims=True)
    )


def half_mean_matrix(scale):
    row = lax.broadcasted_iota(jnp.int32, (128, 128), 0)
    col = lax.broadcasted_iota(jnp.int32, (128, 128), 1)
    return jnp.where((row >= 64) == (col >= 64), scale, 0.0).astype(LOW)


def half_sum(values, block):
    high, low = split_two(values)
    return mm(high, block) + mm(low, block)


def half_norm(values, block):
    center = values - half_sum(values, block)
    inverse = lax.rsqrt(half_sum(center * center, block) + NORM_EPS)
    return center * inverse, inverse


def half_norm_back(gradient, gain_row, normed, inverse, block):
    scaled = gradient * gain_row
    return inverse * (scaled - half_sum(scaled, block) - normed * half_sum(scaled * normed, block))


def gelu_pair(inner):
    size = jnp.abs(inner)
    near = 1.0 / (1.0 + TAIL_P * size)
    bell = jnp.exp(-0.5 * inner * inner)
    poly = TAIL[-1]
    for factor in TAIL[-2::-1]:
        poly = poly * near + factor
    tail = poly * near * bell
    share = jnp.where(inner >= 0, 1.0 - tail, tail)
    return inner * share, share + inner * bell * 0.3989422804014327


def embed_kernel(pack_ref, pix_ref, coord_ref, wp_ref, win_ref, gain_ref, emb_ref, h1_ref, q_ref, k_ref, v_ref):
    rows = pix_ref.shape[0]
    pixels = pix_ref.shape[1]
    groups = win_ref.shape[0]
    part = win_ref.shape[2] // 3
    spots = (wp_ref.shape[1] - pixels) // 2
    lane = lax.broadcasted_iota(jnp.int32, (rows, 2 * spots), 1)
    hot = ((lane == coord_ref[:, 0:1]) | (lane - spots == coord_ref[:, 1:2])).astype(F32).astype(LOW)
    embedded = mm_nt(pix_ref[...], wp_ref[:, :pixels]) + mm_nt(hot, wp_ref[:, pixels:])
    emb_ref[...] = embedded
    normed, _ = row_norm(embedded)
    first = (normed * gain_ref[0:1]).astype(LOW)
    h1_ref[...] = first
    parts = [mm(first, win_ref[group]) for group in range(groups)]
    q_ref[...] = jnp.concatenate([entry[:, :part] for entry in parts], axis=1)
    k_ref[...] = jnp.concatenate([entry[:, part : 2 * part] for entry in parts], axis=1)
    v_ref[...] = jnp.concatenate([entry[:, 2 * part :].astype(LOW) for entry in parts], axis=1)


def embed_call(pack, pixels, coords, w_pp, w_in, vectors, rows):
    width = vectors.shape[1]
    tile = 256
    steps = rows // tile
    whole2 = lambda i, p: (0, 0)
    tiled = pl.BlockSpec((tile, width), lambda i, p: (i, 0))
    return pl.pallas_call(
        embed_kernel,
        grid_spec=pltpu.PrefetchScalarGridSpec(
            num_scalar_prefetch=1,
            grid=(steps,),
            in_specs=[
                pl.BlockSpec((tile, pixels.shape[1]), lambda i, p: (p[0] * steps + i, 0)),
                pl.BlockSpec((tile, 2), lambda i, p: (p[0] * steps + i, 0)),
                pl.BlockSpec(w_pp.shape, whole2),
                pl.BlockSpec(w_in.shape, lambda i, p: (0, 0, 0)),
                pl.BlockSpec(vectors.shape, whole2),
            ],
            out_specs=[tiled] * 5,
        ),
        out_shape=[
            jax.ShapeDtypeStruct((rows, width), F32),
            jax.ShapeDtypeStruct((rows, width), LOW),
            jax.ShapeDtypeStruct((rows, width), F32),
            jax.ShapeDtypeStruct((rows, width), F32),
            jax.ShapeDtypeStruct((rows, width), LOW),
        ],
        compiler_params=pltpu.CompilerParams(vmem_limit_bytes=VMEM_BYTES),
        name="embed",
    )(pack, pixels, coords, w_pp, w_in, vectors)


def image_marks(bound_ref, rows):
    place = lax.broadcasted_iota(jnp.int32, (rows, 128), 0)
    return (place >= bound_ref[0:1, :]) & (place < bound_ref[1:2, :])


def half_lane(rows):
    lane = lax.broadcasted_iota(jnp.int32, (rows, 128), 1)
    return lane, jnp.where(lane >= 64, lane - 64, lane)


def attend_kernel(
    q_ref, k_ref, v_ref, gain_ref, bound_ref, o_ref, lse_ref, ka_ref, va_ref, qa_ref, between=None
):
    rows = q_ref.shape[0]
    tile = 256
    block = half_mean_matrix(1.0 / 64)
    lane, inner = half_lane(rows)
    marks = image_marks(bound_ref, rows)
    one = jnp.where(inner == 8, 1.0, 0.0)
    query_feature = jnp.where(marks, 1.0, one)
    key_feature = jnp.where(marks, APART, -APART * one)
    k_normed, _ = half_norm(k_ref[...], block)
    ka_ref[:, :128] = (k_normed * gain_ref[1:2]).astype(LOW)
    ka_ref[:, 128:] = key_feature.astype(LOW)
    va_ref[:, :128] = v_ref[...]
    va_ref[:, 128:] = jnp.ones((rows, 128), LOW)
    q_normed, _ = half_norm(q_ref[...], block)
    query = (q_normed * gain_ref[0:1]).astype(LOW).astype(F32) * 0.125
    for head in range(2):
        mine = (lane < 64) if head == 0 else (lane >= 64)
        qa_ref[head, :, :128] = jnp.where(mine, query, 0.0).astype(LOW)
        qa_ref[head, :, 128:] = jnp.where(mine, query_feature, 0.0).astype(LOW)
    keys = ka_ref[...]
    values = va_ref[...]
    first = lane[:tile] < 64
    for step in range(rows // tile):
        part = slice(step * tile, (step + 1) * tile)
        outs = []
        for head in range(2):
            score = mm_nt(qa_ref[head, part, :], keys)
            outs.append(mm(jnp.exp(score).astype(LOW), values))
        total = jnp.where(first, outs[0][:, 128:], outs[1][:, 128:])
        o_ref[part, :] = (jnp.where(first, outs[0][:, :128], outs[1][:, :128]) / total).astype(LOW)
        lse_ref[part, :] = jnp.log(total)
        if between is not None and step % 2 == 1:
            between(step // 2)


def attend_call(q_raw, k_raw, value, gains, bounds):
    rows, width = q_raw.shape
    pair = pl.BlockSpec((rows, 128), lambda j: (0, j))
    small = lambda a: pl.BlockSpec(a.shape, lambda j: (0, 0))
    return pl.pallas_call(
        attend_kernel,
        grid=(width // 128,),
        in_specs=[pair, pair, pair, small(gains), small(bounds)],
        out_specs=[pair, pair],
        out_shape=[
            jax.ShapeDtypeStruct((rows, width), LOW),
            jax.ShapeDtypeStruct((rows, width), F32),
        ],
        scratch_shapes=[
            pltpu.VMEM((rows, 256), LOW),
            pltpu.VMEM((rows, 256), LOW),
            pltpu.VMEM((2, rows, 256), LOW),
        ],
        compiler_params=pltpu.CompilerParams(vmem_limit_bytes=VMEM_BYTES),
        name="attend",
    )(q_raw, k_raw, value, gains, bounds)


def attend_back_kernel(
    q_ref, k_ref, v_ref, o_ref, lse_ref, do_ref, gain_ref, bound_ref,
    dq_ref, dk_ref, dv_ref, dgain_ref,
    ka_ref, va_ref, qa_ref, da_ref, qt_ref, dot_ref, dqs_ref, dkt_ref, dvt_ref,
    between=None,
):
    rows = q_ref.shape[0]
    tile = 256
    block = half_mean_matrix(1.0 / 64)
    block_sum = half_mean_matrix(1.0)
    lane, inner = half_lane(rows)
    marks = image_marks(bound_ref, rows)
    one = jnp.where(inner == 8, 1.0, 0.0)
    three = (inner >= 9) & (inner < 12)
    key_feature = jnp.where(marks, APART, jnp.where(three, 1.0, -APART * one))

    def spread(values):
        high, middle, low = split_three(values)
        return jnp.where(
            inner == 9, high.astype(F32), jnp.where(inner == 10, middle.astype(F32), low.astype(F32))
        )

    query_feature = jnp.where(three, spread(-lse_ref[...]), jnp.where(marks, 1.0, one))
    k_normed, k_inverse = half_norm(k_ref[...], block)
    ka_ref[:, :128] = (k_normed * gain_ref[1:2]).astype(LOW)
    ka_ref[:, 128:] = key_feature.astype(LOW)
    va_ref[:, :128] = v_ref[...]
    va_ref[:, 128:] = jnp.where(three, 1.0, 0.0).astype(LOW)
    q_normed, q_inverse = half_norm(q_ref[...], block)
    query = (q_normed * gain_ref[0:1]).astype(LOW).astype(F32)
    qt_ref[...] = jnp.transpose(query).astype(LOW)
    query = query * 0.125
    above = do_ref[...].astype(F32)
    dot_ref[...] = jnp.transpose(above).astype(LOW)
    inside = half_sum(above * o_ref[...].astype(F32), block_sum)
    above_feature = jnp.where(three, spread(inside * -0.125), 0.0)
    above = above * 0.125
    for head in range(2):
        mine = (lane < 64) if head == 0 else (lane >= 64)
        qa_ref[head, :, :128] = jnp.where(mine, query, 0.0).astype(LOW)
        qa_ref[head, :, 128:] = jnp.where(mine, query_feature, 0.0).astype(LOW)
        da_ref[head, :, :128] = jnp.where(mine, above, 0.0).astype(LOW)
        da_ref[head, :, 128:] = jnp.where(mine, above_feature, 0.0).astype(LOW)
    keys = ka_ref[...]
    values = va_ref[...]
    key_low = ka_ref[:, :128]
    first = lane[:tile] < 64
    for step in range(rows // tile):
        part = slice(step * tile, (step + 1) * tile)
        outs = []
        for head in range(2):
            mine = slice(64 * head, 64 * head + 64)
            prob = jnp.exp(mm_nt(qa_ref[head, part, :], keys))
            d_prob = mm_nt(da_ref[head, part, :], values)
            d_score = (prob * d_prob).astype(LOW)
            outs.append(mm(d_score, key_low))
            d_key = mm(qt_ref[mine, part], d_score)
            d_value = mm(dot_ref[mine, part], prob.astype(LOW))
            if step == 0:
                dkt_ref[mine, :] = d_key
                dvt_ref[mine, :] = d_value
            else:
                dkt_ref[mine, :] += d_key
                dvt_ref[mine, :] += d_value
        dqs_ref[part, :] = jnp.where(first, outs[0], outs[1])
        if between is not None and step % 2 == 1:
            between(step // 2)
    d_query = dqs_ref[...]
    d_key = jnp.transpose(dkt_ref[...])
    dv_ref[...] = jnp.transpose(dvt_ref[...]).astype(LOW)
    dq_ref[...] = half_norm_back(d_query, gain_ref[0:1], q_normed, q_inverse, block).astype(LOW)
    dk_ref[...] = half_norm_back(d_key, gain_ref[1:2], k_normed, k_inverse, block).astype(LOW)
    dgain_ref[0, 0:1] = jnp.sum(d_query * q_normed, axis=0, keepdims=True)
    dgain_ref[0, 1:2] = jnp.sum(d_key * k_normed, axis=0, keepdims=True)


ATTEND_BACK_SCRATCH = 9


def attend_back_scratch(rows):
    return [
        pltpu.VMEM((rows, 256), LOW),
        pltpu.VMEM((rows, 256), LOW),
        pltpu.VMEM((2, rows, 256), LOW),
        pltpu.VMEM((2, rows, 256), LOW),
        pltpu.VMEM((128, rows), LOW),
        pltpu.VMEM((128, rows), LOW),
        pltpu.VMEM((rows, 128), F32),
        pltpu.VMEM((128, rows), F32),
        pltpu.VMEM((128, rows), F32),
    ]


def attend_back_sum_kernel(*refs):
    inputs, grads, dout_ref, before_ref = refs[:8], refs[8], refs[9], refs[10]
    outputs, share_ref, out_ref = refs[11:15], refs[15], refs[16]
    scratch, rest = refs[17 : 17 + ATTEND_BACK_SCRATCH], refs[17 + ATTEND_BACK_SCRATCH :]
    mlp_own, mlp_load, mlp_refs = rest[0], rest[1], rest[2:9]
    out_own, out_load, out_refs = rest[9], rest[10], rest[11:18]
    step = pl.program_id(0)
    seat = Seat()
    c = seat.c
    mlp = Flow(
        seat, lambda i: lax.rem(4 - lax.div(i, 2), 4), lambda i: mlp_own.at[i], *mlp_refs[:5], mlp_refs[5:]
    )
    out = Flow(seat, lambda i: i, lambda i: out_own.at[i], *out_refs[:5], out_refs[5:])
    chunks, levels = mlp_own.shape[0], out_own.shape[0]

    def mlp_at(i):
        return lax.rem(i, 2) * 3 + lax.div(i, 2)

    def mlp_loading(i):
        return pltpu.make_async_copy(grads.at[mlp_at(i), :, :, c], mlp_own.at[i], mlp_load.at[i])

    def mlp_to_core(i):
        return mlp.to_core(i, grads.at[mlp_at(i), :, :, 1 - c])

    def out_loading(i):
        return pltpu.make_async_copy(dout_ref.at[i, :, :, c], out_own.at[i], out_load.at[i])

    def out_to_core(i):
        return out.to_core(i, dout_ref.at[i, :, :, 1 - c])

    def every(count, action):
        lax.fori_loop(0, count, lambda i, carry: (action(i), carry)[1], 0)

    @pl.when(step == 0)
    def _():
        every(chunks, lambda i: mlp_loading(i).start())
        every(levels, lambda i: out_loading(i).start())
        greet(seat, 4)
        every(chunks, lambda i: mlp_to_core(i).start())
        every(levels, lambda i: out_to_core(i).start())
        share_ref[...] = before_ref[...]

    def mlp_one(i):
        mlp_loading(i).wait()
        mlp_to_core(i).wait_recv()
        mlp.one(i)

    def mlp_last(i):
        @pl.when(mlp.level_of(i) == seat.z)
        def _():
            share_ref[lax.rem(i, 2)] = mlp.total(i)

    def out_one(i):
        out_loading(i).wait()
        out_to_core(i).wait_recv()
        out.one(i)

    def out_last(i):
        @pl.when(out.level_of(i) == seat.z)
        def _():
            out_ref[...] = out.total(i)

    def pair(action, number):
        return lambda: every(2, lambda i: action(2 * number + i))

    hop_one, hop_two = (functools.partial(mlp.hop, reach=reach) for reach in (1, 2))
    out_hop_one, out_hop_two = (functools.partial(out.hop, reach=reach) for reach in (1, 2))
    plan = {
        0: [pair(mlp_one, 0)],
        1: [lambda: every(levels, out_one)],
        2: [pair(mlp.two, 0), pair(mlp_one, 1)],
        3: [lambda: every(levels, out.two)],
        4: [pair(mlp.three, 0)],
        5: [pair(mlp.two, 1), pair(mlp_one, 2)],
        6: [pair(hop_one, 0), lambda: every(levels, out.three)],
        7: [pair(mlp.three, 1), lambda: every(levels, out_hop_one)],
        8: [pair(mlp.two, 2), pair(hop_two, 0)],
        9: [pair(hop_one, 1), lambda: every(levels, out_hop_two)],
        10: [pair(mlp.three, 2)],
        11: [pair(hop_two, 1), pair(hop_one, 2)],
    }

    def between(slot):
        for number, actions in plan.items():
            if number % 2 == slot:

                @pl.when(2 * step + slot == number)
                def _():
                    for action in actions:
                        action()

    attend_back_kernel(*inputs, *outputs, *scratch, between=between)

    @pl.when(step == pl.num_programs(0) - 1)
    def _():
        every(chunks, mlp_last)
        every(levels, out_last)

        def drain(i):
            mlp_to_core(i).wait_send()
            mlp.drain(i)

        def out_drain(i):
            out_to_core(i).wait_send()
            out.drain(i)

        every(chunks, drain)
        every(levels, out_drain)


def attend_back_sum_call(
    q_raw, k_raw, value, attended, lse, d_attended, gains, bounds, grads, d_out, before, collective_id
):
    rows, width = q_raw.shape
    pairs = width // 128
    share, cols = grads.shape[-2:]
    pair = pl.BlockSpec((rows, 128), lambda j: (0, j))
    small = lambda a: pl.BlockSpec(a.shape, lambda j: (0,) * a.ndim)
    anywhere = pl.BlockSpec(memory_space=pl.ANY)
    low = jax.ShapeDtypeStruct((rows, width), LOW)

    def scratch(chunks, cols):
        own = [pltpu.VMEM((chunks, 2, 2, share, cols), LOW), pltpu.SemaphoreType.DMA((chunks,))]
        return own + flow_scratch(chunks, share, cols)

    return pl.pallas_call(
        attend_back_sum_kernel,
        grid=(pairs,),
        in_specs=[pair] * 6 + [small(gains), small(bounds), anywhere, anywhere, small(before)],
        out_specs=[
            pair, pair, pair,
            pl.BlockSpec((1, 2, 128), lambda j: (j, 0, 0)),
            small(before),
            pl.BlockSpec((share, d_out.shape[-1]), lambda j: (0, 0)),
        ],
        out_shape=[
            low, low, low,
            jax.ShapeDtypeStruct((pairs, 2, 128), F32),
            jax.ShapeDtypeStruct(before.shape, F32),
            jax.ShapeDtypeStruct((share, d_out.shape[-1]), F32),
        ],
        scratch_shapes=attend_back_scratch(rows)
        + scratch(grads.shape[0], cols)
        + scratch(d_out.shape[0], d_out.shape[-1]),
        compiler_params=pltpu.CompilerParams(
            collective_id=collective_id, has_side_effects=True, vmem_limit_bytes=VMEM_BYTES
        ),
        name="attend_back_sum",
    )(q_raw, k_raw, value, attended, lse, d_attended, gains, bounds, grads, d_out, before)


def attend_back_call(q_raw, k_raw, value, attended, lse, d_attended, gains, bounds):
    rows, width = q_raw.shape
    pairs = width // 128
    pair = pl.BlockSpec((rows, 128), lambda j: (0, j))
    small = lambda a: pl.BlockSpec(a.shape, lambda j: (0, 0))
    low = jax.ShapeDtypeStruct((rows, width), LOW)
    return pl.pallas_call(
        attend_back_kernel,
        grid=(pairs,),
        in_specs=[pair] * 6 + [small(gains), small(bounds)],
        out_specs=[pair, pair, pair, pl.BlockSpec((1, 2, 128), lambda j: (j, 0, 0))],
        out_shape=[low, low, low, jax.ShapeDtypeStruct((pairs, 2, 128), F32)],
        scratch_shapes=attend_back_scratch(rows),
        compiler_params=pltpu.CompilerParams(vmem_limit_bytes=VMEM_BYTES),
        name="attend_back",
    )(q_raw, k_raw, value, attended, lse, d_attended, gains, bounds)


def mlp_kernel(o_ref, emb_ref, wout_ref, wup_ref, wdn_ref, vec_ref, x1_ref, h2_ref, act_ref, slope_ref, x2_ref):
    step = pl.program_id(0)
    rows, _ = o_ref.shape
    groups, _, part = wout_ref.shape
    tile = 256

    @pl.when(step == 0)
    def _():
        for at in range(rows // tile):
            span = slice(at * tile, (at + 1) * tile)
            branch = mm_nt(o_ref[span, :part], wout_ref[0])
            for group in range(1, groups):
                branch += mm_nt(o_ref[span, group * part : (group + 1) * part], wout_ref[group])
            middle = emb_ref[span, :] + branch
            x1_ref[span, :] = middle
            x2_ref[span, :] = middle
            normed, _ = row_norm(middle)
            h2_ref[span, :] = (normed * vec_ref[1:2]).astype(LOW)

    for at in range(rows // tile):
        span = slice(at * tile, (at + 1) * tile)
        active, slope = gelu_pair(mm(h2_ref[span, :], wup_ref[0]))
        active = active.astype(LOW)
        act_ref[span, :] = active
        slope_ref[span, :] = slope.astype(LOW)
        x2_ref[span, :] += mm_nt(active, wdn_ref[0])


def mlp_call(attended, embedded, w_out, w_up, w_dn, vectors):
    rows, width = embedded.shape
    groups, _, per = w_up.shape
    chunk = per // 2
    hidden = groups * per
    whole = lambda a: pl.BlockSpec(a.shape, lambda j: (0,) * a.ndim)
    weight = pl.BlockSpec((1, width, chunk), lambda j: (j // 2, 0, j % 2))
    full = pl.BlockSpec((rows, width), lambda j: (0, 0))
    piece = pl.BlockSpec((rows, chunk), lambda j: (0, j))
    return pl.pallas_call(
        mlp_kernel,
        grid=(hidden // chunk,),
        in_specs=[whole(attended), whole(embedded), whole(w_out), weight, weight, whole(vectors)],
        out_specs=[full, full, piece, piece, full],
        out_shape=[
            jax.ShapeDtypeStruct((rows, width), F32),
            jax.ShapeDtypeStruct((rows, width), LOW),
            jax.ShapeDtypeStruct((rows, hidden), LOW),
            jax.ShapeDtypeStruct((rows, hidden), LOW),
            jax.ShapeDtypeStruct((rows, width), F32),
        ],
        compiler_params=pltpu.CompilerParams(vmem_limit_bytes=VMEM_BYTES),
        name="mlp",
    )(attended, embedded, w_out, w_up, w_dn, vectors)


def pool_kernel(
    pack_ref, x2_ref, label_ref, wcls_ref, vec_ref, bound_ref, valid_ref,
    dx2_ref, dcls_ref, loss_ref, dvec_ref,
    norm_ref, inv_ref,
    *, images, image_count,
):
    rows, width = x2_ref.shape
    tile = 256
    root = width**0.5
    gain = vec_ref[2:3]
    query = vec_ref[3:4]
    lane = lax.broadcasted_iota(jnp.int32, (rows, 128), 1)
    marks = image_marks(bound_ref, rows) & (lane < 64)
    logits = []
    for at in range(rows // tile):
        span = slice(at * tile, (at + 1) * tile)
        normed, inverse = row_norm(x2_ref[span, :])
        norm_ref[span, :] = normed
        inv_ref[span, :] = jnp.broadcast_to(inverse, (tile, 128))
        logits.append(jnp.sum(normed * gain * query, axis=-1, keepdims=True) / root)
    logit = jnp.concatenate(logits, axis=0)
    masked = jnp.where(marks, logit, NEGATIVE)
    grown = jnp.exp(masked - jnp.max(masked, axis=0, keepdims=True))
    shares = jnp.where(marks, grown / jnp.sum(grown, axis=0, keepdims=True), 0.0)
    weight = jnp.sum(shares, axis=-1, keepdims=True)
    member = jnp.transpose(marks.astype(F32))[:16].astype(LOW)
    pooled = jnp.zeros((16, width), F32)
    for at in range(rows // tile):
        span = slice(at * tile, (at + 1) * tile)
        for entry in split_three(norm_ref[span, :] * gain * weight[span]):
            pooled += mm(member[:, span], entry)
    pooled_low = pooled.astype(LOW)
    scores = mm(pooled_low, wcls_ref[...])[:images] + SHIFT
    target = label_ref[...].astype(F32)
    valid = valid_ref[0, 0]
    soft = jnp.maximum(scores, 0.0) + jnp.log1p(jnp.exp(-jnp.abs(scores)))
    loss_rows = jnp.sum(soft - target * scores, axis=-1, keepdims=True)
    loss_ref[...] = jnp.broadcast_to(jnp.sum(loss_rows, axis=0, keepdims=True) * valid, loss_ref.shape)
    d_score = (1.0 / (1.0 + jnp.exp(-scores)) - target) / image_count * valid
    d_score = jnp.concatenate([d_score, jnp.zeros((16 - images, d_score.shape[1]), F32)], axis=0).astype(LOW)
    dcls_ref[...] = mm(jnp.transpose(pooled).astype(LOW), d_score).astype(LOW)
    d_pooled = mm_nt(d_score, wcls_ref[...])[:images]
    parts = jnp.concatenate(
        [entry.astype(F32) for entry in split_three(d_pooled)]
        + [jnp.zeros((128 - 3 * images, width), F32)],
        axis=0,
    ).astype(LOW)
    marks_f = marks.astype(F32)
    thrice = (
        marks_f + pltpu.roll(marks_f, images, 1) + pltpu.roll(marks_f, 2 * images, 1)
    ).astype(LOW)
    d_weights = []
    for at in range(rows // tile):
        span = slice(at * tile, (at + 1) * tile)
        spread = mm(thrice[span], parts)
        dx2_ref[span, :] = spread
        d_weights.append(jnp.sum(spread * (norm_ref[span, :] * gain), axis=-1, keepdims=True))
    d_weight = jnp.concatenate(d_weights, axis=0)
    inside = jnp.sum(shares * d_weight, axis=0, keepdims=True)
    d_logit = weight * (d_weight - jnp.sum(marks_f * inside, axis=-1, keepdims=True))
    gain_sum = jnp.zeros((1, width), F32)
    query_sum = jnp.zeros((1, width), F32)
    for at in range(rows // tile):
        span = slice(at * tile, (at + 1) * tile)
        normed = norm_ref[span, :]
        inverse = inv_ref[span, 0:1]
        d_last = dx2_ref[span, :] * weight[span] + d_logit[span] * (query / root)
        gain_sum += jnp.sum(d_last * normed, axis=0, keepdims=True)
        query_sum += jnp.sum(d_logit[span] * normed, axis=0, keepdims=True)
        dx2_ref[span, :] = row_norm_back(d_last, gain, normed, inverse)
    dvec_ref[0:1, :] = gain_sum
    dvec_ref[1:2, :] = query_sum * gain / root


def pool_call(pack, x2, labels, w_cls, vectors, bounds, valid, images, image_count):
    rows, width = x2.shape
    classes = labels.shape[1]
    whole = lambda a: pl.BlockSpec(a.shape, lambda j, p: (0,) * a.ndim)
    full = lambda *shape: pl.BlockSpec(shape, lambda j, p: (0,) * len(shape))
    return pl.pallas_call(
        functools.partial(pool_kernel, images=images, image_count=image_count),
        grid_spec=pltpu.PrefetchScalarGridSpec(
            num_scalar_prefetch=1,
            grid=(1,),
            in_specs=[
                whole(x2),
                pl.BlockSpec((images, classes), lambda j, p: (p[0], 0)),
                whole(w_cls),
                whole(vectors),
                whole(bounds),
                pl.BlockSpec(memory_space=pltpu.SMEM),
            ],
            out_specs=[full(rows, width), full(width, classes), full(8, 128), full(2, width)],
            scratch_shapes=[pltpu.VMEM((rows, width), F32), pltpu.VMEM((rows, 128), F32)],
        ),
        out_shape=[
            jax.ShapeDtypeStruct((rows, width), F32),
            jax.ShapeDtypeStruct((width, classes), LOW),
            jax.ShapeDtypeStruct((8, 128), F32),
            jax.ShapeDtypeStruct((2, width), F32),
        ],
        compiler_params=pltpu.CompilerParams(vmem_limit_bytes=VMEM_BYTES),
        name="pool",
    )(pack, x2, labels, w_cls, vectors, bounds, valid)


def mlp_back_kernel(
    dx2_ref, act_ref, slope_ref, h2_ref, x1_ref, o_ref, wout_ref, wup_ref, wdn_ref, vec_ref,
    dmlp_ref, dout_ref, do_ref, dmid_ref, dvec_ref,
    low_ref, lowt_ref, h2t_ref, acc_ref, dh_ref,
    keep=None, between=None,
):
    step = pl.program_id(0)
    rows, width = dx2_ref.shape
    groups, _, part = wout_ref.shape
    tile = 256

    @pl.when(step == 0)
    def _():
        for at in range(rows // tile):
            span = slice(at * tile, (at + 1) * tile)
            values = dx2_ref[span, :]
            low_ref[span, :] = values.astype(LOW)
            lowt_ref[:, span] = jnp.transpose(values).astype(LOW)
            h2t_ref[:, span] = jnp.transpose(h2_ref[span, :].astype(F32)).astype(LOW)
            acc_ref[span, :] = jnp.zeros((tile, width), F32)

    for at in range(rows // tile):
        span = slice(at * tile, (at + 1) * tile)
        d_hidden = (mm(low_ref[span, :], wdn_ref[0]) * slope_ref[span, :].astype(F32)).astype(LOW)
        dh_ref[span, :] = d_hidden
        acc_ref[span, :] += mm_nt(d_hidden, wup_ref[0])

    def grads(put):
        for at in range(width // 192):
            span = slice(at * 192, (at + 1) * 192)
            put(0, at, mm(lowt_ref[span, :], act_ref[...]).astype(LOW))
            put(1, at, mm(h2t_ref[span, :], dh_ref[...]).astype(LOW))

    def put_out(kind, at, value):
        dmlp_ref[kind, 0, at * 192 : (at + 1) * 192, :] = value

    if keep is None:
        grads(put_out)
    else:
        pl.when(step < 2)(lambda: grads(keep))
        pl.when(step >= 2)(lambda: grads(put_out))
        between(step)

    @pl.when(step == pl.num_programs(0) - 1)
    def _():
        gain = vec_ref[1:2]
        gain_sum = jnp.zeros((1, width), F32)
        for at in range(rows // tile):
            span = slice(at * tile, (at + 1) * tile)
            normed, inverse = row_norm(x1_ref[span, :])
            d_second = acc_ref[span, :]
            gain_sum += jnp.sum(d_second * normed, axis=0, keepdims=True)
            d_middle = dx2_ref[span, :] + row_norm_back(d_second, gain, normed, inverse)
            dmid_ref[span, :] = d_middle
            low = d_middle.astype(LOW)
            lowt_ref[:, span] = jnp.transpose(d_middle).astype(LOW)
            do_ref[span, :] = jnp.concatenate(
                [mm(low, wout_ref[group]) for group in range(groups)], axis=1
            ).astype(LOW)
        dvec_ref[...] = gain_sum
        for group in range(groups):
            piece = o_ref[:, group * part : (group + 1) * part]
            for at in range(width // tile):
                span = slice(at * tile, (at + 1) * tile)
                dout_ref[group, span, :] = mm(lowt_ref[span, :], piece).astype(LOW)


def mlp_back_call(dx2, active, slope, h2, x1, attended, w_out, w_up, w_dn, vectors):
    rows, width = dx2.shape
    groups, _, per = w_up.shape
    chunk = per // 2
    hidden = groups * per
    whole = lambda a: pl.BlockSpec(a.shape, lambda j: (0,) * a.ndim, pipeline_mode=pl.Buffered(1))
    weight = pl.BlockSpec((1, width, chunk), lambda j: (j // 2, 0, j % 2))
    piece = pl.BlockSpec((rows, chunk), lambda j: (0, j))
    full = lambda *shape: pl.BlockSpec(shape, lambda j: (0,) * len(shape))
    return pl.pallas_call(
        mlp_back_kernel,
        grid=(hidden // chunk,),
        in_specs=[
            whole(dx2), piece, piece, whole(h2), whole(x1), whole(attended), whole(w_out),
            weight, weight, whole(vectors),
        ],
        out_specs=[
            pl.BlockSpec((2, 1, width, chunk), lambda j: (0, j // 2, 0, j % 2)),
            full(*w_out.shape),
            full(rows, width),
            full(rows, width),
            full(1, width),
        ],
        out_shape=[
            jax.ShapeDtypeStruct((2,) + w_up.shape, LOW),
            jax.ShapeDtypeStruct(w_out.shape, LOW),
            jax.ShapeDtypeStruct((rows, width), LOW),
            jax.ShapeDtypeStruct((rows, width), F32),
            jax.ShapeDtypeStruct((1, width), F32),
        ],
        scratch_shapes=[
            pltpu.VMEM((rows, width), LOW),
            pltpu.VMEM((width, rows), LOW),
            pltpu.VMEM((width, rows), LOW),
            pltpu.VMEM((rows, width), F32),
            pltpu.VMEM((rows, chunk), LOW),
        ],
        compiler_params=pltpu.CompilerParams(vmem_limit_bytes=VMEM_BYTES),
        name="mlp_back",
    )(dx2, active, slope, h2, x1, attended, w_out, w_up, w_dn, vectors)


def embed_back_kernel(
    pack_ref, dq_ref, dk_ref, dv_ref, h1_ref, emb_ref, dmid_ref, pix_ref, coord_ref, win_ref, vec_ref,
    din_ref, dpp_ref, dvec_ref,
    h1t_ref, join_ref, acc_ref,
):
    step = pl.program_id(0)
    rows, width = h1_ref.shape
    groups = pl.num_programs(0)
    part = win_ref.shape[2] // 3
    tile = 256

    @pl.when(step == 0)
    def _():
        for at in range(rows // tile):
            span = slice(at * tile, (at + 1) * tile)
            h1t_ref[:, span] = jnp.transpose(h1_ref[span, :].astype(F32)).astype(LOW)
            acc_ref[span, :] = jnp.zeros((tile, width), F32)

    for group in range(width // part):

        @pl.when(step == group)
        def _():
            mine = slice(group * part, (group + 1) * part)
            join_ref[...] = jnp.concatenate([dq_ref[:, mine], dk_ref[:, mine], dv_ref[:, mine]], axis=1)

    for at in range(rows // tile):
        span = slice(at * tile, (at + 1) * tile)
        acc_ref[span, :] += mm_nt(join_ref[span, :], win_ref[0])
    for at in range(width // tile):
        span = slice(at * tile, (at + 1) * tile)
        din_ref[0, span, :] = mm(h1t_ref[span, :], join_ref[...]).astype(LOW)

    @pl.when(step == groups - 1)
    def _():
        gain = vec_ref[0:1]
        pixels = pix_ref.shape[1]
        spots = (dpp_ref.shape[1] - pixels) // 2
        gain_sum = jnp.zeros((1, width), F32)
        for at in range(rows // tile):
            span = slice(at * tile, (at + 1) * tile)
            normed, inverse = row_norm(emb_ref[span, :])
            d_first = acc_ref[span, :]
            gain_sum += jnp.sum(d_first * normed, axis=0, keepdims=True)
            d_embed = dmid_ref[span, :] + row_norm_back(d_first, gain, normed, inverse)
            h1t_ref[:, span] = jnp.transpose(d_embed).astype(LOW)
        dvec_ref[...] = gain_sum
        lane = lax.broadcasted_iota(jnp.int32, (rows, 2 * spots), 1)
        hot = ((lane == coord_ref[:, 0:1]) | (lane - spots == coord_ref[:, 1:2])).astype(F32).astype(LOW)
        for at in range(width // tile):
            span = slice(at * tile, (at + 1) * tile)
            dpp_ref[span, :pixels] = mm(h1t_ref[span, :], pix_ref[...]).astype(LOW)
            dpp_ref[span, pixels:] = mm(h1t_ref[span, :], hot).astype(LOW)


def embed_back_call(pack, dq, dk, dv, h1, embedded, d_middle, pixels, coords, w_in, w_pp_shape, vectors):
    rows, width = h1.shape
    groups = w_in.shape[0]
    whole = lambda a: pl.BlockSpec(a.shape, lambda j, p: (0,) * a.ndim, pipeline_mode=pl.Buffered(1))
    full = lambda *shape: pl.BlockSpec(shape, lambda j, p: (0,) * len(shape))
    weight = pl.BlockSpec((1,) + w_in.shape[1:], lambda j, p: (j, 0, 0))
    return pl.pallas_call(
        embed_back_kernel,
        grid_spec=pltpu.PrefetchScalarGridSpec(
            num_scalar_prefetch=1,
            grid=(groups,),
            in_specs=[
                whole(dq), whole(dk), whole(dv), whole(h1), whole(embedded), whole(d_middle),
                pl.BlockSpec((rows, pixels.shape[1]), lambda j, p: (p[0], 0)),
                pl.BlockSpec((rows, 2), lambda j, p: (p[0], 0)),
                weight,
                whole(vectors),
            ],
            out_specs=[weight, full(*w_pp_shape), full(1, width)],
            scratch_shapes=[
                pltpu.VMEM((width, rows), LOW),
                pltpu.VMEM((rows, w_in.shape[2]), LOW),
                pltpu.VMEM((rows, width), F32),
            ],
        ),
        out_shape=[
            jax.ShapeDtypeStruct(w_in.shape, LOW),
            jax.ShapeDtypeStruct(w_pp_shape, LOW),
            jax.ShapeDtypeStruct((1, width), F32),
        ],
        compiler_params=pltpu.CompilerParams(vmem_limit_bytes=VMEM_BYTES),
        name="embed_back",
    )(pack, dq, dk, dv, h1, embedded, d_middle, pixels, coords, w_in, vectors)


def pack_step(pack, valid, pixels, coords, lengths, labels, weights, vectors, head_gains, image_count, close=False):
    w_pp, w_in, w_out, w_up, w_dn, w_cls = weights
    packs, images = lengths.shape
    rows = pixels.shape[0] // packs
    width = vectors.shape[1]
    mine = lax.dynamic_index_in_dim(lengths, pack[0], 0, keepdims=False)
    ends = jnp.cumsum(mine)
    fill = jnp.full((64 - images,), 1 << 30, jnp.int32)
    starts = jnp.concatenate([ends - mine, fill])
    ends = jnp.concatenate([ends, fill])
    bounds = jnp.stack([jnp.tile(starts, 2), jnp.tile(ends, 2)])
    gains = jnp.tile(head_gains, (1, 2))
    if close:
        embedded, h1, q_raw, k_raw, value, attended, lse, w_in, w_out, w_up, w_dn, w_cls = forward_call(
            weights, pixels, coords, vectors, gains, bounds, packs, 0
        )
    else:
        places = coords.T
        embedded, h1, q_raw, k_raw, value = embed_call(pack, pixels, places, w_pp, w_in, vectors, rows)
        attended, lse = attend_call(q_raw, k_raw, value, gains, bounds)
    x1, h2, active, slope, x2 = mlp_call(attended, embedded, w_out, w_up, w_dn, vectors)
    dx2, d_cls, loss, dvec_pool = pool_call(
        pack, x2, labels, w_cls, vectors, bounds, valid, images, image_count
    )
    if close:
        share = width // 8
        cut = lambda entry: entry.reshape(entry.shape[:-2] + (2, 2, 2, share) + entry.shape[-1:])
        d_mlp, d_out, d_attended, d_middle, dvec_two, share_mlp, share_cls = mlp_back_sum_call(
            dx2, active, slope, h2, x1, attended, w_out, w_up, w_dn, vectors, cut(d_cls), 1
        )
        d_mlp = d_mlp.reshape((-1, 2, 2, 2, share, width))
        dq, dk, dv, d_gain, share_mlp, share_out = attend_back_sum_call(
            q_raw, k_raw, value, attended, lse, d_attended, gains, bounds, d_mlp, cut(d_out), share_mlp, 2
        )
        d_gain = jnp.sum(d_gain.reshape(-1, 2, 2, 64), axis=(0, 2))
        small = jnp.concatenate(
            [
                jnp.zeros_like(dvec_two),
                dvec_two,
                dvec_pool,
                jnp.pad(d_gain.reshape(1, -1), ((0, 0), (0, width - d_gain.size))),
                jnp.broadcast_to(loss[0:1, 0:1], (1, width)),
                jnp.zeros((2, width), F32),
            ],
            axis=0,
        )
        share_in, share_pp, small, squares = embed_back_sum_call(
            dq, dk, dv, h1, embedded, d_middle,
            pixels, coords, w_in, w_pp.shape[1], vectors, small, share_mlp, share_cls, share_out, packs, 3,
        )
        shares = (share_pp, share_in, share_out, share_mlp[1], share_mlp[0], share_cls)
        return shares, small[:4], small[4, : d_gain.size].reshape(d_gain.shape), small[5, 0], squares[0, 0]
    d_mlp, d_out, d_attended, d_middle, dvec_two = mlp_back_call(
        dx2, active, slope, h2, x1, attended, w_out, w_up, w_dn, vectors
    )
    d_vec = jnp.concatenate([jnp.zeros_like(dvec_two), dvec_two, dvec_pool], axis=0)
    dq, dk, dv, d_gain = attend_back_call(q_raw, k_raw, value, attended, lse, d_attended, gains, bounds)
    d_in, d_pp, dvec_one = embed_back_call(
        pack, dq, dk, dv, h1, embedded, d_middle, pixels, places, w_in, w_pp.shape, vectors
    )
    d_gains = jnp.sum(d_gain.reshape(-1, 2, 2, 64), axis=(0, 2))
    return (d_pp, d_in, d_out, d_mlp[1], d_mlp[0], d_cls), d_vec.at[0].set(dvec_one[0]), d_gains, loss[0, 0], None


MESH = pl.DeviceIdType.MESH


class Seat:
    def __init__(self):
        self.me = lax.axis_index("dp")
        self.z = lax.axis_index("tensor")
        self.c = lax.rem(self.me, 2)
        self.x = lax.rem(lax.div(self.me, 2), 2)
        self.y = lax.div(self.me, 4)
        self.core = self.me + 1 - 2 * self.c
        self.xn = self.me + 2 - 4 * self.x
        self.yn = self.me + 4 - 8 * self.y
        self.diag = self.xn + 4 - 8 * self.y


def link(src, dst, sems, at, device):
    return pltpu.make_async_remote_copy(
        src_ref=src,
        dst_ref=dst,
        send_sem=sems[0].at[at],
        recv_sem=sems[1].at[at],
        device_id=device,
        device_id_type=MESH,
    )


def greet(seat, depth):
    barrier = pltpu.get_barrier_semaphore()
    for ahead in range(1, 8):
        pl.semaphore_signal(
            barrier, inc=1, device_id={"dp": lax.rem(seat.me + ahead, 8)}, device_id_type=MESH
        )
    for ahead in range(1, depth):
        pl.semaphore_signal(
            barrier, inc=1, device_id={"tensor": lax.rem(seat.z + ahead, depth)}, device_id_type=MESH
        )
    pl.semaphore_wait(barrier, 6 + depth)


class Gather:
    def __init__(self, seat, shards, outs, split, units, own_sem, sems):
        self.seat, self.shards, self.outs, self.split, self.units = seat, shards, outs, split, units
        self.own_sem, self.sems = own_sem, sems
        self.share = shards[0].shape[0]

    def rows(self, owner):
        return pl.ds(pl.multiple_of(owner * self.share, self.share), self.share)

    def column(self, u, owner):
        k, cols = self.units[u]
        if self.split[k]:
            return self.outs[k].at[:, self.rows(owner), cols]
        return self.outs[k].at[self.rows(owner), cols]

    def halves(self, u, owner, which):
        k, cols = self.units[u]
        if self.split[k]:
            return self.outs[k].at[2 * which : 2 * which + 2, self.rows(owner), cols]
        half = self.share // 2
        start = pl.multiple_of(owner * self.share + which * half, half)
        return self.outs[k].at[pl.ds(start, half), cols]

    def block(self, u, level):
        k, cols = self.units[u]
        return self.outs[k].at[level, self.rows(self.seat.me), cols]

    def keep(self, u):
        k, cols = self.units[u]
        mine = self.block(u, self.seat.z) if self.split[k] else self.column(u, self.seat.me)
        return pltpu.make_async_copy(self.shards[k].at[:, cols], mine, self.own_sem.at[u])

    def along(self, u, hop, way):
        k, cols = self.units[u]
        level = self.seat.z - way * hop
        source = self.shards[k].at[:, cols] if hop == 0 else self.block(u, level)
        at = (u, hop + (0 if way > 0 else 3))
        return link(source, self.block(u, level), self.sems, at, {"tensor": self.seat.z + way})

    def arrives(self, u, hop, way):
        level = self.seat.z - way * (hop + 1)
        at = (u, hop + (0 if way > 0 else 3))
        return link(self.block(u, level), self.block(u, level), self.sems, at, {"tensor": self.seat.z - way})

    def sends(self, hop, way):
        level, to = self.seat.z - way * hop, self.seat.z + way
        return (level >= 0) & (level < 4) & (to >= 0) & (to < 4)

    def gets(self, hop, way):
        level = self.seat.z - way * (hop + 1)
        return (level >= 0) & (level < 4)

    def z(self, u, hop):
        for way in (1, -1):
            if hop > 0:

                @pl.when(self.gets(hop - 1, way))
                def _():
                    self.arrives(u, hop - 1, way).wait_recv()

            if hop < 3:

                @pl.when(self.sends(hop, way))
                def _():
                    self.along(u, hop, way).start()

    def copy(self, u, region, at, device):
        return link(region, region, self.sems, (u, at), {"dp": device})

    def own_x(self, u):
        return self.copy(u, self.column(u, self.seat.me), 6, self.seat.xn)

    def own_y(self, u):
        return self.copy(u, self.column(u, self.seat.me), 7, self.seat.yn)

    def pass_x(self, u):
        return self.copy(u, self.halves(u, self.seat.yn, 1), 8, self.seat.xn)

    def pass_y(self, u):
        return self.copy(u, self.halves(u, self.seat.xn, 0), 9, self.seat.yn)

    def owner(self, which):
        return (self.seat.me, self.seat.xn, self.seat.yn, self.seat.diag)[which]

    def over(self, u, which):
        return self.copy(u, self.column(u, self.owner(which)), 10 + which, self.seat.core)

    def plane(self, u):
        self.keep(u).wait()
        self.own_x(u).start()
        self.own_y(u).start()
        self.over(u, 0).start()

    def relay(self, u):
        s = self.seat
        self.copy(u, self.column(u, s.xn), 6, s.xn).wait_recv()
        self.pass_y(u).start()
        self.over(u, 1).start()
        self.copy(u, self.column(u, s.yn), 7, s.yn).wait_recv()
        self.pass_x(u).start()
        self.over(u, 2).start()

    def corner(self, u):
        s = self.seat
        self.copy(u, self.halves(u, s.diag, 1), 8, s.xn).wait_recv()
        self.copy(u, self.halves(u, s.diag, 0), 9, s.yn).wait_recv()
        self.over(u, 3).start()

    def arrived(self, u):
        s = self.seat
        for which in range(4):
            theirs = self.column(u, self.owner(which) + 1 - 2 * s.c)
            self.copy(u, theirs, 10 + which, s.core).wait_recv()

    def drain(self, u):
        if self.split[self.units[u][0]]:
            for hop in range(3):
                for way in (1, -1):

                    @pl.when(self.sends(hop, way))
                    def _():
                        self.along(u, hop, way).wait_send()

        for copy in (self.own_x(u), self.own_y(u), self.pass_x(u), self.pass_y(u)):
            copy.wait_send()
        for which in range(4):
            self.over(u, which).wait_send()


FORWARD_SPLIT = (False, True, True, True, True, False)


def forward_kernel(
    pp_in, in_in, out_in, up_in, dn_in, cls_in, pix_hbm, coord_ref, vec_ref, gain_ref, bound_ref,
    emb_hbm, h1_hbm, q_hbm, k_hbm, v_hbm, o_ref, lse_ref, win_hbm, wout_hbm, wup_hbm, wdn_hbm, wcls_hbm,
    wp_ref, win_ref, pix_ref, emb_ref, h1_ref, q_ref, k_ref, v_ref, ka_ref, va_ref, qa_ref,
    own_sem, send_sem, recv_sem, copy_sem,
    *, packs,
):
    step = pl.program_id(0)
    rows, pixels = pix_ref.shape
    groups = win_ref.shape[0]
    part = win_ref.shape[2] // 3
    spots = (wp_ref.shape[1] - pixels) // 2
    half = wup_hbm.shape[2] // 2
    tile = 256
    seat = Seat()
    everything, left, right = slice(None), slice(0, half), slice(half, 2 * half)
    units = (
        (0, everything), (1, everything), (2, everything),
        (3, left), (3, right), (4, left), (4, right), (5, everything),
    )
    pp, w_in, out, up_a, up_b, dn_a, dn_b, cls = range(8)
    flow = Gather(
        seat,
        (pp_in, in_in, out_in, up_in, dn_in, cls_in),
        (wp_ref, win_ref, wout_hbm, wup_hbm, wdn_hbm, wcls_hbm),
        FORWARD_SPLIT,
        units,
        own_sem,
        (send_sem, recv_sem),
    )
    pack = jnp.minimum(seat.z, packs - 1)
    pix_copy = pltpu.make_async_copy(
        pix_hbm.at[pl.ds(pl.multiple_of(pack * rows, rows), rows)], pix_ref, copy_sem.at[0]
    )
    results = [
        pltpu.make_async_copy(source, target, copy_sem.at[1 + n])
        for n, (source, target) in enumerate(
            ((emb_ref, emb_hbm), (h1_ref, h1_hbm), (q_ref, q_hbm), (k_ref, k_hbm), (v_ref, v_hbm), (win_ref, win_hbm))
        )
    ]

    def embed(at):
        span = slice(at * tile, (at + 1) * tile)
        start = pl.multiple_of(pack * rows + at * tile, tile)
        place = lax.broadcasted_iota(jnp.int32, (2 * spots, tile), 0)
        across = coord_ref[0:1, pl.ds(start, tile)]
        down = coord_ref[1:2, pl.ds(start, tile)]
        hot = jnp.transpose(((place == across) | (place - spots == down)).astype(F32)).astype(LOW)
        embedded = mm_nt(pix_ref[span, :], wp_ref[:, :pixels]) + mm_nt(hot, wp_ref[:, pixels:])
        emb_ref[span, :] = embedded
        normed, _ = row_norm(embedded)
        h1_ref[span, :] = (normed * vec_ref[0:1]).astype(LOW)

    def project(at):
        span = slice(at * tile, (at + 1) * tile)
        first = h1_ref[span, :]
        parts = [mm(first, win_ref[group]) for group in range(groups)]
        q_ref[span, :] = jnp.concatenate([entry[:, :part] for entry in parts], axis=1)
        k_ref[span, :] = jnp.concatenate([entry[:, part : 2 * part] for entry in parts], axis=1)
        v_ref[span, :] = jnp.concatenate([entry[:, 2 * part :].astype(LOW) for entry in parts], axis=1)

    @pl.when(step == 0)
    def _():
        pix_copy.start()
        for u in range(8):
            flow.keep(u).start()
        greet(seat, 4)
        flow.z(w_in, 0)
        flow.plane(pp)
        flow.z(w_in, 1)
        flow.relay(pp)
        flow.z(w_in, 2)
        flow.corner(pp)
        flow.z(w_in, 3)
        flow.plane(w_in)
        flow.z(out, 0)
        flow.arrived(pp)
        pix_copy.wait()
        embed(0)
        flow.z(out, 1)
        embed(1)
        flow.z(out, 2)
        embed(2)
        flow.z(out, 3)
        flow.z(up_a, 0)
        embed(3)
        results[0].start()
        results[1].start()
        flow.z(up_a, 1)
        flow.relay(w_in)
        flow.plane(out)
        flow.z(up_a, 2)
        flow.corner(w_in)
        flow.z(up_a, 3)
        flow.relay(out)
        flow.plane(up_a)
        flow.z(up_b, 0)
        flow.arrived(w_in)
        results[5].start()
        project(0)
        flow.z(up_b, 1)
        flow.corner(out)
        project(1)
        flow.z(up_b, 2)
        project(2)
        flow.z(up_b, 3)
        flow.relay(up_a)
        flow.plane(up_b)
        flow.z(dn_a, 0)
        project(3)
        for n in (2, 3, 4):
            results[n].start()

    plan = {
        0: [lambda: flow.z(dn_a, 1)],
        1: [lambda: flow.corner(up_a), lambda: flow.z(dn_a, 2)],
        2: [lambda: flow.z(dn_a, 3)],
        3: [lambda: flow.relay(up_b), lambda: flow.plane(dn_a), lambda: flow.z(dn_b, 0)],
        4: [lambda: flow.z(dn_b, 1)],
        5: [lambda: flow.corner(up_b), lambda: flow.z(dn_b, 2)],
        6: [lambda: flow.z(dn_b, 3)],
        7: [lambda: flow.relay(dn_a), lambda: flow.plane(dn_b)],
        9: [lambda: flow.corner(dn_a)],
        11: [lambda: flow.relay(dn_b), lambda: flow.plane(cls)],
    }

    def between(slot):
        for number, actions in plan.items():
            if number % 2 == slot:

                @pl.when(2 * step + slot == number)
                def _():
                    for action in actions:
                        action()

    mine = pl.ds(pl.multiple_of(step * 128, 128), 128)
    attend_kernel(
        q_ref.at[:, mine], k_ref.at[:, mine], v_ref.at[:, mine], gain_ref, bound_ref, o_ref, lse_ref,
        ka_ref, va_ref, qa_ref, between=between,
    )

    @pl.when(step == pl.num_programs(0) - 1)
    def _():
        flow.corner(dn_b)
        flow.relay(cls)
        flow.corner(cls)
        for u in (out, up_a, up_b, dn_a, dn_b, cls):
            flow.arrived(u)
        for u in range(8):
            flow.drain(u)
        for copy in results:
            copy.wait()


def forward_call(shards, pixels, coords, vectors, gains, bounds, packs, collective_id):
    depth, width = 4, vectors.shape[1]
    rows = pixels.shape[0] // packs
    anywhere = pl.BlockSpec(memory_space=pl.ANY)
    small = lambda a: pl.BlockSpec(a.shape, lambda j: (0, 0))
    pair = pl.BlockSpec((rows, 128), lambda j: (0, j))
    weights = [
        jax.ShapeDtypeStruct(((depth, width) if apart else (width,)) + entry.shape[1:], LOW)
        for entry, apart in zip(shards, FORWARD_SPLIT)
    ]
    token = lambda dtype: jax.ShapeDtypeStruct((rows, width), dtype)
    held = lambda dtype: pltpu.VMEM((rows, width), dtype)
    return pl.pallas_call(
        functools.partial(forward_kernel, packs=packs),
        grid=(width // 128,),
        in_specs=[anywhere] * 7 + [small(coords), small(vectors), small(gains), small(bounds)],
        out_specs=[anywhere] * 5 + [pair, pair] + [anywhere] * 5,
        out_shape=[token(F32), token(LOW), token(F32), token(F32), token(LOW), token(LOW), token(F32)]
        + weights[1:],
        scratch_shapes=[
            pltpu.VMEM(weights[0].shape, LOW),
            pltpu.VMEM(weights[1].shape, LOW),
            pltpu.VMEM((rows, pixels.shape[1]), LOW),
            held(F32), held(LOW), held(F32), held(F32), held(LOW),
            pltpu.VMEM((rows, 256), LOW),
            pltpu.VMEM((rows, 256), LOW),
            pltpu.VMEM((2, rows, 256), LOW),
            pltpu.SemaphoreType.DMA((8,)),
            pltpu.SemaphoreType.DMA((8, 14)),
            pltpu.SemaphoreType.DMA((8, 14)),
            pltpu.SemaphoreType.DMA((7,)),
        ],
        compiler_params=pltpu.CompilerParams(
            collective_id=collective_id, has_side_effects=True, vmem_limit_bytes=VMEM_BYTES
        ),
        name="forward",
    )(*shards, pixels, coords, vectors, gains, bounds)


class Flow:
    def __init__(self, seat, level_of, own, core_in, plane_in, last_in, up_in, down_in, sems):
        self.seat, self.level_of, self.own, self.sems = seat, level_of, own, sems
        self.core_in, self.plane_in, self.last_in = core_in, plane_in, last_in
        self.up_in, self.down_in = up_in, down_in

    def to_core(self, i, source):
        return link(source, self.core_in.at[i], self.sems, (i, 0), {"dp": self.seat.core})

    def first(self, i, along_x):
        s = self.seat
        source = self.own(i).at[:, 1 - s.x] if along_x else self.own(i).at[1 - s.y]
        return link(source, self.plane_in.at[i], self.sems, (i, 1), {"dp": s.xn if along_x else s.yn})

    def second(self, i, along_x):
        s = self.seat
        source = self.own(i).at[s.y, 1 - s.x] if along_x else self.own(i).at[1 - s.y, s.x]
        return link(source, self.last_in.at[i], self.sems, (i, 2), {"dp": s.xn if along_x else s.yn})

    def along(self, i, way):
        s = self.seat
        buffer = self.up_in if way > 0 else self.down_in
        at = (i, 3 if way > 0 else 4)
        return link(self.own(i).at[s.y, s.x], buffer.at[i], self.sems, at, {"tensor": s.z + way})

    def x_first(self, i, then, other):
        pl.when(lax.rem(i, 2) == 0)(then)
        pl.when(lax.rem(i, 2) == 1)(other)

    def one(self, i):
        mine = self.own(i)
        mine[...] = mine[...] + self.core_in[i]
        self.x_first(i, lambda: self.first(i, True).start(), lambda: self.first(i, False).start())

    def two(self, i):
        s, mine = self.seat, self.own(i)

        def from_x():
            self.first(i, True).wait_recv()
            mine[:, s.x] = mine[:, s.x] + self.plane_in[i]
            self.second(i, False).start()

        def from_y():
            self.first(i, False).wait_recv()
            mine[s.y] = mine[s.y] + self.plane_in[i]
            self.second(i, True).start()

        self.x_first(i, from_x, from_y)

    def three(self, i):
        s, mine = self.seat, self.own(i)
        self.second(i, False).wait_recv()
        mine[s.y, s.x] = mine[s.y, s.x] + self.last_in[i]

        @pl.when((s.z == 0) & (self.level_of(i) > 0))
        def _():
            self.along(i, 1).start()

        @pl.when((s.z == 3) & (self.level_of(i) < 3))
        def _():
            self.along(i, -1).start()

    def hop(self, i, reach):
        s, mine = self.seat, self.own(i)

        @pl.when((s.z == reach) & (self.level_of(i) > reach))
        def _():
            self.along(i, 1).wait_recv()
            mine[s.y, s.x] = mine[s.y, s.x] + self.up_in[i]
            self.along(i, 1).start()

        @pl.when((s.z == 3 - reach) & (self.level_of(i) < 3 - reach))
        def _():
            self.along(i, -1).wait_recv()
            mine[s.y, s.x] = mine[s.y, s.x] + self.down_in[i]
            self.along(i, -1).start()

    def total(self, i):
        s = self.seat
        values = self.own(i)[s.y, s.x].astype(F32)

        @pl.when(s.z > 0)
        def _():
            self.along(i, 1).wait_recv()

        @pl.when(s.z < 3)
        def _():
            self.along(i, -1).wait_recv()

        @pl.when(s.z == 0)
        def _():
            self.up_in[i] = jnp.zeros(self.up_in.shape[1:], LOW)

        @pl.when(s.z == 3)
        def _():
            self.down_in[i] = jnp.zeros(self.down_in.shape[1:], LOW)

        return values + self.up_in[i].astype(F32) + self.down_in[i].astype(F32)

    def drain(self, i):
        s = self.seat
        self.first(i, True).wait_send()
        self.second(i, True).wait_send()

        @pl.when(s.z < self.level_of(i))
        def _():
            self.along(i, 1).wait_send()

        @pl.when(s.z > self.level_of(i))
        def _():
            self.along(i, -1).wait_send()


class Whole:
    def __init__(self, seat, own, core_in, plane_in, last_in, level_in, sems):
        self.seat, self.own, self.sems = seat, own, sems
        self.core_in, self.plane_in, self.last_in, self.level_in = core_in, plane_in, last_in, level_in
        self.half = core_in.shape[2] // 2

    def to_core(self, source):
        return link(source, self.core_in, self.sems, 0, {"dp": self.seat.core})

    def rows(self, which):
        return slice(which * self.half, (which + 1) * self.half)

    def first(self, which):
        s = self.seat
        rows = self.rows(which)
        source = self.own.at[1 - s.y, :, rows] if which else self.own.at[:, 1 - s.x, rows]
        return link(source, self.plane_in.at[which], self.sems, 1 + which, {"dp": s.yn if which else s.xn})

    def second(self, which):
        s = self.seat
        rows = self.rows(which)
        source = self.own.at[s.y, 1 - s.x, rows] if which else self.own.at[1 - s.y, s.x, rows]
        return link(source, self.last_in.at[which], self.sems, 3 + which, {"dp": s.xn if which else s.yn})

    def lift(self):
        s = self.seat
        return link(self.own.at[s.y, s.x], self.level_in.at[0], self.sems, 5, {"tensor": s.z + 1 - 2 * (s.z % 2)})

    def cross(self):
        s = self.seat
        return link(self.own.at[s.y, s.x], self.level_in.at[1], self.sems, 6, {"tensor": 3 - s.z})

    def give(self):
        s = self.seat
        return link(self.own.at[s.y, s.x], self.level_in.at[1], self.sems, 7, {"tensor": s.z + 1 - 2 * (s.z % 2)})

    def middle(self):
        return (self.seat.z == 1) | (self.seat.z == 2)

    def ends(self):
        return (self.seat.z == 0) | (self.seat.z == 3)

    def one(self):
        for a in range(2):
            for b in range(2):
                self.own[a, b] = self.own[a, b] + self.core_in[a, b]
        self.first(0).start()
        self.first(1).start()

    def two(self):
        s, own = self.seat, self.own
        for which in range(2):
            rows = self.rows(which)
            self.first(which).wait_recv()
            for a in range(2):
                if which:
                    own[s.y, a, rows] = own[s.y, a, rows] + self.plane_in[which, a]
                else:
                    own[a, s.x, rows] = own[a, s.x, rows] + self.plane_in[which, a]
            self.second(which).start()

    def three(self):
        s, own = self.seat, self.own
        for which in range(2):
            rows = self.rows(which)
            self.second(which).wait_recv()
            own[s.y, s.x, rows] = own[s.y, s.x, rows] + self.last_in[which]
        pl.when(self.ends())(lambda: self.lift().start())

    def four(self):
        s, own = self.seat, self.own

        @pl.when(self.middle())
        def _():
            self.lift().wait_recv()
            own[s.y, s.x] = own[s.y, s.x] + self.level_in[0]
            self.cross().start()

    def five(self):
        s, own = self.seat, self.own

        @pl.when(self.middle())
        def _():
            self.cross().wait_recv()
            self.cross().wait_send()
            own[s.y, s.x] = own[s.y, s.x] + self.level_in[1]
            self.give().start()

    def total(self):
        s = self.seat

        @pl.when(self.ends())
        def _():
            self.give().wait_recv()

        @pl.when(self.middle())
        def _():
            self.level_in[1] = self.own[s.y, s.x]

        return self.level_in[1].astype(F32)

    def drain(self):
        for which in range(2):
            self.first(which).wait_send()
            self.second(which).wait_send()
        pl.when(self.ends())(lambda: self.lift().wait_send())
        pl.when(self.middle())(lambda: self.give().wait_send())


class Tiny:
    def __init__(self, seat, value, came, sems):
        self.seat, self.value, self.came, self.sems = seat, value, came, sems

    def near(self, ahead, own):
        s = self.seat
        other = lax.rem(s.me + (ahead if own else 8 - ahead), 8)
        place = self.came.at[s.me if own else other]
        return link(self.value.at[0], place, self.sems, ahead - 1, {"dp": other})

    def far(self, ahead, own):
        s = self.seat
        other = lax.rem(s.z + (ahead if own else 4 - ahead), 4)
        place = self.came.at[8 + (s.z if own else other)]
        return link(self.value.at[1], place, self.sems, 6 + ahead, {"tensor": other})

    def start_plane(self):
        for ahead in range(1, 8):
            self.near(ahead, True).start()

    def total(self, first, count):
        total = self.came[first]
        for n in range(1, count):
            total = total + self.came[first + n]
        return total

    def turn_levels(self):
        for ahead in range(1, 8):
            self.near(ahead, False).wait_recv()
        self.came[self.seat.me] = self.value[0]
        self.value[1] = self.total(0, 8)
        for ahead in range(1, 4):
            self.far(ahead, True).start()

    def finish(self):
        for ahead in range(1, 4):
            self.far(ahead, False).wait_recv()
        self.came[8 + self.seat.z] = self.value[1]
        return self.total(8, 4)

    def drain(self):
        for ahead in range(1, 8):
            self.near(ahead, True).wait_send()
        for ahead in range(1, 4):
            self.far(ahead, True).wait_send()


def flow_scratch(chunks, share, cols):
    low = lambda *shape: pltpu.VMEM(shape, LOW)
    sems = lambda: pltpu.SemaphoreType.DMA((chunks, 5))
    return [
        low(chunks, 2, 2, share, cols),
        low(chunks, 2, share, cols),
        low(chunks, share, cols),
        low(chunks, share, cols),
        low(chunks, share, cols),
        sems(),
        sems(),
    ]


def whole_scratch(share, cols):
    low = lambda *shape: pltpu.VMEM(shape, LOW)
    return [
        low(2, 2, share, cols),
        low(2, 2, share // 2, cols),
        low(2, share // 2, cols),
        low(2, share, cols),
        pltpu.SemaphoreType.DMA((8,)),
        pltpu.SemaphoreType.DMA((8,)),
    ]


def tiny_scratch(shape):
    sems = lambda: pltpu.SemaphoreType.DMA((10,))
    return [pltpu.VMEM((2,) + shape, F32), pltpu.VMEM((12,) + shape, F32), sems(), sems()]


MLP_BACK_IO = (10, 5)
MLP_BACK_SCRATCH = 5


def mlp_back_sum_kernel(*refs):
    ins, outs = MLP_BACK_IO
    inputs, dcls_ref = refs[:ins], refs[ins]
    outputs = refs[ins + 1 : ins + 1 + outs]
    share_ref, cls_ref = refs[ins + 1 + outs : ins + 3 + outs]
    rest = refs[ins + 3 + outs :]
    scratch, rest = rest[:MLP_BACK_SCRATCH], rest[MLP_BACK_SCRATCH:]
    full, flow_refs = rest[0], rest[1:8]
    cls_own, cls_load, cls_refs = rest[8], rest[9], rest[10:16]
    step = pl.program_id(0)
    seat = Seat()
    c = seat.c
    share, half = full.shape[-2], inputs[1].shape[1]
    flow = Flow(
        seat, lambda i: 1, lambda i: full.at[i, :, :, c], *flow_refs[:5], flow_refs[5:]
    )
    cls = Whole(seat, cls_own, *cls_refs[:4], cls_refs[4:])
    loading = pltpu.make_async_copy(dcls_ref.at[:, :, c], cls_own, cls_load)
    cls_to_core = cls.to_core(dcls_ref.at[:, :, 1 - c])

    def to_core(i):
        return flow.to_core(i, full.at[i, :, :, 1 - c])

    def one(i):
        to_core(i).wait_recv()
        flow.one(i)

    def last(i):
        @pl.when(seat.z == flow.level_of(i))
        def _():
            share_ref[i] = flow.total(i)

    @pl.when(step == 0)
    def _():
        loading.start()
        greet(seat, 4)
        cls_to_core.start()
        share_ref[...] = jnp.zeros(share_ref.shape, F32)

    def keep(kind, at, value):
        columns = pl.ds(pl.multiple_of(lax.rem(step, 2) * half, half), half)
        full[kind, at // 2, at % 2, :, :, columns] = value.reshape(2, share, half)

    def cls_total():
        cls_ref[...] = cls.total()

    def cls_one():
        loading.wait()
        cls_to_core.wait_recv()
        cls.one()

    plan = {
        0: [cls_one],
        1: [lambda: to_core(0).start(), lambda: to_core(1).start(), cls.two],
        2: [lambda: one(0), lambda: one(1), cls.three],
        4: [lambda: flow.two(0), lambda: flow.two(1), cls.four],
        5: [lambda: flow.three(0), lambda: flow.three(1)],
        6: [cls.five],
        7: [lambda: flow.hop(0, 1), lambda: flow.hop(1, 1)],
    }

    def between(now):
        for number, actions in plan.items():

            @pl.when(now == number)
            def _():
                for action in actions:
                    action()

    mlp_back_kernel(*inputs, *outputs, *scratch, keep=keep, between=between)

    @pl.when(step == pl.num_programs(0) - 1)
    def _():
        cls_total()
        for i in range(2):
            last(i)
        for i in range(2):
            to_core(i).wait_send()
            flow.drain(i)
        cls_to_core.wait_send()
        cls.drain()


def mlp_back_sum_call(dx2, active, slope, h2, x1, attended, w_out, w_up, w_dn, vectors, d_cls, collective_id):
    rows, width = dx2.shape
    groups, _, per = w_up.shape
    chunk = per // 2
    hidden = groups * per
    share, classes = d_cls.shape[-2:]
    turned = lambda j: j // 2 + 1 - 2 * ((j // 2) % 2)
    whole = lambda a: pl.BlockSpec(a.shape, lambda j: (0,) * a.ndim, pipeline_mode=pl.Buffered(1))
    weight = pl.BlockSpec((1, width, chunk), lambda j: (turned(j), 0, j % 2))
    piece = pl.BlockSpec((rows, chunk), lambda j: (0, turned(j) * 2 + j % 2))
    full = lambda *shape: pl.BlockSpec(shape, lambda j: (0,) * len(shape))
    late = lambda j: jnp.where(j < 2, 0, j - 2)
    return pl.pallas_call(
        mlp_back_sum_kernel,
        grid=(hidden // chunk,),
        in_specs=[
            whole(dx2), piece, piece, whole(h2), whole(x1), whole(attended), whole(w_out),
            weight, weight, whole(vectors), pl.BlockSpec(memory_space=pl.ANY),
        ],
        out_specs=[
            pl.BlockSpec((2, 1, width, chunk), lambda j: (0, late(j) // 2, 0, late(j) % 2)),
            full(*w_out.shape),
            full(rows, width),
            full(rows, width),
            full(1, width),
            full(2, share, width),
            full(share, classes),
        ],
        out_shape=[
            jax.ShapeDtypeStruct((2, groups - 1) + w_up.shape[1:], LOW),
            jax.ShapeDtypeStruct(w_out.shape, LOW),
            jax.ShapeDtypeStruct((rows, width), LOW),
            jax.ShapeDtypeStruct((rows, width), F32),
            jax.ShapeDtypeStruct((1, width), F32),
            jax.ShapeDtypeStruct((2, share, width), F32),
            jax.ShapeDtypeStruct((share, classes), F32),
        ],
        scratch_shapes=[
            pltpu.VMEM((rows, width), LOW),
            pltpu.VMEM((width, rows), LOW),
            pltpu.VMEM((width, rows), LOW),
            pltpu.VMEM((rows, width), F32),
            pltpu.VMEM((rows, chunk), LOW),
            pltpu.VMEM((2, 2, 2, 2, share, width), LOW),
        ]
        + flow_scratch(2, share, width)
        + [pltpu.VMEM((2, 2, share, classes), LOW), pltpu.SemaphoreType.DMA]
        + whole_scratch(share, classes),
        compiler_params=pltpu.CompilerParams(
            collective_id=collective_id, has_side_effects=True, vmem_limit_bytes=VMEM_BYTES
        ),
        name="mlp_back_sum",
    )(dx2, active, slope, h2, x1, attended, w_out, w_up, w_dn, vectors, d_cls)


def embed_back_sum_kernel(
    dq_hbm, dk_hbm, dv_hbm, h1_hbm, emb_hbm, dmid_hbm, pix_hbm, coord_ref, win_hbm, vec_ref,
    small_ref, mlp_ref, cls_ref, out_ref,
    in_ref, pp_ref, small_out, square_out,
    dq_ref, dk_ref, dv_ref, h1_ref, emb_ref, dmid_ref, pix_ref, win_ref, tile_sem, load_sem,
    h1t_ref, embt_ref, join_ref, hot_ref, in_full, pp_full,
    *rest, packs,
):
    rows, width = h1_ref.shape
    groups = 4
    part = win_ref.shape[2] // 3
    tile = 256
    seat = Seat()
    c = seat.c
    share = in_full.shape[-2]
    flow = Flow(
        seat, lambda i: (3 * i) % 4, lambda i: in_full.at[i, :, :, c], *rest[:5], rest[5:7]
    )
    pp = Whole(seat, pp_full.at[:, :, c], *rest[7:11], rest[11:13])
    small = Tiny(seat, rest[13], rest[14], rest[15:17])
    square = Tiny(seat, rest[17], rest[18], rest[19:21])
    small_value, square_value = rest[13], rest[17]
    pp_to_core = pp.to_core(pp_full.at[:, :, 1 - c])
    leader = jnp.where(seat.z == 0, 1.0, 0.0)

    def in_to_core(i):
        return flow.to_core(i, in_full.at[i, :, :, 1 - c])

    def one(i):
        in_to_core(i).wait_recv()
        flow.one(i)

    def last(i):
        @pl.when(flow.level_of(i) == seat.z)
        def _():
            in_ref[...] = flow.total(i)

    tiled = (
        (dq_hbm, dq_ref), (dk_hbm, dk_ref), (dv_hbm, dv_ref),
        (emb_hbm, emb_ref), (dmid_hbm, dmid_ref), (h1_hbm, h1_ref),
    )

    def tile_copies(at):
        span = pl.ds(at * tile, tile)
        return [
            pltpu.make_async_copy(source.at[span], target.at[span], tile_sem.at[n, at])
            for n, (source, target) in enumerate(tiled)
        ]

    win_copy = pltpu.make_async_copy(win_hbm, win_ref, load_sem.at[0])
    pack = jnp.minimum(seat.z, packs - 1)
    pix_copy = pltpu.make_async_copy(
        pix_hbm.at[pl.ds(pl.multiple_of(pack * rows, rows), rows)], pix_ref, load_sem.at[1]
    )
    win_copy.start()
    for at in range(rows // tile):
        for copy in tile_copies(at):
            copy.start()
    pix_copy.start()
    greet(seat, 4)
    gain = vec_ref[0:1]
    pixels = pix_ref.shape[1]
    spots = (pp_ref.shape[1] - pixels) // 2
    gain_sum = jnp.zeros((1, width), F32)
    win_copy.wait()
    for at in range(rows // tile):
        for copy in tile_copies(at):
            copy.wait()
        span = slice(at * tile, (at + 1) * tile)
        d_first = jnp.zeros((tile, width), F32)
        for group in range(groups):
            mine = slice(group * part, (group + 1) * part)
            join = jnp.concatenate([dq_ref[span, mine], dk_ref[span, mine], dv_ref[span, mine]], axis=1)
            join_ref[group, span, :] = join
            d_first += mm_nt(join, win_ref[group])
        normed, inverse = row_norm(emb_ref[span, :])
        gain_sum += jnp.sum(d_first * normed, axis=0, keepdims=True)
        d_embed = dmid_ref[span, :] + row_norm_back(d_first, gain, normed, inverse)
        embt_ref[:, span] = jnp.transpose(d_embed).astype(LOW)
        h1t_ref[:, span] = jnp.transpose(h1_ref[span, :].astype(F32)).astype(LOW)
    small_value[0] = small_ref[...]
    small_value[0, 0:1] = gain_sum
    small.start_plane()
    place = lax.broadcasted_iota(jnp.int32, (2 * spots, rows), 0)
    mine = pl.ds(pl.multiple_of(pack * rows, rows), rows)
    hot = (place == coord_ref[0:1, mine]) | (place - spots == coord_ref[1:2, mine])
    hot_ref[...] = hot.astype(F32).astype(LOW)
    pix_copy.wait()
    for at in range(4):
        span = slice(at * 2 * share, (at + 1) * 2 * share)
        picture = mm(embt_ref[span, :], pix_ref[...]).astype(LOW)
        pp_full[at // 2, at % 2, :, :, :pixels] = picture.reshape(2, share, pixels)
        place = mm_nt(embt_ref[span, :], hot_ref[...]).astype(LOW)
        pp_full[at // 2, at % 2, :, :, pixels:] = place.reshape(2, share, 2 * spots)
    pp_to_core.start()

    def project(i):
        group = flow.level_of(i)
        for at in range(4):
            span = slice(at * 2 * share, (at + 1) * 2 * share)
            value = mm(h1t_ref[span, :], join_ref[group]).astype(LOW)
            in_full[i, at // 2, at % 2] = value.reshape(2, share, value.shape[1])
        in_to_core(i).start()

    project(0)
    pp_to_core.wait_recv()
    pp.one()
    small.turn_levels()
    project(1)
    one(0)
    project(2)
    one(1)
    pp.two()
    project(3)
    one(2)
    flow.two(0)
    pp.three()
    small_out[...] = small.finish()
    one(3)
    flow.two(1)
    flow.three(0)
    mlp_sum = mlp_ref[...]
    out_sum = out_ref[...]
    squares = jnp.sum(mlp_sum[0] * mlp_sum[0] + mlp_sum[1] * mlp_sum[1], axis=0, keepdims=True)
    total = jnp.sum(squares, axis=1, keepdims=True)
    total = total + jnp.sum(jnp.sum(out_sum * out_sum, axis=0, keepdims=True), axis=1, keepdims=True)
    cls_sum = cls_ref[...]
    shared = jnp.sum(jnp.sum(cls_sum * cls_sum, axis=0, keepdims=True), axis=1, keepdims=True)
    pp.four()
    flow.three(1)
    flow.two(2)
    flow.hop(0, 1)
    flow.two(3)
    flow.hop(1, 1)
    pp.five()
    flow.three(2)
    flow.hop(0, 2)
    flow.three(3)
    flow.hop(1, 2)
    flow.hop(2, 1)
    pp_sum = pp.total()
    pp_ref[...] = pp_sum
    shared += jnp.sum(jnp.sum(pp_sum * pp_sum, axis=0, keepdims=True), axis=1, keepdims=True)
    flow.hop(3, 1)
    for i in range(groups):
        last(i)
    in_sum = in_ref[...]
    total = total + jnp.sum(jnp.sum(in_sum * in_sum, axis=0, keepdims=True), axis=1, keepdims=True)
    square_value[0] = jnp.broadcast_to(total + leader * shared, (8, 128))
    square.start_plane()
    square.turn_levels()
    square_out[...] = square.finish()
    pp_to_core.wait_send()
    for entry in (pp, small, square):
        entry.drain()
    for i in range(groups):
        in_to_core(i).wait_send()
        flow.drain(i)


def embed_back_sum_call(
    dq, dk, dv, h1, embedded, d_middle, pixels, coords, w_in, pp_cols, vectors,
    small, share_mlp, share_cls, share_out, packs, collective_id,
):
    rows, width = h1.shape
    groups, share = w_in.shape[0], width // 8
    cols = w_in.shape[2]
    low = lambda *shape: pltpu.VMEM(shape, LOW)
    inside = pl.BlockSpec(memory_space=pltpu.VMEM)
    anywhere = pl.BlockSpec(memory_space=pl.ANY)
    loaded = (dq, dk, dv, h1, embedded, d_middle, pixels, w_in)
    return pl.pallas_call(
        functools.partial(embed_back_sum_kernel, packs=packs),
        in_specs=[anywhere] * 7 + [inside, anywhere] + [inside] * 5,
        out_specs=[inside] * 4,
        out_shape=[
            jax.ShapeDtypeStruct((share, cols), F32),
            jax.ShapeDtypeStruct((share, pp_cols), F32),
            jax.ShapeDtypeStruct(small.shape, F32),
            jax.ShapeDtypeStruct((8, 128), F32),
        ],
        scratch_shapes=[pltpu.VMEM((rows,) + a.shape[1:] if a is pixels else a.shape, a.dtype) for a in loaded]
        + [pltpu.SemaphoreType.DMA((6, rows // 256)), pltpu.SemaphoreType.DMA((2,))]
        + [
            low(width, rows),
            low(width, rows),
            low(groups, rows, cols),
            low(pp_cols - pixels.shape[1], rows),
            low(groups, 2, 2, 2, share, cols),
            low(2, 2, 2, share, pp_cols),
        ]
        + flow_scratch(groups, share, cols)
        + whole_scratch(share, pp_cols)
        + tiny_scratch(small.shape)
        + tiny_scratch((8, 128)),
        compiler_params=pltpu.CompilerParams(
            collective_id=collective_id, has_side_effects=True, vmem_limit_bytes=VMEM_BYTES
        ),
        name="embed_back_sum",
    )(
        dq, dk, dv, h1, embedded, d_middle, pixels, coords, w_in, vectors,
        small, share_mlp, share_cls, share_out,
    )


def adam(master, first_moment, second_moment, gradient, clip_scale, rate, decay_rate):
    gradient = gradient * clip_scale
    first_new = BETA_ONE * first_moment + (1 - BETA_ONE) * gradient
    second_new = BETA_TWO * second_moment + (1 - BETA_TWO) * gradient * gradient
    update = (
        first_new / (1 - BETA_ONE**STEP) / (jnp.sqrt(second_new / (1 - BETA_TWO**STEP)) + ADAM_EPS)
    )
    return (master - rate * (update + decay_rate * master), first_new, second_new)


def squared(entry):
    return jnp.sum(entry * entry)


def per_device(
    pixels, coords, lengths, labels,
    patch_table, patch_first, patch_second,
    position_table, position_first, position_second,
    attend_in, attend_in_first, attend_in_second,
    attend_out, attend_out_first, attend_out_second,
    expand, expand_first, expand_second,
    shrink, shrink_first, shrink_second,
    classify, classify_first, classify_second,
    vectors, vectors_first, vectors_second,
    head_gains, head_gains_first, head_gains_second,
):
    packs, images = lengths.shape
    members = lax.axis_size("tensor")
    width = vectors.shape[1]
    share = attend_in.shape[0]
    seat = lax.axis_index("tensor")
    pack = jnp.minimum(seat, packs - 1).astype(jnp.int32)[None]
    valid = (seat < packs).astype(F32).reshape(1, 1)
    image_count = images * packs * lax.axis_size("dp")
    shards = (
        jnp.concatenate(
            [patch_table.T, jnp.transpose(position_table, (2, 0, 1)).reshape(share, -1)], axis=1
        ).astype(LOW),
        attend_in.reshape(share, -1).astype(LOW),
        attend_out.T.astype(LOW),
        expand.astype(LOW),
        shrink.T.astype(LOW),
        classify.astype(LOW),
    )
    both = ("tensor", "dp")
    close = lax.axis_size("dp") == 8 and members == 4
    if close:
        weights = shards
    else:

        def gather(shard):
            return lax.all_gather(shard, both, axis=0, tiled=True).reshape(members, width, -1)

        weights = (
            lax.all_gather(shards[0], "dp", axis=0, tiled=True),
            gather(shards[1]),
            gather(shards[2]),
            gather(shards[3]),
            gather(shards[4]),
            lax.all_gather(shards[5], "dp", axis=0, tiled=True),
        )
    grads, grad_vectors, grad_gains, loss_local, squares = pack_step(
        pack, valid, pixels, coords, lengths, labels, weights, vectors, head_gains, image_count, close
    )
    if close:
        share_pp, share_in, share_out, share_up, share_dn, share_cls = grads
        loss_total = loss_local
    else:
        grad_vectors, grad_gains, loss_total = lax.psum((grad_vectors, grad_gains, loss_local), both)

        def scatter(grad):
            return lax.psum_scatter(
                grad.reshape(members * width, -1), both, scatter_dimension=0, tiled=True
            ).astype(F32)

        def scatter_whole(grad):
            part = lax.psum_scatter(grad, "dp", scatter_dimension=0, tiled=True)
            return lax.psum(part, "tensor").astype(F32)

        share_pp = scatter_whole(grads[0])
        share_in, share_out, share_up, share_dn = (scatter(entry) for entry in grads[1:5])
        share_cls = scatter_whole(grads[5])
        leader = (seat == 0).astype(F32)
        split_squares = squared(share_in) + squared(share_out) + squared(share_up) + squared(share_dn)
        squares = lax.psum(split_squares + leader * (squared(share_pp) + squared(share_cls)), both)
    grad_norm = jnp.sqrt(squares + squared(grad_vectors) + squared(grad_gains))
    clip_scale = CLIP / jnp.maximum(grad_norm, CLIP)
    pixel_width = patch_table.shape[0]
    share_patch = share_pp[:, :pixel_width].T
    share_pos = jnp.transpose(
        share_pp[:, pixel_width:].reshape(share, position_table.shape[0], position_table.shape[1]), (1, 2, 0)
    )
    results = (
        adam(patch_table, patch_first, patch_second, share_patch, clip_scale, RATE_BASE, DECAY),
        adam(position_table, position_first, position_second, share_pos, clip_scale, RATE_POSITION, DECAY),
        adam(
            attend_in, attend_in_first, attend_in_second,
            share_in.reshape(attend_in.shape), clip_scale, RATE_BASE, DECAY,
        ),
        adam(attend_out, attend_out_first, attend_out_second, share_out.T, clip_scale, RATE_MIDDLE, DECAY),
        adam(expand, expand_first, expand_second, share_up, clip_scale, RATE_BASE, DECAY),
        adam(shrink, shrink_first, shrink_second, share_dn.T, clip_scale, RATE_BASE, DECAY),
        adam(classify, classify_first, classify_second, share_cls, clip_scale, RATE_MIDDLE, DECAY),
        adam(vectors, vectors_first, vectors_second, grad_vectors, clip_scale, RATE_VECTOR, 0.0),
        adam(head_gains, head_gains_first, head_gains_second, grad_gains, clip_scale, RATE_VECTOR, 0.0),
    )
    return tuple(entry for group in results for entry in group) + (loss_total, grad_norm)


def solution(mesh):
    data = P("dp", None)
    in_specs = (
        (data, P(None, "dp"), data, data)
        + (P(None, "dp"),) * 3
        + (P(None, None, "dp"),) * 3
        + (P("dp", None, "tensor"),) * 3
        + (P("tensor", "dp"),) * 3
        + (P("dp", "tensor"),) * 3
        + (P("tensor", "dp"),) * 3
        + (data,) * 3
        + (P(),) * 6
    )
    out_specs = in_specs[4:] + (P(), P())
    return jax.shard_map(per_device, mesh=mesh, in_specs=in_specs, out_specs=out_specs, check_vma=False)
```

```python
import functools

import jax
import jax.numpy as jnp
from jax import lax
from jax.experimental import pallas as pl
from jax.experimental.pallas import tpu as pltpu
from jax.sharding import PartitionSpec as P

STEP = 10
NORM_EPS = 1e-06
CLIP = 0.05
RATE_BASE = 0.03
RATE_POSITION = 0.2
RATE_MIDDLE = 0.1
RATE_VECTOR = 1.0
DECAY = 0.05
BETA_ONE = 0.5
BETA_TWO = 0.5
ADAM_EPS = 1e-08
SHIFT = -4.0
NEGATIVE = -1e30
APART = 128.0
LOW = jnp.bfloat16
F32 = jnp.float32
VMEM_BYTES = 60 * 1024 * 1024
TAIL_P = 0.3
TAIL = (
    0.1196293,
    0.12075397,
    0.09991341,
    0.12856192,
    -0.05368424,
    0.20635419,
    -0.1572035,
    0.03567488,
)


def mm(left, right):
    return lax.dot_general(left, right, (((1,), (0,)), ((), ())), preferred_element_type=F32)


def mm_nt(left, right):
    return lax.dot_general(left, right, (((1,), (1,)), ((), ())), preferred_element_type=F32)


def split_two(values):
    high = values.astype(LOW)
    return high, (values - high.astype(F32)).astype(LOW)


def split_three(values):
    high = values.astype(LOW)
    rest = values - high.astype(F32)
    middle = rest.astype(LOW)
    return high, middle, (rest - middle.astype(F32)).astype(LOW)


def row_norm(values):
    center = values - jnp.mean(values, axis=-1, keepdims=True)
    inverse = lax.rsqrt(jnp.mean(center * center, axis=-1, keepdims=True) + NORM_EPS)
    return center * inverse, inverse


def row_norm_back(gradient, gain_row, normed, inverse):
    scaled = gradient * gain_row
    return inverse * (
        scaled
        - jnp.mean(scaled, axis=-1, keepdims=True)
        - normed * jnp.mean(scaled * normed, axis=-1, keepdims=True)
    )


def half_mean_matrix(scale):
    row = lax.broadcasted_iota(jnp.int32, (128, 128), 0)
    col = lax.broadcasted_iota(jnp.int32, (128, 128), 1)
    return jnp.where((row >= 64) == (col >= 64), scale, 0.0).astype(LOW)


def half_sum(values, block):
    high, low = split_two(values)
    return mm(high, block) + mm(low, block)


def half_norm(values, block):
    center = values - half_sum(values, block)
    inverse = lax.rsqrt(half_sum(center * center, block) + NORM_EPS)
    return center * inverse, inverse


def half_norm_back(gradient, gain_row, normed, inverse, block):
    scaled = gradient * gain_row
    return inverse * (scaled - half_sum(scaled, block) - normed * half_sum(scaled * normed, block))


def gelu_pair(inner):
    size = jnp.abs(inner)
    near = 1.0 / (1.0 + TAIL_P * size)
    bell = jnp.exp(-0.5 * inner * inner)
    poly = TAIL[-1]
    for factor in TAIL[-2::-1]:
        poly = poly * near + factor
    tail = poly * near * bell
    share = jnp.where(inner >= 0, 1.0 - tail, tail)
    return inner * share, share + inner * bell * 0.3989422804014327


def embed_kernel(pack_ref, pix_ref, coord_ref, wp_ref, win_ref, gain_ref, emb_ref, h1_ref, q_ref, k_ref, v_ref):
    rows = pix_ref.shape[0]
    pixels = pix_ref.shape[1]
    groups = win_ref.shape[0]
    part = win_ref.shape[2] // 3
    spots = (wp_ref.shape[1] - pixels) // 2
    lane = lax.broadcasted_iota(jnp.int32, (rows, 2 * spots), 1)
    hot = ((lane == coord_ref[:, 0:1]) | (lane - spots == coord_ref[:, 1:2])).astype(F32).astype(LOW)
    embedded = mm_nt(pix_ref[...], wp_ref[:, :pixels]) + mm_nt(hot, wp_ref[:, pixels:])
    emb_ref[...] = embedded
    normed, _ = row_norm(embedded)
    first = (normed * gain_ref[0:1]).astype(LOW)
    h1_ref[...] = first
    parts = [mm(first, win_ref[group]) for group in range(groups)]
    q_ref[...] = jnp.concatenate([entry[:, :part] for entry in parts], axis=1)
    k_ref[...] = jnp.concatenate([entry[:, part : 2 * part] for entry in parts], axis=1)
    v_ref[...] = jnp.concatenate([entry[:, 2 * part :].astype(LOW) for entry in parts], axis=1)


def embed_call(pack, pixels, coords, w_pp, w_in, vectors, rows):
    width = vectors.shape[1]
    tile = 256
    steps = rows // tile
    whole2 = lambda i, p: (0, 0)
    tiled = pl.BlockSpec((tile, width), lambda i, p: (i, 0))
    return pl.pallas_call(
        embed_kernel,
        grid_spec=pltpu.PrefetchScalarGridSpec(
            num_scalar_prefetch=1,
            grid=(steps,),
            in_specs=[
                pl.BlockSpec((tile, pixels.shape[1]), lambda i, p: (p[0] * steps + i, 0)),
                pl.BlockSpec((tile, 2), lambda i, p: (p[0] * steps + i, 0)),
                pl.BlockSpec(w_pp.shape, whole2),
                pl.BlockSpec(w_in.shape, lambda i, p: (0, 0, 0)),
                pl.BlockSpec(vectors.shape, whole2),
            ],
            out_specs=[tiled] * 5,
        ),
        out_shape=[
            jax.ShapeDtypeStruct((rows, width), F32),
            jax.ShapeDtypeStruct((rows, width), LOW),
            jax.ShapeDtypeStruct((rows, width), F32),
            jax.ShapeDtypeStruct((rows, width), F32),
            jax.ShapeDtypeStruct((rows, width), LOW),
        ],
        compiler_params=pltpu.CompilerParams(vmem_limit_bytes=VMEM_BYTES),
        name="embed",
    )(pack, pixels, coords, w_pp, w_in, vectors)


def image_marks(bound_ref, rows):
    place = lax.broadcasted_iota(jnp.int32, (rows, 128), 0)
    return (place >= bound_ref[0:1, :]) & (place < bound_ref[1:2, :])


def half_lane(rows):
    lane = lax.broadcasted_iota(jnp.int32, (rows, 128), 1)
    return lane, jnp.where(lane >= 64, lane - 64, lane)


def attend_kernel(
    q_ref, k_ref, v_ref, gain_ref, bound_ref, o_ref, lse_ref, ka_ref, va_ref, qa_ref, between=None
):
    rows = q_ref.shape[0]
    tile = 256
    block = half_mean_matrix(1.0 / 64)
    lane, inner = half_lane(rows)
    marks = image_marks(bound_ref, rows)
    one = jnp.where(inner == 8, 1.0, 0.0)
    query_feature = jnp.where(marks, 1.0, one)
    key_feature = jnp.where(marks, APART, -APART * one)
    k_normed, _ = half_norm(k_ref[...], block)
    ka_ref[:, :128] = (k_normed * gain_ref[1:2]).astype(LOW)
    ka_ref[:, 128:] = key_feature.astype(LOW)
    va_ref[:, :128] = v_ref[...]
    va_ref[:, 128:] = jnp.ones((rows, 128), LOW)
    q_normed, _ = half_norm(q_ref[...], block)
    query = (q_normed * gain_ref[0:1]).astype(LOW).astype(F32) * 0.125
    for head in range(2):
        mine = (lane < 64) if head == 0 else (lane >= 64)
        qa_ref[head, :, :128] = jnp.where(mine, query, 0.0).astype(LOW)
        qa_ref[head, :, 128:] = jnp.where(mine, query_feature, 0.0).astype(LOW)
    keys = ka_ref[...]
    values = va_ref[...]
    first = lane[:tile] < 64
    for step in range(rows // tile):
        part = slice(step * tile, (step + 1) * tile)
        outs = []
        for head in range(2):
            score = mm_nt(qa_ref[head, part, :], keys)
            outs.append(mm(jnp.exp(score).astype(LOW), values))
        total = jnp.where(first, outs[0][:, 128:], outs[1][:, 128:])
        o_ref[part, :] = (jnp.where(first, outs[0][:, :128], outs[1][:, :128]) / total).astype(LOW)
        lse_ref[part, :] = jnp.log(total)
        if between is not None and step % 2 == 1:
            between(step // 2)


def attend_call(q_raw, k_raw, value, gains, bounds):
    rows, width = q_raw.shape
    pair = pl.BlockSpec((rows, 128), lambda j: (0, j))
    small = lambda a: pl.BlockSpec(a.shape, lambda j: (0, 0))
    return pl.pallas_call(
        attend_kernel,
        grid=(width // 128,),
        in_specs=[pair, pair, pair, small(gains), small(bounds)],
        out_specs=[pair, pair],
        out_shape=[
            jax.ShapeDtypeStruct((rows, width), LOW),
            jax.ShapeDtypeStruct((rows, width), F32),
        ],
        scratch_shapes=[
            pltpu.VMEM((rows, 256), LOW),
            pltpu.VMEM((rows, 256), LOW),
            pltpu.VMEM((2, rows, 256), LOW),
        ],
        compiler_params=pltpu.CompilerParams(vmem_limit_bytes=VMEM_BYTES),
        name="attend",
    )(q_raw, k_raw, value, gains, bounds)


def attend_back_kernel(
    q_ref, k_ref, v_ref, o_ref, lse_ref, do_ref, gain_ref, bound_ref,
    dq_ref, dk_ref, dv_ref, dgain_ref,
    ka_ref, va_ref, qa_ref, da_ref, qt_ref, dot_ref, dqs_ref, dkt_ref, dvt_ref,
    between=None,
):
    rows = q_ref.shape[0]
    tile = 256
    block = half_mean_matrix(1.0 / 64)
    block_sum = half_mean_matrix(1.0)
    lane, inner = half_lane(rows)
    marks = image_marks(bound_ref, rows)
    one = jnp.where(inner == 8, 1.0, 0.0)
    three = (inner >= 9) & (inner < 12)
    key_feature = jnp.where(marks, APART, jnp.where(three, 1.0, -APART * one))

    def spread(values):
        high, middle, low = split_three(values)
        return jnp.where(
            inner == 9, high.astype(F32), jnp.where(inner == 10, middle.astype(F32), low.astype(F32))
        )

    query_feature = jnp.where(three, spread(-lse_ref[...]), jnp.where(marks, 1.0, one))
    k_normed, k_inverse = half_norm(k_ref[...], block)
    ka_ref[:, :128] = (k_normed * gain_ref[1:2]).astype(LOW)
    ka_ref[:, 128:] = key_feature.astype(LOW)
    va_ref[:, :128] = v_ref[...]
    va_ref[:, 128:] = jnp.where(three, 1.0, 0.0).astype(LOW)
    q_normed, q_inverse = half_norm(q_ref[...], block)
    query = (q_normed * gain_ref[0:1]).astype(LOW).astype(F32)
    qt_ref[...] = jnp.transpose(query).astype(LOW)
    query = query * 0.125
    above = do_ref[...].astype(F32)
    dot_ref[...] = jnp.transpose(above).astype(LOW)
    inside = half_sum(above * o_ref[...].astype(F32), block_sum)
    above_feature = jnp.where(three, spread(inside * -0.125), 0.0)
    above = above * 0.125
    for head in range(2):
        mine = (lane < 64) if head == 0 else (lane >= 64)
        qa_ref[head, :, :128] = jnp.where(mine, query, 0.0).astype(LOW)
        qa_ref[head, :, 128:] = jnp.where(mine, query_feature, 0.0).astype(LOW)
        da_ref[head, :, :128] = jnp.where(mine, above, 0.0).astype(LOW)
        da_ref[head, :, 128:] = jnp.where(mine, above_feature, 0.0).astype(LOW)
    keys = ka_ref[...]
    values = va_ref[...]
    key_low = ka_ref[:, :128]
    first = lane[:tile] < 64
    for step in range(rows // tile):
        part = slice(step * tile, (step + 1) * tile)
        outs = []
        for head in range(2):
            mine = slice(64 * head, 64 * head + 64)
            prob = jnp.exp(mm_nt(qa_ref[head, part, :], keys))
            d_prob = mm_nt(da_ref[head, part, :], values)
            d_score = (prob * d_prob).astype(LOW)
            outs.append(mm(d_score, key_low))
            d_key = mm(qt_ref[mine, part], d_score)
            d_value = mm(dot_ref[mine, part], prob.astype(LOW))
            if step == 0:
                dkt_ref[mine, :] = d_key
                dvt_ref[mine, :] = d_value
            else:
                dkt_ref[mine, :] += d_key
                dvt_ref[mine, :] += d_value
        dqs_ref[part, :] = jnp.where(first, outs[0], outs[1])
        if between is not None and step % 2 == 1:
            between(step // 2)
    d_query = dqs_ref[...]
    d_key = jnp.transpose(dkt_ref[...])
    dv_ref[...] = jnp.transpose(dvt_ref[...]).astype(LOW)
    dq_ref[...] = half_norm_back(d_query, gain_ref[0:1], q_normed, q_inverse, block).astype(LOW)
    dk_ref[...] = half_norm_back(d_key, gain_ref[1:2], k_normed, k_inverse, block).astype(LOW)
    dgain_ref[0, 0:1] = jnp.sum(d_query * q_normed, axis=0, keepdims=True)
    dgain_ref[0, 1:2] = jnp.sum(d_key * k_normed, axis=0, keepdims=True)


ATTEND_BACK_SCRATCH = 9


def attend_back_scratch(rows):
    return [
        pltpu.VMEM((rows, 256), LOW),
        pltpu.VMEM((rows, 256), LOW),
        pltpu.VMEM((2, rows, 256), LOW),
        pltpu.VMEM((2, rows, 256), LOW),
        pltpu.VMEM((128, rows), LOW),
        pltpu.VMEM((128, rows), LOW),
        pltpu.VMEM((rows, 128), F32),
        pltpu.VMEM((128, rows), F32),
        pltpu.VMEM((128, rows), F32),
    ]


def attend_back_sum_kernel(*refs):
    inputs, grads, dout_ref, before_ref = refs[:8], refs[8], refs[9], refs[10]
    outputs, share_ref, out_ref = refs[11:15], refs[15], refs[16]
    scratch, rest = refs[17 : 17 + ATTEND_BACK_SCRATCH], refs[17 + ATTEND_BACK_SCRATCH :]
    mlp_own, mlp_load, mlp_refs = rest[0], rest[1], rest[2:9]
    out_own, out_load, out_refs = rest[9], rest[10], rest[11:18]
    step = pl.program_id(0)
    seat = Seat()
    c = seat.c
    mlp = Flow(
        seat, lambda i: lax.rem(4 - lax.div(i, 2), 4), lambda i: mlp_own.at[i], *mlp_refs[:5], mlp_refs[5:]
    )
    out = Flow(seat, lambda i: i, lambda i: out_own.at[i], *out_refs[:5], out_refs[5:])
    chunks, levels = mlp_own.shape[0], out_own.shape[0]

    def mlp_at(i):
        return lax.rem(i, 2) * 3 + lax.div(i, 2)

    def mlp_loading(i):
        return pltpu.make_async_copy(grads.at[mlp_at(i), :, :, c], mlp_own.at[i], mlp_load.at[i])

    def mlp_to_core(i):
        return mlp.to_core(i, grads.at[mlp_at(i), :, :, 1 - c])

    def out_loading(i):
        return pltpu.make_async_copy(dout_ref.at[i, :, :, c], out_own.at[i], out_load.at[i])

    def out_to_core(i):
        return out.to_core(i, dout_ref.at[i, :, :, 1 - c])

    def every(count, action):
        lax.fori_loop(0, count, lambda i, carry: (action(i), carry)[1], 0)

    @pl.when(step == 0)
    def _():
        every(chunks, lambda i: mlp_loading(i).start())
        every(levels, lambda i: out_loading(i).start())
        greet(seat, 4)
        every(chunks, lambda i: mlp_to_core(i).start())
        every(levels, lambda i: out_to_core(i).start())
        share_ref[...] = before_ref[...]

    def mlp_one(i):
        mlp_loading(i).wait()
        mlp_to_core(i).wait_recv()
        mlp.one(i)

    def mlp_last(i):
        @pl.when(mlp.level_of(i) == seat.z)
        def _():
            share_ref[lax.rem(i, 2)] = mlp.total(i)

    def out_one(i):
        out_loading(i).wait()
        out_to_core(i).wait_recv()
        out.one(i)

    def out_last(i):
        @pl.when(out.level_of(i) == seat.z)
        def _():
            out_ref[...] = out.total(i)

    def pair(action, number):
        return lambda: every(2, lambda i: action(2 * number + i))

    hop_one, hop_two = (functools.partial(mlp.hop, reach=reach) for reach in (1, 2))
    out_hop_one, out_hop_two = (functools.partial(out.hop, reach=reach) for reach in (1, 2))
    plan = {
        0: [pair(mlp_one, 0)],
        1: [lambda: every(levels, out_one)],
        2: [pair(mlp.two, 0), pair(mlp_one, 1)],
        3: [lambda: every(levels, out.two)],
        4: [pair(mlp.three, 0)],
        5: [pair(mlp.two, 1), pair(mlp_one, 2)],
        6: [pair(hop_one, 0), lambda: every(levels, out.three)],
        7: [pair(mlp.three, 1), lambda: every(levels, out_hop_one)],
        8: [pair(mlp.two, 2), pair(hop_two, 0)],
        9: [pair(hop_one, 1), lambda: every(levels, out_hop_two)],
        10: [pair(mlp.three, 2)],
        11: [pair(hop_two, 1), pair(hop_one, 2)],
    }

    def between(slot):
        for number, actions in plan.items():
            if number % 2 == slot:

                @pl.when(2 * step + slot == number)
                def _():
                    for action in actions:
                        action()

    attend_back_kernel(*inputs, *outputs, *scratch, between=between)

    @pl.when(step == pl.num_programs(0) - 1)
    def _():
        every(chunks, mlp_last)
        every(levels, out_last)

        def drain(i):
            mlp_to_core(i).wait_send()
            mlp.drain(i)

        def out_drain(i):
            out_to_core(i).wait_send()
            out.drain(i)

        every(chunks, drain)
        every(levels, out_drain)


def attend_back_sum_call(
    q_raw, k_raw, value, attended, lse, d_attended, gains, bounds, grads, d_out, before, collective_id
):
    rows, width = q_raw.shape
    pairs = width // 128
    share, cols = grads.shape[-2:]
    pair = pl.BlockSpec((rows, 128), lambda j: (0, j))
    small = lambda a: pl.BlockSpec(a.shape, lambda j: (0,) * a.ndim)
    anywhere = pl.BlockSpec(memory_space=pl.ANY)
    low = jax.ShapeDtypeStruct((rows, width), LOW)

    def scratch(chunks, cols):
        own = [pltpu.VMEM((chunks, 2, 2, share, cols), LOW), pltpu.SemaphoreType.DMA((chunks,))]
        return own + flow_scratch(chunks, share, cols)

    return pl.pallas_call(
        attend_back_sum_kernel,
        grid=(pairs,),
        in_specs=[pair] * 6 + [small(gains), small(bounds), anywhere, anywhere, small(before)],
        out_specs=[
            pair, pair, pair,
            pl.BlockSpec((1, 2, 128), lambda j: (j, 0, 0)),
            small(before),
            pl.BlockSpec((share, d_out.shape[-1]), lambda j: (0, 0)),
        ],
        out_shape=[
            low, low, low,
            jax.ShapeDtypeStruct((pairs, 2, 128), F32),
            jax.ShapeDtypeStruct(before.shape, F32),
            jax.ShapeDtypeStruct((share, d_out.shape[-1]), F32),
        ],
        scratch_shapes=attend_back_scratch(rows)
        + scratch(grads.shape[0], cols)
        + scratch(d_out.shape[0], d_out.shape[-1]),
        compiler_params=pltpu.CompilerParams(
            collective_id=collective_id, has_side_effects=True, vmem_limit_bytes=VMEM_BYTES
        ),
        name="attend_back_sum",
    )(q_raw, k_raw, value, attended, lse, d_attended, gains, bounds, grads, d_out, before)


def attend_back_call(q_raw, k_raw, value, attended, lse, d_attended, gains, bounds):
    rows, width = q_raw.shape
    pairs = width // 128
    pair = pl.BlockSpec((rows, 128), lambda j: (0, j))
    small = lambda a: pl.BlockSpec(a.shape, lambda j: (0, 0))
    low = jax.ShapeDtypeStruct((rows, width), LOW)
    return pl.pallas_call(
        attend_back_kernel,
        grid=(pairs,),
        in_specs=[pair] * 6 + [small(gains), small(bounds)],
        out_specs=[pair, pair, pair, pl.BlockSpec((1, 2, 128), lambda j: (j, 0, 0))],
        out_shape=[low, low, low, jax.ShapeDtypeStruct((pairs, 2, 128), F32)],
        scratch_shapes=attend_back_scratch(rows),
        compiler_params=pltpu.CompilerParams(vmem_limit_bytes=VMEM_BYTES),
        name="attend_back",
    )(q_raw, k_raw, value, attended, lse, d_attended, gains, bounds)


def mlp_kernel(o_ref, emb_ref, wout_ref, wup_ref, wdn_ref, vec_ref, x1_ref, h2_ref, act_ref, slope_ref, x2_ref):
    step = pl.program_id(0)
    rows, _ = o_ref.shape
    groups, _, part = wout_ref.shape
    tile = 256

    @pl.when(step == 0)
    def _():
        for at in range(rows // tile):
            span = slice(at * tile, (at + 1) * tile)
            branch = mm_nt(o_ref[span, :part], wout_ref[0])
            for group in range(1, groups):
                branch += mm_nt(o_ref[span, group * part : (group + 1) * part], wout_ref[group])
            middle = emb_ref[span, :] + branch
            x1_ref[span, :] = middle
            x2_ref[span, :] = middle
            normed, _ = row_norm(middle)
            h2_ref[span, :] = (normed * vec_ref[1:2]).astype(LOW)

    tile = 256
    spans = [slice(at * tile, (at + 1) * tile) for at in range(rows // tile)]
    hidden = mm(h2_ref[spans[0], :], wup_ref[0])
    for at, span in enumerate(spans):
        now = hidden
        if at + 1 < len(spans):
            hidden = mm(h2_ref[spans[at + 1], :], wup_ref[0])
        active, slope = gelu_pair(now)
        active = active.astype(LOW)
        act_ref[span, :] = active
        slope_ref[span, :] = slope.astype(LOW)
        x2_ref[span, :] += mm_nt(active, wdn_ref[0])


def mlp_call(attended, embedded, w_out, w_up, w_dn, vectors):
    rows, width = embedded.shape
    groups, _, per = w_up.shape
    chunk = per
    hidden = groups * per
    whole = lambda a: pl.BlockSpec(a.shape, lambda j: (0,) * a.ndim)
    weight = pl.BlockSpec((1, width, chunk), lambda j: (j, 0, 0))
    full = pl.BlockSpec((rows, width), lambda j: (0, 0))
    piece = pl.BlockSpec((rows, chunk), lambda j: (0, j))
    return pl.pallas_call(
        mlp_kernel,
        grid=(hidden // chunk,),
        in_specs=[whole(attended), whole(embedded), whole(w_out), weight, weight, whole(vectors)],
        out_specs=[full, full, piece, piece, full],
        out_shape=[
            jax.ShapeDtypeStruct((rows, width), F32),
            jax.ShapeDtypeStruct((rows, width), LOW),
            jax.ShapeDtypeStruct((rows, hidden), LOW),
            jax.ShapeDtypeStruct((rows, hidden), LOW),
            jax.ShapeDtypeStruct((rows, width), F32),
        ],
        compiler_params=pltpu.CompilerParams(vmem_limit_bytes=VMEM_BYTES),
        name="mlp",
    )(attended, embedded, w_out, w_up, w_dn, vectors)


def pool_kernel(
    pack_ref, x2_ref, label_ref, wcls_ref, vec_ref, bound_ref, valid_ref,
    dx2_ref, dcls_ref, loss_ref, dvec_ref,
    norm_ref, inv_ref,
    *, images, image_count,
):
    rows, width = x2_ref.shape
    tile = 256
    root = width**0.5
    gain = vec_ref[2:3]
    query = vec_ref[3:4]
    lane = lax.broadcasted_iota(jnp.int32, (rows, 128), 1)
    marks = image_marks(bound_ref, rows) & (lane < 64)
    logits = []
    for at in range(rows // tile):
        span = slice(at * tile, (at + 1) * tile)
        normed, inverse = row_norm(x2_ref[span, :])
        norm_ref[span, :] = normed
        inv_ref[span, :] = jnp.broadcast_to(inverse, (tile, 128))
        logits.append(jnp.sum(normed * gain * query, axis=-1, keepdims=True) / root)
    logit = jnp.concatenate(logits, axis=0)
    masked = jnp.where(marks, logit, NEGATIVE)
    grown = jnp.exp(masked - jnp.max(masked, axis=0, keepdims=True))
    shares = jnp.where(marks, grown / jnp.sum(grown, axis=0, keepdims=True), 0.0)
    weight = jnp.sum(shares, axis=-1, keepdims=True)
    member = jnp.transpose(marks.astype(F32))[:16].astype(LOW)
    pooled = jnp.zeros((16, width), F32)
    for at in range(rows // tile):
        span = slice(at * tile, (at + 1) * tile)
        for entry in split_three(norm_ref[span, :] * gain * weight[span]):
            pooled += mm(member[:, span], entry)
    pooled_low = pooled.astype(LOW)
    scores = mm(pooled_low, wcls_ref[...])[:images] + SHIFT
    target = label_ref[...].astype(F32)
    valid = valid_ref[0, 0]
    soft = jnp.maximum(scores, 0.0) + jnp.log1p(jnp.exp(-jnp.abs(scores)))
    loss_rows = jnp.sum(soft - target * scores, axis=-1, keepdims=True)
    loss_ref[...] = jnp.broadcast_to(jnp.sum(loss_rows, axis=0, keepdims=True) * valid, loss_ref.shape)
    d_score = (1.0 / (1.0 + jnp.exp(-scores)) - target) / image_count * valid
    d_score = jnp.concatenate([d_score, jnp.zeros((16 - images, d_score.shape[1]), F32)], axis=0).astype(LOW)
    dcls_ref[...] = mm(jnp.transpose(pooled).astype(LOW), d_score).astype(LOW)
    d_pooled = mm_nt(d_score, wcls_ref[...])[:images]
    parts = jnp.concatenate(
        [entry.astype(F32) for entry in split_three(d_pooled)]
        + [jnp.zeros((128 - 3 * images, width), F32)],
        axis=0,
    ).astype(LOW)
    marks_f = marks.astype(F32)
    thrice = (
        marks_f + pltpu.roll(marks_f, images, 1) + pltpu.roll(marks_f, 2 * images, 1)
    ).astype(LOW)
    d_weights = []
    for at in range(rows // tile):
        span = slice(at * tile, (at + 1) * tile)
        spread = mm(thrice[span], parts)
        dx2_ref[span, :] = spread
        d_weights.append(jnp.sum(spread * (norm_ref[span, :] * gain), axis=-1, keepdims=True))
    d_weight = jnp.concatenate(d_weights, axis=0)
    inside = jnp.sum(shares * d_weight, axis=0, keepdims=True)
    d_logit = weight * (d_weight - jnp.sum(marks_f * inside, axis=-1, keepdims=True))
    gain_sum = jnp.zeros((1, width), F32)
    query_sum = jnp.zeros((1, width), F32)
    for at in range(rows // tile):
        span = slice(at * tile, (at + 1) * tile)
        normed = norm_ref[span, :]
        inverse = inv_ref[span, 0:1]
        d_last = dx2_ref[span, :] * weight[span] + d_logit[span] * (query / root)
        gain_sum += jnp.sum(d_last * normed, axis=0, keepdims=True)
        query_sum += jnp.sum(d_logit[span] * normed, axis=0, keepdims=True)
        dx2_ref[span, :] = row_norm_back(d_last, gain, normed, inverse)
    dvec_ref[0:1, :] = gain_sum
    dvec_ref[1:2, :] = query_sum * gain / root


def pool_call(pack, x2, labels, w_cls, vectors, bounds, valid, images, image_count):
    rows, width = x2.shape
    classes = labels.shape[1]
    whole = lambda a: pl.BlockSpec(a.shape, lambda j, p: (0,) * a.ndim)
    full = lambda *shape: pl.BlockSpec(shape, lambda j, p: (0,) * len(shape))
    return pl.pallas_call(
        functools.partial(pool_kernel, images=images, image_count=image_count),
        grid_spec=pltpu.PrefetchScalarGridSpec(
            num_scalar_prefetch=1,
            grid=(1,),
            in_specs=[
                whole(x2),
                pl.BlockSpec((images, classes), lambda j, p: (p[0], 0)),
                whole(w_cls),
                whole(vectors),
                whole(bounds),
                pl.BlockSpec(memory_space=pltpu.SMEM),
            ],
            out_specs=[full(rows, width), full(width, classes), full(8, 128), full(2, width)],
            scratch_shapes=[pltpu.VMEM((rows, width), F32), pltpu.VMEM((rows, 128), F32)],
        ),
        out_shape=[
            jax.ShapeDtypeStruct((rows, width), F32),
            jax.ShapeDtypeStruct((width, classes), LOW),
            jax.ShapeDtypeStruct((8, 128), F32),
            jax.ShapeDtypeStruct((2, width), F32),
        ],
        compiler_params=pltpu.CompilerParams(vmem_limit_bytes=VMEM_BYTES),
        name="pool",
    )(pack, x2, labels, w_cls, vectors, bounds, valid)


def mlp_back_kernel(
    dx2_ref, act_ref, slope_ref, h2_ref, x1_ref, o_ref, wout_ref, wup_ref, wdn_ref, vec_ref,
    dmlp_ref, dout_ref, do_ref, dmid_ref, dvec_ref,
    low_ref, lowt_ref, h2t_ref, acc_ref, dh_ref,
    keep=None, between=None,
):
    step = pl.program_id(0)
    rows, width = dx2_ref.shape
    groups, _, part = wout_ref.shape
    tile = 256

    @pl.when(step == 0)
    def _():
        for at in range(rows // tile):
            span = slice(at * tile, (at + 1) * tile)
            values = dx2_ref[span, :]
            low_ref[span, :] = values.astype(LOW)
            lowt_ref[:, span] = jnp.transpose(values).astype(LOW)
            h2t_ref[:, span] = jnp.transpose(h2_ref[span, :].astype(F32)).astype(LOW)
            acc_ref[span, :] = jnp.zeros((tile, width), F32)

    wide = 512
    for at in range(rows // wide):
        span = slice(at * wide, (at + 1) * wide)
        d_hidden = (mm(low_ref[span, :], wdn_ref[0]) * slope_ref[span, :].astype(F32)).astype(LOW)
        dh_ref[span, :] = d_hidden
        acc_ref[span, :] += mm_nt(d_hidden, wup_ref[0])

    def grads(put):
        for at in range(width // 192):
            span = slice(at * 192, (at + 1) * 192)
            put(0, at, mm(lowt_ref[span, :], act_ref[...]).astype(LOW))
            put(1, at, mm(h2t_ref[span, :], dh_ref[...]).astype(LOW))

    def put_out(kind, at, value):
        dmlp_ref[kind, 0, at * 192 : (at + 1) * 192, :] = value

    if keep is None:
        grads(put_out)
    else:
        between(2 * step, 0)
        pl.when(step < 1)(lambda: grads(keep))
        pl.when(step >= 1)(lambda: grads(put_out))
        between(2 * step + 1, 1)

    @pl.when(step == pl.num_programs(0) - 1)
    def _():
        gain = vec_ref[1:2]
        gain_sum = jnp.zeros((1, width), F32)
        for at in range(rows // tile):
            span = slice(at * tile, (at + 1) * tile)
            normed, inverse = row_norm(x1_ref[span, :])
            d_second = acc_ref[span, :]
            gain_sum += jnp.sum(d_second * normed, axis=0, keepdims=True)
            d_middle = dx2_ref[span, :] + row_norm_back(d_second, gain, normed, inverse)
            dmid_ref[span, :] = d_middle
            low = d_middle.astype(LOW)
            lowt_ref[:, span] = jnp.transpose(d_middle).astype(LOW)
            do_ref[span, :] = jnp.concatenate(
                [mm(low, wout_ref[group]) for group in range(groups)], axis=1
            ).astype(LOW)
        dvec_ref[...] = gain_sum
        for group in range(groups):
            piece = o_ref[:, group * part : (group + 1) * part]
            for at in range(width // tile):
                span = slice(at * tile, (at + 1) * tile)
                dout_ref[group, span, :] = mm(lowt_ref[span, :], piece).astype(LOW)


def mlp_back_call(dx2, active, slope, h2, x1, attended, w_out, w_up, w_dn, vectors):
    rows, width = dx2.shape
    groups, _, per = w_up.shape
    chunk = per
    hidden = groups * per
    whole = lambda a: pl.BlockSpec(a.shape, lambda j: (0,) * a.ndim, pipeline_mode=pl.Buffered(1))
    weight = pl.BlockSpec((1, width, chunk), lambda j: (j, 0, 0))
    piece = pl.BlockSpec((rows, chunk), lambda j: (0, j))
    full = lambda *shape: pl.BlockSpec(shape, lambda j: (0,) * len(shape))
    return pl.pallas_call(
        mlp_back_kernel,
        grid=(hidden // chunk,),
        in_specs=[
            whole(dx2), piece, piece, whole(h2), whole(x1), whole(attended), whole(w_out),
            weight, weight, whole(vectors),
        ],
        out_specs=[
            pl.BlockSpec((2, 1, width, chunk), lambda j: (0, j, 0, 0)),
            full(*w_out.shape),
            full(rows, width),
            full(rows, width),
            full(1, width),
        ],
        out_shape=[
            jax.ShapeDtypeStruct((2,) + w_up.shape, LOW),
            jax.ShapeDtypeStruct(w_out.shape, LOW),
            jax.ShapeDtypeStruct((rows, width), LOW),
            jax.ShapeDtypeStruct((rows, width), F32),
            jax.ShapeDtypeStruct((1, width), F32),
        ],
        scratch_shapes=[
            pltpu.VMEM((rows, width), LOW),
            pltpu.VMEM((width, rows), LOW),
            pltpu.VMEM((width, rows), LOW),
            pltpu.VMEM((rows, width), F32),
            pltpu.VMEM((rows, chunk), LOW),
        ],
        compiler_params=pltpu.CompilerParams(vmem_limit_bytes=VMEM_BYTES),
        name="mlp_back",
    )(dx2, active, slope, h2, x1, attended, w_out, w_up, w_dn, vectors)


def embed_back_kernel(
    pack_ref, dq_ref, dk_ref, dv_ref, h1_ref, emb_ref, dmid_ref, pix_ref, coord_ref, win_ref, vec_ref,
    din_ref, dpp_ref, dvec_ref,
    h1t_ref, join_ref, acc_ref,
):
    step = pl.program_id(0)
    rows, width = h1_ref.shape
    groups = pl.num_programs(0)
    part = win_ref.shape[2] // 3
    tile = 256

    @pl.when(step == 0)
    def _():
        for at in range(rows // tile):
            span = slice(at * tile, (at + 1) * tile)
            h1t_ref[:, span] = jnp.transpose(h1_ref[span, :].astype(F32)).astype(LOW)
            acc_ref[span, :] = jnp.zeros((tile, width), F32)

    for group in range(width // part):

        @pl.when(step == group)
        def _():
            mine = slice(group * part, (group + 1) * part)
            join_ref[...] = jnp.concatenate([dq_ref[:, mine], dk_ref[:, mine], dv_ref[:, mine]], axis=1)

    for at in range(rows // tile):
        span = slice(at * tile, (at + 1) * tile)
        acc_ref[span, :] += mm_nt(join_ref[span, :], win_ref[0])
    for at in range(width // tile):
        span = slice(at * tile, (at + 1) * tile)
        din_ref[0, span, :] = mm(h1t_ref[span, :], join_ref[...]).astype(LOW)

    @pl.when(step == groups - 1)
    def _():
        gain = vec_ref[0:1]
        pixels = pix_ref.shape[1]
        spots = (dpp_ref.shape[1] - pixels) // 2
        gain_sum = jnp.zeros((1, width), F32)
        for at in range(rows // tile):
            span = slice(at * tile, (at + 1) * tile)
            normed, inverse = row_norm(emb_ref[span, :])
            d_first = acc_ref[span, :]
            gain_sum += jnp.sum(d_first * normed, axis=0, keepdims=True)
            d_embed = dmid_ref[span, :] + row_norm_back(d_first, gain, normed, inverse)
            h1t_ref[:, span] = jnp.transpose(d_embed).astype(LOW)
        dvec_ref[...] = gain_sum
        lane = lax.broadcasted_iota(jnp.int32, (rows, 2 * spots), 1)
        hot = ((lane == coord_ref[:, 0:1]) | (lane - spots == coord_ref[:, 1:2])).astype(F32).astype(LOW)
        for at in range(width // tile):
            span = slice(at * tile, (at + 1) * tile)
            dpp_ref[span, :pixels] = mm(h1t_ref[span, :], pix_ref[...]).astype(LOW)
            dpp_ref[span, pixels:] = mm(h1t_ref[span, :], hot).astype(LOW)


def embed_back_call(pack, dq, dk, dv, h1, embedded, d_middle, pixels, coords, w_in, w_pp_shape, vectors):
    rows, width = h1.shape
    groups = w_in.shape[0]
    whole = lambda a: pl.BlockSpec(a.shape, lambda j, p: (0,) * a.ndim, pipeline_mode=pl.Buffered(1))
    full = lambda *shape: pl.BlockSpec(shape, lambda j, p: (0,) * len(shape))
    weight = pl.BlockSpec((1,) + w_in.shape[1:], lambda j, p: (j, 0, 0))
    return pl.pallas_call(
        embed_back_kernel,
        grid_spec=pltpu.PrefetchScalarGridSpec(
            num_scalar_prefetch=1,
            grid=(groups,),
            in_specs=[
                whole(dq), whole(dk), whole(dv), whole(h1), whole(embedded), whole(d_middle),
                pl.BlockSpec((rows, pixels.shape[1]), lambda j, p: (p[0], 0)),
                pl.BlockSpec((rows, 2), lambda j, p: (p[0], 0)),
                weight,
                whole(vectors),
            ],
            out_specs=[weight, full(*w_pp_shape), full(1, width)],
            scratch_shapes=[
                pltpu.VMEM((width, rows), LOW),
                pltpu.VMEM((rows, w_in.shape[2]), LOW),
                pltpu.VMEM((rows, width), F32),
            ],
        ),
        out_shape=[
            jax.ShapeDtypeStruct(w_in.shape, LOW),
            jax.ShapeDtypeStruct(w_pp_shape, LOW),
            jax.ShapeDtypeStruct((1, width), F32),
        ],
        compiler_params=pltpu.CompilerParams(vmem_limit_bytes=VMEM_BYTES),
        name="embed_back",
    )(pack, dq, dk, dv, h1, embedded, d_middle, pixels, coords, w_in, vectors)


def pack_step(pack, valid, pixels, coords, lengths, labels, weights, vectors, head_gains, image_count, close=False):
    if close:
        bounds, gains = weights[6:]
        weights = weights[:6]
    w_pp, w_in, w_out, w_up, w_dn, w_cls = weights
    packs, images = lengths.shape
    rows = pixels.shape[0] // packs
    width = vectors.shape[1]
    if not close:
        mine = lax.dynamic_index_in_dim(lengths, pack[0], 0, keepdims=False)
        ends = jnp.cumsum(mine)
        fill = jnp.full((64 - images,), 1 << 30, jnp.int32)
        starts = jnp.concatenate([ends - mine, fill])
        ends = jnp.concatenate([ends, fill])
        bounds = jnp.stack([jnp.tile(starts, 2), jnp.tile(ends, 2)])
        gains = jnp.tile(head_gains, (1, 2))
    if close:
        embedded, h1, q_raw, k_raw, value, attended, lse, w_in, w_out, w_up, w_dn, w_cls = forward_call(
            weights, pixels, coords, vectors, gains, bounds, packs, 0
        )
    else:
        places = coords.T
        embedded, h1, q_raw, k_raw, value = embed_call(pack, pixels, places, w_pp, w_in, vectors, rows)
        attended, lse = attend_call(q_raw, k_raw, value, gains, bounds)
    x1, h2, active, slope, x2 = mlp_call(attended, embedded, w_out, w_up, w_dn, vectors)
    dx2, d_cls, loss, dvec_pool = pool_call(
        pack, x2, labels, w_cls, vectors, bounds, valid, images, image_count
    )
    if close:
        share = width // 8
        cut = lambda entry: entry.reshape(entry.shape[:-2] + (2, 2, 2, share) + entry.shape[-1:])
        d_mlp, d_out, d_attended, d_middle, dvec_two, share_mlp, share_cls = mlp_back_sum_call(
            dx2, active, slope, h2, x1, attended, w_out, w_up, w_dn, vectors, cut(d_cls), 1
        )
        d_mlp = d_mlp.reshape((-1, 2, 2, 2, share, width))
        dq, dk, dv, d_gain, share_mlp, share_out = attend_back_sum_call(
            q_raw, k_raw, value, attended, lse, d_attended, gains, bounds, d_mlp, cut(d_out), share_mlp, 2
        )
        share_in, share_pp, small, squares = embed_back_sum_call(
            dq, dk, dv, h1, embedded, d_middle, pixels, coords, w_in, weights[0].shape[1], vectors,
            dvec_two, dvec_pool, d_gain, loss, share_mlp, share_cls, share_out, packs, 3,
        )
        return share_pp, share_in, share_out, share_mlp, share_cls, small, squares
    d_mlp, d_out, d_attended, d_middle, dvec_two = mlp_back_call(
        dx2, active, slope, h2, x1, attended, w_out, w_up, w_dn, vectors
    )
    d_vec = jnp.concatenate([jnp.zeros_like(dvec_two), dvec_two, dvec_pool], axis=0)
    dq, dk, dv, d_gain = attend_back_call(q_raw, k_raw, value, attended, lse, d_attended, gains, bounds)
    d_in, d_pp, dvec_one = embed_back_call(
        pack, dq, dk, dv, h1, embedded, d_middle, pixels, places, w_in, w_pp.shape, vectors
    )
    d_gains = jnp.sum(d_gain.reshape(-1, 2, 2, 64), axis=(0, 2))
    return (d_pp, d_in, d_out, d_mlp[1], d_mlp[0], d_cls), d_vec.at[0].set(dvec_one[0]), d_gains, loss[0, 0]


MESH = pl.DeviceIdType.MESH


class Seat:
    def __init__(self):
        self.me = lax.axis_index("dp")
        self.z = lax.axis_index("tensor")
        self.c = lax.rem(self.me, 2)
        self.x = lax.rem(lax.div(self.me, 2), 2)
        self.y = lax.div(self.me, 4)
        self.core = self.me + 1 - 2 * self.c
        self.xn = self.me + 2 - 4 * self.x
        self.yn = self.me + 4 - 8 * self.y
        self.diag = self.xn + 4 - 8 * self.y


def link(src, dst, sems, at, device):
    return pltpu.make_async_remote_copy(
        src_ref=src,
        dst_ref=dst,
        send_sem=sems[0].at[at],
        recv_sem=sems[1].at[at],
        device_id=device,
        device_id_type=MESH,
    )


def greet(seat, depth):
    barrier = pltpu.get_barrier_semaphore()
    for ahead in range(1, 8):
        pl.semaphore_signal(
            barrier, inc=1, device_id={"dp": lax.rem(seat.me + ahead, 8)}, device_id_type=MESH
        )
    for ahead in range(1, depth):
        pl.semaphore_signal(
            barrier, inc=1, device_id={"tensor": lax.rem(seat.z + ahead, depth)}, device_id_type=MESH
        )
    pl.semaphore_wait(barrier, 6 + depth)


class Gather:
    def __init__(self, seat, shards, outs, split, units, own_sem, sems):
        self.seat, self.shards, self.outs, self.split, self.units = seat, shards, outs, split, units
        self.own_sem, self.sems = own_sem, sems
        self.share = shards[0].shape[0]

    def rows(self, owner):
        return pl.ds(pl.multiple_of(owner * self.share, self.share), self.share)

    def column(self, u, owner):
        k, cols = self.units[u]
        if self.split[k]:
            return self.outs[k].at[:, self.rows(owner), cols]
        return self.outs[k].at[self.rows(owner), cols]

    def halves(self, u, owner, which):
        k, cols = self.units[u]
        if self.split[k]:
            return self.outs[k].at[2 * which : 2 * which + 2, self.rows(owner), cols]
        half = self.share // 2
        start = pl.multiple_of(owner * self.share + which * half, half)
        return self.outs[k].at[pl.ds(start, half), cols]

    def block(self, u, level):
        k, cols = self.units[u]
        return self.outs[k].at[level, self.rows(self.seat.me), cols]

    def keep(self, u):
        k, cols = self.units[u]
        mine = self.block(u, self.seat.z) if self.split[k] else self.column(u, self.seat.me)
        return pltpu.make_async_copy(self.shards[k].at[:, cols], mine, self.own_sem.at[u])

    def along(self, u, hop, way):
        k, cols = self.units[u]
        level = self.seat.z - way * hop
        source = self.shards[k].at[:, cols] if hop == 0 else self.block(u, level)
        at = (u, hop + (0 if way > 0 else 3))
        return link(source, self.block(u, level), self.sems, at, {"tensor": self.seat.z + way})

    def arrives(self, u, hop, way):
        level = self.seat.z - way * (hop + 1)
        at = (u, hop + (0 if way > 0 else 3))
        return link(self.block(u, level), self.block(u, level), self.sems, at, {"tensor": self.seat.z - way})

    def sends(self, hop, way):
        level, to = self.seat.z - way * hop, self.seat.z + way
        return (level >= 0) & (level < 4) & (to >= 0) & (to < 4)

    def gets(self, hop, way):
        level = self.seat.z - way * (hop + 1)
        return (level >= 0) & (level < 4)

    def z(self, u, hop):
        for way in (1, -1):
            if hop > 0:

                @pl.when(self.gets(hop - 1, way))
                def _():
                    self.arrives(u, hop - 1, way).wait_recv()

            if hop < 3:

                @pl.when(self.sends(hop, way))
                def _():
                    self.along(u, hop, way).start()

    def copy(self, u, region, at, device):
        return link(region, region, self.sems, (u, at), {"dp": device})

    def own_x(self, u):
        return self.copy(u, self.column(u, self.seat.me), 6, self.seat.xn)

    def own_y(self, u):
        return self.copy(u, self.column(u, self.seat.me), 7, self.seat.yn)

    def pass_x(self, u):
        return self.copy(u, self.halves(u, self.seat.yn, 1), 8, self.seat.xn)

    def pass_y(self, u):
        return self.copy(u, self.halves(u, self.seat.xn, 0), 9, self.seat.yn)

    def owner(self, which):
        return (self.seat.me, self.seat.xn, self.seat.yn, self.seat.diag)[which]

    def over(self, u, which):
        return self.copy(u, self.column(u, self.owner(which)), 10 + which, self.seat.core)

    def plane(self, u):
        self.keep(u).wait()
        self.own_x(u).start()
        self.own_y(u).start()
        self.over(u, 0).start()

    def relay(self, u):
        s = self.seat
        self.copy(u, self.column(u, s.xn), 6, s.xn).wait_recv()
        self.pass_y(u).start()
        self.over(u, 1).start()
        self.copy(u, self.column(u, s.yn), 7, s.yn).wait_recv()
        self.pass_x(u).start()
        self.over(u, 2).start()

    def corner(self, u):
        s = self.seat
        self.copy(u, self.halves(u, s.diag, 1), 8, s.xn).wait_recv()
        self.copy(u, self.halves(u, s.diag, 0), 9, s.yn).wait_recv()
        self.over(u, 3).start()

    def arrived(self, u):
        s = self.seat
        for which in range(4):
            theirs = self.column(u, self.owner(which) + 1 - 2 * s.c)
            self.copy(u, theirs, 10 + which, s.core).wait_recv()

    def drain(self, u):
        if self.split[self.units[u][0]]:
            for hop in range(3):
                for way in (1, -1):

                    @pl.when(self.sends(hop, way))
                    def _():
                        self.along(u, hop, way).wait_send()

        for copy in (self.own_x(u), self.own_y(u), self.pass_x(u), self.pass_y(u)):
            copy.wait_send()
        for which in range(4):
            self.over(u, which).wait_send()


FORWARD_SPLIT = (False, True, True, True, True, False)


def forward_kernel(
    pp_in, in_in, out_in, up_in, dn_in, cls_in, pix_hbm, coord_ref, vec_ref, gain_ref, bound_ref,
    emb_hbm, h1_hbm, q_hbm, k_hbm, v_hbm, o_ref, lse_ref, win_hbm, wout_hbm, wup_hbm, wdn_hbm, wcls_hbm,
    wp_ref, win_ref, pix_ref, emb_ref, h1_ref, q_ref, k_ref, v_ref, ka_ref, va_ref, qa_ref,
    own_sem, send_sem, recv_sem, copy_sem,
    *, packs,
):
    step = pl.program_id(0)
    rows, pixels = pix_ref.shape
    groups = win_ref.shape[0]
    part = win_ref.shape[2] // 3
    spots = (wp_ref.shape[1] - pixels) // 2
    half = wup_hbm.shape[2] // 2
    tile = 256
    seat = Seat()
    everything, left, right = slice(None), slice(0, half), slice(half, 2 * half)
    units = (
        (0, everything), (1, everything), (2, everything),
        (3, left), (3, right), (4, left), (4, right), (5, everything),
    )
    pp, w_in, out, up_a, up_b, dn_a, dn_b, cls = range(8)
    flow = Gather(
        seat,
        (pp_in, in_in, out_in, up_in, dn_in, cls_in),
        (wp_ref, win_ref, wout_hbm, wup_hbm, wdn_hbm, wcls_hbm),
        FORWARD_SPLIT,
        units,
        own_sem,
        (send_sem, recv_sem),
    )
    pack = jnp.minimum(seat.z, packs - 1)
    pix_copy = pltpu.make_async_copy(
        pix_hbm.at[pl.ds(pl.multiple_of(pack * rows, rows), rows)], pix_ref, copy_sem.at[0]
    )
    results = [
        pltpu.make_async_copy(source, target, copy_sem.at[1 + n])
        for n, (source, target) in enumerate(
            ((emb_ref, emb_hbm), (h1_ref, h1_hbm), (q_ref, q_hbm), (k_ref, k_hbm), (v_ref, v_hbm), (win_ref, win_hbm))
        )
    ]

    def embed(at):
        span = slice(at * tile, (at + 1) * tile)
        start = pl.multiple_of(pack * rows + at * tile, tile)
        place = lax.broadcasted_iota(jnp.int32, (2 * spots, tile), 0)
        across = coord_ref[0:1, pl.ds(start, tile)]
        down = coord_ref[1:2, pl.ds(start, tile)]
        hot = jnp.transpose(((place == across) | (place - spots == down)).astype(F32)).astype(LOW)
        embedded = mm_nt(pix_ref[span, :], wp_ref[:, :pixels]) + mm_nt(hot, wp_ref[:, pixels:])
        emb_ref[span, :] = embedded
        normed, _ = row_norm(embedded)
        h1_ref[span, :] = (normed * vec_ref[0:1]).astype(LOW)

    def project(at):
        span = slice(at * tile, (at + 1) * tile)
        first = h1_ref[span, :]
        parts = [mm(first, win_ref[group]) for group in range(groups)]
        q_ref[span, :] = jnp.concatenate([entry[:, :part] for entry in parts], axis=1)
        k_ref[span, :] = jnp.concatenate([entry[:, part : 2 * part] for entry in parts], axis=1)
        v_ref[span, :] = jnp.concatenate([entry[:, 2 * part :].astype(LOW) for entry in parts], axis=1)

    @pl.when(step == 0)
    def _():
        pix_copy.start()
        for u in range(8):
            flow.keep(u).start()
        greet(seat, 4)
        flow.z(w_in, 0)
        flow.plane(pp)
        flow.z(w_in, 1)
        flow.relay(pp)
        flow.z(w_in, 2)
        flow.corner(pp)
        flow.z(w_in, 3)
        flow.plane(w_in)
        flow.z(out, 0)
        flow.arrived(pp)
        pix_copy.wait()
        embed(0)
        flow.z(out, 1)
        embed(1)
        flow.z(out, 2)
        flow.z(up_a, 0)
        embed(2)
        flow.z(out, 3)
        flow.plane(out)
        flow.z(up_a, 1)
        embed(3)
        flow.z(up_a, 2)
        results[0].start()
        results[1].start()
        flow.relay(w_in)
        flow.z(up_a, 3)
        flow.z(up_b, 0)
        flow.relay(out)
        flow.plane(up_a)
        flow.corner(w_in)
        flow.z(up_b, 1)
        flow.arrived(w_in)
        results[5].start()
        project(0)
        flow.corner(out)
        flow.z(up_b, 2)
        project(1)
        flow.z(up_b, 3)
        flow.plane(up_b)
        flow.z(dn_a, 0)
        project(2)
        flow.relay(up_a)
        flow.z(dn_a, 1)
        project(3)
        for n in (2, 3, 4):
            results[n].start()

    plan = {
        0: [lambda: flow.z(dn_a, 2)],
        1: [lambda: flow.corner(up_a), lambda: flow.z(dn_a, 3), lambda: flow.plane(dn_a)],
        2: [lambda: flow.z(dn_b, 0)],
        3: [lambda: flow.relay(up_b), lambda: flow.z(dn_b, 1)],
        4: [lambda: flow.z(dn_b, 2)],
        5: [lambda: flow.corner(up_b), lambda: flow.z(dn_b, 3), lambda: flow.plane(dn_b)],
        7: [lambda: flow.relay(dn_a)],
        9: [lambda: flow.corner(dn_a), lambda: flow.plane(cls)],
        11: [lambda: flow.relay(dn_b)],
    }

    def between(slot):
        for number, actions in plan.items():
            if number % 2 == slot:

                @pl.when(2 * step + slot == number)
                def _():
                    for action in actions:
                        action()

    mine = pl.ds(pl.multiple_of(step * 128, 128), 128)
    attend_kernel(
        q_ref.at[:, mine], k_ref.at[:, mine], v_ref.at[:, mine], gain_ref, bound_ref, o_ref, lse_ref,
        ka_ref, va_ref, qa_ref, between=between,
    )

    @pl.when(step == pl.num_programs(0) - 1)
    def _():
        flow.corner(dn_b)
        flow.relay(cls)
        flow.corner(cls)
        for u in (out, up_a, up_b, dn_a, dn_b, cls):
            flow.arrived(u)
        for u in range(8):
            flow.drain(u)
        for copy in results:
            copy.wait()


def forward_call(shards, pixels, coords, vectors, gains, bounds, packs, collective_id):
    depth, width = 4, vectors.shape[1]
    rows = pixels.shape[0] // packs
    anywhere = pl.BlockSpec(memory_space=pl.ANY)
    small = lambda a: pl.BlockSpec(a.shape, lambda j: (0, 0))
    pair = pl.BlockSpec((rows, 128), lambda j: (0, j))
    weights = [
        jax.ShapeDtypeStruct(((depth, width) if apart else (width,)) + entry.shape[1:], LOW)
        for entry, apart in zip(shards, FORWARD_SPLIT)
    ]
    token = lambda dtype: jax.ShapeDtypeStruct((rows, width), dtype)
    held = lambda dtype: pltpu.VMEM((rows, width), dtype)
    return pl.pallas_call(
        functools.partial(forward_kernel, packs=packs),
        grid=(width // 128,),
        in_specs=[anywhere] * 7 + [small(coords), small(vectors), small(gains), small(bounds)],
        out_specs=[anywhere] * 5 + [pair, pair] + [anywhere] * 5,
        out_shape=[token(F32), token(LOW), token(F32), token(F32), token(LOW), token(LOW), token(F32)]
        + weights[1:],
        scratch_shapes=[
            pltpu.VMEM(weights[0].shape, LOW),
            pltpu.VMEM(weights[1].shape, LOW),
            pltpu.VMEM((rows, pixels.shape[1]), LOW),
            held(F32), held(LOW), held(F32), held(F32), held(LOW),
            pltpu.VMEM((rows, 256), LOW),
            pltpu.VMEM((rows, 256), LOW),
            pltpu.VMEM((2, rows, 256), LOW),
            pltpu.SemaphoreType.DMA((8,)),
            pltpu.SemaphoreType.DMA((8, 14)),
            pltpu.SemaphoreType.DMA((8, 14)),
            pltpu.SemaphoreType.DMA((7,)),
        ],
        compiler_params=pltpu.CompilerParams(
            collective_id=collective_id, has_side_effects=True, vmem_limit_bytes=VMEM_BYTES
        ),
        name="forward",
    )(*shards, pixels, coords, vectors, gains, bounds)


class Flow:
    def __init__(self, seat, level_of, own, core_in, plane_in, last_in, up_in, down_in, sems):
        self.seat, self.level_of, self.own, self.sems = seat, level_of, own, sems
        self.core_in, self.plane_in, self.last_in = core_in, plane_in, last_in
        self.up_in, self.down_in = up_in, down_in

    def to_core(self, i, source):
        return link(source, self.core_in.at[i], self.sems, (i, 0), {"dp": self.seat.core})

    def first(self, i, along_x):
        s = self.seat
        source = self.own(i).at[:, 1 - s.x] if along_x else self.own(i).at[1 - s.y]
        return link(source, self.plane_in.at[i], self.sems, (i, 1), {"dp": s.xn if along_x else s.yn})

    def second(self, i, along_x):
        s = self.seat
        source = self.own(i).at[s.y, 1 - s.x] if along_x else self.own(i).at[1 - s.y, s.x]
        return link(source, self.last_in.at[i], self.sems, (i, 2), {"dp": s.xn if along_x else s.yn})

    def along(self, i, way):
        s = self.seat
        buffer = self.up_in if way > 0 else self.down_in
        at = (i, 3 if way > 0 else 4)
        return link(self.own(i).at[s.y, s.x], buffer.at[i], self.sems, at, {"tensor": s.z + way})

    def x_first(self, i, then, other):
        pl.when(lax.rem(i, 2) == 0)(then)
        pl.when(lax.rem(i, 2) == 1)(other)

    def one(self, i):
        mine = self.own(i)
        mine[...] = mine[...] + self.core_in[i]
        self.x_first(i, lambda: self.first(i, True).start(), lambda: self.first(i, False).start())

    def two(self, i):
        s, mine = self.seat, self.own(i)

        def from_x():
            self.first(i, True).wait_recv()
            mine[:, s.x] = mine[:, s.x] + self.plane_in[i]
            self.second(i, False).start()

        def from_y():
            self.first(i, False).wait_recv()
            mine[s.y] = mine[s.y] + self.plane_in[i]
            self.second(i, True).start()

        self.x_first(i, from_x, from_y)

    def three(self, i):
        s, mine = self.seat, self.own(i)
        self.second(i, False).wait_recv()
        mine[s.y, s.x] = mine[s.y, s.x] + self.last_in[i]

        @pl.when((s.z == 0) & (self.level_of(i) > 0))
        def _():
            self.along(i, 1).start()

        @pl.when((s.z == 3) & (self.level_of(i) < 3))
        def _():
            self.along(i, -1).start()

    def hop(self, i, reach):
        s, mine = self.seat, self.own(i)

        @pl.when((s.z == reach) & (self.level_of(i) > reach))
        def _():
            self.along(i, 1).wait_recv()
            mine[s.y, s.x] = mine[s.y, s.x] + self.up_in[i]
            self.along(i, 1).start()

        @pl.when((s.z == 3 - reach) & (self.level_of(i) < 3 - reach))
        def _():
            self.along(i, -1).wait_recv()
            mine[s.y, s.x] = mine[s.y, s.x] + self.down_in[i]
            self.along(i, -1).start()

    def total(self, i):
        s = self.seat
        values = self.own(i)[s.y, s.x].astype(F32)

        @pl.when(s.z > 0)
        def _():
            self.along(i, 1).wait_recv()

        @pl.when(s.z < 3)
        def _():
            self.along(i, -1).wait_recv()

        @pl.when(s.z == 0)
        def _():
            self.up_in[i] = jnp.zeros(self.up_in.shape[1:], LOW)

        @pl.when(s.z == 3)
        def _():
            self.down_in[i] = jnp.zeros(self.down_in.shape[1:], LOW)

        return values + self.up_in[i].astype(F32) + self.down_in[i].astype(F32)

    def drain(self, i):
        s = self.seat
        self.first(i, True).wait_send()
        self.second(i, True).wait_send()

        @pl.when(s.z < self.level_of(i))
        def _():
            self.along(i, 1).wait_send()

        @pl.when(s.z > self.level_of(i))
        def _():
            self.along(i, -1).wait_send()


class Whole:
    def __init__(self, seat, own, core_in, plane_in, last_in, level_in, sems):
        self.seat, self.own, self.sems = seat, own, sems
        self.core_in, self.plane_in, self.last_in, self.level_in = core_in, plane_in, last_in, level_in
        self.half = core_in.shape[2] // 2

    def to_core(self, source):
        return link(source, self.core_in, self.sems, 0, {"dp": self.seat.core})

    def rows(self, which):
        return slice(which * self.half, (which + 1) * self.half)

    def first(self, which):
        s = self.seat
        rows = self.rows(which)
        source = self.own.at[1 - s.y, :, rows] if which else self.own.at[:, 1 - s.x, rows]
        return link(source, self.plane_in.at[which], self.sems, 1 + which, {"dp": s.yn if which else s.xn})

    def second(self, which):
        s = self.seat
        rows = self.rows(which)
        source = self.own.at[s.y, 1 - s.x, rows] if which else self.own.at[1 - s.y, s.x, rows]
        return link(source, self.last_in.at[which], self.sems, 3 + which, {"dp": s.xn if which else s.yn})

    def lift(self):
        s = self.seat
        return link(self.own.at[s.y, s.x], self.level_in.at[0], self.sems, 5, {"tensor": s.z + 1 - 2 * (s.z % 2)})

    def cross(self):
        s = self.seat
        return link(self.own.at[s.y, s.x], self.level_in.at[1], self.sems, 6, {"tensor": 3 - s.z})

    def give(self):
        s = self.seat
        return link(self.own.at[s.y, s.x], self.level_in.at[1], self.sems, 7, {"tensor": s.z + 1 - 2 * (s.z % 2)})

    def middle(self):
        return (self.seat.z == 1) | (self.seat.z == 2)

    def ends(self):
        return (self.seat.z == 0) | (self.seat.z == 3)

    def one(self):
        for a in range(2):
            for b in range(2):
                self.own[a, b] = self.own[a, b] + self.core_in[a, b]
        self.first(0).start()
        self.first(1).start()

    def two(self):
        s, own = self.seat, self.own
        for which in range(2):
            rows = self.rows(which)
            self.first(which).wait_recv()
            for a in range(2):
                if which:
                    own[s.y, a, rows] = own[s.y, a, rows] + self.plane_in[which, a]
                else:
                    own[a, s.x, rows] = own[a, s.x, rows] + self.plane_in[which, a]
            self.second(which).start()

    def three(self):
        s, own = self.seat, self.own
        for which in range(2):
            rows = self.rows(which)
            self.second(which).wait_recv()
            own[s.y, s.x, rows] = own[s.y, s.x, rows] + self.last_in[which]
        pl.when(self.ends())(lambda: self.lift().start())

    def four(self):
        s, own = self.seat, self.own

        @pl.when(self.middle())
        def _():
            self.lift().wait_recv()
            own[s.y, s.x] = own[s.y, s.x] + self.level_in[0]
            self.cross().start()

    def five(self):
        s, own = self.seat, self.own

        @pl.when(self.middle())
        def _():
            self.cross().wait_recv()
            self.cross().wait_send()
            own[s.y, s.x] = own[s.y, s.x] + self.level_in[1]
            self.give().start()

    def total(self):
        s = self.seat

        @pl.when(self.ends())
        def _():
            self.give().wait_recv()

        @pl.when(self.middle())
        def _():
            self.level_in[1] = self.own[s.y, s.x]

        return self.level_in[1].astype(F32)

    def drain(self):
        for which in range(2):
            self.first(which).wait_send()
            self.second(which).wait_send()
        pl.when(self.ends())(lambda: self.lift().wait_send())
        pl.when(self.middle())(lambda: self.give().wait_send())


class Tiny:
    def __init__(self, seat, value, came, sems):
        self.seat, self.value, self.came, self.sems = seat, value, came, sems

    def near(self, ahead, own):
        s = self.seat
        other = lax.rem(s.me + (ahead if own else 8 - ahead), 8)
        place = self.came.at[s.me if own else other]
        return link(self.value.at[0], place, self.sems, ahead - 1, {"dp": other})

    def far(self, ahead, own):
        s = self.seat
        other = lax.rem(s.z + (ahead if own else 4 - ahead), 4)
        place = self.came.at[8 + (s.z if own else other)]
        return link(self.value.at[1], place, self.sems, 6 + ahead, {"tensor": other})

    def start_plane(self):
        for ahead in range(1, 8):
            self.near(ahead, True).start()

    def total(self, first, count):
        total = self.came[first]
        for n in range(1, count):
            total = total + self.came[first + n]
        return total

    def turn_levels(self):
        for ahead in range(1, 8):
            self.near(ahead, False).wait_recv()
        self.came[self.seat.me] = self.value[0]
        self.value[1] = self.total(0, 8)
        for ahead in range(1, 4):
            self.far(ahead, True).start()

    def finish(self):
        for ahead in range(1, 4):
            self.far(ahead, False).wait_recv()
        self.came[8 + self.seat.z] = self.value[1]
        return self.total(8, 4)

    def drain(self):
        for ahead in range(1, 8):
            self.near(ahead, True).wait_send()
        for ahead in range(1, 4):
            self.far(ahead, True).wait_send()


def flow_scratch(chunks, share, cols):
    low = lambda *shape: pltpu.VMEM(shape, LOW)
    sems = lambda: pltpu.SemaphoreType.DMA((chunks, 5))
    return [
        low(chunks, 2, 2, share, cols),
        low(chunks, 2, share, cols),
        low(chunks, share, cols),
        low(chunks, share, cols),
        low(chunks, share, cols),
        sems(),
        sems(),
    ]


def whole_scratch(share, cols):
    low = lambda *shape: pltpu.VMEM(shape, LOW)
    return [
        low(2, 2, share, cols),
        low(2, 2, share // 2, cols),
        low(2, share // 2, cols),
        low(2, share, cols),
        pltpu.SemaphoreType.DMA((8,)),
        pltpu.SemaphoreType.DMA((8,)),
    ]


def tiny_scratch(shape):
    sems = lambda: pltpu.SemaphoreType.DMA((10,))
    return [pltpu.VMEM((2,) + shape, F32), pltpu.VMEM((12,) + shape, F32), sems(), sems()]


MLP_BACK_IO = (10, 5)
MLP_BACK_SCRATCH = 5


def mlp_back_sum_kernel(*refs):
    ins, outs = MLP_BACK_IO
    inputs, dcls_ref = refs[:ins], refs[ins]
    outputs = refs[ins + 1 : ins + 1 + outs]
    share_ref, cls_ref = refs[ins + 1 + outs : ins + 3 + outs]
    rest = refs[ins + 3 + outs :]
    scratch, rest = rest[:MLP_BACK_SCRATCH], rest[MLP_BACK_SCRATCH:]
    full, flow_refs = rest[0], rest[1:8]
    cls_own, cls_load, cls_refs = rest[8], rest[9], rest[10:16]
    step = pl.program_id(0)
    seat = Seat()
    c = seat.c
    share = full.shape[-2]
    flow = Flow(
        seat, lambda i: 1, lambda i: full.at[i, :, :, c], *flow_refs[:5], flow_refs[5:]
    )
    cls = Whole(seat, cls_own, *cls_refs[:4], cls_refs[4:])
    loading = pltpu.make_async_copy(dcls_ref.at[:, :, c], cls_own, cls_load)
    cls_to_core = cls.to_core(dcls_ref.at[:, :, 1 - c])

    def to_core(i):
        return flow.to_core(i, full.at[i, :, :, 1 - c])

    def one(i):
        to_core(i).wait_recv()
        flow.one(i)

    def last(i):
        @pl.when(seat.z == flow.level_of(i))
        def _():
            share_ref[i] = flow.total(i)

    @pl.when(step == 0)
    def _():
        loading.start()
        greet(seat, 4)
        cls_to_core.start()
        share_ref[...] = jnp.zeros(share_ref.shape, F32)

    def keep(kind, at, value):
        full[kind, at // 2, at % 2] = value.reshape(2, share, value.shape[1])

    def cls_total():
        cls_ref[...] = cls.total()

    def cls_one():
        loading.wait()
        cls_to_core.wait_recv()
        cls.one()

    plan = {
        0: [cls_one],
        1: [lambda: to_core(0).start(), lambda: to_core(1).start(), cls.two],
        2: [lambda: one(0), lambda: one(1), cls.three],
        4: [lambda: flow.two(0), lambda: flow.two(1), cls.four],
        5: [lambda: flow.three(0), lambda: flow.three(1)],
        6: [cls.five],
        7: [lambda: flow.hop(0, 1), lambda: flow.hop(1, 1)],
    }

    def between(now, odd):
        for number, actions in plan.items():
            if number % 2 != odd:
                continue

            @pl.when(now == number)
            def _():
                for action in actions:
                    action()

    mlp_back_kernel(*inputs, *outputs, *scratch, keep=keep, between=between)

    @pl.when(step == pl.num_programs(0) - 1)
    def _():
        cls_total()
        for i in range(2):
            last(i)
        for i in range(2):
            to_core(i).wait_send()
            flow.drain(i)
        cls_to_core.wait_send()
        cls.drain()


def mlp_back_sum_call(dx2, active, slope, h2, x1, attended, w_out, w_up, w_dn, vectors, d_cls, collective_id):
    rows, width = dx2.shape
    groups, _, per = w_up.shape
    chunk = per
    hidden = groups * per
    share, classes = d_cls.shape[-2:]
    turned = lambda j: j + 1 - 2 * (j % 2)
    whole = lambda a: pl.BlockSpec(a.shape, lambda j: (0,) * a.ndim, pipeline_mode=pl.Buffered(1))
    weight = pl.BlockSpec((1, width, chunk), lambda j: (turned(j), 0, 0))
    piece = pl.BlockSpec((rows, chunk), lambda j: (0, turned(j)))
    full = lambda *shape: pl.BlockSpec(shape, lambda j: (0,) * len(shape))
    late = lambda j: jnp.maximum(j - 1, 0)
    return pl.pallas_call(
        mlp_back_sum_kernel,
        grid=(hidden // chunk,),
        in_specs=[
            whole(dx2), piece, piece, whole(h2), whole(x1), whole(attended), whole(w_out),
            weight, weight, whole(vectors), pl.BlockSpec(memory_space=pl.ANY),
        ],
        out_specs=[
            pl.BlockSpec((2, 1, width, chunk), lambda j: (0, late(j), 0, 0)),
            full(*w_out.shape),
            full(rows, width),
            full(rows, width),
            full(1, width),
            full(2, share, width),
            full(share, classes),
        ],
        out_shape=[
            jax.ShapeDtypeStruct((2, groups - 1) + w_up.shape[1:], LOW),
            jax.ShapeDtypeStruct(w_out.shape, LOW),
            jax.ShapeDtypeStruct((rows, width), LOW),
            jax.ShapeDtypeStruct((rows, width), F32),
            jax.ShapeDtypeStruct((1, width), F32),
            jax.ShapeDtypeStruct((2, share, width), F32),
            jax.ShapeDtypeStruct((share, classes), F32),
        ],
        scratch_shapes=[
            pltpu.VMEM((rows, width), LOW),
            pltpu.VMEM((width, rows), LOW),
            pltpu.VMEM((width, rows), LOW),
            pltpu.VMEM((rows, width), F32),
            pltpu.VMEM((rows, chunk), LOW),
            pltpu.VMEM((2, 2, 2, 2, share, width), LOW),
        ]
        + flow_scratch(2, share, width)
        + [pltpu.VMEM((2, 2, share, classes), LOW), pltpu.SemaphoreType.DMA]
        + whole_scratch(share, classes),
        compiler_params=pltpu.CompilerParams(
            collective_id=collective_id, has_side_effects=True, vmem_limit_bytes=VMEM_BYTES
        ),
        name="mlp_back_sum",
    )(dx2, active, slope, h2, x1, attended, w_out, w_up, w_dn, vectors, d_cls)


def embed_back_sum_kernel(
    dq_hbm, dk_hbm, dv_hbm, h1_hbm, emb_hbm, dmid_hbm, pix_hbm, coord_ref, win_hbm, vec_ref,
    two_ref, pool_ref, gains_ref, loss_ref, mlp_ref, cls_ref, out_ref,
    in_ref, pp_ref, small_out, square_out,
    dq_ref, dk_ref, dv_ref, h1_ref, emb_ref, dmid_ref, pix_ref, win_ref, tile_sem, load_sem,
    h1t_ref, embt_ref, join_ref, hot_ref, in_full, pp_full,
    *rest, packs,
):
    rows, width = h1_ref.shape
    groups = 4
    part = win_ref.shape[2] // 3
    tile = 256
    seat = Seat()
    c = seat.c
    share = in_full.shape[-2]
    flow = Flow(
        seat, lambda i: (3 * i) % 4, lambda i: in_full.at[i, :, :, c], *rest[:5], rest[5:7]
    )
    pp = Whole(seat, pp_full.at[:, :, c], *rest[7:11], rest[11:13])
    small = Tiny(seat, rest[13], rest[14], rest[15:17])
    square = Tiny(seat, rest[17], rest[18], rest[19:21])
    small_value, square_value = rest[13], rest[17]
    pp_to_core = pp.to_core(pp_full.at[:, :, 1 - c])
    leader = jnp.where(seat.z == 0, 1.0, 0.0)

    def in_to_core(i):
        return flow.to_core(i, in_full.at[i, :, :, 1 - c])

    def one(i):
        in_to_core(i).wait_recv()
        flow.one(i)

    def last(i):
        @pl.when(flow.level_of(i) == seat.z)
        def _():
            in_ref[...] = flow.total(i)

    tiled = (
        (dq_hbm, dq_ref), (dk_hbm, dk_ref), (dv_hbm, dv_ref), (h1_hbm, h1_ref),
        (emb_hbm, emb_ref), (dmid_hbm, dmid_ref),
    )

    def tile_copies(at, numbers):
        span = pl.ds(at * tile, tile)
        return [
            pltpu.make_async_copy(tiled[n][0].at[span], tiled[n][1].at[span], tile_sem.at[n, at])
            for n in numbers
        ]

    win_copy = pltpu.make_async_copy(win_hbm, win_ref, load_sem.at[0])
    pack = jnp.minimum(seat.z, packs - 1)
    pix_copy = pltpu.make_async_copy(
        pix_hbm.at[pl.ds(pl.multiple_of(pack * rows, rows), rows)], pix_ref, load_sem.at[1]
    )
    for at in range(rows // tile):
        for copy in tile_copies(at, range(4)):
            copy.start()
    win_copy.start()
    for at in range(rows // tile):
        for copy in tile_copies(at, range(4, 6)):
            copy.start()
    pix_copy.start()
    greet(seat, 4)
    gain = vec_ref[0:1]
    pixels = pix_ref.shape[1]
    spots = (pp_ref.shape[1] - pixels) // 2
    gain_sum = jnp.zeros((1, width), F32)
    for at in range(rows // tile):
        for copy in tile_copies(at, range(4)):
            copy.wait()
        span = slice(at * tile, (at + 1) * tile)
        for group in range(groups):
            mine = slice(group * part, (group + 1) * part)
            join_ref[group, span, :] = jnp.concatenate(
                [dq_ref[span, mine], dk_ref[span, mine], dv_ref[span, mine]], axis=1
            )
        h1t_ref[:, span] = jnp.transpose(h1_ref[span, :].astype(F32)).astype(LOW)

    def project(i):
        group = flow.level_of(i)
        for at in range(4):
            span = slice(at * 2 * share, (at + 1) * 2 * share)
            value = mm(h1t_ref[span, :], join_ref[group]).astype(LOW)
            in_full[i, at // 2, at % 2] = value.reshape(2, share, value.shape[1])
        in_to_core(i).start()

    project(0)
    project(1)
    win_copy.wait()
    for at in range(rows // tile):
        for copy in tile_copies(at, range(4, 6)):
            copy.wait()
        span = slice(at * tile, (at + 1) * tile)
        d_first = jnp.zeros((tile, width), F32)
        for group in range(groups):
            d_first += mm_nt(join_ref[group, span, :], win_ref[group])
        normed, inverse = row_norm(emb_ref[span, :])
        gain_sum += jnp.sum(d_first * normed, axis=0, keepdims=True)
        d_embed = dmid_ref[span, :] + row_norm_back(d_first, gain, normed, inverse)
        embt_ref[:, span] = jnp.transpose(d_embed).astype(LOW)
        if at < 2:
            one(at)
    flow.two(0)
    small_value[0] = jnp.zeros(small_out.shape, F32)
    small_value[0, 0:1] = gain_sum
    small_value[0, 1:2] = two_ref[...]
    small_value[0, 2:4] = pool_ref[...]
    heads = jnp.sum(gains_ref[...], axis=0)
    small_value[0, 4:5, :128] = heads[0:1]
    small_value[0, 4:5, 128:256] = heads[1:2]
    small_value[0, 5:6, :128] = loss_ref[0:1, :]
    small.start_plane()
    place = lax.broadcasted_iota(jnp.int32, (2 * spots, rows), 0)
    mine = pl.ds(pl.multiple_of(pack * rows, rows), rows)
    hot = (place == coord_ref[0:1, mine]) | (place - spots == coord_ref[1:2, mine])
    hot_ref[...] = hot.astype(F32).astype(LOW)
    pix_copy.wait()
    for at in range(4):
        span = slice(at * 2 * share, (at + 1) * 2 * share)
        picture = mm(embt_ref[span, :], pix_ref[...]).astype(LOW)
        pp_full[at // 2, at % 2, :, :, :pixels] = picture.reshape(2, share, pixels)
        place = mm_nt(embt_ref[span, :], hot_ref[...]).astype(LOW)
        pp_full[at // 2, at % 2, :, :, pixels:] = place.reshape(2, share, 2 * spots)
    pp_to_core.start()
    flow.two(1)
    project(2)
    pp_to_core.wait_recv()
    pp.one()
    flow.three(0)
    small.turn_levels()
    project(3)
    one(2)
    flow.three(1)
    flow.hop(0, 1)
    pp.two()
    one(3)
    flow.hop(1, 1)
    flow.hop(0, 2)
    small_out[...] = small.finish()
    mlp_sum = mlp_ref[...]
    out_sum = out_ref[...]
    squares = jnp.sum(mlp_sum[0] * mlp_sum[0] + mlp_sum[1] * mlp_sum[1], axis=0, keepdims=True)
    total = jnp.sum(squares, axis=1, keepdims=True)
    total = total + jnp.sum(jnp.sum(out_sum * out_sum, axis=0, keepdims=True), axis=1, keepdims=True)
    cls_sum = cls_ref[...]
    shared = jnp.sum(jnp.sum(cls_sum * cls_sum, axis=0, keepdims=True), axis=1, keepdims=True)
    pp.three()
    flow.two(2)
    flow.hop(1, 2)
    flow.two(3)
    pp.four()
    flow.three(2)
    flow.three(3)
    pp.five()
    flow.hop(2, 1)
    flow.hop(3, 1)
    pp_sum = pp.total()
    pp_ref[...] = pp_sum
    shared += jnp.sum(jnp.sum(pp_sum * pp_sum, axis=0, keepdims=True), axis=1, keepdims=True)
    for i in range(groups):
        last(i)
    in_sum = in_ref[...]
    total = total + jnp.sum(jnp.sum(in_sum * in_sum, axis=0, keepdims=True), axis=1, keepdims=True)
    square_value[0] = jnp.broadcast_to(total + leader * shared, (8, 128))
    square.start_plane()
    square.turn_levels()
    square_out[...] = square.finish()
    pp_to_core.wait_send()
    for entry in (pp, small, square):
        entry.drain()
    for i in range(groups):
        in_to_core(i).wait_send()
        flow.drain(i)


def embed_back_sum_call(
    dq, dk, dv, h1, embedded, d_middle, pixels, coords, w_in, pp_cols, vectors,
    d_two, d_pool, d_gain, loss, share_mlp, share_cls, share_out, packs, collective_id,
):
    rows, width = h1.shape
    groups, share = w_in.shape[0], width // 8
    cols = w_in.shape[2]
    low = lambda *shape: pltpu.VMEM(shape, LOW)
    inside = pl.BlockSpec(memory_space=pltpu.VMEM)
    anywhere = pl.BlockSpec(memory_space=pl.ANY)
    loaded = (dq, dk, dv, h1, embedded, d_middle, pixels, w_in)
    return pl.pallas_call(
        functools.partial(embed_back_sum_kernel, packs=packs),
        in_specs=[anywhere] * 7 + [inside, anywhere] + [inside] * 8,
        out_specs=[inside] * 4,
        out_shape=[
            jax.ShapeDtypeStruct((share, cols), F32),
            jax.ShapeDtypeStruct((share, pp_cols), F32),
            jax.ShapeDtypeStruct((8, width), F32),
            jax.ShapeDtypeStruct((8, 128), F32),
        ],
        scratch_shapes=[pltpu.VMEM((rows,) + a.shape[1:] if a is pixels else a.shape, a.dtype) for a in loaded]
        + [pltpu.SemaphoreType.DMA((6, rows // 256)), pltpu.SemaphoreType.DMA((2,))]
        + [
            low(width, rows),
            low(width, rows),
            low(groups, rows, cols),
            low(pp_cols - pixels.shape[1], rows),
            low(groups, 2, 2, 2, share, cols),
            low(2, 2, 2, share, pp_cols),
        ]
        + flow_scratch(groups, share, cols)
        + whole_scratch(share, pp_cols)
        + tiny_scratch((8, width))
        + tiny_scratch((8, 128)),
        compiler_params=pltpu.CompilerParams(
            collective_id=collective_id, has_side_effects=True, vmem_limit_bytes=VMEM_BYTES
        ),
        name="embed_back_sum",
    )(
        dq, dk, dv, h1, embedded, d_middle, pixels, coords, w_in, vectors,
        d_two, d_pool, d_gain, loss, share_mlp, share_cls, share_out,
    )


def prepare_kernel(
    length_ref, patch_ref, pos_ref, in_ref, out_ref, up_ref, dn_ref, cls_ref, gain_ref,
    pp_low, in_low, out_low, up_low, dn_low, cls_low, bound_out, gain_out,
):
    packs, images = length_ref.shape
    pixels = patch_ref.shape[1]
    kinds, spots, share = pos_ref.shape
    pp_low[:, :pixels] = patch_ref[...].astype(LOW)
    pp_low[:, pixels:] = jnp.transpose(pos_ref[...].reshape(kinds * spots, share)).astype(LOW)
    in_low[...] = jnp.concatenate([in_ref[n] for n in range(in_ref.shape[0])], axis=1).astype(LOW)
    out_low[...] = jnp.transpose(out_ref[...]).astype(LOW)
    up_low[...] = up_ref[...].astype(LOW)
    dn_low[...] = dn_ref[...].astype(LOW)
    cls_low[...] = cls_ref[...].astype(LOW)
    gain_out[...] = jnp.concatenate([gain_ref[...], gain_ref[...]], axis=1)
    pack = jnp.minimum(lax.axis_index("tensor"), packs - 1)
    lane = lax.broadcasted_iota(jnp.int32, (1, 128), 1)
    slot = jnp.where(lane >= 64, lane - 64, lane)
    starts = jnp.full((1, 128), 1 << 30, jnp.int32)
    ends = starts
    place = jnp.int32(0)
    for n in range(images):
        after = place + length_ref[pack, n]
        starts = jnp.where(slot == n, place, starts)
        ends = jnp.where(slot == n, after, ends)
        place = after
    bound_out[0:1, :] = starts
    bound_out[1:2, :] = ends


def prepare_call(lengths, patch, pos, w_in, w_out, up, dn, cls, gains):
    share, width = up.shape
    low = lambda cols: jax.ShapeDtypeStruct((share, cols), LOW)
    inside = pl.BlockSpec(memory_space=pltpu.VMEM)
    return pl.pallas_call(
        prepare_kernel,
        in_specs=[pl.BlockSpec(memory_space=pltpu.SMEM)] + [inside] * 8,
        out_specs=[inside] * 8,
        out_shape=[
            low(patch.shape[1] + pos.shape[0] * pos.shape[1]),
            low(w_in.shape[0] * w_in.shape[2]),
            low(w_out.shape[0]),
            low(width),
            low(width),
            low(cls.shape[1]),
            jax.ShapeDtypeStruct((2, 128), jnp.int32),
            jax.ShapeDtypeStruct((2, 128), F32),
        ],
        compiler_params=pltpu.CompilerParams(vmem_limit_bytes=VMEM_BYTES),
        name="prepare",
    )(lengths, patch, pos, w_in, w_out, up, dn, cls, gains)


RATES = (RATE_BASE, RATE_POSITION, RATE_BASE, RATE_MIDDLE, RATE_BASE, RATE_BASE, RATE_MIDDLE, RATE_VECTOR, RATE_VECTOR)


def update_kernel(*refs):
    states, shares, outs = refs[:27], refs[27:34], refs[34:61]
    loss_ref, norm_ref = refs[61:]
    pp_ref, in_ref, out_ref, mlp_ref, cls_ref, small_ref, square_ref = shares
    pixels = states[0].shape[1]
    kinds, spots, share = states[3].shape
    part = states[6].shape[2]
    vectors = small_ref[0:4, :]
    row = small_ref[4:5, :]
    head = states[24].shape[1]
    gains = jnp.concatenate(
        [row[:, :head] + row[:, head : 2 * head], row[:, 2 * head : 3 * head] + row[:, 3 * head : 4 * head]],
        axis=0,
    )

    def square_sum(entry):
        return jnp.sum(jnp.sum(entry * entry, axis=0, keepdims=True), axis=1, keepdims=True)

    norm = jnp.sqrt(square_ref[0:1, 0:1] + square_sum(vectors) + square_sum(gains))
    clip = CLIP / jnp.maximum(norm, CLIP)
    grads = (
        pp_ref[:, :pixels],
        jnp.transpose(pp_ref[:, pixels:]).reshape(kinds, spots, share),
        None,
        jnp.transpose(out_ref[...]),
        mlp_ref[1],
        mlp_ref[0],
        cls_ref[...],
        vectors,
        gains,
    )
    for n, grad in enumerate(grads):
        decay = DECAY if n < 7 else 0.0
        if n == 2:
            for kind in range(states[6].shape[0]):
                results = adam(
                    *(state[kind] for state in states[6:9]),
                    in_ref[:, kind * part : (kind + 1) * part], clip, RATES[n], decay,
                )
                for result, out in zip(results, outs[6:9]):
                    out[kind] = result
        else:
            mine = clip.reshape(1, 1, 1) if grad.ndim == 3 else clip
            results = adam(*(state[...] for state in states[3 * n : 3 * n + 3]), grad, mine, RATES[n], decay)
            for result, out in zip(results, outs[3 * n : 3 * n + 3]):
                out[...] = result
    loss_ref[...] = small_ref[5:6, 0:1]
    norm_ref[...] = norm


def update_call(states, shares):
    inside = pl.BlockSpec(memory_space=pltpu.VMEM)
    scalar = jax.ShapeDtypeStruct((1, 1), F32)
    return pl.pallas_call(
        update_kernel,
        in_specs=[inside] * (len(states) + len(shares)),
        out_specs=[inside] * (len(states) + 2),
        out_shape=[jax.ShapeDtypeStruct(a.shape, F32) for a in states] + [scalar, scalar],
        compiler_params=pltpu.CompilerParams(vmem_limit_bytes=VMEM_BYTES),
        name="update",
    )(*states, *shares)


def adam(master, first_moment, second_moment, gradient, clip_scale, rate, decay_rate):
    gradient = gradient * clip_scale
    first_new = BETA_ONE * first_moment + (1 - BETA_ONE) * gradient
    second_new = BETA_TWO * second_moment + (1 - BETA_TWO) * gradient * gradient
    update = (
        first_new / (1 - BETA_ONE**STEP) / (jnp.sqrt(second_new / (1 - BETA_TWO**STEP)) + ADAM_EPS)
    )
    return (master - rate * (update + decay_rate * master), first_new, second_new)


def squared(entry):
    return jnp.sum(entry * entry)


def per_device(
    pixels, coords, lengths, labels,
    patch_table, patch_first, patch_second,
    position_table, position_first, position_second,
    attend_in, attend_in_first, attend_in_second,
    attend_out, attend_out_first, attend_out_second,
    expand, expand_first, expand_second,
    shrink, shrink_first, shrink_second,
    classify, classify_first, classify_second,
    vectors, vectors_first, vectors_second,
    head_gains, head_gains_first, head_gains_second,
):
    packs, images = lengths.shape
    members = lax.axis_size("tensor")
    width = vectors.shape[1]
    share = attend_in.shape[0]
    seat = lax.axis_index("tensor")
    pack = jnp.minimum(seat, packs - 1).astype(jnp.int32)[None]
    valid = (seat < packs).astype(F32).reshape(1, 1)
    image_count = images * packs * lax.axis_size("dp")
    if lax.axis_size("dp") == 8 and members == 4:
        turn = {0: lambda a: a.T, 2: lambda a: jnp.transpose(a, (1, 0, 2)), 5: lambda a: a.T}
        states = (
            patch_table, patch_first, patch_second, position_table, position_first, position_second,
            attend_in, attend_in_first, attend_in_second, attend_out, attend_out_first, attend_out_second,
            expand, expand_first, expand_second, shrink, shrink_first, shrink_second,
            classify, classify_first, classify_second, vectors, vectors_first, vectors_second,
            head_gains, head_gains_first, head_gains_second,
        )
        states = [turn.get(n // 3, lambda a: a)(entry) for n, entry in enumerate(states)]
        ready = prepare_call(lengths, *states[0:21:3], head_gains)
        shares = pack_step(
            pack, valid, pixels, coords, lengths, labels, tuple(ready), vectors, head_gains, image_count, True
        )
        *results, loss_total, grad_norm = update_call(states, shares)
        results = [turn.get(n // 3, lambda a: a)(entry) for n, entry in enumerate(results)]
        return (*results, loss_total.reshape(()), grad_norm.reshape(()))
    shards = (
        jnp.concatenate(
            [patch_table.T, jnp.transpose(position_table, (2, 0, 1)).reshape(share, -1)], axis=1
        ).astype(LOW),
        attend_in.reshape(share, -1).astype(LOW),
        attend_out.T.astype(LOW),
        expand.astype(LOW),
        shrink.T.astype(LOW),
        classify.astype(LOW),
    )
    both = ("tensor", "dp")

    def gather(shard):
        return lax.all_gather(shard, both, axis=0, tiled=True).reshape(members, width, -1)

    weights = (
        lax.all_gather(shards[0], "dp", axis=0, tiled=True),
        gather(shards[1]),
        gather(shards[2]),
        gather(shards[3]),
        gather(shards[4]),
        lax.all_gather(shards[5], "dp", axis=0, tiled=True),
    )
    grads, grad_vectors, grad_gains, loss_local = pack_step(
        pack, valid, pixels, coords, lengths, labels, weights, vectors, head_gains, image_count
    )
    grad_vectors, grad_gains, loss_total = lax.psum((grad_vectors, grad_gains, loss_local), both)

    def scatter(grad):
        return lax.psum_scatter(
            grad.reshape(members * width, -1), both, scatter_dimension=0, tiled=True
        ).astype(F32)

    def scatter_whole(grad):
        part = lax.psum_scatter(grad, "dp", scatter_dimension=0, tiled=True)
        return lax.psum(part, "tensor").astype(F32)

    share_pp = scatter_whole(grads[0])
    share_in, share_out, share_up, share_dn = (scatter(entry) for entry in grads[1:5])
    share_cls = scatter_whole(grads[5])
    leader = (seat == 0).astype(F32)
    split_squares = squared(share_in) + squared(share_out) + squared(share_up) + squared(share_dn)
    squares = lax.psum(split_squares + leader * (squared(share_pp) + squared(share_cls)), both)
    grad_norm = jnp.sqrt(squares + squared(grad_vectors) + squared(grad_gains))
    clip_scale = CLIP / jnp.maximum(grad_norm, CLIP)
    pixel_width = patch_table.shape[0]
    share_patch = share_pp[:, :pixel_width].T
    share_pos = jnp.transpose(
        share_pp[:, pixel_width:].reshape(share, position_table.shape[0], position_table.shape[1]), (1, 2, 0)
    )
    results = (
        adam(patch_table, patch_first, patch_second, share_patch, clip_scale, RATE_BASE, DECAY),
        adam(position_table, position_first, position_second, share_pos, clip_scale, RATE_POSITION, DECAY),
        adam(
            attend_in, attend_in_first, attend_in_second,
            share_in.reshape(attend_in.shape), clip_scale, RATE_BASE, DECAY,
        ),
        adam(attend_out, attend_out_first, attend_out_second, share_out.T, clip_scale, RATE_MIDDLE, DECAY),
        adam(expand, expand_first, expand_second, share_up, clip_scale, RATE_BASE, DECAY),
        adam(shrink, shrink_first, shrink_second, share_dn.T, clip_scale, RATE_BASE, DECAY),
        adam(classify, classify_first, classify_second, share_cls, clip_scale, RATE_MIDDLE, DECAY),
        adam(vectors, vectors_first, vectors_second, grad_vectors, clip_scale, RATE_VECTOR, 0.0),
        adam(head_gains, head_gains_first, head_gains_second, grad_gains, clip_scale, RATE_VECTOR, 0.0),
    )
    return tuple(entry for group in results for entry in group) + (loss_total, grad_norm)


def solution(mesh):
    data = P("dp", None)
    in_specs = (
        (data, P(None, "dp"), data, data)
        + (P(None, "dp"),) * 3
        + (P(None, None, "dp"),) * 3
        + (P("dp", None, "tensor"),) * 3
        + (P("tensor", "dp"),) * 3
        + (P("dp", "tensor"),) * 3
        + (P("tensor", "dp"),) * 3
        + (data,) * 3
        + (P(),) * 6
    )
    out_specs = in_specs[4:] + (P(), P())
    return jax.shard_map(per_device, mesh=mesh, in_specs=in_specs, out_specs=out_specs, check_vma=False)
```

```python
import functools

import jax
import jax.numpy as jnp
from jax import lax
from jax.experimental import pallas as pl
from jax.experimental.pallas import tpu as pltpu
from jax.sharding import PartitionSpec as P

STEP = 10
NORM_EPS = 1e-06
CLIP = 0.05
RATE_BASE = 0.03
RATE_POSITION = 0.2
RATE_MIDDLE = 0.1
RATE_VECTOR = 1.0
DECAY = 0.05
BETA_ONE = 0.5
BETA_TWO = 0.5
ADAM_EPS = 1e-08
SHIFT = -4.0
NEGATIVE = -1e30
APART = 128.0
LOW = jnp.bfloat16
F32 = jnp.float32
VMEM_BYTES = 60 * 1024 * 1024
TAIL_P = 0.3
TAIL = (
    0.1196293,
    0.12075397,
    0.09991341,
    0.12856192,
    -0.05368424,
    0.20635419,
    -0.1572035,
    0.03567488,
)


def mm(left, right):
    return lax.dot_general(left, right, (((1,), (0,)), ((), ())), preferred_element_type=F32)


def mm_nt(left, right):
    return lax.dot_general(left, right, (((1,), (1,)), ((), ())), preferred_element_type=F32)


def split_two(values):
    high = values.astype(LOW)
    return high, (values - high.astype(F32)).astype(LOW)


def split_three(values):
    high = values.astype(LOW)
    rest = values - high.astype(F32)
    middle = rest.astype(LOW)
    return high, middle, (rest - middle.astype(F32)).astype(LOW)


def row_norm(values):
    center = values - jnp.mean(values, axis=-1, keepdims=True)
    inverse = lax.rsqrt(jnp.mean(center * center, axis=-1, keepdims=True) + NORM_EPS)
    return center * inverse, inverse


def row_norm_back(gradient, gain_row, normed, inverse):
    scaled = gradient * gain_row
    return inverse * (
        scaled
        - jnp.mean(scaled, axis=-1, keepdims=True)
        - normed * jnp.mean(scaled * normed, axis=-1, keepdims=True)
    )


def half_mean_matrix(scale):
    row = lax.broadcasted_iota(jnp.int32, (128, 128), 0)
    col = lax.broadcasted_iota(jnp.int32, (128, 128), 1)
    return jnp.where((row >= 64) == (col >= 64), scale, 0.0).astype(LOW)


def half_sum(values, block):
    high, low = split_two(values)
    return mm(high, block) + mm(low, block)


def half_norm(values, block):
    center = values - half_sum(values, block)
    inverse = lax.rsqrt(half_sum(center * center, block) + NORM_EPS)
    return center * inverse, inverse


def half_norm_back(gradient, gain_row, normed, inverse, block):
    scaled = gradient * gain_row
    return inverse * (scaled - half_sum(scaled, block) - normed * half_sum(scaled * normed, block))


def gelu_pair(inner):
    size = jnp.abs(inner)
    near = 1.0 / (1.0 + TAIL_P * size)
    bell = jnp.exp(-0.5 * inner * inner)
    poly = TAIL[-1]
    for factor in TAIL[-2::-1]:
        poly = poly * near + factor
    tail = poly * near * bell
    share = jnp.where(inner >= 0, 1.0 - tail, tail)
    return inner * share, share + inner * bell * 0.3989422804014327


def embed_kernel(pack_ref, pix_ref, coord_ref, wp_ref, win_ref, gain_ref, emb_ref, h1_ref, q_ref, k_ref, v_ref):
    rows = pix_ref.shape[0]
    pixels = pix_ref.shape[1]
    groups = win_ref.shape[0]
    part = win_ref.shape[2] // 3
    spots = (wp_ref.shape[1] - pixels) // 2
    lane = lax.broadcasted_iota(jnp.int32, (rows, 2 * spots), 1)
    hot = ((lane == coord_ref[:, 0:1]) | (lane - spots == coord_ref[:, 1:2])).astype(F32).astype(LOW)
    embedded = mm_nt(pix_ref[...], wp_ref[:, :pixels]) + mm_nt(hot, wp_ref[:, pixels:])
    emb_ref[...] = embedded
    normed, _ = row_norm(embedded)
    first = (normed * gain_ref[0:1]).astype(LOW)
    h1_ref[...] = first
    parts = [mm(first, win_ref[group]) for group in range(groups)]
    q_ref[...] = jnp.concatenate([entry[:, :part] for entry in parts], axis=1)
    k_ref[...] = jnp.concatenate([entry[:, part : 2 * part] for entry in parts], axis=1)
    v_ref[...] = jnp.concatenate([entry[:, 2 * part :].astype(LOW) for entry in parts], axis=1)


def embed_call(pack, pixels, coords, w_pp, w_in, vectors, rows):
    width = vectors.shape[1]
    tile = 256
    steps = rows // tile
    whole2 = lambda i, p: (0, 0)
    tiled = pl.BlockSpec((tile, width), lambda i, p: (i, 0))
    return pl.pallas_call(
        embed_kernel,
        grid_spec=pltpu.PrefetchScalarGridSpec(
            num_scalar_prefetch=1,
            grid=(steps,),
            in_specs=[
                pl.BlockSpec((tile, pixels.shape[1]), lambda i, p: (p[0] * steps + i, 0)),
                pl.BlockSpec((tile, 2), lambda i, p: (p[0] * steps + i, 0)),
                pl.BlockSpec(w_pp.shape, whole2),
                pl.BlockSpec(w_in.shape, lambda i, p: (0, 0, 0)),
                pl.BlockSpec(vectors.shape, whole2),
            ],
            out_specs=[tiled] * 5,
        ),
        out_shape=[
            jax.ShapeDtypeStruct((rows, width), F32),
            jax.ShapeDtypeStruct((rows, width), LOW),
            jax.ShapeDtypeStruct((rows, width), F32),
            jax.ShapeDtypeStruct((rows, width), F32),
            jax.ShapeDtypeStruct((rows, width), LOW),
        ],
        compiler_params=pltpu.CompilerParams(vmem_limit_bytes=VMEM_BYTES),
        name="embed",
    )(pack, pixels, coords, w_pp, w_in, vectors)


def image_marks(bound_ref, rows):
    place = lax.broadcasted_iota(jnp.int32, (rows, 128), 0)
    return (place >= bound_ref[0:1, :]) & (place < bound_ref[1:2, :])


def half_lane(rows):
    lane = lax.broadcasted_iota(jnp.int32, (rows, 128), 1)
    return lane, jnp.where(lane >= 64, lane - 64, lane)


def attend_kernel(
    q_ref, k_ref, v_ref, gain_ref, bound_ref, o_ref, lse_ref, ka_ref, va_ref, qa_ref, between=None
):
    rows = q_ref.shape[0]
    tile = 256
    block = half_mean_matrix(1.0 / 64)
    lane, inner = half_lane(rows)
    marks = image_marks(bound_ref, rows)
    one = jnp.where(inner == 8, 1.0, 0.0)
    query_feature = jnp.where(marks, 1.0, one)
    key_feature = jnp.where(marks, APART, -APART * one)
    k_normed, _ = half_norm(k_ref[...], block)
    ka_ref[:, :128] = (k_normed * gain_ref[1:2]).astype(LOW)
    ka_ref[:, 128:] = key_feature.astype(LOW)
    va_ref[:, :128] = v_ref[...]
    va_ref[:, 128:] = jnp.ones((rows, 128), LOW)
    q_normed, _ = half_norm(q_ref[...], block)
    query = (q_normed * gain_ref[0:1]).astype(LOW).astype(F32) * 0.125
    for head in range(2):
        mine = (lane < 64) if head == 0 else (lane >= 64)
        qa_ref[head, :, :128] = jnp.where(mine, query, 0.0).astype(LOW)
        qa_ref[head, :, 128:] = jnp.where(mine, query_feature, 0.0).astype(LOW)
    keys = ka_ref[...]
    values = va_ref[...]
    first = lane[:tile] < 64
    for step in range(rows // tile):
        part = slice(step * tile, (step + 1) * tile)
        outs = []
        for head in range(2):
            score = mm_nt(qa_ref[head, part, :], keys)
            outs.append(mm(jnp.exp(score).astype(LOW), values))
        total = jnp.where(first, outs[0][:, 128:], outs[1][:, 128:])
        o_ref[part, :] = (jnp.where(first, outs[0][:, :128], outs[1][:, :128]) / total).astype(LOW)
        lse_ref[part, :] = jnp.log(total)
        if between is not None and step % 2 == 1:
            between(step // 2)


def attend_call(q_raw, k_raw, value, gains, bounds):
    rows, width = q_raw.shape
    pair = pl.BlockSpec((rows, 128), lambda j: (0, j))
    small = lambda a: pl.BlockSpec(a.shape, lambda j: (0, 0))
    return pl.pallas_call(
        attend_kernel,
        grid=(width // 128,),
        in_specs=[pair, pair, pair, small(gains), small(bounds)],
        out_specs=[pair, pair],
        out_shape=[
            jax.ShapeDtypeStruct((rows, width), LOW),
            jax.ShapeDtypeStruct((rows, width), F32),
        ],
        scratch_shapes=[
            pltpu.VMEM((rows, 256), LOW),
            pltpu.VMEM((rows, 256), LOW),
            pltpu.VMEM((2, rows, 256), LOW),
        ],
        compiler_params=pltpu.CompilerParams(vmem_limit_bytes=VMEM_BYTES),
        name="attend",
    )(q_raw, k_raw, value, gains, bounds)


def attend_back_kernel(
    q_ref, k_ref, v_ref, o_ref, lse_ref, do_ref, gain_ref, bound_ref,
    dq_ref, dk_ref, dv_ref, dgain_ref,
    ka_ref, va_ref, qa_ref, da_ref, qt_ref, dot_ref, dqs_ref, dkt_ref, dvt_ref,
    between=None,
):
    rows = q_ref.shape[0]
    tile = 256
    block = half_mean_matrix(1.0 / 64)
    block_sum = half_mean_matrix(1.0)
    lane, inner = half_lane(rows)
    marks = image_marks(bound_ref, rows)
    one = jnp.where(inner == 8, 1.0, 0.0)
    three = (inner >= 9) & (inner < 12)
    key_feature = jnp.where(marks, APART, jnp.where(three, 1.0, -APART * one))

    def spread(values):
        high, middle, low = split_three(values)
        return jnp.where(
            inner == 9, high.astype(F32), jnp.where(inner == 10, middle.astype(F32), low.astype(F32))
        )

    query_feature = jnp.where(three, spread(-lse_ref[...]), jnp.where(marks, 1.0, one))
    k_normed, k_inverse = half_norm(k_ref[...], block)
    ka_ref[:, :128] = (k_normed * gain_ref[1:2]).astype(LOW)
    ka_ref[:, 128:] = key_feature.astype(LOW)
    va_ref[:, :128] = v_ref[...]
    va_ref[:, 128:] = jnp.where(three, 1.0, 0.0).astype(LOW)
    q_normed, q_inverse = half_norm(q_ref[...], block)
    query = (q_normed * gain_ref[0:1]).astype(LOW).astype(F32)
    qt_ref[...] = jnp.transpose(query).astype(LOW)
    query = query * 0.125
    above = do_ref[...].astype(F32)
    dot_ref[...] = jnp.transpose(above).astype(LOW)
    inside = half_sum(above * o_ref[...].astype(F32), block_sum)
    above_feature = jnp.where(three, spread(inside * -0.125), 0.0)
    above = above * 0.125
    for head in range(2):
        mine = (lane < 64) if head == 0 else (lane >= 64)
        qa_ref[head, :, :128] = jnp.where(mine, query, 0.0).astype(LOW)
        qa_ref[head, :, 128:] = jnp.where(mine, query_feature, 0.0).astype(LOW)
        da_ref[head, :, :128] = jnp.where(mine, above, 0.0).astype(LOW)
        da_ref[head, :, 128:] = jnp.where(mine, above_feature, 0.0).astype(LOW)
    keys = ka_ref[...]
    values = va_ref[...]
    key_low = ka_ref[:, :128]
    first = lane[:tile] < 64
    for step in range(rows // tile):
        part = slice(step * tile, (step + 1) * tile)
        outs = []
        for head in range(2):
            mine = slice(64 * head, 64 * head + 64)
            prob = jnp.exp(mm_nt(qa_ref[head, part, :], keys))
            d_prob = mm_nt(da_ref[head, part, :], values)
            d_score = (prob * d_prob).astype(LOW)
            outs.append(mm(d_score, key_low))
            d_key = mm(qt_ref[mine, part], d_score)
            d_value = mm(dot_ref[mine, part], prob.astype(LOW))
            if step == 0:
                dkt_ref[mine, :] = d_key
                dvt_ref[mine, :] = d_value
            else:
                dkt_ref[mine, :] += d_key
                dvt_ref[mine, :] += d_value
        dqs_ref[part, :] = jnp.where(first, outs[0], outs[1])
        if between is not None and step % 2 == 1:
            between(step // 2)
    d_query = dqs_ref[...]
    d_key = jnp.transpose(dkt_ref[...])
    dv_ref[...] = jnp.transpose(dvt_ref[...]).astype(LOW)
    dq_ref[...] = half_norm_back(d_query, gain_ref[0:1], q_normed, q_inverse, block).astype(LOW)
    dk_ref[...] = half_norm_back(d_key, gain_ref[1:2], k_normed, k_inverse, block).astype(LOW)
    dgain_ref[0, 0:1] = jnp.sum(d_query * q_normed, axis=0, keepdims=True)
    dgain_ref[0, 1:2] = jnp.sum(d_key * k_normed, axis=0, keepdims=True)


ATTEND_BACK_SCRATCH = 9


def attend_back_scratch(rows):
    return [
        pltpu.VMEM((rows, 256), LOW),
        pltpu.VMEM((rows, 256), LOW),
        pltpu.VMEM((2, rows, 256), LOW),
        pltpu.VMEM((2, rows, 256), LOW),
        pltpu.VMEM((128, rows), LOW),
        pltpu.VMEM((128, rows), LOW),
        pltpu.VMEM((rows, 128), F32),
        pltpu.VMEM((128, rows), F32),
        pltpu.VMEM((128, rows), F32),
    ]


def attend_back_sum_kernel(*refs):
    inputs, grads, dout_ref, before_ref = refs[:8], refs[8], refs[9], refs[10]
    outputs, share_ref, out_ref = refs[11:15], refs[15], refs[16]
    scratch, rest = refs[17 : 17 + ATTEND_BACK_SCRATCH], refs[17 + ATTEND_BACK_SCRATCH :]
    mlp_own, mlp_load, mlp_refs = rest[0], rest[1], rest[2:9]
    out_own, out_load, out_refs = rest[9], rest[10], rest[11:18]
    step = pl.program_id(0)
    seat = Seat()
    c = seat.c
    mlp = Flow(
        seat, lambda i: lax.rem(4 - lax.div(i, 2), 4), lambda i: mlp_own.at[i], *mlp_refs[:5], mlp_refs[5:]
    )
    out = Flow(seat, lambda i: i, lambda i: out_own.at[i], *out_refs[:5], out_refs[5:])
    chunks, levels = mlp_own.shape[0], out_own.shape[0]

    def mlp_at(i):
        return lax.rem(i, 2) * 3 + lax.div(i, 2)

    def mlp_loading(i):
        return pltpu.make_async_copy(grads.at[mlp_at(i), :, :, c], mlp_own.at[i], mlp_load.at[i])

    def mlp_to_core(i):
        return mlp.to_core(i, grads.at[mlp_at(i), :, :, 1 - c])

    def out_loading(i):
        return pltpu.make_async_copy(dout_ref.at[i, :, :, c], out_own.at[i], out_load.at[i])

    def out_to_core(i):
        return out.to_core(i, dout_ref.at[i, :, :, 1 - c])

    def every(count, action):
        lax.fori_loop(0, count, lambda i, carry: (action(i), carry)[1], 0)

    @pl.when(step == 0)
    def _():
        every(chunks, lambda i: mlp_loading(i).start())
        every(levels, lambda i: out_loading(i).start())
        greet(seat, 4)
        every(chunks, lambda i: mlp_to_core(i).start())
        every(levels, lambda i: out_to_core(i).start())
        share_ref[...] = before_ref[...]

    def mlp_one(i):
        mlp_loading(i).wait()
        mlp_to_core(i).wait_recv()
        mlp.one(i)

    def mlp_last(i):
        @pl.when(mlp.level_of(i) == seat.z)
        def _():
            share_ref[lax.rem(i, 2)] = mlp.total(i)

    def out_one(i):
        out_loading(i).wait()
        out_to_core(i).wait_recv()
        out.one(i)

    def out_last(i):
        @pl.when(out.level_of(i) == seat.z)
        def _():
            out_ref[...] = out.total(i)

    def pair(action, number):
        return lambda: every(2, lambda i: action(2 * number + i))

    hop_one, hop_two = (functools.partial(mlp.hop, reach=reach) for reach in (1, 2))
    out_hop_one, out_hop_two = (functools.partial(out.hop, reach=reach) for reach in (1, 2))
    plan = {
        0: [pair(mlp_one, 0)],
        1: [lambda: every(levels, out_one)],
        2: [pair(mlp.two, 0), pair(mlp_one, 1)],
        3: [lambda: every(levels, out.two)],
        4: [pair(mlp.three, 0)],
        5: [pair(mlp.two, 1), pair(mlp_one, 2)],
        6: [pair(hop_one, 0), lambda: every(levels, out.three)],
        7: [pair(mlp.three, 1), lambda: every(levels, out_hop_one)],
        8: [pair(mlp.two, 2), pair(hop_two, 0)],
        9: [pair(hop_one, 1), lambda: every(levels, out_hop_two)],
        10: [pair(mlp.three, 2)],
        11: [pair(hop_two, 1), pair(hop_one, 2)],
    }

    def between(slot):
        for number, actions in plan.items():
            if number % 2 == slot:

                @pl.when(2 * step + slot == number)
                def _():
                    for action in actions:
                        action()

    attend_back_kernel(*inputs, *outputs, *scratch, between=between)

    @pl.when(step == pl.num_programs(0) - 1)
    def _():
        every(chunks, mlp_last)
        every(levels, out_last)

        def drain(i):
            mlp_to_core(i).wait_send()
            mlp.drain(i)

        def out_drain(i):
            out_to_core(i).wait_send()
            out.drain(i)

        every(chunks, drain)
        every(levels, out_drain)


def attend_back_sum_call(
    q_raw, k_raw, value, attended, lse, d_attended, gains, bounds, grads, d_out, before, collective_id
):
    rows, width = q_raw.shape
    pairs = width // 128
    share, cols = grads.shape[-2:]
    pair = pl.BlockSpec((rows, 128), lambda j: (0, j))
    small = lambda a: pl.BlockSpec(a.shape, lambda j: (0,) * a.ndim)
    anywhere = pl.BlockSpec(memory_space=pl.ANY)
    low = jax.ShapeDtypeStruct((rows, width), LOW)

    def scratch(chunks, cols):
        own = [pltpu.VMEM((chunks, 2, 2, share, cols), LOW), pltpu.SemaphoreType.DMA((chunks,))]
        return own + flow_scratch(chunks, share, cols)

    return pl.pallas_call(
        attend_back_sum_kernel,
        grid=(pairs,),
        in_specs=[pair] * 6 + [small(gains), small(bounds), anywhere, anywhere, small(before)],
        out_specs=[
            pair, pair, pair,
            pl.BlockSpec((1, 2, 128), lambda j: (j, 0, 0)),
            small(before),
            pl.BlockSpec((share, d_out.shape[-1]), lambda j: (0, 0)),
        ],
        out_shape=[
            low, low, low,
            jax.ShapeDtypeStruct((pairs, 2, 128), F32),
            jax.ShapeDtypeStruct(before.shape, F32),
            jax.ShapeDtypeStruct((share, d_out.shape[-1]), F32),
        ],
        scratch_shapes=attend_back_scratch(rows)
        + scratch(grads.shape[0], cols)
        + scratch(d_out.shape[0], d_out.shape[-1]),
        compiler_params=pltpu.CompilerParams(
            collective_id=collective_id, has_side_effects=True, vmem_limit_bytes=VMEM_BYTES
        ),
        name="attend_back_sum",
    )(q_raw, k_raw, value, attended, lse, d_attended, gains, bounds, grads, d_out, before)


def attend_back_call(q_raw, k_raw, value, attended, lse, d_attended, gains, bounds):
    rows, width = q_raw.shape
    pairs = width // 128
    pair = pl.BlockSpec((rows, 128), lambda j: (0, j))
    small = lambda a: pl.BlockSpec(a.shape, lambda j: (0, 0))
    low = jax.ShapeDtypeStruct((rows, width), LOW)
    return pl.pallas_call(
        attend_back_kernel,
        grid=(pairs,),
        in_specs=[pair] * 6 + [small(gains), small(bounds)],
        out_specs=[pair, pair, pair, pl.BlockSpec((1, 2, 128), lambda j: (j, 0, 0))],
        out_shape=[low, low, low, jax.ShapeDtypeStruct((pairs, 2, 128), F32)],
        scratch_shapes=attend_back_scratch(rows),
        compiler_params=pltpu.CompilerParams(vmem_limit_bytes=VMEM_BYTES),
        name="attend_back",
    )(q_raw, k_raw, value, attended, lse, d_attended, gains, bounds)


def mlp_kernel(o_ref, emb_ref, wout_ref, wup_ref, wdn_ref, vec_ref, x1_ref, h2_ref, act_ref, slope_ref, x2_ref):
    step = pl.program_id(0)
    rows, _ = o_ref.shape
    groups, _, part = wout_ref.shape
    tile = 256

    @pl.when(step == 0)
    def _():
        for at in range(rows // tile):
            span = slice(at * tile, (at + 1) * tile)
            branch = mm_nt(o_ref[span, :part], wout_ref[0])
            for group in range(1, groups):
                branch += mm_nt(o_ref[span, group * part : (group + 1) * part], wout_ref[group])
            middle = emb_ref[span, :] + branch
            x1_ref[span, :] = middle
            x2_ref[span, :] = middle
            normed, _ = row_norm(middle)
            h2_ref[span, :] = (normed * vec_ref[1:2]).astype(LOW)

    tile = 256
    spans = [slice(at * tile, (at + 1) * tile) for at in range(rows // tile)]
    hidden = mm(h2_ref[spans[0], :], wup_ref[0])
    for at, span in enumerate(spans):
        now = hidden
        if at + 1 < len(spans):
            hidden = mm(h2_ref[spans[at + 1], :], wup_ref[0])
        active, slope = gelu_pair(now)
        active = active.astype(LOW)
        act_ref[span, :] = active
        slope_ref[span, :] = slope.astype(LOW)
        x2_ref[span, :] += mm_nt(active, wdn_ref[0])


def mlp_call(attended, embedded, w_out, w_up, w_dn, vectors):
    rows, width = embedded.shape
    groups, _, per = w_up.shape
    chunk = per
    hidden = groups * per
    whole = lambda a: pl.BlockSpec(a.shape, lambda j: (0,) * a.ndim)
    weight = pl.BlockSpec((1, width, chunk), lambda j: (j, 0, 0))
    full = pl.BlockSpec((rows, width), lambda j: (0, 0))
    piece = pl.BlockSpec((rows, chunk), lambda j: (0, j))
    return pl.pallas_call(
        mlp_kernel,
        grid=(hidden // chunk,),
        in_specs=[whole(attended), whole(embedded), whole(w_out), weight, weight, whole(vectors)],
        out_specs=[full, full, piece, piece, full],
        out_shape=[
            jax.ShapeDtypeStruct((rows, width), F32),
            jax.ShapeDtypeStruct((rows, width), LOW),
            jax.ShapeDtypeStruct((rows, hidden), LOW),
            jax.ShapeDtypeStruct((rows, hidden), LOW),
            jax.ShapeDtypeStruct((rows, width), F32),
        ],
        compiler_params=pltpu.CompilerParams(vmem_limit_bytes=VMEM_BYTES),
        name="mlp",
    )(attended, embedded, w_out, w_up, w_dn, vectors)


def pool_kernel(
    pack_ref, x2_ref, label_ref, wcls_ref, vec_ref, bound_ref, valid_ref,
    dx2_ref, dcls_ref, loss_ref, dvec_ref,
    norm_ref, inv_ref,
    *, images, image_count,
):
    rows, width = x2_ref.shape
    tile = 256
    root = width**0.5
    gain = vec_ref[2:3]
    query = vec_ref[3:4]
    lane = lax.broadcasted_iota(jnp.int32, (rows, 128), 1)
    marks = image_marks(bound_ref, rows) & (lane < 64)
    logits = []
    for at in range(rows // tile):
        span = slice(at * tile, (at + 1) * tile)
        normed, inverse = row_norm(x2_ref[span, :])
        norm_ref[span, :] = normed
        inv_ref[span, :] = jnp.broadcast_to(inverse, (tile, 128))
        logits.append(jnp.sum(normed * gain * query, axis=-1, keepdims=True) / root)
    logit = jnp.concatenate(logits, axis=0)
    masked = jnp.where(marks, logit, NEGATIVE)
    grown = jnp.exp(masked - jnp.max(masked, axis=0, keepdims=True))
    shares = jnp.where(marks, grown / jnp.sum(grown, axis=0, keepdims=True), 0.0)
    weight = jnp.sum(shares, axis=-1, keepdims=True)
    member = jnp.transpose(marks.astype(F32))[:16].astype(LOW)
    pooled = jnp.zeros((16, width), F32)
    for at in range(rows // tile):
        span = slice(at * tile, (at + 1) * tile)
        for entry in split_three(norm_ref[span, :] * gain * weight[span]):
            pooled += mm(member[:, span], entry)
    pooled_low = pooled.astype(LOW)
    scores = mm(pooled_low, wcls_ref[...])[:images] + SHIFT
    target = label_ref[...].astype(F32)
    valid = valid_ref[0, 0]
    soft = jnp.maximum(scores, 0.0) + jnp.log1p(jnp.exp(-jnp.abs(scores)))
    loss_rows = jnp.sum(soft - target * scores, axis=-1, keepdims=True)
    loss_ref[...] = jnp.broadcast_to(jnp.sum(loss_rows, axis=0, keepdims=True) * valid, loss_ref.shape)
    d_score = (1.0 / (1.0 + jnp.exp(-scores)) - target) / image_count * valid
    d_score = jnp.concatenate([d_score, jnp.zeros((16 - images, d_score.shape[1]), F32)], axis=0).astype(LOW)
    dcls_ref[...] = mm(jnp.transpose(pooled).astype(LOW), d_score).astype(LOW)
    d_pooled = mm_nt(d_score, wcls_ref[...])[:images]
    parts = jnp.concatenate(
        [entry.astype(F32) for entry in split_three(d_pooled)]
        + [jnp.zeros((128 - 3 * images, width), F32)],
        axis=0,
    ).astype(LOW)
    marks_f = marks.astype(F32)
    thrice = (
        marks_f + pltpu.roll(marks_f, images, 1) + pltpu.roll(marks_f, 2 * images, 1)
    ).astype(LOW)
    d_weights = []
    for at in range(rows // tile):
        span = slice(at * tile, (at + 1) * tile)
        spread = mm(thrice[span], parts)
        dx2_ref[span, :] = spread
        d_weights.append(jnp.sum(spread * (norm_ref[span, :] * gain), axis=-1, keepdims=True))
    d_weight = jnp.concatenate(d_weights, axis=0)
    inside = jnp.sum(shares * d_weight, axis=0, keepdims=True)
    d_logit = weight * (d_weight - jnp.sum(marks_f * inside, axis=-1, keepdims=True))
    gain_sum = jnp.zeros((1, width), F32)
    query_sum = jnp.zeros((1, width), F32)
    for at in range(rows // tile):
        span = slice(at * tile, (at + 1) * tile)
        normed = norm_ref[span, :]
        inverse = inv_ref[span, 0:1]
        d_last = dx2_ref[span, :] * weight[span] + d_logit[span] * (query / root)
        gain_sum += jnp.sum(d_last * normed, axis=0, keepdims=True)
        query_sum += jnp.sum(d_logit[span] * normed, axis=0, keepdims=True)
        dx2_ref[span, :] = row_norm_back(d_last, gain, normed, inverse)
    dvec_ref[0:1, :] = gain_sum
    dvec_ref[1:2, :] = query_sum * gain / root


def pool_call(pack, x2, labels, w_cls, vectors, bounds, valid, images, image_count):
    rows, width = x2.shape
    classes = labels.shape[1]
    whole = lambda a: pl.BlockSpec(a.shape, lambda j, p: (0,) * a.ndim)
    full = lambda *shape: pl.BlockSpec(shape, lambda j, p: (0,) * len(shape))
    return pl.pallas_call(
        functools.partial(pool_kernel, images=images, image_count=image_count),
        grid_spec=pltpu.PrefetchScalarGridSpec(
            num_scalar_prefetch=1,
            grid=(1,),
            in_specs=[
                whole(x2),
                pl.BlockSpec((images, classes), lambda j, p: (p[0], 0)),
                whole(w_cls),
                whole(vectors),
                whole(bounds),
                pl.BlockSpec(memory_space=pltpu.SMEM),
            ],
            out_specs=[full(rows, width), full(width, classes), full(8, 128), full(2, width)],
            scratch_shapes=[pltpu.VMEM((rows, width), F32), pltpu.VMEM((rows, 128), F32)],
        ),
        out_shape=[
            jax.ShapeDtypeStruct((rows, width), F32),
            jax.ShapeDtypeStruct((width, classes), LOW),
            jax.ShapeDtypeStruct((8, 128), F32),
            jax.ShapeDtypeStruct((2, width), F32),
        ],
        compiler_params=pltpu.CompilerParams(vmem_limit_bytes=VMEM_BYTES),
        name="pool",
    )(pack, x2, labels, w_cls, vectors, bounds, valid)


def mlp_back_kernel(
    dx2_ref, act_ref, slope_ref, h2_ref, x1_ref, o_ref, wout_ref, wup_ref, wdn_ref, vec_ref,
    dmlp_ref, dout_ref, do_ref, dmid_ref, dvec_ref,
    low_ref, lowt_ref, h2t_ref, acc_ref, dh_ref,
    keep=None, between=None,
):
    step = pl.program_id(0)
    rows, width = dx2_ref.shape
    groups, _, part = wout_ref.shape
    tile = 256

    @pl.when(step == 0)
    def _():
        for at in range(rows // tile):
            span = slice(at * tile, (at + 1) * tile)
            values = dx2_ref[span, :]
            low_ref[span, :] = values.astype(LOW)
            lowt_ref[:, span] = jnp.transpose(values).astype(LOW)
            h2t_ref[:, span] = jnp.transpose(h2_ref[span, :].astype(F32)).astype(LOW)
            acc_ref[span, :] = jnp.zeros((tile, width), F32)

    wide = 512
    for at in range(rows // wide):
        span = slice(at * wide, (at + 1) * wide)
        d_hidden = (mm(low_ref[span, :], wdn_ref[0]) * slope_ref[span, :].astype(F32)).astype(LOW)
        dh_ref[span, :] = d_hidden
        acc_ref[span, :] += mm_nt(d_hidden, wup_ref[0])

    def grads(put):
        for at in range(width // 192):
            span = slice(at * 192, (at + 1) * 192)
            put(0, at, mm(lowt_ref[span, :], act_ref[...]).astype(LOW))
            put(1, at, mm(h2t_ref[span, :], dh_ref[...]).astype(LOW))

    def put_out(kind, at, value):
        dmlp_ref[kind, 0, at * 192 : (at + 1) * 192, :] = value

    if keep is None:
        grads(put_out)
    else:
        between(2 * step, 0)
        pl.when(step < 1)(lambda: grads(keep))
        pl.when(step >= 1)(lambda: grads(put_out))
        between(2 * step + 1, 1)

    @pl.when(step == pl.num_programs(0) - 1)
    def _():
        gain = vec_ref[1:2]
        gain_sum = jnp.zeros((1, width), F32)
        for at in range(rows // tile):
            span = slice(at * tile, (at + 1) * tile)
            normed, inverse = row_norm(x1_ref[span, :])
            d_second = acc_ref[span, :]
            gain_sum += jnp.sum(d_second * normed, axis=0, keepdims=True)
            d_middle = dx2_ref[span, :] + row_norm_back(d_second, gain, normed, inverse)
            dmid_ref[span, :] = d_middle
            low = d_middle.astype(LOW)
            lowt_ref[:, span] = jnp.transpose(d_middle).astype(LOW)
            do_ref[span, :] = jnp.concatenate(
                [mm(low, wout_ref[group]) for group in range(groups)], axis=1
            ).astype(LOW)
        dvec_ref[...] = gain_sum
        for group in range(groups):
            piece = o_ref[:, group * part : (group + 1) * part]
            for at in range(width // tile):
                span = slice(at * tile, (at + 1) * tile)
                dout_ref[group, span, :] = mm(lowt_ref[span, :], piece).astype(LOW)


def mlp_back_call(dx2, active, slope, h2, x1, attended, w_out, w_up, w_dn, vectors):
    rows, width = dx2.shape
    groups, _, per = w_up.shape
    chunk = per
    hidden = groups * per
    whole = lambda a: pl.BlockSpec(a.shape, lambda j: (0,) * a.ndim, pipeline_mode=pl.Buffered(1))
    weight = pl.BlockSpec((1, width, chunk), lambda j: (j, 0, 0))
    piece = pl.BlockSpec((rows, chunk), lambda j: (0, j))
    full = lambda *shape: pl.BlockSpec(shape, lambda j: (0,) * len(shape))
    return pl.pallas_call(
        mlp_back_kernel,
        grid=(hidden // chunk,),
        in_specs=[
            whole(dx2), piece, piece, whole(h2), whole(x1), whole(attended), whole(w_out),
            weight, weight, whole(vectors),
        ],
        out_specs=[
            pl.BlockSpec((2, 1, width, chunk), lambda j: (0, j, 0, 0)),
            full(*w_out.shape),
            full(rows, width),
            full(rows, width),
            full(1, width),
        ],
        out_shape=[
            jax.ShapeDtypeStruct((2,) + w_up.shape, LOW),
            jax.ShapeDtypeStruct(w_out.shape, LOW),
            jax.ShapeDtypeStruct((rows, width), LOW),
            jax.ShapeDtypeStruct((rows, width), F32),
            jax.ShapeDtypeStruct((1, width), F32),
        ],
        scratch_shapes=[
            pltpu.VMEM((rows, width), LOW),
            pltpu.VMEM((width, rows), LOW),
            pltpu.VMEM((width, rows), LOW),
            pltpu.VMEM((rows, width), F32),
            pltpu.VMEM((rows, chunk), LOW),
        ],
        compiler_params=pltpu.CompilerParams(vmem_limit_bytes=VMEM_BYTES),
        name="mlp_back",
    )(dx2, active, slope, h2, x1, attended, w_out, w_up, w_dn, vectors)


def embed_back_kernel(
    pack_ref, dq_ref, dk_ref, dv_ref, h1_ref, emb_ref, dmid_ref, pix_ref, coord_ref, win_ref, vec_ref,
    din_ref, dpp_ref, dvec_ref,
    h1t_ref, join_ref, acc_ref,
):
    step = pl.program_id(0)
    rows, width = h1_ref.shape
    groups = pl.num_programs(0)
    part = win_ref.shape[2] // 3
    tile = 256

    @pl.when(step == 0)
    def _():
        for at in range(rows // tile):
            span = slice(at * tile, (at + 1) * tile)
            h1t_ref[:, span] = jnp.transpose(h1_ref[span, :].astype(F32)).astype(LOW)
            acc_ref[span, :] = jnp.zeros((tile, width), F32)

    for group in range(width // part):

        @pl.when(step == group)
        def _():
            mine = slice(group * part, (group + 1) * part)
            join_ref[...] = jnp.concatenate([dq_ref[:, mine], dk_ref[:, mine], dv_ref[:, mine]], axis=1)

    for at in range(rows // tile):
        span = slice(at * tile, (at + 1) * tile)
        acc_ref[span, :] += mm_nt(join_ref[span, :], win_ref[0])
    for at in range(width // tile):
        span = slice(at * tile, (at + 1) * tile)
        din_ref[0, span, :] = mm(h1t_ref[span, :], join_ref[...]).astype(LOW)

    @pl.when(step == groups - 1)
    def _():
        gain = vec_ref[0:1]
        pixels = pix_ref.shape[1]
        spots = (dpp_ref.shape[1] - pixels) // 2
        gain_sum = jnp.zeros((1, width), F32)
        for at in range(rows // tile):
            span = slice(at * tile, (at + 1) * tile)
            normed, inverse = row_norm(emb_ref[span, :])
            d_first = acc_ref[span, :]
            gain_sum += jnp.sum(d_first * normed, axis=0, keepdims=True)
            d_embed = dmid_ref[span, :] + row_norm_back(d_first, gain, normed, inverse)
            h1t_ref[:, span] = jnp.transpose(d_embed).astype(LOW)
        dvec_ref[...] = gain_sum
        lane = lax.broadcasted_iota(jnp.int32, (rows, 2 * spots), 1)
        hot = ((lane == coord_ref[:, 0:1]) | (lane - spots == coord_ref[:, 1:2])).astype(F32).astype(LOW)
        for at in range(width // tile):
            span = slice(at * tile, (at + 1) * tile)
            dpp_ref[span, :pixels] = mm(h1t_ref[span, :], pix_ref[...]).astype(LOW)
            dpp_ref[span, pixels:] = mm(h1t_ref[span, :], hot).astype(LOW)


def embed_back_call(pack, dq, dk, dv, h1, embedded, d_middle, pixels, coords, w_in, w_pp_shape, vectors):
    rows, width = h1.shape
    groups = w_in.shape[0]
    whole = lambda a: pl.BlockSpec(a.shape, lambda j, p: (0,) * a.ndim, pipeline_mode=pl.Buffered(1))
    full = lambda *shape: pl.BlockSpec(shape, lambda j, p: (0,) * len(shape))
    weight = pl.BlockSpec((1,) + w_in.shape[1:], lambda j, p: (j, 0, 0))
    return pl.pallas_call(
        embed_back_kernel,
        grid_spec=pltpu.PrefetchScalarGridSpec(
            num_scalar_prefetch=1,
            grid=(groups,),
            in_specs=[
                whole(dq), whole(dk), whole(dv), whole(h1), whole(embedded), whole(d_middle),
                pl.BlockSpec((rows, pixels.shape[1]), lambda j, p: (p[0], 0)),
                pl.BlockSpec((rows, 2), lambda j, p: (p[0], 0)),
                weight,
                whole(vectors),
            ],
            out_specs=[weight, full(*w_pp_shape), full(1, width)],
            scratch_shapes=[
                pltpu.VMEM((width, rows), LOW),
                pltpu.VMEM((rows, w_in.shape[2]), LOW),
                pltpu.VMEM((rows, width), F32),
            ],
        ),
        out_shape=[
            jax.ShapeDtypeStruct(w_in.shape, LOW),
            jax.ShapeDtypeStruct(w_pp_shape, LOW),
            jax.ShapeDtypeStruct((1, width), F32),
        ],
        compiler_params=pltpu.CompilerParams(vmem_limit_bytes=VMEM_BYTES),
        name="embed_back",
    )(pack, dq, dk, dv, h1, embedded, d_middle, pixels, coords, w_in, vectors)


def pack_step(pack, valid, pixels, coords, lengths, labels, weights, vectors, head_gains, image_count, close=False):
    if close:
        bounds, gains = weights[6:]
        weights = weights[:6]
    w_pp, w_in, w_out, w_up, w_dn, w_cls = weights
    packs, images = lengths.shape
    rows = pixels.shape[0] // packs
    width = vectors.shape[1]
    if not close:
        mine = lax.dynamic_index_in_dim(lengths, pack[0], 0, keepdims=False)
        ends = jnp.cumsum(mine)
        fill = jnp.full((64 - images,), 1 << 30, jnp.int32)
        starts = jnp.concatenate([ends - mine, fill])
        ends = jnp.concatenate([ends, fill])
        bounds = jnp.stack([jnp.tile(starts, 2), jnp.tile(ends, 2)])
        gains = jnp.tile(head_gains, (1, 2))
    if close:
        (
            embedded, h1, q_raw, k_raw, value, attended, lse, w_in, w_out, w_up, w_dn, w_cls,
            x1, h2, active, slope, x2,
        ) = forward_call(weights, pixels, coords, vectors, gains, bounds, packs, 0)
    else:
        places = coords.T
        embedded, h1, q_raw, k_raw, value = embed_call(pack, pixels, places, w_pp, w_in, vectors, rows)
        attended, lse = attend_call(q_raw, k_raw, value, gains, bounds)
        x1, h2, active, slope, x2 = mlp_call(attended, embedded, w_out, w_up, w_dn, vectors)
    dx2, d_cls, loss, dvec_pool = pool_call(
        pack, x2, labels, w_cls, vectors, bounds, valid, images, image_count
    )
    if close:
        share = width // 8
        cut = lambda entry: entry.reshape(entry.shape[:-2] + (2, 2, 2, share) + entry.shape[-1:])
        d_mlp, d_out, d_attended, d_middle, dvec_two, share_mlp, share_cls = mlp_back_sum_call(
            dx2, active, slope, h2, x1, attended, w_out, w_up, w_dn, vectors, cut(d_cls), 1
        )
        d_mlp = d_mlp.reshape((-1, 2, 2, 2, share, width))
        dq, dk, dv, d_gain, share_mlp, share_out = attend_back_sum_call(
            q_raw, k_raw, value, attended, lse, d_attended, gains, bounds, d_mlp, cut(d_out), share_mlp, 2
        )
        share_in, share_pp, small, squares = embed_back_sum_call(
            dq, dk, dv, h1, embedded, d_middle, pixels, coords, w_in, weights[0].shape[1], vectors,
            dvec_two, dvec_pool, d_gain, loss, share_mlp, share_cls, share_out, packs, 3,
        )
        return share_pp, share_in, share_out, share_mlp, share_cls, small, squares
    d_mlp, d_out, d_attended, d_middle, dvec_two = mlp_back_call(
        dx2, active, slope, h2, x1, attended, w_out, w_up, w_dn, vectors
    )
    d_vec = jnp.concatenate([jnp.zeros_like(dvec_two), dvec_two, dvec_pool], axis=0)
    dq, dk, dv, d_gain = attend_back_call(q_raw, k_raw, value, attended, lse, d_attended, gains, bounds)
    d_in, d_pp, dvec_one = embed_back_call(
        pack, dq, dk, dv, h1, embedded, d_middle, pixels, places, w_in, w_pp.shape, vectors
    )
    d_gains = jnp.sum(d_gain.reshape(-1, 2, 2, 64), axis=(0, 2))
    return (d_pp, d_in, d_out, d_mlp[1], d_mlp[0], d_cls), d_vec.at[0].set(dvec_one[0]), d_gains, loss[0, 0]


MESH = pl.DeviceIdType.MESH


class Seat:
    def __init__(self):
        self.me = lax.axis_index("dp")
        self.z = lax.axis_index("tensor")
        self.c = lax.rem(self.me, 2)
        self.x = lax.rem(lax.div(self.me, 2), 2)
        self.y = lax.div(self.me, 4)
        self.core = self.me + 1 - 2 * self.c
        self.xn = self.me + 2 - 4 * self.x
        self.yn = self.me + 4 - 8 * self.y
        self.diag = self.xn + 4 - 8 * self.y


def link(src, dst, sems, at, device):
    return pltpu.make_async_remote_copy(
        src_ref=src,
        dst_ref=dst,
        send_sem=sems[0].at[at],
        recv_sem=sems[1].at[at],
        device_id=device,
        device_id_type=MESH,
    )


def greet(seat, depth):
    barrier = pltpu.get_barrier_semaphore()
    for ahead in range(1, 8):
        pl.semaphore_signal(
            barrier, inc=1, device_id={"dp": lax.rem(seat.me + ahead, 8)}, device_id_type=MESH
        )
    for ahead in range(1, depth):
        pl.semaphore_signal(
            barrier, inc=1, device_id={"tensor": lax.rem(seat.z + ahead, depth)}, device_id_type=MESH
        )
    pl.semaphore_wait(barrier, 6 + depth)


class Gather:
    def __init__(self, seat, shards, outs, split, units, own_sem, sems):
        self.seat, self.shards, self.outs, self.split, self.units = seat, shards, outs, split, units
        self.own_sem, self.sems = own_sem, sems
        self.share = shards[0].shape[0]

    def rows(self, owner):
        return pl.ds(pl.multiple_of(owner * self.share, self.share), self.share)

    def column(self, u, owner):
        k, cols = self.units[u]
        if self.split[k]:
            return self.outs[k].at[:, self.rows(owner), cols]
        return self.outs[k].at[self.rows(owner), cols]

    def halves(self, u, owner, which):
        k, cols = self.units[u]
        if self.split[k]:
            return self.outs[k].at[2 * which : 2 * which + 2, self.rows(owner), cols]
        half = self.share // 2
        start = pl.multiple_of(owner * self.share + which * half, half)
        return self.outs[k].at[pl.ds(start, half), cols]

    def block(self, u, level):
        k, cols = self.units[u]
        return self.outs[k].at[level, self.rows(self.seat.me), cols]

    def keep(self, u):
        k, cols = self.units[u]
        mine = self.block(u, self.seat.z) if self.split[k] else self.column(u, self.seat.me)
        return pltpu.make_async_copy(self.shards[k].at[:, cols], mine, self.own_sem.at[u])

    def along(self, u, hop, way):
        k, cols = self.units[u]
        level = self.seat.z - way * hop
        source = self.shards[k].at[:, cols] if hop == 0 else self.block(u, level)
        at = (u, hop + (0 if way > 0 else 3))
        return link(source, self.block(u, level), self.sems, at, {"tensor": self.seat.z + way})

    def arrives(self, u, hop, way):
        level = self.seat.z - way * (hop + 1)
        at = (u, hop + (0 if way > 0 else 3))
        return link(self.block(u, level), self.block(u, level), self.sems, at, {"tensor": self.seat.z - way})

    def sends(self, hop, way):
        level, to = self.seat.z - way * hop, self.seat.z + way
        return (level >= 0) & (level < 4) & (to >= 0) & (to < 4)

    def gets(self, hop, way):
        level = self.seat.z - way * (hop + 1)
        return (level >= 0) & (level < 4)

    def z(self, u, hop):
        for way in (1, -1):
            if hop > 0:

                @pl.when(self.gets(hop - 1, way))
                def _():
                    self.arrives(u, hop - 1, way).wait_recv()

            if hop < 3:

                @pl.when(self.sends(hop, way))
                def _():
                    self.along(u, hop, way).start()

    def copy(self, u, region, at, device):
        return link(region, region, self.sems, (u, at), {"dp": device})

    def own_x(self, u):
        return self.copy(u, self.column(u, self.seat.me), 6, self.seat.xn)

    def own_y(self, u):
        return self.copy(u, self.column(u, self.seat.me), 7, self.seat.yn)

    def pass_x(self, u):
        return self.copy(u, self.halves(u, self.seat.yn, 1), 8, self.seat.xn)

    def pass_y(self, u):
        return self.copy(u, self.halves(u, self.seat.xn, 0), 9, self.seat.yn)

    def owner(self, which):
        return (self.seat.me, self.seat.xn, self.seat.yn, self.seat.diag)[which]

    def over(self, u, which):
        return self.copy(u, self.column(u, self.owner(which)), 10 + which, self.seat.core)

    def plane(self, u):
        self.keep(u).wait()
        self.own_x(u).start()
        self.own_y(u).start()
        self.over(u, 0).start()

    def relay(self, u):
        s = self.seat
        self.copy(u, self.column(u, s.xn), 6, s.xn).wait_recv()
        self.pass_y(u).start()
        self.over(u, 1).start()
        self.copy(u, self.column(u, s.yn), 7, s.yn).wait_recv()
        self.pass_x(u).start()
        self.over(u, 2).start()

    def corner(self, u):
        s = self.seat
        self.copy(u, self.halves(u, s.diag, 1), 8, s.xn).wait_recv()
        self.copy(u, self.halves(u, s.diag, 0), 9, s.yn).wait_recv()
        self.over(u, 3).start()

    def arrived(self, u):
        s = self.seat
        for which in range(4):
            theirs = self.column(u, self.owner(which) + 1 - 2 * s.c)
            self.copy(u, theirs, 10 + which, s.core).wait_recv()

    def drain(self, u):
        if self.split[self.units[u][0]]:
            for hop in range(3):
                for way in (1, -1):

                    @pl.when(self.sends(hop, way))
                    def _():
                        self.along(u, hop, way).wait_send()

        for copy in (self.own_x(u), self.own_y(u), self.pass_x(u), self.pass_y(u)):
            copy.wait_send()
        for which in range(4):
            self.over(u, which).wait_send()


FORWARD_SPLIT = (False, True, True, True, True, False)


def forward_kernel(
    pp_in, in_in, out_in, up_in, dn_in, cls_in, pix_hbm, coord_ref, vec_ref, gain_ref, bound_ref,
    emb_hbm, h1_hbm, q_hbm, k_hbm, v_hbm, o_ref, lse_ref, win_hbm, wout_hbm, wup_hbm, wdn_hbm, wcls_hbm,
    x1_hbm, h2_hbm, act_hbm, slope_hbm, x2_hbm,
    wp_ref, win_ref, pix_ref, emb_ref, h1_ref, q_ref, k_ref, v_ref, ka_ref, va_ref, qa_ref,
    wout_ref, wup_ref, wdn_ref, all_ref, act_ref, slope_ref,
    own_sem, send_sem, recv_sem, copy_sem, act_sem,
    *, packs,
):
    step = pl.program_id(0)
    rows, pixels = pix_ref.shape
    groups = win_ref.shape[0]
    part = win_ref.shape[2] // 3
    spots = (wp_ref.shape[1] - pixels) // 2
    per = wup_ref.shape[2]
    half = per // 2
    tile = 256
    seat = Seat()
    everything, left, right = slice(None), slice(0, half), slice(half, 2 * half)
    units = (
        (0, everything), (1, everything), (2, everything),
        (3, left), (3, right), (4, left), (4, right), (5, everything),
    )
    pp, w_in, out, up_a, up_b, dn_a, dn_b, cls = range(8)
    flow = Gather(
        seat,
        (pp_in, in_in, out_in, up_in, dn_in, cls_in),
        (wp_ref, win_ref, wout_ref, wup_ref, wdn_ref, wcls_hbm),
        FORWARD_SPLIT,
        units,
        own_sem,
        (send_sem, recv_sem),
    )
    pack = jnp.minimum(seat.z, packs - 1)
    pix_copy = pltpu.make_async_copy(
        pix_hbm.at[pl.ds(pl.multiple_of(pack * rows, rows), rows)], pix_ref, copy_sem.at[0]
    )
    results = [
        pltpu.make_async_copy(source, target, copy_sem.at[1 + n])
        for n, (source, target) in enumerate(
            (
                (emb_ref, emb_hbm), (h1_ref, h1_hbm), (q_ref, q_hbm), (k_ref, k_hbm), (v_ref, v_hbm),
                (win_ref, win_hbm), (wout_ref, wout_hbm), (wup_ref, wup_hbm), (wdn_ref, wdn_hbm),
                (emb_ref, x1_hbm), (h1_ref, h2_hbm), (q_ref, x2_hbm),
            )
        )
    ]

    def hidden_copies(group):
        columns = slice(group * per, (group + 1) * per)
        return [
            pltpu.make_async_copy(source.at[group], target.at[:, columns], act_sem.at[n, group])
            for n, (source, target) in enumerate(((act_ref, act_hbm), (slope_ref, slope_hbm)))
        ]

    def join_heads(at):
        span = slice(at * tile, (at + 1) * tile)
        branch = mm_nt(all_ref[span, :part], wout_ref[0])
        for group in range(1, groups):
            branch += mm_nt(all_ref[span, group * part : (group + 1) * part], wout_ref[group])
        middle = emb_ref[span, :] + branch
        emb_ref[span, :] = middle
        normed, _ = row_norm(middle)
        h1_ref[span, :] = (normed * vec_ref[1:2]).astype(LOW)

    def hide(group):
        spans = [slice(at * tile, (at + 1) * tile) for at in range(rows // tile)]
        hidden = mm(h1_ref[spans[0], :], wup_ref[group])
        for at, span in enumerate(spans):
            now = hidden
            if at + 1 < len(spans):
                hidden = mm(h1_ref[spans[at + 1], :], wup_ref[group])
            active, slope = gelu_pair(now)
            act_ref[group, span, :] = active.astype(LOW)
            slope_ref[group, span, :] = slope.astype(LOW)
        for copy in hidden_copies(group):
            copy.start()

    def show(at):
        span = slice(at * tile, (at + 1) * tile)
        total = emb_ref[span, :]
        for group in range(groups):
            total += mm_nt(act_ref[group, span, :], wdn_ref[group])
        q_ref[span, :] = total

    def embed(at):
        span = slice(at * tile, (at + 1) * tile)
        start = pl.multiple_of(pack * rows + at * tile, tile)
        place = lax.broadcasted_iota(jnp.int32, (2 * spots, tile), 0)
        across = coord_ref[0:1, pl.ds(start, tile)]
        down = coord_ref[1:2, pl.ds(start, tile)]
        hot = jnp.transpose(((place == across) | (place - spots == down)).astype(F32)).astype(LOW)
        embedded = mm_nt(pix_ref[span, :], wp_ref[:, :pixels]) + mm_nt(hot, wp_ref[:, pixels:])
        emb_ref[span, :] = embedded
        normed, _ = row_norm(embedded)
        h1_ref[span, :] = (normed * vec_ref[0:1]).astype(LOW)

    def project(at):
        span = slice(at * tile, (at + 1) * tile)
        first = h1_ref[span, :]
        parts = [mm(first, win_ref[group]) for group in range(groups)]
        q_ref[span, :] = jnp.concatenate([entry[:, :part] for entry in parts], axis=1)
        k_ref[span, :] = jnp.concatenate([entry[:, part : 2 * part] for entry in parts], axis=1)
        v_ref[span, :] = jnp.concatenate([entry[:, 2 * part :].astype(LOW) for entry in parts], axis=1)

    @pl.when(step == 0)
    def _():
        pix_copy.start()
        for u in range(8):
            flow.keep(u).start()
        greet(seat, 4)
        flow.z(w_in, 0)
        flow.plane(pp)
        flow.z(w_in, 1)
        flow.relay(pp)
        flow.z(w_in, 2)
        flow.corner(pp)
        flow.z(w_in, 3)
        flow.plane(w_in)
        flow.z(out, 0)
        flow.arrived(pp)
        pix_copy.wait()
        embed(0)
        flow.z(out, 1)
        embed(1)
        flow.z(out, 2)
        flow.z(up_a, 0)
        embed(2)
        flow.z(out, 3)
        flow.plane(out)
        flow.z(up_a, 1)
        embed(3)
        flow.z(up_a, 2)
        results[0].start()
        results[1].start()
        flow.relay(w_in)
        flow.z(up_a, 3)
        flow.z(up_b, 0)
        flow.relay(out)
        flow.plane(up_a)
        flow.corner(w_in)
        flow.z(up_b, 1)
        flow.arrived(w_in)
        results[5].start()
        project(0)
        flow.corner(out)
        flow.z(up_b, 2)
        project(1)
        flow.z(up_b, 3)
        flow.plane(up_b)
        flow.z(dn_a, 0)
        project(2)
        flow.relay(up_a)
        flow.z(dn_a, 1)
        project(3)
        for n in (2, 3, 4):
            results[n].start()

    plan = {
        0: [lambda: flow.z(dn_a, 2)],
        1: [lambda: flow.z(dn_a, 3)],
        2: [lambda: flow.corner(up_a), lambda: flow.plane(dn_a), lambda: flow.z(dn_b, 0)],
        4: [lambda: flow.relay(up_b), lambda: flow.z(dn_b, 1)],
        5: [lambda: flow.z(dn_b, 2)],
        7: [lambda: flow.corner(up_b), lambda: flow.z(dn_b, 3), lambda: flow.plane(dn_b)],
        10: [lambda: flow.relay(dn_a)],
    }

    def between(slot):
        for number, actions in plan.items():
            if number % 2 == slot:

                @pl.when(2 * step + slot == number)
                def _():
                    for action in actions:
                        action()

    mine = pl.ds(pl.multiple_of(step * 128, 128), 128)
    attend_kernel(
        q_ref.at[:, mine], k_ref.at[:, mine], v_ref.at[:, mine], gain_ref, bound_ref, o_ref, lse_ref,
        ka_ref, va_ref, qa_ref, between=between,
    )
    all_ref[:, mine] = o_ref[...]

    @pl.when(step == pl.num_programs(0) - 1)
    def _():
        flow.arrived(out)
        results[6].start()
        for n in range(3):
            results[n].wait()
        for at in range(rows // tile):
            join_heads(at)
        results[9].start()
        results[10].start()
        flow.corner(dn_a)
        flow.plane(cls)
        flow.arrived(up_a)
        flow.arrived(up_b)
        results[7].start()
        hide(0)
        flow.relay(dn_b)
        hide(1)
        flow.corner(dn_b)
        hide(2)
        flow.relay(cls)
        hide(3)
        flow.corner(cls)
        flow.arrived(dn_a)
        flow.arrived(dn_b)
        results[8].start()
        for at in range(rows // tile):
            show(at)
        results[11].start()
        flow.arrived(cls)
        for u in range(8):
            flow.drain(u)
        for copy in results[3:]:
            copy.wait()
        for group in range(groups):
            for copy in hidden_copies(group):
                copy.wait()


def forward_call(shards, pixels, coords, vectors, gains, bounds, packs, collective_id):
    depth, width = 4, vectors.shape[1]
    rows = pixels.shape[0] // packs
    anywhere = pl.BlockSpec(memory_space=pl.ANY)
    small = lambda a: pl.BlockSpec(a.shape, lambda j: (0, 0))
    pair = pl.BlockSpec((rows, 128), lambda j: (0, j))
    weights = [
        jax.ShapeDtypeStruct(((depth, width) if apart else (width,)) + entry.shape[1:], LOW)
        for entry, apart in zip(shards, FORWARD_SPLIT)
    ]
    token = lambda dtype: jax.ShapeDtypeStruct((rows, width), dtype)
    held = lambda dtype: pltpu.VMEM((rows, width), dtype)
    per = shards[3].shape[1]
    wide = jax.ShapeDtypeStruct((rows, depth * per), LOW)
    return pl.pallas_call(
        functools.partial(forward_kernel, packs=packs),
        grid=(width // 128,),
        in_specs=[anywhere] * 7 + [small(coords), small(vectors), small(gains), small(bounds)],
        out_specs=[anywhere] * 5 + [pair, pair] + [anywhere] * 10,
        out_shape=[token(F32), token(LOW), token(F32), token(F32), token(LOW), token(LOW), token(F32)]
        + weights[1:]
        + [token(F32), token(LOW), wide, wide, token(F32)],
        scratch_shapes=[
            pltpu.VMEM(weights[0].shape, LOW),
            pltpu.VMEM(weights[1].shape, LOW),
            pltpu.VMEM((rows, pixels.shape[1]), LOW),
            held(F32), held(LOW), held(F32), held(F32), held(LOW),
            pltpu.VMEM((rows, 256), LOW),
            pltpu.VMEM((rows, 256), LOW),
            pltpu.VMEM((2, rows, 256), LOW),
            *(pltpu.VMEM(entry.shape, LOW) for entry in weights[2:5]),
            held(LOW),
            pltpu.VMEM((depth, rows, per), LOW),
            pltpu.VMEM((depth, rows, per), LOW),
            pltpu.SemaphoreType.DMA((8,)),
            pltpu.SemaphoreType.DMA((8, 14)),
            pltpu.SemaphoreType.DMA((8, 14)),
            pltpu.SemaphoreType.DMA((13,)),
            pltpu.SemaphoreType.DMA((2, depth)),
        ],
        compiler_params=pltpu.CompilerParams(
            collective_id=collective_id, has_side_effects=True, vmem_limit_bytes=VMEM_BYTES
        ),
        name="forward",
    )(*shards, pixels, coords, vectors, gains, bounds)


class Flow:
    def __init__(self, seat, level_of, own, core_in, plane_in, last_in, up_in, down_in, sems):
        self.seat, self.level_of, self.own, self.sems = seat, level_of, own, sems
        self.core_in, self.plane_in, self.last_in = core_in, plane_in, last_in
        self.up_in, self.down_in = up_in, down_in

    def to_core(self, i, source):
        return link(source, self.core_in.at[i], self.sems, (i, 0), {"dp": self.seat.core})

    def first(self, i, along_x):
        s = self.seat
        source = self.own(i).at[:, 1 - s.x] if along_x else self.own(i).at[1 - s.y]
        return link(source, self.plane_in.at[i], self.sems, (i, 1), {"dp": s.xn if along_x else s.yn})

    def second(self, i, along_x):
        s = self.seat
        source = self.own(i).at[s.y, 1 - s.x] if along_x else self.own(i).at[1 - s.y, s.x]
        return link(source, self.last_in.at[i], self.sems, (i, 2), {"dp": s.xn if along_x else s.yn})

    def along(self, i, way):
        s = self.seat
        buffer = self.up_in if way > 0 else self.down_in
        at = (i, 3 if way > 0 else 4)
        return link(self.own(i).at[s.y, s.x], buffer.at[i], self.sems, at, {"tensor": s.z + way})

    def x_first(self, i, then, other):
        pl.when(lax.rem(i, 2) == 0)(then)
        pl.when(lax.rem(i, 2) == 1)(other)

    def one(self, i):
        mine = self.own(i)
        mine[...] = mine[...] + self.core_in[i]
        self.x_first(i, lambda: self.first(i, True).start(), lambda: self.first(i, False).start())

    def two(self, i):
        s, mine = self.seat, self.own(i)

        def from_x():
            self.first(i, True).wait_recv()
            mine[:, s.x] = mine[:, s.x] + self.plane_in[i]
            self.second(i, False).start()

        def from_y():
            self.first(i, False).wait_recv()
            mine[s.y] = mine[s.y] + self.plane_in[i]
            self.second(i, True).start()

        self.x_first(i, from_x, from_y)

    def three(self, i):
        s, mine = self.seat, self.own(i)
        self.second(i, False).wait_recv()
        mine[s.y, s.x] = mine[s.y, s.x] + self.last_in[i]

        @pl.when((s.z == 0) & (self.level_of(i) > 0))
        def _():
            self.along(i, 1).start()

        @pl.when((s.z == 3) & (self.level_of(i) < 3))
        def _():
            self.along(i, -1).start()

    def hop(self, i, reach):
        s, mine = self.seat, self.own(i)

        @pl.when((s.z == reach) & (self.level_of(i) > reach))
        def _():
            self.along(i, 1).wait_recv()
            mine[s.y, s.x] = mine[s.y, s.x] + self.up_in[i]
            self.along(i, 1).start()

        @pl.when((s.z == 3 - reach) & (self.level_of(i) < 3 - reach))
        def _():
            self.along(i, -1).wait_recv()
            mine[s.y, s.x] = mine[s.y, s.x] + self.down_in[i]
            self.along(i, -1).start()

    def total(self, i):
        s = self.seat
        values = self.own(i)[s.y, s.x].astype(F32)

        @pl.when(s.z > 0)
        def _():
            self.along(i, 1).wait_recv()

        @pl.when(s.z < 3)
        def _():
            self.along(i, -1).wait_recv()

        @pl.when(s.z == 0)
        def _():
            self.up_in[i] = jnp.zeros(self.up_in.shape[1:], LOW)

        @pl.when(s.z == 3)
        def _():
            self.down_in[i] = jnp.zeros(self.down_in.shape[1:], LOW)

        return values + self.up_in[i].astype(F32) + self.down_in[i].astype(F32)

    def drain(self, i):
        s = self.seat
        self.first(i, True).wait_send()
        self.second(i, True).wait_send()

        @pl.when(s.z < self.level_of(i))
        def _():
            self.along(i, 1).wait_send()

        @pl.when(s.z > self.level_of(i))
        def _():
            self.along(i, -1).wait_send()


class Whole:
    def __init__(self, seat, own, core_in, plane_in, last_in, level_in, sems):
        self.seat, self.own, self.sems = seat, own, sems
        self.core_in, self.plane_in, self.last_in, self.level_in = core_in, plane_in, last_in, level_in
        self.half = core_in.shape[2] // 2

    def to_core(self, source):
        return link(source, self.core_in, self.sems, 0, {"dp": self.seat.core})

    def rows(self, which):
        return slice(which * self.half, (which + 1) * self.half)

    def first(self, which):
        s = self.seat
        rows = self.rows(which)
        source = self.own.at[1 - s.y, :, rows] if which else self.own.at[:, 1 - s.x, rows]
        return link(source, self.plane_in.at[which], self.sems, 1 + which, {"dp": s.yn if which else s.xn})

    def second(self, which):
        s = self.seat
        rows = self.rows(which)
        source = self.own.at[s.y, 1 - s.x, rows] if which else self.own.at[1 - s.y, s.x, rows]
        return link(source, self.last_in.at[which], self.sems, 3 + which, {"dp": s.xn if which else s.yn})

    def lift(self):
        s = self.seat
        return link(self.own.at[s.y, s.x], self.level_in.at[0], self.sems, 5, {"tensor": s.z + 1 - 2 * (s.z % 2)})

    def cross(self):
        s = self.seat
        return link(self.own.at[s.y, s.x], self.level_in.at[1], self.sems, 6, {"tensor": 3 - s.z})

    def give(self):
        s = self.seat
        return link(self.own.at[s.y, s.x], self.level_in.at[1], self.sems, 7, {"tensor": s.z + 1 - 2 * (s.z % 2)})

    def middle(self):
        return (self.seat.z == 1) | (self.seat.z == 2)

    def ends(self):
        return (self.seat.z == 0) | (self.seat.z == 3)

    def one(self):
        for a in range(2):
            for b in range(2):
                self.own[a, b] = self.own[a, b] + self.core_in[a, b]
        self.first(0).start()
        self.first(1).start()

    def two(self):
        s, own = self.seat, self.own
        for which in range(2):
            rows = self.rows(which)
            self.first(which).wait_recv()
            for a in range(2):
                if which:
                    own[s.y, a, rows] = own[s.y, a, rows] + self.plane_in[which, a]
                else:
                    own[a, s.x, rows] = own[a, s.x, rows] + self.plane_in[which, a]
            self.second(which).start()

    def three(self):
        s, own = self.seat, self.own
        for which in range(2):
            rows = self.rows(which)
            self.second(which).wait_recv()
            own[s.y, s.x, rows] = own[s.y, s.x, rows] + self.last_in[which]
        pl.when(self.ends())(lambda: self.lift().start())

    def four(self):
        s, own = self.seat, self.own

        @pl.when(self.middle())
        def _():
            self.lift().wait_recv()
            own[s.y, s.x] = own[s.y, s.x] + self.level_in[0]
            self.cross().start()

    def five(self):
        s, own = self.seat, self.own

        @pl.when(self.middle())
        def _():
            self.cross().wait_recv()
            self.cross().wait_send()
            own[s.y, s.x] = own[s.y, s.x] + self.level_in[1]
            self.give().start()

    def total(self):
        s = self.seat

        @pl.when(self.ends())
        def _():
            self.give().wait_recv()

        @pl.when(self.middle())
        def _():
            self.level_in[1] = self.own[s.y, s.x]

        return self.level_in[1].astype(F32)

    def drain(self):
        for which in range(2):
            self.first(which).wait_send()
            self.second(which).wait_send()
        pl.when(self.ends())(lambda: self.lift().wait_send())
        pl.when(self.middle())(lambda: self.give().wait_send())


class Tiny:
    def __init__(self, seat, value, came, sems):
        self.seat, self.value, self.came, self.sems = seat, value, came, sems

    def near(self, ahead, own):
        s = self.seat
        other = lax.rem(s.me + (ahead if own else 8 - ahead), 8)
        place = self.came.at[s.me if own else other]
        return link(self.value.at[0], place, self.sems, ahead - 1, {"dp": other})

    def far(self, ahead, own):
        s = self.seat
        other = lax.rem(s.z + (ahead if own else 4 - ahead), 4)
        place = self.came.at[8 + (s.z if own else other)]
        return link(self.value.at[1], place, self.sems, 6 + ahead, {"tensor": other})

    def start_plane(self):
        for ahead in range(1, 8):
            self.near(ahead, True).start()

    def total(self, first, count):
        total = self.came[first]
        for n in range(1, count):
            total = total + self.came[first + n]
        return total

    def turn_levels(self):
        for ahead in range(1, 8):
            self.near(ahead, False).wait_recv()
        self.came[self.seat.me] = self.value[0]
        self.value[1] = self.total(0, 8)
        for ahead in range(1, 4):
            self.far(ahead, True).start()

    def finish(self):
        for ahead in range(1, 4):
            self.far(ahead, False).wait_recv()
        self.came[8 + self.seat.z] = self.value[1]
        return self.total(8, 4)

    def drain(self):
        for ahead in range(1, 8):
            self.near(ahead, True).wait_send()
        for ahead in range(1, 4):
            self.far(ahead, True).wait_send()


def flow_scratch(chunks, share, cols):
    low = lambda *shape: pltpu.VMEM(shape, LOW)
    sems = lambda: pltpu.SemaphoreType.DMA((chunks, 5))
    return [
        low(chunks, 2, 2, share, cols),
        low(chunks, 2, share, cols),
        low(chunks, share, cols),
        low(chunks, share, cols),
        low(chunks, share, cols),
        sems(),
        sems(),
    ]


def whole_scratch(share, cols):
    low = lambda *shape: pltpu.VMEM(shape, LOW)
    return [
        low(2, 2, share, cols),
        low(2, 2, share // 2, cols),
        low(2, share // 2, cols),
        low(2, share, cols),
        pltpu.SemaphoreType.DMA((8,)),
        pltpu.SemaphoreType.DMA((8,)),
    ]


def tiny_scratch(shape):
    sems = lambda: pltpu.SemaphoreType.DMA((10,))
    return [pltpu.VMEM((2,) + shape, F32), pltpu.VMEM((12,) + shape, F32), sems(), sems()]


MLP_BACK_IO = (10, 5)
MLP_BACK_SCRATCH = 5


def mlp_back_sum_kernel(*refs):
    ins, outs = MLP_BACK_IO
    inputs, dcls_ref = refs[:ins], refs[ins]
    outputs = refs[ins + 1 : ins + 1 + outs]
    share_ref, cls_ref = refs[ins + 1 + outs : ins + 3 + outs]
    rest = refs[ins + 3 + outs :]
    scratch, rest = rest[:MLP_BACK_SCRATCH], rest[MLP_BACK_SCRATCH:]
    full, flow_refs = rest[0], rest[1:8]
    cls_own, cls_load, cls_refs = rest[8], rest[9], rest[10:16]
    step = pl.program_id(0)
    seat = Seat()
    c = seat.c
    share = full.shape[-2]
    flow = Flow(
        seat, lambda i: 1, lambda i: full.at[i, :, :, c], *flow_refs[:5], flow_refs[5:]
    )
    cls = Whole(seat, cls_own, *cls_refs[:4], cls_refs[4:])
    loading = pltpu.make_async_copy(dcls_ref.at[:, :, c], cls_own, cls_load)
    cls_to_core = cls.to_core(dcls_ref.at[:, :, 1 - c])

    def to_core(i):
        return flow.to_core(i, full.at[i, :, :, 1 - c])

    def one(i):
        to_core(i).wait_recv()
        flow.one(i)

    def last(i):
        @pl.when(seat.z == flow.level_of(i))
        def _():
            share_ref[i] = flow.total(i)

    @pl.when(step == 0)
    def _():
        loading.start()
        greet(seat, 4)
        cls_to_core.start()
        share_ref[...] = jnp.zeros(share_ref.shape, F32)

    def keep(kind, at, value):
        full[kind, at // 2, at % 2] = value.reshape(2, share, value.shape[1])

    def cls_total():
        cls_ref[...] = cls.total()

    def cls_one():
        loading.wait()
        cls_to_core.wait_recv()
        cls.one()

    plan = {
        0: [cls_one],
        1: [lambda: to_core(0).start(), lambda: to_core(1).start(), cls.two],
        2: [lambda: one(0), lambda: one(1), cls.three],
        4: [lambda: flow.two(0), lambda: flow.two(1), cls.four],
        5: [lambda: flow.three(0), lambda: flow.three(1)],
        6: [cls.five],
        7: [lambda: flow.hop(0, 1), lambda: flow.hop(1, 1)],
    }

    def between(now, odd):
        for number, actions in plan.items():
            if number % 2 != odd:
                continue

            @pl.when(now == number)
            def _():
                for action in actions:
                    action()

    mlp_back_kernel(*inputs, *outputs, *scratch, keep=keep, between=between)

    @pl.when(step == pl.num_programs(0) - 1)
    def _():
        cls_total()
        for i in range(2):
            last(i)
        for i in range(2):
            to_core(i).wait_send()
            flow.drain(i)
        cls_to_core.wait_send()
        cls.drain()


def mlp_back_sum_call(dx2, active, slope, h2, x1, attended, w_out, w_up, w_dn, vectors, d_cls, collective_id):
    rows, width = dx2.shape
    groups, _, per = w_up.shape
    chunk = per
    hidden = groups * per
    share, classes = d_cls.shape[-2:]
    turned = lambda j: j + 1 - 2 * (j % 2)
    whole = lambda a: pl.BlockSpec(a.shape, lambda j: (0,) * a.ndim, pipeline_mode=pl.Buffered(1))
    weight = pl.BlockSpec((1, width, chunk), lambda j: (turned(j), 0, 0))
    piece = pl.BlockSpec((rows, chunk), lambda j: (0, turned(j)))
    full = lambda *shape: pl.BlockSpec(shape, lambda j: (0,) * len(shape))
    late = lambda j: jnp.maximum(j - 1, 0)
    return pl.pallas_call(
        mlp_back_sum_kernel,
        grid=(hidden // chunk,),
        in_specs=[
            whole(dx2), piece, piece, whole(h2), whole(x1), whole(attended), whole(w_out),
            weight, weight, whole(vectors), pl.BlockSpec(memory_space=pl.ANY),
        ],
        out_specs=[
            pl.BlockSpec((2, 1, width, chunk), lambda j: (0, late(j), 0, 0)),
            full(*w_out.shape),
            full(rows, width),
            full(rows, width),
            full(1, width),
            full(2, share, width),
            full(share, classes),
        ],
        out_shape=[
            jax.ShapeDtypeStruct((2, groups - 1) + w_up.shape[1:], LOW),
            jax.ShapeDtypeStruct(w_out.shape, LOW),
            jax.ShapeDtypeStruct((rows, width), LOW),
            jax.ShapeDtypeStruct((rows, width), F32),
            jax.ShapeDtypeStruct((1, width), F32),
            jax.ShapeDtypeStruct((2, share, width), F32),
            jax.ShapeDtypeStruct((share, classes), F32),
        ],
        scratch_shapes=[
            pltpu.VMEM((rows, width), LOW),
            pltpu.VMEM((width, rows), LOW),
            pltpu.VMEM((width, rows), LOW),
            pltpu.VMEM((rows, width), F32),
            pltpu.VMEM((rows, chunk), LOW),
            pltpu.VMEM((2, 2, 2, 2, share, width), LOW),
        ]
        + flow_scratch(2, share, width)
        + [pltpu.VMEM((2, 2, share, classes), LOW), pltpu.SemaphoreType.DMA]
        + whole_scratch(share, classes),
        compiler_params=pltpu.CompilerParams(
            collective_id=collective_id, has_side_effects=True, vmem_limit_bytes=VMEM_BYTES
        ),
        name="mlp_back_sum",
    )(dx2, active, slope, h2, x1, attended, w_out, w_up, w_dn, vectors, d_cls)


def embed_back_sum_kernel(
    dq_hbm, dk_hbm, dv_hbm, h1_hbm, emb_hbm, dmid_hbm, pix_hbm, coord_ref, win_hbm, vec_ref,
    two_ref, pool_ref, gains_ref, loss_ref, mlp_ref, cls_ref, out_ref,
    in_ref, pp_ref, small_out, square_out,
    dq_ref, dk_ref, dv_ref, h1_ref, emb_ref, dmid_ref, pix_ref, win_ref, tile_sem, load_sem,
    h1t_ref, embt_ref, join_ref, hot_ref, in_full, pp_full,
    *rest, packs,
):
    rows, width = h1_ref.shape
    groups = 4
    part = win_ref.shape[2] // 3
    tile = 256
    seat = Seat()
    c = seat.c
    share = in_full.shape[-2]
    flow = Flow(
        seat, lambda i: (3 * i) % 4, lambda i: in_full.at[i, :, :, c], *rest[:5], rest[5:7]
    )
    pp = Whole(seat, pp_full.at[:, :, c], *rest[7:11], rest[11:13])
    small = Tiny(seat, rest[13], rest[14], rest[15:17])
    square = Tiny(seat, rest[17], rest[18], rest[19:21])
    small_value, square_value = rest[13], rest[17]
    pp_to_core = pp.to_core(pp_full.at[:, :, 1 - c])
    leader = jnp.where(seat.z == 0, 1.0, 0.0)

    def in_to_core(i):
        return flow.to_core(i, in_full.at[i, :, :, 1 - c])

    def one(i):
        in_to_core(i).wait_recv()
        flow.one(i)

    def last(i):
        @pl.when(flow.level_of(i) == seat.z)
        def _():
            in_ref[...] = flow.total(i)

    tiled = (
        (dq_hbm, dq_ref), (dk_hbm, dk_ref), (dv_hbm, dv_ref), (h1_hbm, h1_ref),
        (emb_hbm, emb_ref), (dmid_hbm, dmid_ref),
    )

    def tile_copies(at, numbers):
        span = pl.ds(at * tile, tile)
        return [
            pltpu.make_async_copy(tiled[n][0].at[span], tiled[n][1].at[span], tile_sem.at[n, at])
            for n in numbers
        ]

    win_copy = pltpu.make_async_copy(win_hbm, win_ref, load_sem.at[0])
    pack = jnp.minimum(seat.z, packs - 1)
    pix_copy = pltpu.make_async_copy(
        pix_hbm.at[pl.ds(pl.multiple_of(pack * rows, rows), rows)], pix_ref, load_sem.at[1]
    )
    for at in range(rows // tile):
        for copy in tile_copies(at, range(4)):
            copy.start()
    win_copy.start()
    for at in range(rows // tile):
        for copy in tile_copies(at, range(4, 6)):
            copy.start()
    pix_copy.start()
    greet(seat, 4)
    gain = vec_ref[0:1]
    pixels = pix_ref.shape[1]
    spots = (pp_ref.shape[1] - pixels) // 2
    gain_sum = jnp.zeros((1, width), F32)
    for at in range(rows // tile):
        for copy in tile_copies(at, range(4)):
            copy.wait()
        span = slice(at * tile, (at + 1) * tile)
        for group in range(groups):
            mine = slice(group * part, (group + 1) * part)
            join_ref[group, span, :] = jnp.concatenate(
                [dq_ref[span, mine], dk_ref[span, mine], dv_ref[span, mine]], axis=1
            )
        h1t_ref[:, span] = jnp.transpose(h1_ref[span, :].astype(F32)).astype(LOW)

    def project(i):
        group = flow.level_of(i)
        for at in range(4):
            span = slice(at * 2 * share, (at + 1) * 2 * share)
            value = mm(h1t_ref[span, :], join_ref[group]).astype(LOW)
            in_full[i, at // 2, at % 2] = value.reshape(2, share, value.shape[1])
        in_to_core(i).start()

    project(0)
    project(1)
    win_copy.wait()
    for at in range(rows // tile):
        for copy in tile_copies(at, range(4, 6)):
            copy.wait()
        span = slice(at * tile, (at + 1) * tile)
        d_first = jnp.zeros((tile, width), F32)
        for group in range(groups):
            d_first += mm_nt(join_ref[group, span, :], win_ref[group])
        normed, inverse = row_norm(emb_ref[span, :])
        gain_sum += jnp.sum(d_first * normed, axis=0, keepdims=True)
        d_embed = dmid_ref[span, :] + row_norm_back(d_first, gain, normed, inverse)
        embt_ref[:, span] = jnp.transpose(d_embed).astype(LOW)
        if at < 2:
            one(at)
    flow.two(0)
    small_value[0] = jnp.zeros(small_out.shape, F32)
    small_value[0, 0:1] = gain_sum
    small_value[0, 1:2] = two_ref[...]
    small_value[0, 2:4] = pool_ref[...]
    heads = jnp.sum(gains_ref[...], axis=0)
    small_value[0, 4:5, :128] = heads[0:1]
    small_value[0, 4:5, 128:256] = heads[1:2]
    small_value[0, 5:6, :128] = loss_ref[0:1, :]
    small.start_plane()
    place = lax.broadcasted_iota(jnp.int32, (2 * spots, rows), 0)
    mine = pl.ds(pl.multiple_of(pack * rows, rows), rows)
    hot = (place == coord_ref[0:1, mine]) | (place - spots == coord_ref[1:2, mine])
    hot_ref[...] = hot.astype(F32).astype(LOW)
    pix_copy.wait()
    for at in range(4):
        span = slice(at * 2 * share, (at + 1) * 2 * share)
        picture = mm(embt_ref[span, :], pix_ref[...]).astype(LOW)
        pp_full[at // 2, at % 2, :, :, :pixels] = picture.reshape(2, share, pixels)
        place = mm_nt(embt_ref[span, :], hot_ref[...]).astype(LOW)
        pp_full[at // 2, at % 2, :, :, pixels:] = place.reshape(2, share, 2 * spots)
    pp_to_core.start()
    flow.two(1)
    project(2)
    pp_to_core.wait_recv()
    pp.one()
    flow.three(0)
    small.turn_levels()
    project(3)
    one(2)
    flow.three(1)
    flow.hop(0, 1)
    pp.two()
    one(3)
    flow.hop(1, 1)
    flow.hop(0, 2)
    small_out[...] = small.finish()
    mlp_sum = mlp_ref[...]
    out_sum = out_ref[...]
    squares = jnp.sum(mlp_sum[0] * mlp_sum[0] + mlp_sum[1] * mlp_sum[1], axis=0, keepdims=True)
    total = jnp.sum(squares, axis=1, keepdims=True)
    total = total + jnp.sum(jnp.sum(out_sum * out_sum, axis=0, keepdims=True), axis=1, keepdims=True)
    cls_sum = cls_ref[...]
    shared = jnp.sum(jnp.sum(cls_sum * cls_sum, axis=0, keepdims=True), axis=1, keepdims=True)
    pp.three()
    flow.two(2)
    flow.hop(1, 2)
    flow.two(3)
    pp.four()
    flow.three(2)
    flow.three(3)
    pp.five()
    flow.hop(2, 1)
    flow.hop(3, 1)
    pp_sum = pp.total()
    pp_ref[...] = pp_sum
    shared += jnp.sum(jnp.sum(pp_sum * pp_sum, axis=0, keepdims=True), axis=1, keepdims=True)
    for i in range(groups):
        last(i)
    in_sum = in_ref[...]
    total = total + jnp.sum(jnp.sum(in_sum * in_sum, axis=0, keepdims=True), axis=1, keepdims=True)
    square_value[0] = jnp.broadcast_to(total + leader * shared, (8, 128))
    square.start_plane()
    square.turn_levels()
    square_out[...] = square.finish()
    pp_to_core.wait_send()
    for entry in (pp, small, square):
        entry.drain()
    for i in range(groups):
        in_to_core(i).wait_send()
        flow.drain(i)


def embed_back_sum_call(
    dq, dk, dv, h1, embedded, d_middle, pixels, coords, w_in, pp_cols, vectors,
    d_two, d_pool, d_gain, loss, share_mlp, share_cls, share_out, packs, collective_id,
):
    rows, width = h1.shape
    groups, share = w_in.shape[0], width // 8
    cols = w_in.shape[2]
    low = lambda *shape: pltpu.VMEM(shape, LOW)
    inside = pl.BlockSpec(memory_space=pltpu.VMEM)
    anywhere = pl.BlockSpec(memory_space=pl.ANY)
    loaded = (dq, dk, dv, h1, embedded, d_middle, pixels, w_in)
    return pl.pallas_call(
        functools.partial(embed_back_sum_kernel, packs=packs),
        in_specs=[anywhere] * 7 + [inside, anywhere] + [inside] * 8,
        out_specs=[inside] * 4,
        out_shape=[
            jax.ShapeDtypeStruct((share, cols), F32),
            jax.ShapeDtypeStruct((share, pp_cols), F32),
            jax.ShapeDtypeStruct((8, width), F32),
            jax.ShapeDtypeStruct((8, 128), F32),
        ],
        scratch_shapes=[pltpu.VMEM((rows,) + a.shape[1:] if a is pixels else a.shape, a.dtype) for a in loaded]
        + [pltpu.SemaphoreType.DMA((6, rows // 256)), pltpu.SemaphoreType.DMA((2,))]
        + [
            low(width, rows),
            low(width, rows),
            low(groups, rows, cols),
            low(pp_cols - pixels.shape[1], rows),
            low(groups, 2, 2, 2, share, cols),
            low(2, 2, 2, share, pp_cols),
        ]
        + flow_scratch(groups, share, cols)
        + whole_scratch(share, pp_cols)
        + tiny_scratch((8, width))
        + tiny_scratch((8, 128)),
        compiler_params=pltpu.CompilerParams(
            collective_id=collective_id, has_side_effects=True, vmem_limit_bytes=VMEM_BYTES
        ),
        name="embed_back_sum",
    )(
        dq, dk, dv, h1, embedded, d_middle, pixels, coords, w_in, vectors,
        d_two, d_pool, d_gain, loss, share_mlp, share_cls, share_out,
    )


def prepare_kernel(
    length_ref, patch_ref, pos_ref, in_ref, out_ref, up_ref, dn_ref, cls_ref, gain_ref,
    pp_low, in_low, out_low, up_low, dn_low, cls_low, bound_out, gain_out,
):
    packs, images = length_ref.shape
    pixels = patch_ref.shape[1]
    kinds, spots, share = pos_ref.shape
    pp_low[:, :pixels] = patch_ref[...].astype(LOW)
    pp_low[:, pixels:] = jnp.transpose(pos_ref[...].reshape(kinds * spots, share)).astype(LOW)
    in_low[...] = jnp.concatenate([in_ref[n] for n in range(in_ref.shape[0])], axis=1).astype(LOW)
    out_low[...] = jnp.transpose(out_ref[...]).astype(LOW)
    up_low[...] = up_ref[...].astype(LOW)
    dn_low[...] = dn_ref[...].astype(LOW)
    cls_low[...] = cls_ref[...].astype(LOW)
    gain_out[...] = jnp.concatenate([gain_ref[...], gain_ref[...]], axis=1)
    pack = jnp.minimum(lax.axis_index("tensor"), packs - 1)
    lane = lax.broadcasted_iota(jnp.int32, (1, 128), 1)
    slot = jnp.where(lane >= 64, lane - 64, lane)
    starts = jnp.full((1, 128), 1 << 30, jnp.int32)
    ends = starts
    place = jnp.int32(0)
    for n in range(images):
        after = place + length_ref[pack, n]
        starts = jnp.where(slot == n, place, starts)
        ends = jnp.where(slot == n, after, ends)
        place = after
    bound_out[0:1, :] = starts
    bound_out[1:2, :] = ends


def prepare_call(lengths, patch, pos, w_in, w_out, up, dn, cls, gains):
    share, width = up.shape
    low = lambda cols: jax.ShapeDtypeStruct((share, cols), LOW)
    inside = pl.BlockSpec(memory_space=pltpu.VMEM)
    return pl.pallas_call(
        prepare_kernel,
        in_specs=[pl.BlockSpec(memory_space=pltpu.SMEM)] + [inside] * 8,
        out_specs=[inside] * 8,
        out_shape=[
            low(patch.shape[1] + pos.shape[0] * pos.shape[1]),
            low(w_in.shape[0] * w_in.shape[2]),
            low(w_out.shape[0]),
            low(width),
            low(width),
            low(cls.shape[1]),
            jax.ShapeDtypeStruct((2, 128), jnp.int32),
            jax.ShapeDtypeStruct((2, 128), F32),
        ],
        compiler_params=pltpu.CompilerParams(vmem_limit_bytes=VMEM_BYTES),
        name="prepare",
    )(lengths, patch, pos, w_in, w_out, up, dn, cls, gains)


RATES = (RATE_BASE, RATE_POSITION, RATE_BASE, RATE_MIDDLE, RATE_BASE, RATE_BASE, RATE_MIDDLE, RATE_VECTOR, RATE_VECTOR)


def update_kernel(*refs):
    states, shares, outs = refs[:27], refs[27:34], refs[34:61]
    loss_ref, norm_ref = refs[61:]
    pp_ref, in_ref, out_ref, mlp_ref, cls_ref, small_ref, square_ref = shares
    pixels = states[0].shape[1]
    kinds, spots, share = states[3].shape
    part = states[6].shape[2]
    vectors = small_ref[0:4, :]
    row = small_ref[4:5, :]
    head = states[24].shape[1]
    gains = jnp.concatenate(
        [row[:, :head] + row[:, head : 2 * head], row[:, 2 * head : 3 * head] + row[:, 3 * head : 4 * head]],
        axis=0,
    )

    def square_sum(entry):
        return jnp.sum(jnp.sum(entry * entry, axis=0, keepdims=True), axis=1, keepdims=True)

    norm = jnp.sqrt(square_ref[0:1, 0:1] + square_sum(vectors) + square_sum(gains))
    clip = CLIP / jnp.maximum(norm, CLIP)
    grads = (
        pp_ref[:, :pixels],
        jnp.transpose(pp_ref[:, pixels:]).reshape(kinds, spots, share),
        None,
        jnp.transpose(out_ref[...]),
        mlp_ref[1],
        mlp_ref[0],
        cls_ref[...],
        vectors,
        gains,
    )
    for n, grad in enumerate(grads):
        decay = DECAY if n < 7 else 0.0
        if n == 2:
            for kind in range(states[6].shape[0]):
                results = adam(
                    *(state[kind] for state in states[6:9]),
                    in_ref[:, kind * part : (kind + 1) * part], clip, RATES[n], decay,
                )
                for result, out in zip(results, outs[6:9]):
                    out[kind] = result
        else:
            mine = clip.reshape(1, 1, 1) if grad.ndim == 3 else clip
            results = adam(*(state[...] for state in states[3 * n : 3 * n + 3]), grad, mine, RATES[n], decay)
            for result, out in zip(results, outs[3 * n : 3 * n + 3]):
                out[...] = result
    loss_ref[...] = small_ref[5:6, 0:1]
    norm_ref[...] = norm


def update_call(states, shares):
    inside = pl.BlockSpec(memory_space=pltpu.VMEM)
    scalar = jax.ShapeDtypeStruct((1, 1), F32)
    return pl.pallas_call(
        update_kernel,
        in_specs=[inside] * (len(states) + len(shares)),
        out_specs=[inside] * (len(states) + 2),
        out_shape=[jax.ShapeDtypeStruct(a.shape, F32) for a in states] + [scalar, scalar],
        compiler_params=pltpu.CompilerParams(vmem_limit_bytes=VMEM_BYTES),
        name="update",
    )(*states, *shares)


def adam(master, first_moment, second_moment, gradient, clip_scale, rate, decay_rate):
    gradient = gradient * clip_scale
    first_new = BETA_ONE * first_moment + (1 - BETA_ONE) * gradient
    second_new = BETA_TWO * second_moment + (1 - BETA_TWO) * gradient * gradient
    update = (
        first_new / (1 - BETA_ONE**STEP) / (jnp.sqrt(second_new / (1 - BETA_TWO**STEP)) + ADAM_EPS)
    )
    return (master - rate * (update + decay_rate * master), first_new, second_new)


def squared(entry):
    return jnp.sum(entry * entry)


def per_device(
    pixels, coords, lengths, labels,
    patch_table, patch_first, patch_second,
    position_table, position_first, position_second,
    attend_in, attend_in_first, attend_in_second,
    attend_out, attend_out_first, attend_out_second,
    expand, expand_first, expand_second,
    shrink, shrink_first, shrink_second,
    classify, classify_first, classify_second,
    vectors, vectors_first, vectors_second,
    head_gains, head_gains_first, head_gains_second,
):
    packs, images = lengths.shape
    members = lax.axis_size("tensor")
    width = vectors.shape[1]
    share = attend_in.shape[0]
    seat = lax.axis_index("tensor")
    pack = jnp.minimum(seat, packs - 1).astype(jnp.int32)[None]
    valid = (seat < packs).astype(F32).reshape(1, 1)
    image_count = images * packs * lax.axis_size("dp")
    if lax.axis_size("dp") == 8 and members == 4:
        turn = {0: lambda a: a.T, 2: lambda a: jnp.transpose(a, (1, 0, 2)), 5: lambda a: a.T}
        states = (
            patch_table, patch_first, patch_second, position_table, position_first, position_second,
            attend_in, attend_in_first, attend_in_second, attend_out, attend_out_first, attend_out_second,
            expand, expand_first, expand_second, shrink, shrink_first, shrink_second,
            classify, classify_first, classify_second, vectors, vectors_first, vectors_second,
            head_gains, head_gains_first, head_gains_second,
        )
        states = [turn.get(n // 3, lambda a: a)(entry) for n, entry in enumerate(states)]
        ready = prepare_call(lengths, *states[0:21:3], head_gains)
        shares = pack_step(
            pack, valid, pixels, coords, lengths, labels, tuple(ready), vectors, head_gains, image_count, True
        )
        *results, loss_total, grad_norm = update_call(states, shares)
        results = [turn.get(n // 3, lambda a: a)(entry) for n, entry in enumerate(results)]
        return (*results, loss_total.reshape(()), grad_norm.reshape(()))
    shards = (
        jnp.concatenate(
            [patch_table.T, jnp.transpose(position_table, (2, 0, 1)).reshape(share, -1)], axis=1
        ).astype(LOW),
        attend_in.reshape(share, -1).astype(LOW),
        attend_out.T.astype(LOW),
        expand.astype(LOW),
        shrink.T.astype(LOW),
        classify.astype(LOW),
    )
    both = ("tensor", "dp")

    def gather(shard):
        return lax.all_gather(shard, both, axis=0, tiled=True).reshape(members, width, -1)

    weights = (
        lax.all_gather(shards[0], "dp", axis=0, tiled=True),
        gather(shards[1]),
        gather(shards[2]),
        gather(shards[3]),
        gather(shards[4]),
        lax.all_gather(shards[5], "dp", axis=0, tiled=True),
    )
    grads, grad_vectors, grad_gains, loss_local = pack_step(
        pack, valid, pixels, coords, lengths, labels, weights, vectors, head_gains, image_count
    )
    grad_vectors, grad_gains, loss_total = lax.psum((grad_vectors, grad_gains, loss_local), both)

    def scatter(grad):
        return lax.psum_scatter(
            grad.reshape(members * width, -1), both, scatter_dimension=0, tiled=True
        ).astype(F32)

    def scatter_whole(grad):
        part = lax.psum_scatter(grad, "dp", scatter_dimension=0, tiled=True)
        return lax.psum(part, "tensor").astype(F32)

    share_pp = scatter_whole(grads[0])
    share_in, share_out, share_up, share_dn = (scatter(entry) for entry in grads[1:5])
    share_cls = scatter_whole(grads[5])
    leader = (seat == 0).astype(F32)
    split_squares = squared(share_in) + squared(share_out) + squared(share_up) + squared(share_dn)
    squares = lax.psum(split_squares + leader * (squared(share_pp) + squared(share_cls)), both)
    grad_norm = jnp.sqrt(squares + squared(grad_vectors) + squared(grad_gains))
    clip_scale = CLIP / jnp.maximum(grad_norm, CLIP)
    pixel_width = patch_table.shape[0]
    share_patch = share_pp[:, :pixel_width].T
    share_pos = jnp.transpose(
        share_pp[:, pixel_width:].reshape(share, position_table.shape[0], position_table.shape[1]), (1, 2, 0)
    )
    results = (
        adam(patch_table, patch_first, patch_second, share_patch, clip_scale, RATE_BASE, DECAY),
        adam(position_table, position_first, position_second, share_pos, clip_scale, RATE_POSITION, DECAY),
        adam(
            attend_in, attend_in_first, attend_in_second,
            share_in.reshape(attend_in.shape), clip_scale, RATE_BASE, DECAY,
        ),
        adam(attend_out, attend_out_first, attend_out_second, share_out.T, clip_scale, RATE_MIDDLE, DECAY),
        adam(expand, expand_first, expand_second, share_up, clip_scale, RATE_BASE, DECAY),
        adam(shrink, shrink_first, shrink_second, share_dn.T, clip_scale, RATE_BASE, DECAY),
        adam(classify, classify_first, classify_second, share_cls, clip_scale, RATE_MIDDLE, DECAY),
        adam(vectors, vectors_first, vectors_second, grad_vectors, clip_scale, RATE_VECTOR, 0.0),
        adam(head_gains, head_gains_first, head_gains_second, grad_gains, clip_scale, RATE_VECTOR, 0.0),
    )
    return tuple(entry for group in results for entry in group) + (loss_total, grad_norm)


def solution(mesh):
    data = P("dp", None)
    in_specs = (
        (data, P(None, "dp"), data, data)
        + (P(None, "dp"),) * 3
        + (P(None, None, "dp"),) * 3
        + (P("dp", None, "tensor"),) * 3
        + (P("tensor", "dp"),) * 3
        + (P("dp", "tensor"),) * 3
        + (P("tensor", "dp"),) * 3
        + (data,) * 3
        + (P(),) * 6
    )
    out_specs = in_specs[4:] + (P(), P())
    return jax.shard_map(per_device, mesh=mesh, in_specs=in_specs, out_specs=out_specs, check_vma=False)
```

```python
import functools

import jax
import jax.numpy as jnp
from jax import lax
from jax.experimental import pallas as pl
from jax.experimental.pallas import tpu as pltpu
from jax.sharding import PartitionSpec as P

STEP = 10
NORM_EPS = 1e-06
CLIP = 0.05
RATE_BASE = 0.03
RATE_POSITION = 0.2
RATE_MIDDLE = 0.1
RATE_VECTOR = 1.0
DECAY = 0.05
BETA_ONE = 0.5
BETA_TWO = 0.5
ADAM_EPS = 1e-08
SHIFT = -4.0
NEGATIVE = -1e30
APART = 128.0
LOW = jnp.bfloat16
F32 = jnp.float32
VMEM_BYTES = 60 * 1024 * 1024
TAIL_P = 0.3
TAIL = (
    0.1196293,
    0.12075397,
    0.09991341,
    0.12856192,
    -0.05368424,
    0.20635419,
    -0.1572035,
    0.03567488,
)


def mm(left, right):
    return lax.dot_general(left, right, (((1,), (0,)), ((), ())), preferred_element_type=F32)


def mm_nt(left, right):
    return lax.dot_general(left, right, (((1,), (1,)), ((), ())), preferred_element_type=F32)


def split_two(values):
    high = values.astype(LOW)
    return high, (values - high.astype(F32)).astype(LOW)


def split_three(values):
    high = values.astype(LOW)
    rest = values - high.astype(F32)
    middle = rest.astype(LOW)
    return high, middle, (rest - middle.astype(F32)).astype(LOW)


def row_norm(values):
    center = values - jnp.mean(values, axis=-1, keepdims=True)
    inverse = lax.rsqrt(jnp.mean(center * center, axis=-1, keepdims=True) + NORM_EPS)
    return center * inverse, inverse


def row_norm_back(gradient, gain_row, normed, inverse):
    scaled = gradient * gain_row
    return inverse * (
        scaled
        - jnp.mean(scaled, axis=-1, keepdims=True)
        - normed * jnp.mean(scaled * normed, axis=-1, keepdims=True)
    )


def half_mean_matrix(scale):
    row = lax.broadcasted_iota(jnp.int32, (128, 128), 0)
    col = lax.broadcasted_iota(jnp.int32, (128, 128), 1)
    return jnp.where((row >= 64) == (col >= 64), scale, 0.0).astype(LOW)


def half_sum(values, block):
    high, low = split_two(values)
    return mm(high, block) + mm(low, block)


def half_norm(values, block):
    center = values - half_sum(values, block)
    inverse = lax.rsqrt(half_sum(center * center, block) + NORM_EPS)
    return center * inverse, inverse


def half_norm_back(gradient, gain_row, normed, inverse, block):
    scaled = gradient * gain_row
    return inverse * (scaled - half_sum(scaled, block) - normed * half_sum(scaled * normed, block))


def gelu_pair(inner):
    size = jnp.abs(inner)
    near = 1.0 / (1.0 + TAIL_P * size)
    bell = jnp.exp(-0.5 * inner * inner)
    poly = TAIL[-1]
    for factor in TAIL[-2::-1]:
        poly = poly * near + factor
    tail = poly * near * bell
    share = jnp.where(inner >= 0, 1.0 - tail, tail)
    return inner * share, share + inner * bell * 0.3989422804014327


def embed_kernel(pack_ref, pix_ref, coord_ref, wp_ref, win_ref, gain_ref, emb_ref, h1_ref, q_ref, k_ref, v_ref):
    rows = pix_ref.shape[0]
    pixels = pix_ref.shape[1]
    groups = win_ref.shape[0]
    part = win_ref.shape[2] // 3
    spots = (wp_ref.shape[1] - pixels) // 2
    lane = lax.broadcasted_iota(jnp.int32, (rows, 2 * spots), 1)
    hot = ((lane == coord_ref[:, 0:1]) | (lane - spots == coord_ref[:, 1:2])).astype(F32).astype(LOW)
    embedded = mm_nt(pix_ref[...], wp_ref[:, :pixels]) + mm_nt(hot, wp_ref[:, pixels:])
    emb_ref[...] = embedded
    normed, _ = row_norm(embedded)
    first = (normed * gain_ref[0:1]).astype(LOW)
    h1_ref[...] = first
    parts = [mm(first, win_ref[group]) for group in range(groups)]
    q_ref[...] = jnp.concatenate([entry[:, :part] for entry in parts], axis=1)
    k_ref[...] = jnp.concatenate([entry[:, part : 2 * part] for entry in parts], axis=1)
    v_ref[...] = jnp.concatenate([entry[:, 2 * part :].astype(LOW) for entry in parts], axis=1)


def embed_call(pack, pixels, coords, w_pp, w_in, vectors, rows):
    width = vectors.shape[1]
    tile = 256
    steps = rows // tile
    whole2 = lambda i, p: (0, 0)
    tiled = pl.BlockSpec((tile, width), lambda i, p: (i, 0))
    return pl.pallas_call(
        embed_kernel,
        grid_spec=pltpu.PrefetchScalarGridSpec(
            num_scalar_prefetch=1,
            grid=(steps,),
            in_specs=[
                pl.BlockSpec((tile, pixels.shape[1]), lambda i, p: (p[0] * steps + i, 0)),
                pl.BlockSpec((tile, 2), lambda i, p: (p[0] * steps + i, 0)),
                pl.BlockSpec(w_pp.shape, whole2),
                pl.BlockSpec(w_in.shape, lambda i, p: (0, 0, 0)),
                pl.BlockSpec(vectors.shape, whole2),
            ],
            out_specs=[tiled] * 5,
        ),
        out_shape=[
            jax.ShapeDtypeStruct((rows, width), F32),
            jax.ShapeDtypeStruct((rows, width), LOW),
            jax.ShapeDtypeStruct((rows, width), F32),
            jax.ShapeDtypeStruct((rows, width), F32),
            jax.ShapeDtypeStruct((rows, width), LOW),
        ],
        compiler_params=pltpu.CompilerParams(vmem_limit_bytes=VMEM_BYTES),
        name="embed",
    )(pack, pixels, coords, w_pp, w_in, vectors)


def image_marks(bound_ref, rows):
    place = lax.broadcasted_iota(jnp.int32, (rows, 128), 0)
    return (place >= bound_ref[0:1, :]) & (place < bound_ref[1:2, :])


def half_lane(rows):
    lane = lax.broadcasted_iota(jnp.int32, (rows, 128), 1)
    return lane, jnp.where(lane >= 64, lane - 64, lane)


def attend_kernel(
    q_ref, k_ref, v_ref, gain_ref, bound_ref, o_ref, lse_ref, ka_ref, va_ref, qa_ref, between=None
):
    rows = q_ref.shape[0]
    tile = 256
    block = half_mean_matrix(1.0 / 64)
    lane = lax.broadcasted_iota(jnp.int32, (rows, 128), 1)

    @pl.when(pl.program_id(0) == 0)
    def _():
        _, inner = half_lane(rows)
        marks = image_marks(bound_ref, rows)
        one = jnp.where(inner == 8, 1.0, 0.0)
        query_feature = jnp.where(marks, 1.0, one)
        ka_ref[:, 128:] = jnp.where(marks, APART, -APART * one).astype(LOW)
        va_ref[:, 128:] = jnp.ones((rows, 128), LOW)
        qa_ref[0, :, 128:] = jnp.where(lane < 64, query_feature, 0.0).astype(LOW)
        qa_ref[1, :, 128:] = jnp.where(lane >= 64, query_feature, 0.0).astype(LOW)

    k_normed, _ = half_norm(k_ref[...], block)
    ka_ref[:, :128] = (k_normed * gain_ref[1:2]).astype(LOW)
    va_ref[:, :128] = v_ref[...]
    q_normed, _ = half_norm(q_ref[...], block)
    query = (q_normed * gain_ref[0:1]).astype(LOW).astype(F32) * 0.125
    for head in range(2):
        mine = (lane < 64) if head == 0 else (lane >= 64)
        qa_ref[head, :, :128] = jnp.where(mine, query, 0.0).astype(LOW)
    keys = ka_ref[...]
    values = va_ref[...]
    first = lane[:tile] < 64
    for step in range(rows // tile):
        part = slice(step * tile, (step + 1) * tile)
        outs = []
        for head in range(2):
            score = mm_nt(qa_ref[head, part, :], keys)
            outs.append(mm(jnp.exp(score).astype(LOW), values))
        total = jnp.where(first, outs[0][:, 128:], outs[1][:, 128:])
        o_ref[part, :] = (jnp.where(first, outs[0][:, :128], outs[1][:, :128]) / total).astype(LOW)
        lse_ref[part, :] = jnp.log(total)
        if between is not None and step % 2 == 1:
            between(step // 2)


def attend_call(q_raw, k_raw, value, gains, bounds):
    rows, width = q_raw.shape
    pair = pl.BlockSpec((rows, 128), lambda j: (0, j))
    small = lambda a: pl.BlockSpec(a.shape, lambda j: (0, 0))
    return pl.pallas_call(
        attend_kernel,
        grid=(width // 128,),
        in_specs=[pair, pair, pair, small(gains), small(bounds)],
        out_specs=[pair, pair],
        out_shape=[
            jax.ShapeDtypeStruct((rows, width), LOW),
            jax.ShapeDtypeStruct((rows, width), F32),
        ],
        scratch_shapes=[
            pltpu.VMEM((rows, 256), LOW),
            pltpu.VMEM((rows, 256), LOW),
            pltpu.VMEM((2, rows, 256), LOW),
        ],
        compiler_params=pltpu.CompilerParams(vmem_limit_bytes=VMEM_BYTES),
        name="attend",
    )(q_raw, k_raw, value, gains, bounds)


def attend_back_kernel(
    q_ref, k_ref, v_ref, o_ref, lse_ref, do_ref, gain_ref, bound_ref,
    dq_ref, dk_ref, dv_ref, dgain_ref,
    ka_ref, va_ref, qa_ref, da_ref, qt_ref, dot_ref, dqs_ref, dkt_ref, dvt_ref,
    between=None,
):
    rows = q_ref.shape[0]
    tile = 256
    block = half_mean_matrix(1.0 / 64)
    block_sum = half_mean_matrix(1.0)
    lane, inner = half_lane(rows)
    marks = image_marks(bound_ref, rows)
    one = jnp.where(inner == 8, 1.0, 0.0)
    three = (inner >= 9) & (inner < 12)
    key_feature = jnp.where(marks, APART, jnp.where(three, 1.0, -APART * one))

    def spread(values):
        high, middle, low = split_three(values)
        return jnp.where(
            inner == 9, high.astype(F32), jnp.where(inner == 10, middle.astype(F32), low.astype(F32))
        )

    query_feature = jnp.where(three, spread(-lse_ref[...]), jnp.where(marks, 1.0, one))
    k_normed, k_inverse = half_norm(k_ref[...], block)
    ka_ref[:, :128] = (k_normed * gain_ref[1:2]).astype(LOW)
    ka_ref[:, 128:] = key_feature.astype(LOW)
    va_ref[:, :128] = v_ref[...]
    va_ref[:, 128:] = jnp.where(three, 1.0, 0.0).astype(LOW)
    q_normed, q_inverse = half_norm(q_ref[...], block)
    query = (q_normed * gain_ref[0:1]).astype(LOW).astype(F32)
    qt_ref[...] = jnp.transpose(query).astype(LOW)
    query = query * 0.125
    above = do_ref[...].astype(F32)
    dot_ref[...] = jnp.transpose(above).astype(LOW)
    inside = half_sum(above * o_ref[...].astype(F32), block_sum)
    above_feature = jnp.where(three, spread(inside * -0.125), 0.0)
    above = above * 0.125
    for head in range(2):
        mine = (lane < 64) if head == 0 else (lane >= 64)
        qa_ref[head, :, :128] = jnp.where(mine, query, 0.0).astype(LOW)
        qa_ref[head, :, 128:] = jnp.where(mine, query_feature, 0.0).astype(LOW)
        da_ref[head, :, :128] = jnp.where(mine, above, 0.0).astype(LOW)
        da_ref[head, :, 128:] = jnp.where(mine, above_feature, 0.0).astype(LOW)
    keys = ka_ref[...]
    values = va_ref[...]
    key_low = ka_ref[:, :128]
    first = lane[:tile] < 64
    for step in range(rows // tile):
        part = slice(step * tile, (step + 1) * tile)
        outs = []
        for head in range(2):
            mine = slice(64 * head, 64 * head + 64)
            prob = jnp.exp(mm_nt(qa_ref[head, part, :], keys))
            d_prob = mm_nt(da_ref[head, part, :], values)
            d_score = (prob * d_prob).astype(LOW)
            outs.append(mm(d_score, key_low))
            d_key = mm(qt_ref[mine, part], d_score)
            d_value = mm(dot_ref[mine, part], prob.astype(LOW))
            if step == 0:
                dkt_ref[mine, :] = d_key
                dvt_ref[mine, :] = d_value
            else:
                dkt_ref[mine, :] += d_key
                dvt_ref[mine, :] += d_value
        dqs_ref[part, :] = jnp.where(first, outs[0], outs[1])
        if between is not None and step % 2 == 1:
            between(step // 2)
    d_query = dqs_ref[...]
    d_key = jnp.transpose(dkt_ref[...])
    dv_ref[...] = jnp.transpose(dvt_ref[...]).astype(LOW)
    dq_ref[...] = half_norm_back(d_query, gain_ref[0:1], q_normed, q_inverse, block).astype(LOW)
    dk_ref[...] = half_norm_back(d_key, gain_ref[1:2], k_normed, k_inverse, block).astype(LOW)
    dgain_ref[0, 0:1] = jnp.sum(d_query * q_normed, axis=0, keepdims=True)
    dgain_ref[0, 1:2] = jnp.sum(d_key * k_normed, axis=0, keepdims=True)


ATTEND_BACK_SCRATCH = 9


def attend_back_scratch(rows):
    return [
        pltpu.VMEM((rows, 256), LOW),
        pltpu.VMEM((rows, 256), LOW),
        pltpu.VMEM((2, rows, 256), LOW),
        pltpu.VMEM((2, rows, 256), LOW),
        pltpu.VMEM((128, rows), LOW),
        pltpu.VMEM((128, rows), LOW),
        pltpu.VMEM((rows, 128), F32),
        pltpu.VMEM((128, rows), F32),
        pltpu.VMEM((128, rows), F32),
    ]


def attend_back_sum_kernel(*refs):
    inputs, grads, dout_ref, before_ref = refs[:8], refs[8], refs[9], refs[10]
    outputs, share_ref, out_ref = refs[11:15], refs[15], refs[16]
    scratch, rest = refs[17 : 17 + ATTEND_BACK_SCRATCH], refs[17 + ATTEND_BACK_SCRATCH :]
    mlp_own, mlp_load, mlp_refs = rest[0], rest[1], rest[2:9]
    out_own, out_load, out_refs = rest[9], rest[10], rest[11:18]
    step = pl.program_id(0)
    seat = Seat()
    c = seat.c
    mlp = Flow(
        seat, lambda i: lax.rem(4 - lax.div(i, 2), 4), lambda i: mlp_own.at[i], *mlp_refs[:5], mlp_refs[5:]
    )
    out = Flow(seat, lambda i: i, lambda i: out_own.at[i], *out_refs[:5], out_refs[5:])
    chunks, levels = mlp_own.shape[0], out_own.shape[0]

    def mlp_at(i):
        return lax.rem(i, 2) * 3 + lax.div(i, 2)

    def mlp_loading(i):
        return pltpu.make_async_copy(grads.at[mlp_at(i), :, :, c], mlp_own.at[i], mlp_load.at[i])

    def mlp_to_core(i):
        return mlp.to_core(i, grads.at[mlp_at(i), :, :, 1 - c])

    def out_loading(i):
        return pltpu.make_async_copy(dout_ref.at[i, :, :, c], out_own.at[i], out_load.at[i])

    def out_to_core(i):
        return out.to_core(i, dout_ref.at[i, :, :, 1 - c])

    def every(count, action):
        lax.fori_loop(0, count, lambda i, carry: (action(i), carry)[1], 0)

    @pl.when(step == 0)
    def _():
        every(chunks, lambda i: mlp_loading(i).start())
        every(levels, lambda i: out_loading(i).start())
        greet(seat, 4)
        every(chunks, lambda i: mlp_to_core(i).start())
        every(levels, lambda i: out_to_core(i).start())
        share_ref[...] = before_ref[...]

    def mlp_one(i):
        mlp_loading(i).wait()
        mlp_to_core(i).wait_recv()
        mlp.one(i)

    def mlp_last(i):
        @pl.when(mlp.level_of(i) == seat.z)
        def _():
            share_ref[lax.rem(i, 2)] = mlp.total(i)

    def out_one(i):
        out_loading(i).wait()
        out_to_core(i).wait_recv()
        out.one(i)

    def out_last(i):
        @pl.when(out.level_of(i) == seat.z)
        def _():
            out_ref[...] = out.total(i)

    def pair(action, number):
        return lambda: every(2, lambda i: action(2 * number + i))

    hop_one, hop_two = (functools.partial(mlp.hop, reach=reach) for reach in (1, 2))
    out_hop_one, out_hop_two = (functools.partial(out.hop, reach=reach) for reach in (1, 2))
    plan = {
        0: [pair(mlp_one, 0)],
        1: [lambda: every(levels, out_one)],
        2: [pair(mlp.two, 0), pair(mlp_one, 1)],
        3: [lambda: every(levels, out.two)],
        4: [pair(mlp.three, 0)],
        5: [pair(mlp.two, 1), pair(mlp_one, 2)],
        6: [pair(hop_one, 0), lambda: every(levels, out.three)],
        7: [pair(mlp.three, 1), lambda: every(levels, out_hop_one)],
        8: [pair(mlp.two, 2), pair(hop_two, 0)],
        9: [pair(hop_one, 1), lambda: every(levels, out_hop_two)],
        10: [pair(mlp.three, 2)],
        11: [pair(hop_two, 1), pair(hop_one, 2)],
    }

    def between(slot):
        for number, actions in plan.items():
            if number % 2 == slot:

                @pl.when(2 * step + slot == number)
                def _():
                    for action in actions:
                        action()

    attend_back_kernel(*inputs, *outputs, *scratch, between=between)

    @pl.when(step == pl.num_programs(0) - 1)
    def _():
        every(chunks, mlp_last)
        every(levels, out_last)

        def drain(i):
            mlp_to_core(i).wait_send()
            mlp.drain(i)

        def out_drain(i):
            out_to_core(i).wait_send()
            out.drain(i)

        every(chunks, drain)
        every(levels, out_drain)


def attend_back_sum_call(
    q_raw, k_raw, value, attended, lse, d_attended, gains, bounds, grads, d_out, before, collective_id
):
    rows, width = q_raw.shape
    pairs = width // 128
    share, cols = grads.shape[-2:]
    pair = pl.BlockSpec((rows, 128), lambda j: (0, j))
    small = lambda a: pl.BlockSpec(a.shape, lambda j: (0,) * a.ndim)
    anywhere = pl.BlockSpec(memory_space=pl.ANY)
    low = jax.ShapeDtypeStruct((rows, width), LOW)

    def scratch(chunks, cols):
        own = [pltpu.VMEM((chunks, 2, 2, share, cols), LOW), pltpu.SemaphoreType.DMA((chunks,))]
        return own + flow_scratch(chunks, share, cols)

    return pl.pallas_call(
        attend_back_sum_kernel,
        grid=(pairs,),
        in_specs=[pair] * 6 + [small(gains), small(bounds), anywhere, anywhere, small(before)],
        out_specs=[
            pair, pair, pair,
            pl.BlockSpec((1, 2, 128), lambda j: (j, 0, 0)),
            small(before),
            pl.BlockSpec((share, d_out.shape[-1]), lambda j: (0, 0)),
        ],
        out_shape=[
            low, low, low,
            jax.ShapeDtypeStruct((pairs, 2, 128), F32),
            jax.ShapeDtypeStruct(before.shape, F32),
            jax.ShapeDtypeStruct((share, d_out.shape[-1]), F32),
        ],
        scratch_shapes=attend_back_scratch(rows)
        + scratch(grads.shape[0], cols)
        + scratch(d_out.shape[0], d_out.shape[-1]),
        compiler_params=pltpu.CompilerParams(
            collective_id=collective_id, has_side_effects=True, vmem_limit_bytes=VMEM_BYTES
        ),
        name="attend_back_sum",
    )(q_raw, k_raw, value, attended, lse, d_attended, gains, bounds, grads, d_out, before)


def attend_back_call(q_raw, k_raw, value, attended, lse, d_attended, gains, bounds):
    rows, width = q_raw.shape
    pairs = width // 128
    pair = pl.BlockSpec((rows, 128), lambda j: (0, j))
    small = lambda a: pl.BlockSpec(a.shape, lambda j: (0, 0))
    low = jax.ShapeDtypeStruct((rows, width), LOW)
    return pl.pallas_call(
        attend_back_kernel,
        grid=(pairs,),
        in_specs=[pair] * 6 + [small(gains), small(bounds)],
        out_specs=[pair, pair, pair, pl.BlockSpec((1, 2, 128), lambda j: (j, 0, 0))],
        out_shape=[low, low, low, jax.ShapeDtypeStruct((pairs, 2, 128), F32)],
        scratch_shapes=attend_back_scratch(rows),
        compiler_params=pltpu.CompilerParams(vmem_limit_bytes=VMEM_BYTES),
        name="attend_back",
    )(q_raw, k_raw, value, attended, lse, d_attended, gains, bounds)


def mlp_kernel(o_ref, emb_ref, wout_ref, wup_ref, wdn_ref, vec_ref, x1_ref, h2_ref, act_ref, slope_ref, x2_ref):
    step = pl.program_id(0)
    rows, _ = o_ref.shape
    groups, _, part = wout_ref.shape
    tile = 256

    @pl.when(step == 0)
    def _():
        for at in range(rows // tile):
            span = slice(at * tile, (at + 1) * tile)
            branch = mm_nt(o_ref[span, :part], wout_ref[0])
            for group in range(1, groups):
                branch += mm_nt(o_ref[span, group * part : (group + 1) * part], wout_ref[group])
            middle = emb_ref[span, :] + branch
            x1_ref[span, :] = middle
            x2_ref[span, :] = middle
            normed, _ = row_norm(middle)
            h2_ref[span, :] = (normed * vec_ref[1:2]).astype(LOW)

    tile = 256
    spans = [slice(at * tile, (at + 1) * tile) for at in range(rows // tile)]
    hidden = mm(h2_ref[spans[0], :], wup_ref[0])
    for at, span in enumerate(spans):
        now = hidden
        if at + 1 < len(spans):
            hidden = mm(h2_ref[spans[at + 1], :], wup_ref[0])
        active, slope = gelu_pair(now)
        active = active.astype(LOW)
        act_ref[span, :] = active
        slope_ref[span, :] = slope.astype(LOW)
        x2_ref[span, :] += mm_nt(active, wdn_ref[0])


def mlp_call(attended, embedded, w_out, w_up, w_dn, vectors):
    rows, width = embedded.shape
    groups, _, per = w_up.shape
    chunk = per
    hidden = groups * per
    whole = lambda a: pl.BlockSpec(a.shape, lambda j: (0,) * a.ndim)
    weight = pl.BlockSpec((1, width, chunk), lambda j: (j, 0, 0))
    full = pl.BlockSpec((rows, width), lambda j: (0, 0))
    piece = pl.BlockSpec((rows, chunk), lambda j: (0, j))
    return pl.pallas_call(
        mlp_kernel,
        grid=(hidden // chunk,),
        in_specs=[whole(attended), whole(embedded), whole(w_out), weight, weight, whole(vectors)],
        out_specs=[full, full, piece, piece, full],
        out_shape=[
            jax.ShapeDtypeStruct((rows, width), F32),
            jax.ShapeDtypeStruct((rows, width), LOW),
            jax.ShapeDtypeStruct((rows, hidden), LOW),
            jax.ShapeDtypeStruct((rows, hidden), LOW),
            jax.ShapeDtypeStruct((rows, width), F32),
        ],
        compiler_params=pltpu.CompilerParams(vmem_limit_bytes=VMEM_BYTES),
        name="mlp",
    )(attended, embedded, w_out, w_up, w_dn, vectors)


def pool_kernel(
    pack_ref, x2_ref, label_ref, wcls_ref, vec_ref, bound_ref, valid_ref,
    dx2_ref, dcls_ref, loss_ref, dvec_ref,
    norm_ref, inv_ref,
    *, images, image_count,
):
    rows, width = x2_ref.shape
    tile = 256
    root = width**0.5
    gain = vec_ref[2:3]
    query = vec_ref[3:4]
    lane = lax.broadcasted_iota(jnp.int32, (rows, 128), 1)
    marks = image_marks(bound_ref, rows) & (lane < 64)
    logits = []
    for at in range(rows // tile):
        span = slice(at * tile, (at + 1) * tile)
        normed, inverse = row_norm(x2_ref[span, :])
        norm_ref[span, :] = normed
        inv_ref[span, :] = jnp.broadcast_to(inverse, (tile, 128))
        logits.append(jnp.sum(normed * gain * query, axis=-1, keepdims=True) / root)
    logit = jnp.concatenate(logits, axis=0)
    masked = jnp.where(marks, logit, NEGATIVE)
    grown = jnp.exp(masked - jnp.max(masked, axis=0, keepdims=True))
    shares = jnp.where(marks, grown / jnp.sum(grown, axis=0, keepdims=True), 0.0)
    weight = jnp.sum(shares, axis=-1, keepdims=True)
    member = jnp.transpose(marks.astype(F32))[:16].astype(LOW)
    pooled = jnp.zeros((16, width), F32)
    for at in range(rows // tile):
        span = slice(at * tile, (at + 1) * tile)
        for entry in split_two(norm_ref[span, :] * gain * weight[span]):
            pooled += mm(member[:, span], entry)
    pooled_low = pooled.astype(LOW)
    scores = mm(pooled_low, wcls_ref[...])[:images] + SHIFT
    target = label_ref[...].astype(F32)
    valid = valid_ref[0, 0]
    soft = jnp.maximum(scores, 0.0) + jnp.log1p(jnp.exp(-jnp.abs(scores)))
    loss_rows = jnp.sum(soft - target * scores, axis=-1, keepdims=True)
    loss_ref[...] = jnp.broadcast_to(jnp.sum(loss_rows, axis=0, keepdims=True) * valid, loss_ref.shape)
    d_score = (1.0 / (1.0 + jnp.exp(-scores)) - target) / image_count * valid
    d_score = jnp.concatenate([d_score, jnp.zeros((16 - images, d_score.shape[1]), F32)], axis=0).astype(LOW)
    dcls_ref[...] = mm(jnp.transpose(pooled).astype(LOW), d_score).astype(LOW)
    d_pooled = mm_nt(d_score, wcls_ref[...])[:images]
    parts = jnp.concatenate(
        [entry.astype(F32) for entry in split_three(d_pooled)]
        + [jnp.zeros((128 - 3 * images, width), F32)],
        axis=0,
    ).astype(LOW)
    marks_f = marks.astype(F32)
    thrice = (
        marks_f + pltpu.roll(marks_f, images, 1) + pltpu.roll(marks_f, 2 * images, 1)
    ).astype(LOW)
    d_weights = []
    for at in range(rows // tile):
        span = slice(at * tile, (at + 1) * tile)
        spread = mm(thrice[span], parts)
        dx2_ref[span, :] = spread
        d_weights.append(jnp.sum(spread * (norm_ref[span, :] * gain), axis=-1, keepdims=True))
    d_weight = jnp.concatenate(d_weights, axis=0)
    inside = jnp.sum(shares * d_weight, axis=0, keepdims=True)
    d_logit = weight * (d_weight - jnp.sum(marks_f * inside, axis=-1, keepdims=True))
    gain_sum = jnp.zeros((1, width), F32)
    query_sum = jnp.zeros((1, width), F32)
    for at in range(rows // tile):
        span = slice(at * tile, (at + 1) * tile)
        normed = norm_ref[span, :]
        inverse = inv_ref[span, 0:1]
        d_last = dx2_ref[span, :] * weight[span] + d_logit[span] * (query / root)
        gain_sum += jnp.sum(d_last * normed, axis=0, keepdims=True)
        query_sum += jnp.sum(d_logit[span] * normed, axis=0, keepdims=True)
        dx2_ref[span, :] = row_norm_back(d_last, gain, normed, inverse)
    dvec_ref[0:1, :] = gain_sum
    dvec_ref[1:2, :] = query_sum * gain / root


def pool_call(pack, x2, labels, w_cls, vectors, bounds, valid, images, image_count):
    rows, width = x2.shape
    classes = labels.shape[1]
    whole = lambda a: pl.BlockSpec(a.shape, lambda j, p: (0,) * a.ndim)
    full = lambda *shape: pl.BlockSpec(shape, lambda j, p: (0,) * len(shape))
    return pl.pallas_call(
        functools.partial(pool_kernel, images=images, image_count=image_count),
        grid_spec=pltpu.PrefetchScalarGridSpec(
            num_scalar_prefetch=1,
            grid=(1,),
            in_specs=[
                whole(x2),
                pl.BlockSpec((images, classes), lambda j, p: (p[0], 0)),
                whole(w_cls),
                whole(vectors),
                whole(bounds),
                pl.BlockSpec(memory_space=pltpu.SMEM),
            ],
            out_specs=[full(rows, width), full(width, classes), full(8, 128), full(2, width)],
            scratch_shapes=[pltpu.VMEM((rows, width), F32), pltpu.VMEM((rows, 128), F32)],
        ),
        out_shape=[
            jax.ShapeDtypeStruct((rows, width), F32),
            jax.ShapeDtypeStruct((width, classes), LOW),
            jax.ShapeDtypeStruct((8, 128), F32),
            jax.ShapeDtypeStruct((2, width), F32),
        ],
        compiler_params=pltpu.CompilerParams(vmem_limit_bytes=VMEM_BYTES),
        name="pool",
    )(pack, x2, labels, w_cls, vectors, bounds, valid)


def mlp_back_kernel(
    dx2_ref, act_ref, slope_ref, h2_ref, x1_ref, o_ref, wout_ref, wup_ref, wdn_ref, vec_ref,
    dmlp_ref, dout_ref, do_ref, dmid_ref, dvec_ref,
    low_ref, lowt_ref, h2t_ref, acc_ref, dh_ref,
    keep=None, between=None,
):
    step = pl.program_id(0)
    rows, width = dx2_ref.shape
    groups, _, part = wout_ref.shape
    tile = 256

    @pl.when(step == 0)
    def _():
        for at in range(rows // tile):
            span = slice(at * tile, (at + 1) * tile)
            values = dx2_ref[span, :]
            low_ref[span, :] = values.astype(LOW)
            lowt_ref[:, span] = jnp.transpose(values).astype(LOW)
            h2t_ref[:, span] = jnp.transpose(h2_ref[span, :].astype(F32)).astype(LOW)
            acc_ref[span, :] = jnp.zeros((tile, width), F32)

    wide = 512
    for at in range(rows // wide):
        span = slice(at * wide, (at + 1) * wide)
        d_hidden = (mm(low_ref[span, :], wdn_ref[0]) * slope_ref[span, :].astype(F32)).astype(LOW)
        dh_ref[span, :] = d_hidden
        acc_ref[span, :] += mm_nt(d_hidden, wup_ref[0])

    def grads(put):
        for at in range(width // 192):
            span = slice(at * 192, (at + 1) * 192)
            put(0, at, mm(lowt_ref[span, :], act_ref[...]).astype(LOW))
            put(1, at, mm(h2t_ref[span, :], dh_ref[...]).astype(LOW))

    def put_out(kind, at, value):
        dmlp_ref[kind, 0, at * 192 : (at + 1) * 192, :] = value

    if keep is None:
        grads(put_out)
    else:
        between(2 * step, 0)
        pl.when(step < 1)(lambda: grads(keep))
        pl.when(step >= 1)(lambda: grads(put_out))
        between(2 * step + 1, 1)

    @pl.when(step == pl.num_programs(0) - 1)
    def _():
        gain = vec_ref[1:2]
        gain_sum = jnp.zeros((1, width), F32)
        for at in range(rows // tile):
            span = slice(at * tile, (at + 1) * tile)
            normed, inverse = row_norm(x1_ref[span, :])
            d_second = acc_ref[span, :]
            gain_sum += jnp.sum(d_second * normed, axis=0, keepdims=True)
            d_middle = dx2_ref[span, :] + row_norm_back(d_second, gain, normed, inverse)
            dmid_ref[span, :] = d_middle
            low = d_middle.astype(LOW)
            lowt_ref[:, span] = jnp.transpose(d_middle).astype(LOW)
            do_ref[span, :] = jnp.concatenate(
                [mm(low, wout_ref[group]) for group in range(groups)], axis=1
            ).astype(LOW)
        dvec_ref[...] = gain_sum
        for group in range(groups):
            piece = o_ref[:, group * part : (group + 1) * part]
            for at in range(width // tile):
                span = slice(at * tile, (at + 1) * tile)
                dout_ref[group, span, :] = mm(lowt_ref[span, :], piece).astype(LOW)


def mlp_back_call(dx2, active, slope, h2, x1, attended, w_out, w_up, w_dn, vectors):
    rows, width = dx2.shape
    groups, _, per = w_up.shape
    chunk = per
    hidden = groups * per
    whole = lambda a: pl.BlockSpec(a.shape, lambda j: (0,) * a.ndim, pipeline_mode=pl.Buffered(1))
    weight = pl.BlockSpec((1, width, chunk), lambda j: (j, 0, 0))
    piece = pl.BlockSpec((rows, chunk), lambda j: (0, j))
    full = lambda *shape: pl.BlockSpec(shape, lambda j: (0,) * len(shape))
    return pl.pallas_call(
        mlp_back_kernel,
        grid=(hidden // chunk,),
        in_specs=[
            whole(dx2), piece, piece, whole(h2), whole(x1), whole(attended), whole(w_out),
            weight, weight, whole(vectors),
        ],
        out_specs=[
            pl.BlockSpec((2, 1, width, chunk), lambda j: (0, j, 0, 0)),
            full(*w_out.shape),
            full(rows, width),
            full(rows, width),
            full(1, width),
        ],
        out_shape=[
            jax.ShapeDtypeStruct((2,) + w_up.shape, LOW),
            jax.ShapeDtypeStruct(w_out.shape, LOW),
            jax.ShapeDtypeStruct((rows, width), LOW),
            jax.ShapeDtypeStruct((rows, width), F32),
            jax.ShapeDtypeStruct((1, width), F32),
        ],
        scratch_shapes=[
            pltpu.VMEM((rows, width), LOW),
            pltpu.VMEM((width, rows), LOW),
            pltpu.VMEM((width, rows), LOW),
            pltpu.VMEM((rows, width), F32),
            pltpu.VMEM((rows, chunk), LOW),
        ],
        compiler_params=pltpu.CompilerParams(vmem_limit_bytes=VMEM_BYTES),
        name="mlp_back",
    )(dx2, active, slope, h2, x1, attended, w_out, w_up, w_dn, vectors)


def embed_back_kernel(
    pack_ref, dq_ref, dk_ref, dv_ref, h1_ref, emb_ref, dmid_ref, pix_ref, coord_ref, win_ref, vec_ref,
    din_ref, dpp_ref, dvec_ref,
    h1t_ref, join_ref, acc_ref,
):
    step = pl.program_id(0)
    rows, width = h1_ref.shape
    groups = pl.num_programs(0)
    part = win_ref.shape[2] // 3
    tile = 256

    @pl.when(step == 0)
    def _():
        for at in range(rows // tile):
            span = slice(at * tile, (at + 1) * tile)
            h1t_ref[:, span] = jnp.transpose(h1_ref[span, :].astype(F32)).astype(LOW)
            acc_ref[span, :] = jnp.zeros((tile, width), F32)

    for group in range(width // part):

        @pl.when(step == group)
        def _():
            mine = slice(group * part, (group + 1) * part)
            join_ref[...] = jnp.concatenate([dq_ref[:, mine], dk_ref[:, mine], dv_ref[:, mine]], axis=1)

    for at in range(rows // tile):
        span = slice(at * tile, (at + 1) * tile)
        acc_ref[span, :] += mm_nt(join_ref[span, :], win_ref[0])
    for at in range(width // tile):
        span = slice(at * tile, (at + 1) * tile)
        din_ref[0, span, :] = mm(h1t_ref[span, :], join_ref[...]).astype(LOW)

    @pl.when(step == groups - 1)
    def _():
        gain = vec_ref[0:1]
        pixels = pix_ref.shape[1]
        spots = (dpp_ref.shape[1] - pixels) // 2
        gain_sum = jnp.zeros((1, width), F32)
        for at in range(rows // tile):
            span = slice(at * tile, (at + 1) * tile)
            normed, inverse = row_norm(emb_ref[span, :])
            d_first = acc_ref[span, :]
            gain_sum += jnp.sum(d_first * normed, axis=0, keepdims=True)
            d_embed = dmid_ref[span, :] + row_norm_back(d_first, gain, normed, inverse)
            h1t_ref[:, span] = jnp.transpose(d_embed).astype(LOW)
        dvec_ref[...] = gain_sum
        lane = lax.broadcasted_iota(jnp.int32, (rows, 2 * spots), 1)
        hot = ((lane == coord_ref[:, 0:1]) | (lane - spots == coord_ref[:, 1:2])).astype(F32).astype(LOW)
        for at in range(width // tile):
            span = slice(at * tile, (at + 1) * tile)
            dpp_ref[span, :pixels] = mm(h1t_ref[span, :], pix_ref[...]).astype(LOW)
            dpp_ref[span, pixels:] = mm(h1t_ref[span, :], hot).astype(LOW)


def embed_back_call(pack, dq, dk, dv, h1, embedded, d_middle, pixels, coords, w_in, w_pp_shape, vectors):
    rows, width = h1.shape
    groups = w_in.shape[0]
    whole = lambda a: pl.BlockSpec(a.shape, lambda j, p: (0,) * a.ndim, pipeline_mode=pl.Buffered(1))
    full = lambda *shape: pl.BlockSpec(shape, lambda j, p: (0,) * len(shape))
    weight = pl.BlockSpec((1,) + w_in.shape[1:], lambda j, p: (j, 0, 0))
    return pl.pallas_call(
        embed_back_kernel,
        grid_spec=pltpu.PrefetchScalarGridSpec(
            num_scalar_prefetch=1,
            grid=(groups,),
            in_specs=[
                whole(dq), whole(dk), whole(dv), whole(h1), whole(embedded), whole(d_middle),
                pl.BlockSpec((rows, pixels.shape[1]), lambda j, p: (p[0], 0)),
                pl.BlockSpec((rows, 2), lambda j, p: (p[0], 0)),
                weight,
                whole(vectors),
            ],
            out_specs=[weight, full(*w_pp_shape), full(1, width)],
            scratch_shapes=[
                pltpu.VMEM((width, rows), LOW),
                pltpu.VMEM((rows, w_in.shape[2]), LOW),
                pltpu.VMEM((rows, width), F32),
            ],
        ),
        out_shape=[
            jax.ShapeDtypeStruct(w_in.shape, LOW),
            jax.ShapeDtypeStruct(w_pp_shape, LOW),
            jax.ShapeDtypeStruct((1, width), F32),
        ],
        compiler_params=pltpu.CompilerParams(vmem_limit_bytes=VMEM_BYTES),
        name="embed_back",
    )(pack, dq, dk, dv, h1, embedded, d_middle, pixels, coords, w_in, vectors)


def pack_step(pack, valid, pixels, coords, lengths, labels, weights, vectors, head_gains, image_count, close=False):
    if close:
        bounds, gains = weights[6:]
        weights = weights[:6]
    w_pp, w_in, w_out, w_up, w_dn, w_cls = weights
    packs, images = lengths.shape
    rows = pixels.shape[0] // packs
    width = vectors.shape[1]
    if not close:
        mine = lax.dynamic_index_in_dim(lengths, pack[0], 0, keepdims=False)
        ends = jnp.cumsum(mine)
        fill = jnp.full((64 - images,), 1 << 30, jnp.int32)
        starts = jnp.concatenate([ends - mine, fill])
        ends = jnp.concatenate([ends, fill])
        bounds = jnp.stack([jnp.tile(starts, 2), jnp.tile(ends, 2)])
        gains = jnp.tile(head_gains, (1, 2))
    if close:
        (
            embedded, h1, q_raw, k_raw, value, attended, lse, w_in, w_out, w_up, w_dn, w_cls,
            x1, h2, active, slope, x2,
        ) = forward_call(weights, pixels, coords, vectors, gains, bounds, packs, 0)
    else:
        places = coords.T
        embedded, h1, q_raw, k_raw, value = embed_call(pack, pixels, places, w_pp, w_in, vectors, rows)
        attended, lse = attend_call(q_raw, k_raw, value, gains, bounds)
        x1, h2, active, slope, x2 = mlp_call(attended, embedded, w_out, w_up, w_dn, vectors)
    dx2, d_cls, loss, dvec_pool = pool_call(
        pack, x2, labels, w_cls, vectors, bounds, valid, images, image_count
    )
    if close:
        share = width // 8
        cut = lambda entry: entry.reshape(entry.shape[:-2] + (2, 2, 2, share) + entry.shape[-1:])
        d_mlp, d_out, d_attended, d_middle, dvec_two, share_mlp, share_cls = mlp_back_sum_call(
            dx2, active, slope, h2, x1, attended, w_out, w_up, w_dn, vectors, cut(d_cls), 1
        )
        d_mlp = d_mlp.reshape((-1, 2, 2, 2, share, width))
        dq, dk, dv, d_gain, share_mlp, share_out = attend_back_sum_call(
            q_raw, k_raw, value, attended, lse, d_attended, gains, bounds, d_mlp, cut(d_out), share_mlp, 2
        )
        share_in, share_pp, small, squares = embed_back_sum_call(
            dq, dk, dv, h1, embedded, d_middle, pixels, coords, w_in, weights[0].shape[1], vectors,
            dvec_two, dvec_pool, d_gain, loss, share_mlp, share_cls, share_out, packs, 3,
        )
        return share_pp, share_in, share_out, share_mlp, share_cls, small, squares
    d_mlp, d_out, d_attended, d_middle, dvec_two = mlp_back_call(
        dx2, active, slope, h2, x1, attended, w_out, w_up, w_dn, vectors
    )
    d_vec = jnp.concatenate([jnp.zeros_like(dvec_two), dvec_two, dvec_pool], axis=0)
    dq, dk, dv, d_gain = attend_back_call(q_raw, k_raw, value, attended, lse, d_attended, gains, bounds)
    d_in, d_pp, dvec_one = embed_back_call(
        pack, dq, dk, dv, h1, embedded, d_middle, pixels, places, w_in, w_pp.shape, vectors
    )
    d_gains = jnp.sum(d_gain.reshape(-1, 2, 2, 64), axis=(0, 2))
    return (d_pp, d_in, d_out, d_mlp[1], d_mlp[0], d_cls), d_vec.at[0].set(dvec_one[0]), d_gains, loss[0, 0]


MESH = pl.DeviceIdType.MESH


class Seat:
    def __init__(self):
        self.me = lax.axis_index("dp")
        self.z = lax.axis_index("tensor")
        self.c = lax.rem(self.me, 2)
        self.x = lax.rem(lax.div(self.me, 2), 2)
        self.y = lax.div(self.me, 4)
        self.core = self.me + 1 - 2 * self.c
        self.xn = self.me + 2 - 4 * self.x
        self.yn = self.me + 4 - 8 * self.y
        self.diag = self.xn + 4 - 8 * self.y


def link(src, dst, sems, at, device):
    return pltpu.make_async_remote_copy(
        src_ref=src,
        dst_ref=dst,
        send_sem=sems[0].at[at],
        recv_sem=sems[1].at[at],
        device_id=device,
        device_id_type=MESH,
    )


def greet(seat, depth):
    barrier = pltpu.get_barrier_semaphore()
    for ahead in range(1, 8):
        pl.semaphore_signal(
            barrier, inc=1, device_id={"dp": lax.rem(seat.me + ahead, 8)}, device_id_type=MESH
        )
    for ahead in range(1, depth):
        pl.semaphore_signal(
            barrier, inc=1, device_id={"tensor": lax.rem(seat.z + ahead, depth)}, device_id_type=MESH
        )
    pl.semaphore_wait(barrier, 6 + depth)


class Gather:
    def __init__(self, seat, shards, outs, split, units, own_sem, sems):
        self.seat, self.shards, self.outs, self.split, self.units = seat, shards, outs, split, units
        self.own_sem, self.sems = own_sem, sems
        self.share = shards[0].shape[0]

    def rows(self, owner):
        return pl.ds(pl.multiple_of(owner * self.share, self.share), self.share)

    def column(self, u, owner):
        k, cols = self.units[u]
        if self.split[k]:
            return self.outs[k].at[:, self.rows(owner), cols]
        return self.outs[k].at[self.rows(owner), cols]

    def halves(self, u, owner, which):
        k, cols = self.units[u]
        if self.split[k]:
            return self.outs[k].at[2 * which : 2 * which + 2, self.rows(owner), cols]
        half = self.share // 2
        start = pl.multiple_of(owner * self.share + which * half, half)
        return self.outs[k].at[pl.ds(start, half), cols]

    def block(self, u, level):
        k, cols = self.units[u]
        return self.outs[k].at[level, self.rows(self.seat.me), cols]

    def keep(self, u):
        k, cols = self.units[u]
        mine = self.block(u, self.seat.z) if self.split[k] else self.column(u, self.seat.me)
        return pltpu.make_async_copy(self.shards[k].at[:, cols], mine, self.own_sem.at[u])

    def along(self, u, hop, way):
        k, cols = self.units[u]
        level = self.seat.z - way * hop
        source = self.shards[k].at[:, cols] if hop == 0 else self.block(u, level)
        at = (u, hop + (0 if way > 0 else 3))
        return link(source, self.block(u, level), self.sems, at, {"tensor": self.seat.z + way})

    def arrives(self, u, hop, way):
        level = self.seat.z - way * (hop + 1)
        at = (u, hop + (0 if way > 0 else 3))
        return link(self.block(u, level), self.block(u, level), self.sems, at, {"tensor": self.seat.z - way})

    def sends(self, hop, way):
        level, to = self.seat.z - way * hop, self.seat.z + way
        return (level >= 0) & (level < 4) & (to >= 0) & (to < 4)

    def gets(self, hop, way):
        level = self.seat.z - way * (hop + 1)
        return (level >= 0) & (level < 4)

    def z(self, u, hop):
        for way in (1, -1):
            if hop > 0:

                @pl.when(self.gets(hop - 1, way))
                def _():
                    self.arrives(u, hop - 1, way).wait_recv()

            if hop < 3:

                @pl.when(self.sends(hop, way))
                def _():
                    self.along(u, hop, way).start()

    def copy(self, u, region, at, device):
        return link(region, region, self.sems, (u, at), {"dp": device})

    def own_x(self, u):
        return self.copy(u, self.column(u, self.seat.me), 6, self.seat.xn)

    def own_y(self, u):
        return self.copy(u, self.column(u, self.seat.me), 7, self.seat.yn)

    def pass_x(self, u):
        return self.copy(u, self.halves(u, self.seat.yn, 1), 8, self.seat.xn)

    def pass_y(self, u):
        return self.copy(u, self.halves(u, self.seat.xn, 0), 9, self.seat.yn)

    def owner(self, which):
        return (self.seat.me, self.seat.xn, self.seat.yn, self.seat.diag)[which]

    def over(self, u, which):
        return self.copy(u, self.column(u, self.owner(which)), 10 + which, self.seat.core)

    def plane(self, u):
        self.keep(u).wait()
        self.own_x(u).start()
        self.own_y(u).start()
        self.over(u, 0).start()

    def relay(self, u):
        s = self.seat
        self.copy(u, self.column(u, s.xn), 6, s.xn).wait_recv()
        self.pass_y(u).start()
        self.over(u, 1).start()
        self.copy(u, self.column(u, s.yn), 7, s.yn).wait_recv()
        self.pass_x(u).start()
        self.over(u, 2).start()

    def corner(self, u):
        s = self.seat
        self.copy(u, self.halves(u, s.diag, 1), 8, s.xn).wait_recv()
        self.copy(u, self.halves(u, s.diag, 0), 9, s.yn).wait_recv()
        self.over(u, 3).start()

    def arrived(self, u):
        s = self.seat
        for which in range(4):
            theirs = self.column(u, self.owner(which) + 1 - 2 * s.c)
            self.copy(u, theirs, 10 + which, s.core).wait_recv()

    def drain(self, u):
        if self.split[self.units[u][0]]:
            for hop in range(3):
                for way in (1, -1):

                    @pl.when(self.sends(hop, way))
                    def _():
                        self.along(u, hop, way).wait_send()

        for copy in (self.own_x(u), self.own_y(u), self.pass_x(u), self.pass_y(u)):
            copy.wait_send()
        for which in range(4):
            self.over(u, which).wait_send()


FORWARD_SPLIT = (False, True, True, True, True, False)


def forward_kernel(
    pp_in, in_in, out_in, up_in, dn_in, cls_in, pix_hbm, coord_ref, vec_ref, gain_ref, bound_ref,
    emb_hbm, h1_hbm, q_hbm, k_hbm, v_hbm, o_ref, lse_ref, win_hbm, wout_hbm, wup_hbm, wdn_hbm, wcls_hbm,
    x1_hbm, h2_hbm, act_hbm, slope_hbm, x2_hbm,
    wp_ref, win_ref, pix_ref, emb_ref, h1_ref, q_ref, k_ref, v_ref, ka_ref, va_ref, qa_ref,
    wout_ref, wup_ref, wdn_ref, all_ref, act_ref, slope_ref,
    own_sem, send_sem, recv_sem, copy_sem, act_sem,
    *, packs,
):
    step = pl.program_id(0)
    rows, pixels = pix_ref.shape
    groups = win_ref.shape[0]
    part = win_ref.shape[2] // 3
    spots = (wp_ref.shape[1] - pixels) // 2
    per = wup_ref.shape[2]
    half = per // 2
    tile = 256
    seat = Seat()
    everything, left, right = slice(None), slice(0, half), slice(half, 2 * half)
    units = (
        (0, everything), (1, everything), (2, everything),
        (3, left), (3, right), (4, left), (4, right), (5, everything),
    )
    pp, w_in, out, up_a, up_b, dn_a, dn_b, cls = range(8)
    flow = Gather(
        seat,
        (pp_in, in_in, out_in, up_in, dn_in, cls_in),
        (wp_ref, win_ref, wout_ref, wup_ref, wdn_ref, wcls_hbm),
        FORWARD_SPLIT,
        units,
        own_sem,
        (send_sem, recv_sem),
    )
    pack = jnp.minimum(seat.z, packs - 1)
    pix_copy = pltpu.make_async_copy(
        pix_hbm.at[pl.ds(pl.multiple_of(pack * rows, rows), rows)], pix_ref, copy_sem.at[0]
    )
    results = [
        pltpu.make_async_copy(source, target, copy_sem.at[1 + n])
        for n, (source, target) in enumerate(
            (
                (emb_ref, emb_hbm), (h1_ref, h1_hbm), (q_ref, q_hbm), (k_ref, k_hbm), (v_ref, v_hbm),
                (win_ref, win_hbm), (wout_ref, wout_hbm), (wup_ref, wup_hbm), (wdn_ref, wdn_hbm),
                (emb_ref, x1_hbm), (h1_ref, h2_hbm), (q_ref, x2_hbm),
            )
        )
    ]

    def hidden_copies(group):
        columns = slice(group * per, (group + 1) * per)
        return [
            pltpu.make_async_copy(source.at[group], target.at[:, columns], act_sem.at[n, group])
            for n, (source, target) in enumerate(((act_ref, act_hbm), (slope_ref, slope_hbm)))
        ]

    def join_heads(at):
        span = slice(at * tile, (at + 1) * tile)
        branch = mm_nt(all_ref[span, :part], wout_ref[0])
        for group in range(1, groups):
            branch += mm_nt(all_ref[span, group * part : (group + 1) * part], wout_ref[group])
        middle = emb_ref[span, :] + branch
        emb_ref[span, :] = middle
        normed, _ = row_norm(middle)
        h1_ref[span, :] = (normed * vec_ref[1:2]).astype(LOW)

    def hide(group):
        spans = [slice(at * tile, (at + 1) * tile) for at in range(rows // tile)]
        hidden = mm(h1_ref[spans[0], :], wup_ref[group])
        for at, span in enumerate(spans):
            now = hidden
            if at + 1 < len(spans):
                hidden = mm(h1_ref[spans[at + 1], :], wup_ref[group])
            active, slope = gelu_pair(now)
            act_ref[group, span, :] = active.astype(LOW)
            slope_ref[group, span, :] = slope.astype(LOW)
        for copy in hidden_copies(group):
            copy.start()

    def show(at):
        span = slice(at * tile, (at + 1) * tile)
        total = emb_ref[span, :]
        for group in range(groups):
            total += mm_nt(act_ref[group, span, :], wdn_ref[group])
        q_ref[span, :] = total

    def embed(at):
        span = slice(at * tile, (at + 1) * tile)
        start = pl.multiple_of(pack * rows + at * tile, tile)
        place = lax.broadcasted_iota(jnp.int32, (2 * spots, tile), 0)
        across = coord_ref[0:1, pl.ds(start, tile)]
        down = coord_ref[1:2, pl.ds(start, tile)]
        hot = jnp.transpose(((place == across) | (place - spots == down)).astype(F32)).astype(LOW)
        embedded = mm_nt(pix_ref[span, :], wp_ref[:, :pixels]) + mm_nt(hot, wp_ref[:, pixels:])
        emb_ref[span, :] = embedded
        normed, _ = row_norm(embedded)
        h1_ref[span, :] = (normed * vec_ref[0:1]).astype(LOW)

    def project(at):
        span = slice(at * tile, (at + 1) * tile)
        first = h1_ref[span, :]
        parts = [mm(first, win_ref[group]) for group in range(groups)]
        q_ref[span, :] = jnp.concatenate([entry[:, :part] for entry in parts], axis=1)
        k_ref[span, :] = jnp.concatenate([entry[:, part : 2 * part] for entry in parts], axis=1)
        v_ref[span, :] = jnp.concatenate([entry[:, 2 * part :].astype(LOW) for entry in parts], axis=1)

    @pl.when(step == 0)
    def _():
        pix_copy.start()
        for u in range(8):
            flow.keep(u).start()
        greet(seat, 4)
        flow.z(w_in, 0)
        flow.plane(pp)
        flow.z(w_in, 1)
        flow.relay(pp)
        flow.z(w_in, 2)
        flow.corner(pp)
        flow.z(w_in, 3)
        flow.plane(w_in)
        flow.z(out, 0)
        flow.arrived(pp)
        pix_copy.wait()
        embed(0)
        flow.z(out, 1)
        embed(1)
        flow.z(out, 2)
        flow.z(up_a, 0)
        embed(2)
        flow.z(out, 3)
        flow.plane(out)
        flow.z(up_a, 1)
        embed(3)
        flow.z(up_a, 2)
        results[0].start()
        results[1].start()
        flow.relay(w_in)
        flow.z(up_a, 3)
        flow.z(up_b, 0)
        flow.relay(out)
        flow.plane(up_a)
        flow.corner(w_in)
        flow.z(up_b, 1)
        flow.arrived(w_in)
        results[5].start()
        project(0)
        flow.corner(out)
        flow.z(up_b, 2)
        project(1)
        flow.z(up_b, 3)
        flow.plane(up_b)
        flow.z(dn_a, 0)
        project(2)
        flow.relay(up_a)
        flow.z(dn_a, 1)
        project(3)
        for n in (2, 3, 4):
            results[n].start()

    plan = {
        0: [lambda: flow.z(dn_a, 2)],
        1: [lambda: flow.z(dn_a, 3)],
        2: [lambda: flow.corner(up_a), lambda: flow.plane(dn_a), lambda: flow.z(dn_b, 0)],
        4: [lambda: flow.relay(up_b), lambda: flow.z(dn_b, 1)],
        5: [lambda: flow.z(dn_b, 2)],
        7: [lambda: flow.corner(up_b), lambda: flow.z(dn_b, 3), lambda: flow.plane(dn_b)],
        10: [lambda: flow.relay(dn_a)],
    }

    def between(slot):
        for number, actions in plan.items():
            if number % 2 == slot:

                @pl.when(2 * step + slot == number)
                def _():
                    for action in actions:
                        action()

    mine = pl.ds(pl.multiple_of(step * 128, 128), 128)
    attend_kernel(
        q_ref.at[:, mine], k_ref.at[:, mine], v_ref.at[:, mine], gain_ref, bound_ref, o_ref, lse_ref,
        ka_ref, va_ref, qa_ref, between=between,
    )
    all_ref[:, mine] = o_ref[...]

    @pl.when(step == pl.num_programs(0) - 1)
    def _():
        flow.arrived(out)
        results[6].start()
        for n in range(3):
            results[n].wait()
        for at in range(rows // tile):
            join_heads(at)
        results[9].start()
        results[10].start()
        flow.corner(dn_a)
        flow.plane(cls)
        flow.arrived(up_a)
        flow.arrived(up_b)
        results[7].start()
        hide(0)
        flow.relay(dn_b)
        hide(1)
        flow.corner(dn_b)
        hide(2)
        flow.relay(cls)
        hide(3)
        flow.corner(cls)
        flow.arrived(dn_a)
        flow.arrived(dn_b)
        results[8].start()
        for at in range(rows // tile):
            show(at)
        results[11].start()
        flow.arrived(cls)
        for u in range(8):
            flow.drain(u)
        for copy in results[3:]:
            copy.wait()
        for group in range(groups):
            for copy in hidden_copies(group):
                copy.wait()


def forward_call(shards, pixels, coords, vectors, gains, bounds, packs, collective_id):
    depth, width = 4, vectors.shape[1]
    rows = pixels.shape[0] // packs
    anywhere = pl.BlockSpec(memory_space=pl.ANY)
    small = lambda a: pl.BlockSpec(a.shape, lambda j: (0, 0))
    pair = pl.BlockSpec((rows, 128), lambda j: (0, j))
    weights = [
        jax.ShapeDtypeStruct(((depth, width) if apart else (width,)) + entry.shape[1:], LOW)
        for entry, apart in zip(shards, FORWARD_SPLIT)
    ]
    token = lambda dtype: jax.ShapeDtypeStruct((rows, width), dtype)
    held = lambda dtype: pltpu.VMEM((rows, width), dtype)
    per = shards[3].shape[1]
    wide = jax.ShapeDtypeStruct((rows, depth * per), LOW)
    return pl.pallas_call(
        functools.partial(forward_kernel, packs=packs),
        grid=(width // 128,),
        in_specs=[anywhere] * 7 + [small(coords), small(vectors), small(gains), small(bounds)],
        out_specs=[anywhere] * 5 + [pair, pair] + [anywhere] * 10,
        out_shape=[token(F32), token(LOW), token(F32), token(F32), token(LOW), token(LOW), token(F32)]
        + weights[1:]
        + [token(F32), token(LOW), wide, wide, token(F32)],
        scratch_shapes=[
            pltpu.VMEM(weights[0].shape, LOW),
            pltpu.VMEM(weights[1].shape, LOW),
            pltpu.VMEM((rows, pixels.shape[1]), LOW),
            held(F32), held(LOW), held(F32), held(F32), held(LOW),
            pltpu.VMEM((rows, 256), LOW),
            pltpu.VMEM((rows, 256), LOW),
            pltpu.VMEM((2, rows, 256), LOW),
            *(pltpu.VMEM(entry.shape, LOW) for entry in weights[2:5]),
            held(LOW),
            pltpu.VMEM((depth, rows, per), LOW),
            pltpu.VMEM((depth, rows, per), LOW),
            pltpu.SemaphoreType.DMA((8,)),
            pltpu.SemaphoreType.DMA((8, 14)),
            pltpu.SemaphoreType.DMA((8, 14)),
            pltpu.SemaphoreType.DMA((13,)),
            pltpu.SemaphoreType.DMA((2, depth)),
        ],
        compiler_params=pltpu.CompilerParams(
            collective_id=collective_id, has_side_effects=True, vmem_limit_bytes=VMEM_BYTES
        ),
        name="forward",
    )(*shards, pixels, coords, vectors, gains, bounds)


class Flow:
    def __init__(self, seat, level_of, own, core_in, plane_in, last_in, up_in, down_in, sems):
        self.seat, self.level_of, self.own, self.sems = seat, level_of, own, sems
        self.core_in, self.plane_in, self.last_in = core_in, plane_in, last_in
        self.up_in, self.down_in = up_in, down_in

    def to_core(self, i, source):
        return link(source, self.core_in.at[i], self.sems, (i, 0), {"dp": self.seat.core})

    def first(self, i, along_x):
        s = self.seat
        source = self.own(i).at[:, 1 - s.x] if along_x else self.own(i).at[1 - s.y]
        return link(source, self.plane_in.at[i], self.sems, (i, 1), {"dp": s.xn if along_x else s.yn})

    def second(self, i, along_x):
        s = self.seat
        source = self.own(i).at[s.y, 1 - s.x] if along_x else self.own(i).at[1 - s.y, s.x]
        return link(source, self.last_in.at[i], self.sems, (i, 2), {"dp": s.xn if along_x else s.yn})

    def along(self, i, way):
        s = self.seat
        buffer = self.up_in if way > 0 else self.down_in
        at = (i, 3 if way > 0 else 4)
        return link(self.own(i).at[s.y, s.x], buffer.at[i], self.sems, at, {"tensor": s.z + way})

    def x_first(self, i, then, other):
        pl.when(lax.rem(i, 2) == 0)(then)
        pl.when(lax.rem(i, 2) == 1)(other)

    def one(self, i):
        mine = self.own(i)
        mine[...] = mine[...] + self.core_in[i]
        self.x_first(i, lambda: self.first(i, True).start(), lambda: self.first(i, False).start())

    def two(self, i):
        s, mine = self.seat, self.own(i)

        def from_x():
            self.first(i, True).wait_recv()
            mine[:, s.x] = mine[:, s.x] + self.plane_in[i]
            self.second(i, False).start()

        def from_y():
            self.first(i, False).wait_recv()
            mine[s.y] = mine[s.y] + self.plane_in[i]
            self.second(i, True).start()

        self.x_first(i, from_x, from_y)

    def three(self, i):
        s, mine = self.seat, self.own(i)
        self.second(i, False).wait_recv()
        mine[s.y, s.x] = mine[s.y, s.x] + self.last_in[i]

        @pl.when((s.z == 0) & (self.level_of(i) > 0))
        def _():
            self.along(i, 1).start()

        @pl.when((s.z == 3) & (self.level_of(i) < 3))
        def _():
            self.along(i, -1).start()

    def hop(self, i, reach):
        s, mine = self.seat, self.own(i)

        @pl.when((s.z == reach) & (self.level_of(i) > reach))
        def _():
            self.along(i, 1).wait_recv()
            mine[s.y, s.x] = mine[s.y, s.x] + self.up_in[i]
            self.along(i, 1).start()

        @pl.when((s.z == 3 - reach) & (self.level_of(i) < 3 - reach))
        def _():
            self.along(i, -1).wait_recv()
            mine[s.y, s.x] = mine[s.y, s.x] + self.down_in[i]
            self.along(i, -1).start()

    def total(self, i):
        s = self.seat
        values = self.own(i)[s.y, s.x].astype(F32)

        @pl.when(s.z > 0)
        def _():
            self.along(i, 1).wait_recv()

        @pl.when(s.z < 3)
        def _():
            self.along(i, -1).wait_recv()

        @pl.when(s.z == 0)
        def _():
            self.up_in[i] = jnp.zeros(self.up_in.shape[1:], LOW)

        @pl.when(s.z == 3)
        def _():
            self.down_in[i] = jnp.zeros(self.down_in.shape[1:], LOW)

        return values + self.up_in[i].astype(F32) + self.down_in[i].astype(F32)

    def drain(self, i):
        s = self.seat
        self.first(i, True).wait_send()
        self.second(i, True).wait_send()

        @pl.when(s.z < self.level_of(i))
        def _():
            self.along(i, 1).wait_send()

        @pl.when(s.z > self.level_of(i))
        def _():
            self.along(i, -1).wait_send()


class Whole:
    def __init__(self, seat, own, core_in, plane_in, last_in, level_in, sems):
        self.seat, self.own, self.sems = seat, own, sems
        self.core_in, self.plane_in, self.last_in, self.level_in = core_in, plane_in, last_in, level_in
        self.half = core_in.shape[2] // 2

    def to_core(self, source):
        return link(source, self.core_in, self.sems, 0, {"dp": self.seat.core})

    def rows(self, which):
        return slice(which * self.half, (which + 1) * self.half)

    def first(self, which):
        s = self.seat
        rows = self.rows(which)
        source = self.own.at[1 - s.y, :, rows] if which else self.own.at[:, 1 - s.x, rows]
        return link(source, self.plane_in.at[which], self.sems, 1 + which, {"dp": s.yn if which else s.xn})

    def second(self, which):
        s = self.seat
        rows = self.rows(which)
        source = self.own.at[s.y, 1 - s.x, rows] if which else self.own.at[1 - s.y, s.x, rows]
        return link(source, self.last_in.at[which], self.sems, 3 + which, {"dp": s.xn if which else s.yn})

    def lift(self):
        s = self.seat
        return link(self.own.at[s.y, s.x], self.level_in.at[0], self.sems, 5, {"tensor": s.z + 1 - 2 * (s.z % 2)})

    def cross(self):
        s = self.seat
        return link(self.own.at[s.y, s.x], self.level_in.at[1], self.sems, 6, {"tensor": 3 - s.z})

    def give(self):
        s = self.seat
        return link(self.own.at[s.y, s.x], self.level_in.at[1], self.sems, 7, {"tensor": s.z + 1 - 2 * (s.z % 2)})

    def middle(self):
        return (self.seat.z == 1) | (self.seat.z == 2)

    def ends(self):
        return (self.seat.z == 0) | (self.seat.z == 3)

    def one(self):
        for a in range(2):
            for b in range(2):
                self.own[a, b] = self.own[a, b] + self.core_in[a, b]
        self.first(0).start()
        self.first(1).start()

    def two(self):
        s, own = self.seat, self.own
        for which in range(2):
            rows = self.rows(which)
            self.first(which).wait_recv()
            for a in range(2):
                if which:
                    own[s.y, a, rows] = own[s.y, a, rows] + self.plane_in[which, a]
                else:
                    own[a, s.x, rows] = own[a, s.x, rows] + self.plane_in[which, a]
            self.second(which).start()

    def three(self):
        s, own = self.seat, self.own
        for which in range(2):
            rows = self.rows(which)
            self.second(which).wait_recv()
            own[s.y, s.x, rows] = own[s.y, s.x, rows] + self.last_in[which]
        pl.when(self.ends())(lambda: self.lift().start())

    def four(self):
        s, own = self.seat, self.own

        @pl.when(self.middle())
        def _():
            self.lift().wait_recv()
            own[s.y, s.x] = own[s.y, s.x] + self.level_in[0]
            self.cross().start()

    def five(self):
        s, own = self.seat, self.own

        @pl.when(self.middle())
        def _():
            self.cross().wait_recv()
            self.cross().wait_send()
            own[s.y, s.x] = own[s.y, s.x] + self.level_in[1]
            self.give().start()

    def total(self):
        s = self.seat

        @pl.when(self.ends())
        def _():
            self.give().wait_recv()

        @pl.when(self.middle())
        def _():
            self.level_in[1] = self.own[s.y, s.x]

        return self.level_in[1].astype(F32)

    def drain(self):
        for which in range(2):
            self.first(which).wait_send()
            self.second(which).wait_send()
        pl.when(self.ends())(lambda: self.lift().wait_send())
        pl.when(self.middle())(lambda: self.give().wait_send())


class Tiny:
    def __init__(self, seat, value, came, sems):
        self.seat, self.value, self.came, self.sems = seat, value, came, sems

    def near(self, ahead, own):
        s = self.seat
        other = lax.rem(s.me + (ahead if own else 8 - ahead), 8)
        place = self.came.at[s.me if own else other]
        return link(self.value.at[0], place, self.sems, ahead - 1, {"dp": other})

    def far(self, ahead, own):
        s = self.seat
        other = lax.rem(s.z + (ahead if own else 4 - ahead), 4)
        place = self.came.at[8 + (s.z if own else other)]
        return link(self.value.at[1], place, self.sems, 6 + ahead, {"tensor": other})

    def start_plane(self):
        for ahead in range(1, 8):
            self.near(ahead, True).start()

    def total(self, first, count):
        total = self.came[first]
        for n in range(1, count):
            total = total + self.came[first + n]
        return total

    def turn_levels(self):
        for ahead in range(1, 8):
            self.near(ahead, False).wait_recv()
        self.came[self.seat.me] = self.value[0]
        self.value[1] = self.total(0, 8)
        for ahead in range(1, 4):
            self.far(ahead, True).start()

    def finish(self):
        for ahead in range(1, 4):
            self.far(ahead, False).wait_recv()
        self.came[8 + self.seat.z] = self.value[1]
        return self.total(8, 4)

    def drain(self):
        for ahead in range(1, 8):
            self.near(ahead, True).wait_send()
        for ahead in range(1, 4):
            self.far(ahead, True).wait_send()


def flow_scratch(chunks, share, cols):
    low = lambda *shape: pltpu.VMEM(shape, LOW)
    sems = lambda: pltpu.SemaphoreType.DMA((chunks, 5))
    return [
        low(chunks, 2, 2, share, cols),
        low(chunks, 2, share, cols),
        low(chunks, share, cols),
        low(chunks, share, cols),
        low(chunks, share, cols),
        sems(),
        sems(),
    ]


def whole_scratch(share, cols):
    low = lambda *shape: pltpu.VMEM(shape, LOW)
    return [
        low(2, 2, share, cols),
        low(2, 2, share // 2, cols),
        low(2, share // 2, cols),
        low(2, share, cols),
        pltpu.SemaphoreType.DMA((8,)),
        pltpu.SemaphoreType.DMA((8,)),
    ]


def tiny_scratch(shape):
    sems = lambda: pltpu.SemaphoreType.DMA((10,))
    return [pltpu.VMEM((2,) + shape, F32), pltpu.VMEM((12,) + shape, F32), sems(), sems()]


MLP_BACK_IO = (10, 5)
MLP_BACK_SCRATCH = 5


def mlp_back_sum_kernel(*refs):
    ins, outs = MLP_BACK_IO
    inputs, dcls_ref = refs[:ins], refs[ins]
    outputs = refs[ins + 1 : ins + 1 + outs]
    share_ref, cls_ref = refs[ins + 1 + outs : ins + 3 + outs]
    rest = refs[ins + 3 + outs :]
    scratch, rest = rest[:MLP_BACK_SCRATCH], rest[MLP_BACK_SCRATCH:]
    full, flow_refs = rest[0], rest[1:8]
    cls_own, cls_load, cls_refs = rest[8], rest[9], rest[10:16]
    step = pl.program_id(0)
    seat = Seat()
    c = seat.c
    share = full.shape[-2]
    flow = Flow(
        seat, lambda i: 1, lambda i: full.at[i, :, :, c], *flow_refs[:5], flow_refs[5:]
    )
    cls = Whole(seat, cls_own, *cls_refs[:4], cls_refs[4:])
    loading = pltpu.make_async_copy(dcls_ref.at[:, :, c], cls_own, cls_load)
    cls_to_core = cls.to_core(dcls_ref.at[:, :, 1 - c])

    def to_core(i):
        return flow.to_core(i, full.at[i, :, :, 1 - c])

    def one(i):
        to_core(i).wait_recv()
        flow.one(i)

    def last(i):
        @pl.when(seat.z == flow.level_of(i))
        def _():
            share_ref[i] = flow.total(i)

    @pl.when(step == 0)
    def _():
        loading.start()
        greet(seat, 4)
        cls_to_core.start()
        share_ref[...] = jnp.zeros(share_ref.shape, F32)

    def keep(kind, at, value):
        full[kind, at // 2, at % 2] = value.reshape(2, share, value.shape[1])

    def cls_total():
        cls_ref[...] = cls.total()

    def cls_one():
        loading.wait()
        cls_to_core.wait_recv()
        cls.one()

    plan = {
        0: [cls_one],
        1: [lambda: to_core(0).start(), lambda: to_core(1).start(), cls.two],
        2: [lambda: one(0), lambda: one(1), cls.three],
        4: [lambda: flow.two(0), lambda: flow.two(1), cls.four],
        5: [lambda: flow.three(0), lambda: flow.three(1)],
        6: [cls.five],
        7: [lambda: flow.hop(0, 1), lambda: flow.hop(1, 1)],
    }

    def between(now, odd):
        for number, actions in plan.items():
            if number % 2 != odd:
                continue

            @pl.when(now == number)
            def _():
                for action in actions:
                    action()

    mlp_back_kernel(*inputs, *outputs, *scratch, keep=keep, between=between)

    @pl.when(step == pl.num_programs(0) - 1)
    def _():
        cls_total()
        for i in range(2):
            last(i)
        for i in range(2):
            to_core(i).wait_send()
            flow.drain(i)
        cls_to_core.wait_send()
        cls.drain()


def mlp_back_sum_call(dx2, active, slope, h2, x1, attended, w_out, w_up, w_dn, vectors, d_cls, collective_id):
    rows, width = dx2.shape
    groups, _, per = w_up.shape
    chunk = per
    hidden = groups * per
    share, classes = d_cls.shape[-2:]
    turned = lambda j: j + 1 - 2 * (j % 2)
    whole = lambda a: pl.BlockSpec(a.shape, lambda j: (0,) * a.ndim, pipeline_mode=pl.Buffered(1))
    weight = pl.BlockSpec((1, width, chunk), lambda j: (turned(j), 0, 0))
    piece = pl.BlockSpec((rows, chunk), lambda j: (0, turned(j)))
    full = lambda *shape: pl.BlockSpec(shape, lambda j: (0,) * len(shape))
    late = lambda j: jnp.maximum(j - 1, 0)
    return pl.pallas_call(
        mlp_back_sum_kernel,
        grid=(hidden // chunk,),
        in_specs=[
            whole(dx2), piece, piece, whole(h2), whole(x1), whole(attended), whole(w_out),
            weight, weight, whole(vectors), pl.BlockSpec(memory_space=pl.ANY),
        ],
        out_specs=[
            pl.BlockSpec((2, 1, width, chunk), lambda j: (0, late(j), 0, 0)),
            full(*w_out.shape),
            full(rows, width),
            full(rows, width),
            full(1, width),
            full(2, share, width),
            full(share, classes),
        ],
        out_shape=[
            jax.ShapeDtypeStruct((2, groups - 1) + w_up.shape[1:], LOW),
            jax.ShapeDtypeStruct(w_out.shape, LOW),
            jax.ShapeDtypeStruct((rows, width), LOW),
            jax.ShapeDtypeStruct((rows, width), F32),
            jax.ShapeDtypeStruct((1, width), F32),
            jax.ShapeDtypeStruct((2, share, width), F32),
            jax.ShapeDtypeStruct((share, classes), F32),
        ],
        scratch_shapes=[
            pltpu.VMEM((rows, width), LOW),
            pltpu.VMEM((width, rows), LOW),
            pltpu.VMEM((width, rows), LOW),
            pltpu.VMEM((rows, width), F32),
            pltpu.VMEM((rows, chunk), LOW),
            pltpu.VMEM((2, 2, 2, 2, share, width), LOW),
        ]
        + flow_scratch(2, share, width)
        + [pltpu.VMEM((2, 2, share, classes), LOW), pltpu.SemaphoreType.DMA]
        + whole_scratch(share, classes),
        compiler_params=pltpu.CompilerParams(
            collective_id=collective_id, has_side_effects=True, vmem_limit_bytes=VMEM_BYTES
        ),
        name="mlp_back_sum",
    )(dx2, active, slope, h2, x1, attended, w_out, w_up, w_dn, vectors, d_cls)


def embed_back_sum_kernel(
    dq_hbm, dk_hbm, dv_hbm, h1_hbm, emb_hbm, dmid_hbm, pix_hbm, coord_ref, win_hbm, vec_ref,
    two_ref, pool_ref, gains_ref, loss_ref, mlp_ref, cls_ref, out_ref,
    in_ref, pp_ref, small_out, square_out,
    dq_ref, dk_ref, dv_ref, h1_ref, emb_ref, dmid_ref, pix_ref, win_ref, tile_sem, load_sem,
    h1t_ref, embt_ref, join_ref, hot_ref, in_full, pp_full,
    *rest, packs,
):
    rows, width = h1_ref.shape
    groups = 4
    part = win_ref.shape[2] // 3
    tile = 256
    seat = Seat()
    c = seat.c
    share = in_full.shape[-2]
    flow = Flow(
        seat, lambda i: (3 * i) % 4, lambda i: in_full.at[i, :, :, c], *rest[:5], rest[5:7]
    )
    pp = Whole(seat, pp_full.at[:, :, c], *rest[7:11], rest[11:13])
    small = Tiny(seat, rest[13], rest[14], rest[15:17])
    square = Tiny(seat, rest[17], rest[18], rest[19:21])
    small_value, square_value = rest[13], rest[17]
    pp_to_core = pp.to_core(pp_full.at[:, :, 1 - c])
    leader = jnp.where(seat.z == 0, 1.0, 0.0)

    def in_to_core(i):
        return flow.to_core(i, in_full.at[i, :, :, 1 - c])

    def one(i):
        in_to_core(i).wait_recv()
        flow.one(i)

    def last(i):
        @pl.when(flow.level_of(i) == seat.z)
        def _():
            in_ref[...] = flow.total(i)

    tiled = (
        (dq_hbm, dq_ref), (dk_hbm, dk_ref), (dv_hbm, dv_ref), (h1_hbm, h1_ref),
        (emb_hbm, emb_ref), (dmid_hbm, dmid_ref),
    )

    def tile_copies(at, numbers):
        span = pl.ds(at * tile, tile)
        return [
            pltpu.make_async_copy(tiled[n][0].at[span], tiled[n][1].at[span], tile_sem.at[n, at])
            for n in numbers
        ]

    win_copy = pltpu.make_async_copy(win_hbm, win_ref, load_sem.at[0])
    pack = jnp.minimum(seat.z, packs - 1)
    pix_copy = pltpu.make_async_copy(
        pix_hbm.at[pl.ds(pl.multiple_of(pack * rows, rows), rows)], pix_ref, load_sem.at[1]
    )
    for at in range(rows // tile):
        for copy in tile_copies(at, range(4)):
            copy.start()
    win_copy.start()
    for at in range(rows // tile):
        for copy in tile_copies(at, range(4, 6)):
            copy.start()
    pix_copy.start()
    greet(seat, 4)
    gain = vec_ref[0:1]
    pixels = pix_ref.shape[1]
    spots = (pp_ref.shape[1] - pixels) // 2
    gain_sum = jnp.zeros((1, width), F32)
    for at in range(rows // tile):
        for copy in tile_copies(at, range(4)):
            copy.wait()
        span = slice(at * tile, (at + 1) * tile)
        for group in range(groups):
            mine = slice(group * part, (group + 1) * part)
            join_ref[group, span, :] = jnp.concatenate(
                [dq_ref[span, mine], dk_ref[span, mine], dv_ref[span, mine]], axis=1
            )
        h1t_ref[:, span] = jnp.transpose(h1_ref[span, :].astype(F32)).astype(LOW)

    def project(i):
        group = flow.level_of(i)
        for at in range(4):
            span = slice(at * 2 * share, (at + 1) * 2 * share)
            value = mm(h1t_ref[span, :], join_ref[group]).astype(LOW)
            in_full[i, at // 2, at % 2] = value.reshape(2, share, value.shape[1])
        in_to_core(i).start()

    project(0)
    project(1)
    win_copy.wait()
    for at in range(rows // tile):
        for copy in tile_copies(at, range(4, 6)):
            copy.wait()
        span = slice(at * tile, (at + 1) * tile)
        d_first = jnp.zeros((tile, width), F32)
        for group in range(groups):
            d_first += mm_nt(join_ref[group, span, :], win_ref[group])
        normed, inverse = row_norm(emb_ref[span, :])
        gain_sum += jnp.sum(d_first * normed, axis=0, keepdims=True)
        d_embed = dmid_ref[span, :] + row_norm_back(d_first, gain, normed, inverse)
        embt_ref[:, span] = jnp.transpose(d_embed).astype(LOW)
        if at < 2:
            one(at)
    flow.two(0)
    small_value[0] = jnp.zeros(small_out.shape, F32)
    small_value[0, 0:1] = gain_sum
    small_value[0, 1:2] = two_ref[...]
    small_value[0, 2:4] = pool_ref[...]
    heads = jnp.sum(gains_ref[...], axis=0)
    small_value[0, 4:5, :128] = heads[0:1]
    small_value[0, 4:5, 128:256] = heads[1:2]
    small_value[0, 5:6, :128] = loss_ref[0:1, :]
    small.start_plane()
    place = lax.broadcasted_iota(jnp.int32, (2 * spots, rows), 0)
    mine = pl.ds(pl.multiple_of(pack * rows, rows), rows)
    hot = (place == coord_ref[0:1, mine]) | (place - spots == coord_ref[1:2, mine])
    hot_ref[...] = hot.astype(F32).astype(LOW)
    pix_copy.wait()
    for at in range(4):
        span = slice(at * 2 * share, (at + 1) * 2 * share)
        picture = mm(embt_ref[span, :], pix_ref[...]).astype(LOW)
        pp_full[at // 2, at % 2, :, :, :pixels] = picture.reshape(2, share, pixels)
        place = mm_nt(embt_ref[span, :], hot_ref[...]).astype(LOW)
        pp_full[at // 2, at % 2, :, :, pixels:] = place.reshape(2, share, 2 * spots)
    pp_to_core.start()
    flow.two(1)
    project(2)
    pp_to_core.wait_recv()
    pp.one()
    flow.three(0)
    small.turn_levels()
    project(3)
    one(2)
    flow.three(1)
    flow.hop(0, 1)
    pp.two()
    one(3)
    flow.hop(1, 1)
    flow.hop(0, 2)
    small_out[...] = small.finish()
    mlp_sum = mlp_ref[...]
    out_sum = out_ref[...]
    squares = jnp.sum(mlp_sum[0] * mlp_sum[0] + mlp_sum[1] * mlp_sum[1], axis=0, keepdims=True)
    total = jnp.sum(squares, axis=1, keepdims=True)
    total = total + jnp.sum(jnp.sum(out_sum * out_sum, axis=0, keepdims=True), axis=1, keepdims=True)
    cls_sum = cls_ref[...]
    shared = jnp.sum(jnp.sum(cls_sum * cls_sum, axis=0, keepdims=True), axis=1, keepdims=True)
    pp.three()
    flow.two(2)
    flow.hop(1, 2)
    flow.two(3)
    pp.four()
    flow.three(2)
    flow.three(3)
    pp.five()
    flow.hop(2, 1)
    flow.hop(3, 1)
    pp_sum = pp.total()
    pp_ref[...] = pp_sum
    shared += jnp.sum(jnp.sum(pp_sum * pp_sum, axis=0, keepdims=True), axis=1, keepdims=True)
    for i in range(groups):
        last(i)
    in_sum = in_ref[...]
    total = total + jnp.sum(jnp.sum(in_sum * in_sum, axis=0, keepdims=True), axis=1, keepdims=True)
    square_value[0] = jnp.broadcast_to(total + leader * shared, (8, 128))
    square.start_plane()
    square.turn_levels()
    square_out[...] = square.finish()
    pp_to_core.wait_send()
    for entry in (pp, small, square):
        entry.drain()
    for i in range(groups):
        in_to_core(i).wait_send()
        flow.drain(i)


def embed_back_sum_call(
    dq, dk, dv, h1, embedded, d_middle, pixels, coords, w_in, pp_cols, vectors,
    d_two, d_pool, d_gain, loss, share_mlp, share_cls, share_out, packs, collective_id,
):
    rows, width = h1.shape
    groups, share = w_in.shape[0], width // 8
    cols = w_in.shape[2]
    low = lambda *shape: pltpu.VMEM(shape, LOW)
    inside = pl.BlockSpec(memory_space=pltpu.VMEM)
    anywhere = pl.BlockSpec(memory_space=pl.ANY)
    loaded = (dq, dk, dv, h1, embedded, d_middle, pixels, w_in)
    return pl.pallas_call(
        functools.partial(embed_back_sum_kernel, packs=packs),
        in_specs=[anywhere] * 7 + [inside, anywhere] + [inside] * 8,
        out_specs=[inside] * 4,
        out_shape=[
            jax.ShapeDtypeStruct((share, cols), F32),
            jax.ShapeDtypeStruct((share, pp_cols), F32),
            jax.ShapeDtypeStruct((8, width), F32),
            jax.ShapeDtypeStruct((8, 128), F32),
        ],
        scratch_shapes=[pltpu.VMEM((rows,) + a.shape[1:] if a is pixels else a.shape, a.dtype) for a in loaded]
        + [pltpu.SemaphoreType.DMA((6, rows // 256)), pltpu.SemaphoreType.DMA((2,))]
        + [
            low(width, rows),
            low(width, rows),
            low(groups, rows, cols),
            low(pp_cols - pixels.shape[1], rows),
            low(groups, 2, 2, 2, share, cols),
            low(2, 2, 2, share, pp_cols),
        ]
        + flow_scratch(groups, share, cols)
        + whole_scratch(share, pp_cols)
        + tiny_scratch((8, width))
        + tiny_scratch((8, 128)),
        compiler_params=pltpu.CompilerParams(
            collective_id=collective_id, has_side_effects=True, vmem_limit_bytes=VMEM_BYTES
        ),
        name="embed_back_sum",
    )(
        dq, dk, dv, h1, embedded, d_middle, pixels, coords, w_in, vectors,
        d_two, d_pool, d_gain, loss, share_mlp, share_cls, share_out,
    )


def prepare_kernel(
    length_ref, patch_ref, pos_ref, in_ref, out_ref, up_ref, dn_ref, cls_ref, gain_ref,
    pp_low, in_low, out_low, up_low, dn_low, cls_low, bound_out, gain_out,
):
    packs, images = length_ref.shape
    pixels = patch_ref.shape[1]
    kinds, spots, share = pos_ref.shape
    pp_low[:, :pixels] = patch_ref[...].astype(LOW)
    pp_low[:, pixels:] = jnp.transpose(pos_ref[...].reshape(kinds * spots, share)).astype(LOW)
    in_low[...] = jnp.concatenate([in_ref[n] for n in range(in_ref.shape[0])], axis=1).astype(LOW)
    out_low[...] = jnp.transpose(out_ref[...]).astype(LOW)
    up_low[...] = up_ref[...].astype(LOW)
    dn_low[...] = dn_ref[...].astype(LOW)
    cls_low[...] = cls_ref[...].astype(LOW)
    gain_out[...] = jnp.concatenate([gain_ref[...], gain_ref[...]], axis=1)
    pack = jnp.minimum(lax.axis_index("tensor"), packs - 1)
    lane = lax.broadcasted_iota(jnp.int32, (1, 128), 1)
    slot = jnp.where(lane >= 64, lane - 64, lane)
    starts = jnp.full((1, 128), 1 << 30, jnp.int32)
    ends = starts
    place = jnp.int32(0)
    for n in range(images):
        after = place + length_ref[pack, n]
        starts = jnp.where(slot == n, place, starts)
        ends = jnp.where(slot == n, after, ends)
        place = after
    bound_out[0:1, :] = starts
    bound_out[1:2, :] = ends


def prepare_call(lengths, patch, pos, w_in, w_out, up, dn, cls, gains):
    share, width = up.shape
    low = lambda cols: jax.ShapeDtypeStruct((share, cols), LOW)
    inside = pl.BlockSpec(memory_space=pltpu.VMEM)
    return pl.pallas_call(
        prepare_kernel,
        in_specs=[pl.BlockSpec(memory_space=pltpu.SMEM)] + [inside] * 8,
        out_specs=[inside] * 8,
        out_shape=[
            low(patch.shape[1] + pos.shape[0] * pos.shape[1]),
            low(w_in.shape[0] * w_in.shape[2]),
            low(w_out.shape[0]),
            low(width),
            low(width),
            low(cls.shape[1]),
            jax.ShapeDtypeStruct((2, 128), jnp.int32),
            jax.ShapeDtypeStruct((2, 128), F32),
        ],
        compiler_params=pltpu.CompilerParams(vmem_limit_bytes=VMEM_BYTES),
        name="prepare",
    )(lengths, patch, pos, w_in, w_out, up, dn, cls, gains)


RATES = (RATE_BASE, RATE_POSITION, RATE_BASE, RATE_MIDDLE, RATE_BASE, RATE_BASE, RATE_MIDDLE, RATE_VECTOR, RATE_VECTOR)


def update_kernel(*refs):
    states, shares, outs = refs[:27], refs[27:34], refs[34:61]
    loss_ref, norm_ref = refs[61:]
    pp_ref, in_ref, out_ref, mlp_ref, cls_ref, small_ref, square_ref = shares
    pixels = states[0].shape[1]
    kinds, spots, share = states[3].shape
    part = states[6].shape[2]
    vectors = small_ref[0:4, :]
    row = small_ref[4:5, :]
    head = states[24].shape[1]
    gains = jnp.concatenate(
        [row[:, :head] + row[:, head : 2 * head], row[:, 2 * head : 3 * head] + row[:, 3 * head : 4 * head]],
        axis=0,
    )

    def square_sum(entry):
        return jnp.sum(jnp.sum(entry * entry, axis=0, keepdims=True), axis=1, keepdims=True)

    norm = jnp.sqrt(square_ref[0:1, 0:1] + square_sum(vectors) + square_sum(gains))
    clip = CLIP / jnp.maximum(norm, CLIP)
    grads = (
        pp_ref[:, :pixels],
        jnp.transpose(pp_ref[:, pixels:]).reshape(kinds, spots, share),
        None,
        jnp.transpose(out_ref[...]),
        mlp_ref[1],
        mlp_ref[0],
        cls_ref[...],
        vectors,
        gains,
    )
    for n, grad in enumerate(grads):
        decay = DECAY if n < 7 else 0.0
        if n == 2:
            for kind in range(states[6].shape[0]):
                results = adam(
                    *(state[kind] for state in states[6:9]),
                    in_ref[:, kind * part : (kind + 1) * part], clip, RATES[n], decay,
                )
                for result, out in zip(results, outs[6:9]):
                    out[kind] = result
        else:
            mine = clip.reshape(1, 1, 1) if grad.ndim == 3 else clip
            results = adam(*(state[...] for state in states[3 * n : 3 * n + 3]), grad, mine, RATES[n], decay)
            for result, out in zip(results, outs[3 * n : 3 * n + 3]):
                out[...] = result
    loss_ref[...] = small_ref[5:6, 0:1]
    norm_ref[...] = norm


def update_call(states, shares):
    inside = pl.BlockSpec(memory_space=pltpu.VMEM)
    scalar = jax.ShapeDtypeStruct((1, 1), F32)
    return pl.pallas_call(
        update_kernel,
        in_specs=[inside] * (len(states) + len(shares)),
        out_specs=[inside] * (len(states) + 2),
        out_shape=[jax.ShapeDtypeStruct(a.shape, F32) for a in states] + [scalar, scalar],
        compiler_params=pltpu.CompilerParams(vmem_limit_bytes=VMEM_BYTES),
        name="update",
    )(*states, *shares)


def adam(master, first_moment, second_moment, gradient, clip_scale, rate, decay_rate):
    gradient = gradient * clip_scale
    first_new = BETA_ONE * first_moment + (1 - BETA_ONE) * gradient
    second_new = BETA_TWO * second_moment + (1 - BETA_TWO) * gradient * gradient
    update = (
        first_new / (1 - BETA_ONE**STEP) / (jnp.sqrt(second_new / (1 - BETA_TWO**STEP)) + ADAM_EPS)
    )
    return (master - rate * (update + decay_rate * master), first_new, second_new)


def squared(entry):
    return jnp.sum(entry * entry)


def per_device(
    pixels, coords, lengths, labels,
    patch_table, patch_first, patch_second,
    position_table, position_first, position_second,
    attend_in, attend_in_first, attend_in_second,
    attend_out, attend_out_first, attend_out_second,
    expand, expand_first, expand_second,
    shrink, shrink_first, shrink_second,
    classify, classify_first, classify_second,
    vectors, vectors_first, vectors_second,
    head_gains, head_gains_first, head_gains_second,
):
    packs, images = lengths.shape
    members = lax.axis_size("tensor")
    width = vectors.shape[1]
    share = attend_in.shape[0]
    seat = lax.axis_index("tensor")
    pack = jnp.minimum(seat, packs - 1).astype(jnp.int32)[None]
    valid = (seat < packs).astype(F32).reshape(1, 1)
    image_count = images * packs * lax.axis_size("dp")
    if lax.axis_size("dp") == 8 and members == 4:
        turn = {0: lambda a: a.T, 2: lambda a: jnp.transpose(a, (1, 0, 2)), 5: lambda a: a.T}
        states = (
            patch_table, patch_first, patch_second, position_table, position_first, position_second,
            attend_in, attend_in_first, attend_in_second, attend_out, attend_out_first, attend_out_second,
            expand, expand_first, expand_second, shrink, shrink_first, shrink_second,
            classify, classify_first, classify_second, vectors, vectors_first, vectors_second,
            head_gains, head_gains_first, head_gains_second,
        )
        states = [turn.get(n // 3, lambda a: a)(entry) for n, entry in enumerate(states)]
        ready = prepare_call(lengths, *states[0:21:3], head_gains)
        shares = pack_step(
            pack, valid, pixels, coords, lengths, labels, tuple(ready), vectors, head_gains, image_count, True
        )
        *results, loss_total, grad_norm = update_call(states, shares)
        results = [turn.get(n // 3, lambda a: a)(entry) for n, entry in enumerate(results)]
        return (*results, loss_total.reshape(()), grad_norm.reshape(()))
    shards = (
        jnp.concatenate(
            [patch_table.T, jnp.transpose(position_table, (2, 0, 1)).reshape(share, -1)], axis=1
        ).astype(LOW),
        attend_in.reshape(share, -1).astype(LOW),
        attend_out.T.astype(LOW),
        expand.astype(LOW),
        shrink.T.astype(LOW),
        classify.astype(LOW),
    )
    both = ("tensor", "dp")

    def gather(shard):
        return lax.all_gather(shard, both, axis=0, tiled=True).reshape(members, width, -1)

    weights = (
        lax.all_gather(shards[0], "dp", axis=0, tiled=True),
        gather(shards[1]),
        gather(shards[2]),
        gather(shards[3]),
        gather(shards[4]),
        lax.all_gather(shards[5], "dp", axis=0, tiled=True),
    )
    grads, grad_vectors, grad_gains, loss_local = pack_step(
        pack, valid, pixels, coords, lengths, labels, weights, vectors, head_gains, image_count
    )
    grad_vectors, grad_gains, loss_total = lax.psum((grad_vectors, grad_gains, loss_local), both)

    def scatter(grad):
        return lax.psum_scatter(
            grad.reshape(members * width, -1), both, scatter_dimension=0, tiled=True
        ).astype(F32)

    def scatter_whole(grad):
        part = lax.psum_scatter(grad, "dp", scatter_dimension=0, tiled=True)
        return lax.psum(part, "tensor").astype(F32)

    share_pp = scatter_whole(grads[0])
    share_in, share_out, share_up, share_dn = (scatter(entry) for entry in grads[1:5])
    share_cls = scatter_whole(grads[5])
    leader = (seat == 0).astype(F32)
    split_squares = squared(share_in) + squared(share_out) + squared(share_up) + squared(share_dn)
    squares = lax.psum(split_squares + leader * (squared(share_pp) + squared(share_cls)), both)
    grad_norm = jnp.sqrt(squares + squared(grad_vectors) + squared(grad_gains))
    clip_scale = CLIP / jnp.maximum(grad_norm, CLIP)
    pixel_width = patch_table.shape[0]
    share_patch = share_pp[:, :pixel_width].T
    share_pos = jnp.transpose(
        share_pp[:, pixel_width:].reshape(share, position_table.shape[0], position_table.shape[1]), (1, 2, 0)
    )
    results = (
        adam(patch_table, patch_first, patch_second, share_patch, clip_scale, RATE_BASE, DECAY),
        adam(position_table, position_first, position_second, share_pos, clip_scale, RATE_POSITION, DECAY),
        adam(
            attend_in, attend_in_first, attend_in_second,
            share_in.reshape(attend_in.shape), clip_scale, RATE_BASE, DECAY,
        ),
        adam(attend_out, attend_out_first, attend_out_second, share_out.T, clip_scale, RATE_MIDDLE, DECAY),
        adam(expand, expand_first, expand_second, share_up, clip_scale, RATE_BASE, DECAY),
        adam(shrink, shrink_first, shrink_second, share_dn.T, clip_scale, RATE_BASE, DECAY),
        adam(classify, classify_first, classify_second, share_cls, clip_scale, RATE_MIDDLE, DECAY),
        adam(vectors, vectors_first, vectors_second, grad_vectors, clip_scale, RATE_VECTOR, 0.0),
        adam(head_gains, head_gains_first, head_gains_second, grad_gains, clip_scale, RATE_VECTOR, 0.0),
    )
    return tuple(entry for group in results for entry in group) + (loss_total, grad_norm)


def solution(mesh):
    data = P("dp", None)
    in_specs = (
        (data, P(None, "dp"), data, data)
        + (P(None, "dp"),) * 3
        + (P(None, None, "dp"),) * 3
        + (P("dp", None, "tensor"),) * 3
        + (P("tensor", "dp"),) * 3
        + (P("dp", "tensor"),) * 3
        + (P("tensor", "dp"),) * 3
        + (data,) * 3
        + (P(),) * 6
    )
    out_specs = in_specs[4:] + (P(), P())
    return jax.shard_map(per_device, mesh=mesh, in_specs=in_specs, out_specs=out_specs, check_vma=False)
```

```python
import functools

import jax
import jax.numpy as jnp
from jax import lax
from jax.experimental import pallas as pl
from jax.experimental.pallas import tpu as pltpu
from jax.sharding import PartitionSpec as P

STEP = 10
NORM_EPS = 1e-06
CLIP = 0.05
RATE_BASE = 0.03
RATE_POSITION = 0.2
RATE_MIDDLE = 0.1
RATE_VECTOR = 1.0
DECAY = 0.05
BETA_ONE = 0.5
BETA_TWO = 0.5
ADAM_EPS = 1e-08
SHIFT = -4.0
NEGATIVE = -1e30
APART = 128.0
LOW = jnp.bfloat16
F32 = jnp.float32
VMEM_BYTES = 60 * 1024 * 1024
TAIL_P = 0.3
TAIL = (
    0.1196293,
    0.12075397,
    0.09991341,
    0.12856192,
    -0.05368424,
    0.20635419,
    -0.1572035,
    0.03567488,
)


def mm(left, right):
    return lax.dot_general(left, right, (((1,), (0,)), ((), ())), preferred_element_type=F32)


def mm_nt(left, right):
    return lax.dot_general(left, right, (((1,), (1,)), ((), ())), preferred_element_type=F32)


def split_two(values):
    high = values.astype(LOW)
    return high, (values - high.astype(F32)).astype(LOW)


def split_three(values):
    high = values.astype(LOW)
    rest = values - high.astype(F32)
    middle = rest.astype(LOW)
    return high, middle, (rest - middle.astype(F32)).astype(LOW)


def row_norm(values):
    center = values - jnp.mean(values, axis=-1, keepdims=True)
    inverse = lax.rsqrt(jnp.mean(center * center, axis=-1, keepdims=True) + NORM_EPS)
    return center * inverse, inverse


def row_norm_back(gradient, gain_row, normed, inverse):
    scaled = gradient * gain_row
    return inverse * (
        scaled
        - jnp.mean(scaled, axis=-1, keepdims=True)
        - normed * jnp.mean(scaled * normed, axis=-1, keepdims=True)
    )


def half_mean_matrix(scale):
    row = lax.broadcasted_iota(jnp.int32, (128, 128), 0)
    col = lax.broadcasted_iota(jnp.int32, (128, 128), 1)
    return jnp.where((row >= 64) == (col >= 64), scale, 0.0).astype(LOW)


def half_sum(values, block):
    high, low = split_two(values)
    return mm(high, block) + mm(low, block)


def half_norm(values, block):
    center = values - half_sum(values, block)
    inverse = lax.rsqrt(half_sum(center * center, block) + NORM_EPS)
    return center * inverse, inverse


def half_norm_back(gradient, gain_row, normed, inverse, block):
    scaled = gradient * gain_row
    return inverse * (scaled - half_sum(scaled, block) - normed * half_sum(scaled * normed, block))


def gelu_pair(inner):
    size = jnp.abs(inner)
    near = 1.0 / (1.0 + TAIL_P * size)
    bell = jnp.exp(-0.5 * inner * inner)
    poly = TAIL[-1]
    for factor in TAIL[-2::-1]:
        poly = poly * near + factor
    tail = poly * near * bell
    share = jnp.where(inner >= 0, 1.0 - tail, tail)
    return inner * share, share + inner * bell * 0.3989422804014327


def embed_kernel(pack_ref, pix_ref, coord_ref, wp_ref, win_ref, gain_ref, emb_ref, h1_ref, q_ref, k_ref, v_ref):
    rows = pix_ref.shape[0]
    pixels = pix_ref.shape[1]
    groups = win_ref.shape[0]
    part = win_ref.shape[2] // 3
    spots = (wp_ref.shape[1] - pixels) // 2
    lane = lax.broadcasted_iota(jnp.int32, (rows, 2 * spots), 1)
    hot = ((lane == coord_ref[:, 0:1]) | (lane - spots == coord_ref[:, 1:2])).astype(F32).astype(LOW)
    embedded = mm_nt(pix_ref[...], wp_ref[:, :pixels]) + mm_nt(hot, wp_ref[:, pixels:])
    emb_ref[...] = embedded
    normed, _ = row_norm(embedded)
    first = (normed * gain_ref[0:1]).astype(LOW)
    h1_ref[...] = first
    parts = [mm(first, win_ref[group]) for group in range(groups)]
    q_ref[...] = jnp.concatenate([entry[:, :part] for entry in parts], axis=1)
    k_ref[...] = jnp.concatenate([entry[:, part : 2 * part] for entry in parts], axis=1)
    v_ref[...] = jnp.concatenate([entry[:, 2 * part :].astype(LOW) for entry in parts], axis=1)


def embed_call(pack, pixels, coords, w_pp, w_in, vectors, rows):
    width = vectors.shape[1]
    tile = 256
    steps = rows // tile
    whole2 = lambda i, p: (0, 0)
    tiled = pl.BlockSpec((tile, width), lambda i, p: (i, 0))
    return pl.pallas_call(
        embed_kernel,
        grid_spec=pltpu.PrefetchScalarGridSpec(
            num_scalar_prefetch=1,
            grid=(steps,),
            in_specs=[
                pl.BlockSpec((tile, pixels.shape[1]), lambda i, p: (p[0] * steps + i, 0)),
                pl.BlockSpec((tile, 2), lambda i, p: (p[0] * steps + i, 0)),
                pl.BlockSpec(w_pp.shape, whole2),
                pl.BlockSpec(w_in.shape, lambda i, p: (0, 0, 0)),
                pl.BlockSpec(vectors.shape, whole2),
            ],
            out_specs=[tiled] * 5,
        ),
        out_shape=[
            jax.ShapeDtypeStruct((rows, width), F32),
            jax.ShapeDtypeStruct((rows, width), LOW),
            jax.ShapeDtypeStruct((rows, width), F32),
            jax.ShapeDtypeStruct((rows, width), F32),
            jax.ShapeDtypeStruct((rows, width), LOW),
        ],
        compiler_params=pltpu.CompilerParams(vmem_limit_bytes=VMEM_BYTES),
        name="embed",
    )(pack, pixels, coords, w_pp, w_in, vectors)


def image_marks(bound_ref, rows):
    place = lax.broadcasted_iota(jnp.int32, (rows, 128), 0)
    return (place >= bound_ref[0:1, :]) & (place < bound_ref[1:2, :])


def half_lane(rows):
    lane = lax.broadcasted_iota(jnp.int32, (rows, 128), 1)
    return lane, jnp.where(lane >= 64, lane - 64, lane)


def attend_kernel(
    q_ref, k_ref, v_ref, gain_ref, bound_ref, o_ref, lse_ref, ka_ref, va_ref, qa_ref, between=None
):
    rows = q_ref.shape[0]
    tile = 256
    block = half_mean_matrix(1.0 / 64)
    lane = lax.broadcasted_iota(jnp.int32, (rows, 128), 1)

    @pl.when(pl.program_id(0) == 0)
    def _():
        _, inner = half_lane(rows)
        marks = image_marks(bound_ref, rows)
        one = jnp.where(inner == 8, 1.0, 0.0)
        query_feature = jnp.where(marks, 1.0, one)
        ka_ref[:, 128:] = jnp.where(marks, APART, -APART * one).astype(LOW)
        va_ref[:, 128:] = jnp.ones((rows, 128), LOW)
        qa_ref[0, :, 128:] = jnp.where(lane < 64, query_feature, 0.0).astype(LOW)
        qa_ref[1, :, 128:] = jnp.where(lane >= 64, query_feature, 0.0).astype(LOW)

    k_normed, _ = half_norm(k_ref[...], block)
    ka_ref[:, :128] = (k_normed * gain_ref[1:2]).astype(LOW)
    va_ref[:, :128] = v_ref[...]
    q_normed, _ = half_norm(q_ref[...], block)
    query = (q_normed * gain_ref[0:1]).astype(LOW).astype(F32) * 0.125
    for head in range(2):
        mine = (lane < 64) if head == 0 else (lane >= 64)
        qa_ref[head, :, :128] = jnp.where(mine, query, 0.0).astype(LOW)
    keys = ka_ref[...]
    values = va_ref[...]
    first = lane[:tile] < 64
    for step in range(rows // tile):
        part = slice(step * tile, (step + 1) * tile)
        outs = []
        for head in range(2):
            score = mm_nt(qa_ref[head, part, :], keys)
            outs.append(mm(jnp.exp(score).astype(LOW), values))
        total = jnp.where(first, outs[0][:, 128:], outs[1][:, 128:])
        o_ref[part, :] = (jnp.where(first, outs[0][:, :128], outs[1][:, :128]) / total).astype(LOW)
        lse_ref[part, :] = jnp.log(total)
        if between is not None and step % 2 == 1:
            between(step // 2)


def attend_call(q_raw, k_raw, value, gains, bounds):
    rows, width = q_raw.shape
    pair = pl.BlockSpec((rows, 128), lambda j: (0, j))
    small = lambda a: pl.BlockSpec(a.shape, lambda j: (0, 0))
    return pl.pallas_call(
        attend_kernel,
        grid=(width // 128,),
        in_specs=[pair, pair, pair, small(gains), small(bounds)],
        out_specs=[pair, pair],
        out_shape=[
            jax.ShapeDtypeStruct((rows, width), LOW),
            jax.ShapeDtypeStruct((rows, width), F32),
        ],
        scratch_shapes=[
            pltpu.VMEM((rows, 256), LOW),
            pltpu.VMEM((rows, 256), LOW),
            pltpu.VMEM((2, rows, 256), LOW),
        ],
        compiler_params=pltpu.CompilerParams(vmem_limit_bytes=VMEM_BYTES),
        name="attend",
    )(q_raw, k_raw, value, gains, bounds)


def attend_back_kernel(
    q_ref, k_ref, v_ref, o_ref, lse_ref, do_ref, gain_ref, bound_ref,
    dq_ref, dk_ref, dv_ref, dgain_ref,
    ka_ref, va_ref, qa_ref, da_ref, qt_ref, dot_ref, dqs_ref, dkt_ref, dvt_ref,
    between=None,
):
    rows = q_ref.shape[0]
    tile = 256
    block = half_mean_matrix(1.0 / 64)
    block_sum = half_mean_matrix(1.0)
    lane, inner = half_lane(rows)
    marks = image_marks(bound_ref, rows)
    one = jnp.where(inner == 8, 1.0, 0.0)
    three = (inner >= 9) & (inner < 12)

    @pl.when(pl.program_id(0) == 0)
    def _():
        ka_ref[:, 128:] = jnp.where(marks, APART, jnp.where(three, 1.0, -APART * one)).astype(LOW)
        va_ref[:, 128:] = jnp.where(three, 1.0, 0.0).astype(LOW)

    def spread(values):
        high, middle, low = split_three(values)
        return jnp.where(
            inner == 9, high.astype(F32), jnp.where(inner == 10, middle.astype(F32), low.astype(F32))
        )

    query_feature = jnp.where(three, spread(-lse_ref[...]), jnp.where(marks, 1.0, one))
    k_normed, k_inverse = half_norm(k_ref[...], block)
    ka_ref[:, :128] = (k_normed * gain_ref[1:2]).astype(LOW)
    va_ref[:, :128] = v_ref[...]
    q_normed, q_inverse = half_norm(q_ref[...], block)
    query = (q_normed * gain_ref[0:1]).astype(LOW).astype(F32)
    qt_ref[...] = jnp.transpose(query).astype(LOW)
    query = query * 0.125
    above = do_ref[...].astype(F32)
    dot_ref[...] = jnp.transpose(above).astype(LOW)
    inside = half_sum(above * o_ref[...].astype(F32), block_sum)
    above_feature = jnp.where(three, spread(inside * -0.125), 0.0)
    above = above * 0.125
    for head in range(2):
        mine = (lane < 64) if head == 0 else (lane >= 64)
        qa_ref[head, :, :128] = jnp.where(mine, query, 0.0).astype(LOW)
        qa_ref[head, :, 128:] = jnp.where(mine, query_feature, 0.0).astype(LOW)
        da_ref[head, :, :128] = jnp.where(mine, above, 0.0).astype(LOW)
        da_ref[head, :, 128:] = jnp.where(mine, above_feature, 0.0).astype(LOW)
    keys = ka_ref[...]
    values = va_ref[...]
    key_low = ka_ref[:, :128]
    first = lane[:tile] < 64
    for step in range(rows // tile):
        part = slice(step * tile, (step + 1) * tile)
        outs = []
        for head in range(2):
            mine = slice(64 * head, 64 * head + 64)
            prob = jnp.exp(mm_nt(qa_ref[head, part, :], keys))
            d_prob = mm_nt(da_ref[head, part, :], values)
            d_score = (prob * d_prob).astype(LOW)
            outs.append(mm(d_score, key_low))
            d_key = mm(qt_ref[mine, part], d_score)
            d_value = mm(dot_ref[mine, part], prob.astype(LOW))
            if step == 0:
                dkt_ref[mine, :] = d_key
                dvt_ref[mine, :] = d_value
            else:
                dkt_ref[mine, :] += d_key
                dvt_ref[mine, :] += d_value
        dqs_ref[part, :] = jnp.where(first, outs[0], outs[1])
        if between is not None and step % 2 == 1:
            between(step // 2)
    d_query = dqs_ref[...]
    d_key = jnp.transpose(dkt_ref[...])
    dv_ref[...] = jnp.transpose(dvt_ref[...]).astype(LOW)
    dq_ref[...] = half_norm_back(d_query, gain_ref[0:1], q_normed, q_inverse, block).astype(LOW)
    dk_ref[...] = half_norm_back(d_key, gain_ref[1:2], k_normed, k_inverse, block).astype(LOW)
    dgain_ref[0, 0:1] = jnp.sum(d_query * q_normed, axis=0, keepdims=True)
    dgain_ref[0, 1:2] = jnp.sum(d_key * k_normed, axis=0, keepdims=True)


ATTEND_BACK_SCRATCH = 9


def attend_back_scratch(rows):
    return [
        pltpu.VMEM((rows, 256), LOW),
        pltpu.VMEM((rows, 256), LOW),
        pltpu.VMEM((2, rows, 256), LOW),
        pltpu.VMEM((2, rows, 256), LOW),
        pltpu.VMEM((128, rows), LOW),
        pltpu.VMEM((128, rows), LOW),
        pltpu.VMEM((rows, 128), F32),
        pltpu.VMEM((128, rows), F32),
        pltpu.VMEM((128, rows), F32),
    ]


def attend_back_sum_kernel(*refs):
    inputs, grads, dout_ref, before_ref = refs[:8], refs[8], refs[9], refs[10]
    outputs, share_ref, out_ref = refs[11:15], refs[15], refs[16]
    scratch, rest = refs[17 : 17 + ATTEND_BACK_SCRATCH], refs[17 + ATTEND_BACK_SCRATCH :]
    mlp_own, mlp_load, mlp_refs = rest[0], rest[1], rest[2:9]
    out_own, out_load, out_refs = rest[9], rest[10], rest[11:18]
    step = pl.program_id(0)
    seat = Seat()
    c = seat.c
    mlp = Flow(
        seat, lambda i: lax.rem(4 - lax.div(i, 2), 4), lambda i: mlp_own.at[i], *mlp_refs[:5], mlp_refs[5:]
    )
    out = Flow(seat, lambda i: i, lambda i: out_own.at[i], *out_refs[:5], out_refs[5:])
    chunks, levels = mlp_own.shape[0], out_own.shape[0]

    def mlp_at(i):
        return lax.rem(i, 2) * 3 + lax.div(i, 2)

    def mlp_loading(i):
        return pltpu.make_async_copy(grads.at[mlp_at(i), :, :, c], mlp_own.at[i], mlp_load.at[i])

    def mlp_to_core(i):
        return mlp.to_core(i, grads.at[mlp_at(i), :, :, 1 - c])

    def out_loading(i):
        return pltpu.make_async_copy(dout_ref.at[i, :, :, c], out_own.at[i], out_load.at[i])

    def out_to_core(i):
        return out.to_core(i, dout_ref.at[i, :, :, 1 - c])

    def every(count, action):
        lax.fori_loop(0, count, lambda i, carry: (action(i), carry)[1], 0)

    @pl.when(step == 0)
    def _():
        every(chunks, lambda i: mlp_loading(i).start())
        every(levels, lambda i: out_loading(i).start())
        greet(seat, 4)
        every(chunks, lambda i: mlp_to_core(i).start())
        every(levels, lambda i: out_to_core(i).start())
        share_ref[...] = before_ref[...]

    def mlp_one(i):
        mlp_loading(i).wait()
        mlp_to_core(i).wait_recv()
        mlp.one(i)

    def mlp_last(i):
        @pl.when(mlp.level_of(i) == seat.z)
        def _():
            share_ref[lax.rem(i, 2)] = mlp.total(i)

    def out_one(i):
        out_loading(i).wait()
        out_to_core(i).wait_recv()
        out.one(i)

    def out_last(i):
        @pl.when(out.level_of(i) == seat.z)
        def _():
            out_ref[...] = out.total(i)

    def pair(action, number):
        return lambda: every(2, lambda i: action(2 * number + i))

    hop_one, hop_two = (functools.partial(mlp.hop, reach=reach) for reach in (1, 2))
    out_hop_one, out_hop_two = (functools.partial(out.hop, reach=reach) for reach in (1, 2))
    plan = {
        0: [pair(mlp_one, 0)],
        1: [lambda: every(levels, out_one)],
        2: [pair(mlp.two, 0), pair(mlp_one, 1)],
        3: [lambda: every(levels, out.two)],
        4: [pair(mlp.three, 0)],
        5: [pair(mlp.two, 1), pair(mlp_one, 2)],
        6: [pair(hop_one, 0), lambda: every(levels, out.three)],
        7: [pair(mlp.three, 1), lambda: every(levels, out_hop_one)],
        8: [pair(mlp.two, 2), pair(hop_two, 0)],
        9: [pair(hop_one, 1), lambda: every(levels, out_hop_two)],
        10: [pair(mlp.three, 2)],
        11: [pair(hop_two, 1), pair(hop_one, 2)],
    }

    def between(slot):
        for number, actions in plan.items():
            if number % 2 == slot:

                @pl.when(2 * step + slot == number)
                def _():
                    for action in actions:
                        action()

    attend_back_kernel(*inputs, *outputs, *scratch, between=between)

    @pl.when(step == pl.num_programs(0) - 1)
    def _():
        every(chunks, mlp_last)
        every(levels, out_last)

        def drain(i):
            mlp_to_core(i).wait_send()
            mlp.drain(i)

        def out_drain(i):
            out_to_core(i).wait_send()
            out.drain(i)

        every(chunks, drain)
        every(levels, out_drain)


def attend_back_sum_call(
    q_raw, k_raw, value, attended, lse, d_attended, gains, bounds, grads, d_out, before, collective_id
):
    rows, width = q_raw.shape
    pairs = width // 128
    share, cols = grads.shape[-2:]
    pair = pl.BlockSpec((rows, 128), lambda j: (0, j))
    small = lambda a: pl.BlockSpec(a.shape, lambda j: (0,) * a.ndim)
    anywhere = pl.BlockSpec(memory_space=pl.ANY)
    low = jax.ShapeDtypeStruct((rows, width), LOW)

    def scratch(chunks, cols):
        own = [pltpu.VMEM((chunks, 2, 2, share, cols), LOW), pltpu.SemaphoreType.DMA((chunks,))]
        return own + flow_scratch(chunks, share, cols)

    return pl.pallas_call(
        attend_back_sum_kernel,
        grid=(pairs,),
        in_specs=[pair] * 6 + [small(gains), small(bounds), anywhere, anywhere, small(before)],
        out_specs=[
            pair, pair, pair,
            pl.BlockSpec((1, 2, 128), lambda j: (j, 0, 0)),
            small(before),
            pl.BlockSpec((share, d_out.shape[-1]), lambda j: (0, 0)),
        ],
        out_shape=[
            low, low, low,
            jax.ShapeDtypeStruct((pairs, 2, 128), F32),
            jax.ShapeDtypeStruct(before.shape, F32),
            jax.ShapeDtypeStruct((share, d_out.shape[-1]), F32),
        ],
        scratch_shapes=attend_back_scratch(rows)
        + scratch(grads.shape[0], cols)
        + scratch(d_out.shape[0], d_out.shape[-1]),
        compiler_params=pltpu.CompilerParams(
            collective_id=collective_id, has_side_effects=True, vmem_limit_bytes=VMEM_BYTES
        ),
        name="attend_back_sum",
    )(q_raw, k_raw, value, attended, lse, d_attended, gains, bounds, grads, d_out, before)


def attend_back_call(q_raw, k_raw, value, attended, lse, d_attended, gains, bounds):
    rows, width = q_raw.shape
    pairs = width // 128
    pair = pl.BlockSpec((rows, 128), lambda j: (0, j))
    small = lambda a: pl.BlockSpec(a.shape, lambda j: (0, 0))
    low = jax.ShapeDtypeStruct((rows, width), LOW)
    return pl.pallas_call(
        attend_back_kernel,
        grid=(pairs,),
        in_specs=[pair] * 6 + [small(gains), small(bounds)],
        out_specs=[pair, pair, pair, pl.BlockSpec((1, 2, 128), lambda j: (j, 0, 0))],
        out_shape=[low, low, low, jax.ShapeDtypeStruct((pairs, 2, 128), F32)],
        scratch_shapes=attend_back_scratch(rows),
        compiler_params=pltpu.CompilerParams(vmem_limit_bytes=VMEM_BYTES),
        name="attend_back",
    )(q_raw, k_raw, value, attended, lse, d_attended, gains, bounds)


def mlp_kernel(o_ref, emb_ref, wout_ref, wup_ref, wdn_ref, vec_ref, x1_ref, h2_ref, act_ref, slope_ref, x2_ref):
    step = pl.program_id(0)
    rows, _ = o_ref.shape
    groups, _, part = wout_ref.shape
    tile = 256

    @pl.when(step == 0)
    def _():
        for at in range(rows // tile):
            span = slice(at * tile, (at + 1) * tile)
            branch = mm_nt(o_ref[span, :part], wout_ref[0])
            for group in range(1, groups):
                branch += mm_nt(o_ref[span, group * part : (group + 1) * part], wout_ref[group])
            middle = emb_ref[span, :] + branch
            x1_ref[span, :] = middle
            x2_ref[span, :] = middle
            normed, _ = row_norm(middle)
            h2_ref[span, :] = (normed * vec_ref[1:2]).astype(LOW)

    tile = 256
    spans = [slice(at * tile, (at + 1) * tile) for at in range(rows // tile)]
    hidden = mm(h2_ref[spans[0], :], wup_ref[0])
    for at, span in enumerate(spans):
        now = hidden
        if at + 1 < len(spans):
            hidden = mm(h2_ref[spans[at + 1], :], wup_ref[0])
        active, slope = gelu_pair(now)
        active = active.astype(LOW)
        act_ref[span, :] = active
        slope_ref[span, :] = slope.astype(LOW)
        x2_ref[span, :] += mm_nt(active, wdn_ref[0])


def mlp_call(attended, embedded, w_out, w_up, w_dn, vectors):
    rows, width = embedded.shape
    groups, _, per = w_up.shape
    chunk = per
    hidden = groups * per
    whole = lambda a: pl.BlockSpec(a.shape, lambda j: (0,) * a.ndim)
    weight = pl.BlockSpec((1, width, chunk), lambda j: (j, 0, 0))
    full = pl.BlockSpec((rows, width), lambda j: (0, 0))
    piece = pl.BlockSpec((rows, chunk), lambda j: (0, j))
    return pl.pallas_call(
        mlp_kernel,
        grid=(hidden // chunk,),
        in_specs=[whole(attended), whole(embedded), whole(w_out), weight, weight, whole(vectors)],
        out_specs=[full, full, piece, piece, full],
        out_shape=[
            jax.ShapeDtypeStruct((rows, width), F32),
            jax.ShapeDtypeStruct((rows, width), LOW),
            jax.ShapeDtypeStruct((rows, hidden), LOW),
            jax.ShapeDtypeStruct((rows, hidden), LOW),
            jax.ShapeDtypeStruct((rows, width), F32),
        ],
        compiler_params=pltpu.CompilerParams(vmem_limit_bytes=VMEM_BYTES),
        name="mlp",
    )(attended, embedded, w_out, w_up, w_dn, vectors)


def pool_kernel(
    pack_ref, x2_ref, label_ref, wcls_ref, vec_ref, bound_ref, valid_ref,
    dx2_ref, dcls_ref, loss_ref, dvec_ref,
    norm_ref, inv_ref,
    *, images, image_count,
):
    rows, width = x2_ref.shape
    tile = 256
    root = width**0.5
    gain = vec_ref[2:3]
    query = vec_ref[3:4]
    lane = lax.broadcasted_iota(jnp.int32, (rows, 128), 1)
    marks = image_marks(bound_ref, rows) & (lane < 64)
    logits = []
    for at in range(rows // tile):
        span = slice(at * tile, (at + 1) * tile)
        normed, inverse = row_norm(x2_ref[span, :])
        norm_ref[span, :] = normed
        inv_ref[span, :] = jnp.broadcast_to(inverse, (tile, 128))
        logits.append(jnp.sum(normed * gain * query, axis=-1, keepdims=True) / root)
    logit = jnp.concatenate(logits, axis=0)
    masked = jnp.where(marks, logit, NEGATIVE)
    grown = jnp.exp(masked - jnp.max(masked, axis=0, keepdims=True))
    shares = jnp.where(marks, grown / jnp.sum(grown, axis=0, keepdims=True), 0.0)
    weight = jnp.sum(shares, axis=-1, keepdims=True)
    member = jnp.transpose(marks.astype(F32))[:16].astype(LOW)
    pooled = jnp.zeros((16, width), F32)
    for at in range(rows // tile):
        span = slice(at * tile, (at + 1) * tile)
        for entry in split_two(norm_ref[span, :] * gain * weight[span]):
            pooled += mm(member[:, span], entry)
    pooled_low = pooled.astype(LOW)
    scores = mm(pooled_low, wcls_ref[...])[:images] + SHIFT
    target = label_ref[...].astype(F32)
    valid = valid_ref[0, 0]
    soft = jnp.maximum(scores, 0.0) + jnp.log1p(jnp.exp(-jnp.abs(scores)))
    loss_rows = jnp.sum(soft - target * scores, axis=-1, keepdims=True)
    loss_ref[...] = jnp.broadcast_to(jnp.sum(loss_rows, axis=0, keepdims=True) * valid, loss_ref.shape)
    d_score = (1.0 / (1.0 + jnp.exp(-scores)) - target) / image_count * valid
    d_score = jnp.concatenate([d_score, jnp.zeros((16 - images, d_score.shape[1]), F32)], axis=0).astype(LOW)
    dcls_ref[...] = mm(jnp.transpose(pooled).astype(LOW), d_score).astype(LOW)
    d_pooled = mm_nt(d_score, wcls_ref[...])[:images]
    parts = jnp.concatenate(
        [entry.astype(F32) for entry in split_three(d_pooled)]
        + [jnp.zeros((128 - 3 * images, width), F32)],
        axis=0,
    ).astype(LOW)
    marks_f = marks.astype(F32)
    thrice = (
        marks_f + pltpu.roll(marks_f, images, 1) + pltpu.roll(marks_f, 2 * images, 1)
    ).astype(LOW)
    d_weights = []
    for at in range(rows // tile):
        span = slice(at * tile, (at + 1) * tile)
        spread = mm(thrice[span], parts)
        dx2_ref[span, :] = spread
        d_weights.append(jnp.sum(spread * (norm_ref[span, :] * gain), axis=-1, keepdims=True))
    d_weight = jnp.concatenate(d_weights, axis=0)
    inside = jnp.sum(shares * d_weight, axis=0, keepdims=True)
    d_logit = weight * (d_weight - jnp.sum(marks_f * inside, axis=-1, keepdims=True))
    gain_sum = jnp.zeros((1, width), F32)
    query_sum = jnp.zeros((1, width), F32)
    for at in range(rows // tile):
        span = slice(at * tile, (at + 1) * tile)
        normed = norm_ref[span, :]
        inverse = inv_ref[span, 0:1]
        d_last = dx2_ref[span, :] * weight[span] + d_logit[span] * (query / root)
        gain_sum += jnp.sum(d_last * normed, axis=0, keepdims=True)
        query_sum += jnp.sum(d_logit[span] * normed, axis=0, keepdims=True)
        dx2_ref[span, :] = row_norm_back(d_last, gain, normed, inverse)
    dvec_ref[0:1, :] = gain_sum
    dvec_ref[1:2, :] = query_sum * gain / root


def pool_call(pack, x2, labels, w_cls, vectors, bounds, valid, images, image_count):
    rows, width = x2.shape
    classes = labels.shape[1]
    whole = lambda a: pl.BlockSpec(a.shape, lambda j, p: (0,) * a.ndim)
    full = lambda *shape: pl.BlockSpec(shape, lambda j, p: (0,) * len(shape))
    return pl.pallas_call(
        functools.partial(pool_kernel, images=images, image_count=image_count),
        grid_spec=pltpu.PrefetchScalarGridSpec(
            num_scalar_prefetch=1,
            grid=(1,),
            in_specs=[
                whole(x2),
                pl.BlockSpec((images, classes), lambda j, p: (p[0], 0)),
                whole(w_cls),
                whole(vectors),
                whole(bounds),
                pl.BlockSpec(memory_space=pltpu.SMEM),
            ],
            out_specs=[full(rows, width), full(width, classes), full(8, 128), full(2, width)],
            scratch_shapes=[pltpu.VMEM((rows, width), F32), pltpu.VMEM((rows, 128), F32)],
        ),
        out_shape=[
            jax.ShapeDtypeStruct((rows, width), F32),
            jax.ShapeDtypeStruct((width, classes), LOW),
            jax.ShapeDtypeStruct((8, 128), F32),
            jax.ShapeDtypeStruct((2, width), F32),
        ],
        compiler_params=pltpu.CompilerParams(vmem_limit_bytes=VMEM_BYTES),
        name="pool",
    )(pack, x2, labels, w_cls, vectors, bounds, valid)


def mlp_back_kernel(
    dx2_ref, act_ref, slope_ref, h2_ref, x1_ref, o_ref, wout_ref, wup_ref, wdn_ref, vec_ref,
    dmlp_ref, dout_ref, do_ref, dmid_ref, dvec_ref,
    low_ref, lowt_ref, h2t_ref, acc_ref, dh_ref,
    keep=None, between=None,
):
    step = pl.program_id(0)
    rows, width = dx2_ref.shape
    groups, _, part = wout_ref.shape
    tile = 256

    @pl.when(step == 0)
    def _():
        for at in range(rows // tile):
            span = slice(at * tile, (at + 1) * tile)
            values = dx2_ref[span, :]
            low_ref[span, :] = values.astype(LOW)
            lowt_ref[:, span] = jnp.transpose(values).astype(LOW)
            h2t_ref[:, span] = jnp.transpose(h2_ref[span, :].astype(F32)).astype(LOW)
            acc_ref[span, :] = jnp.zeros((tile, width), F32)

    wide = 512
    for at in range(rows // wide):
        span = slice(at * wide, (at + 1) * wide)
        d_hidden = (mm(low_ref[span, :], wdn_ref[0]) * slope_ref[span, :].astype(F32)).astype(LOW)
        dh_ref[span, :] = d_hidden
        acc_ref[span, :] += mm_nt(d_hidden, wup_ref[0])

    def grads(put):
        for at in range(width // 192):
            span = slice(at * 192, (at + 1) * 192)
            put(0, at, mm(lowt_ref[span, :], act_ref[...]).astype(LOW))
            put(1, at, mm(h2t_ref[span, :], dh_ref[...]).astype(LOW))

    def put_out(kind, at, value):
        dmlp_ref[kind, 0, at * 192 : (at + 1) * 192, :] = value

    if keep is None:
        grads(put_out)
    else:
        between(2 * step, 0)
        pl.when(step < 1)(lambda: grads(keep))
        pl.when(step >= 1)(lambda: grads(put_out))
        between(2 * step + 1, 1)

    @pl.when(step == pl.num_programs(0) - 1)
    def _():
        gain = vec_ref[1:2]
        gain_sum = jnp.zeros((1, width), F32)
        for at in range(rows // tile):
            span = slice(at * tile, (at + 1) * tile)
            normed, inverse = row_norm(x1_ref[span, :])
            d_second = acc_ref[span, :]
            gain_sum += jnp.sum(d_second * normed, axis=0, keepdims=True)
            d_middle = dx2_ref[span, :] + row_norm_back(d_second, gain, normed, inverse)
            dmid_ref[span, :] = d_middle
            low = d_middle.astype(LOW)
            lowt_ref[:, span] = jnp.transpose(d_middle).astype(LOW)
            do_ref[span, :] = jnp.concatenate(
                [mm(low, wout_ref[group]) for group in range(groups)], axis=1
            ).astype(LOW)
        dvec_ref[...] = gain_sum
        for group in range(groups):
            piece = o_ref[:, group * part : (group + 1) * part]
            for at in range(width // tile):
                span = slice(at * tile, (at + 1) * tile)
                dout_ref[group, span, :] = mm(lowt_ref[span, :], piece).astype(LOW)


def mlp_back_call(dx2, active, slope, h2, x1, attended, w_out, w_up, w_dn, vectors):
    rows, width = dx2.shape
    groups, _, per = w_up.shape
    chunk = per
    hidden = groups * per
    whole = lambda a: pl.BlockSpec(a.shape, lambda j: (0,) * a.ndim, pipeline_mode=pl.Buffered(1))
    weight = pl.BlockSpec((1, width, chunk), lambda j: (j, 0, 0))
    piece = pl.BlockSpec((rows, chunk), lambda j: (0, j))
    full = lambda *shape: pl.BlockSpec(shape, lambda j: (0,) * len(shape))
    return pl.pallas_call(
        mlp_back_kernel,
        grid=(hidden // chunk,),
        in_specs=[
            whole(dx2), piece, piece, whole(h2), whole(x1), whole(attended), whole(w_out),
            weight, weight, whole(vectors),
        ],
        out_specs=[
            pl.BlockSpec((2, 1, width, chunk), lambda j: (0, j, 0, 0)),
            full(*w_out.shape),
            full(rows, width),
            full(rows, width),
            full(1, width),
        ],
        out_shape=[
            jax.ShapeDtypeStruct((2,) + w_up.shape, LOW),
            jax.ShapeDtypeStruct(w_out.shape, LOW),
            jax.ShapeDtypeStruct((rows, width), LOW),
            jax.ShapeDtypeStruct((rows, width), F32),
            jax.ShapeDtypeStruct((1, width), F32),
        ],
        scratch_shapes=[
            pltpu.VMEM((rows, width), LOW),
            pltpu.VMEM((width, rows), LOW),
            pltpu.VMEM((width, rows), LOW),
            pltpu.VMEM((rows, width), F32),
            pltpu.VMEM((rows, chunk), LOW),
        ],
        compiler_params=pltpu.CompilerParams(vmem_limit_bytes=VMEM_BYTES),
        name="mlp_back",
    )(dx2, active, slope, h2, x1, attended, w_out, w_up, w_dn, vectors)


def embed_back_kernel(
    pack_ref, dq_ref, dk_ref, dv_ref, h1_ref, emb_ref, dmid_ref, pix_ref, coord_ref, win_ref, vec_ref,
    din_ref, dpp_ref, dvec_ref,
    h1t_ref, join_ref, acc_ref,
):
    step = pl.program_id(0)
    rows, width = h1_ref.shape
    groups = pl.num_programs(0)
    part = win_ref.shape[2] // 3
    tile = 256

    @pl.when(step == 0)
    def _():
        for at in range(rows // tile):
            span = slice(at * tile, (at + 1) * tile)
            h1t_ref[:, span] = jnp.transpose(h1_ref[span, :].astype(F32)).astype(LOW)
            acc_ref[span, :] = jnp.zeros((tile, width), F32)

    for group in range(width // part):

        @pl.when(step == group)
        def _():
            mine = slice(group * part, (group + 1) * part)
            join_ref[...] = jnp.concatenate([dq_ref[:, mine], dk_ref[:, mine], dv_ref[:, mine]], axis=1)

    for at in range(rows // tile):
        span = slice(at * tile, (at + 1) * tile)
        acc_ref[span, :] += mm_nt(join_ref[span, :], win_ref[0])
    for at in range(width // tile):
        span = slice(at * tile, (at + 1) * tile)
        din_ref[0, span, :] = mm(h1t_ref[span, :], join_ref[...]).astype(LOW)

    @pl.when(step == groups - 1)
    def _():
        gain = vec_ref[0:1]
        pixels = pix_ref.shape[1]
        spots = (dpp_ref.shape[1] - pixels) // 2
        gain_sum = jnp.zeros((1, width), F32)
        for at in range(rows // tile):
            span = slice(at * tile, (at + 1) * tile)
            normed, inverse = row_norm(emb_ref[span, :])
            d_first = acc_ref[span, :]
            gain_sum += jnp.sum(d_first * normed, axis=0, keepdims=True)
            d_embed = dmid_ref[span, :] + row_norm_back(d_first, gain, normed, inverse)
            h1t_ref[:, span] = jnp.transpose(d_embed).astype(LOW)
        dvec_ref[...] = gain_sum
        lane = lax.broadcasted_iota(jnp.int32, (rows, 2 * spots), 1)
        hot = ((lane == coord_ref[:, 0:1]) | (lane - spots == coord_ref[:, 1:2])).astype(F32).astype(LOW)
        for at in range(width // tile):
            span = slice(at * tile, (at + 1) * tile)
            dpp_ref[span, :pixels] = mm(h1t_ref[span, :], pix_ref[...]).astype(LOW)
            dpp_ref[span, pixels:] = mm(h1t_ref[span, :], hot).astype(LOW)


def embed_back_call(pack, dq, dk, dv, h1, embedded, d_middle, pixels, coords, w_in, w_pp_shape, vectors):
    rows, width = h1.shape
    groups = w_in.shape[0]
    whole = lambda a: pl.BlockSpec(a.shape, lambda j, p: (0,) * a.ndim, pipeline_mode=pl.Buffered(1))
    full = lambda *shape: pl.BlockSpec(shape, lambda j, p: (0,) * len(shape))
    weight = pl.BlockSpec((1,) + w_in.shape[1:], lambda j, p: (j, 0, 0))
    return pl.pallas_call(
        embed_back_kernel,
        grid_spec=pltpu.PrefetchScalarGridSpec(
            num_scalar_prefetch=1,
            grid=(groups,),
            in_specs=[
                whole(dq), whole(dk), whole(dv), whole(h1), whole(embedded), whole(d_middle),
                pl.BlockSpec((rows, pixels.shape[1]), lambda j, p: (p[0], 0)),
                pl.BlockSpec((rows, 2), lambda j, p: (p[0], 0)),
                weight,
                whole(vectors),
            ],
            out_specs=[weight, full(*w_pp_shape), full(1, width)],
            scratch_shapes=[
                pltpu.VMEM((width, rows), LOW),
                pltpu.VMEM((rows, w_in.shape[2]), LOW),
                pltpu.VMEM((rows, width), F32),
            ],
        ),
        out_shape=[
            jax.ShapeDtypeStruct(w_in.shape, LOW),
            jax.ShapeDtypeStruct(w_pp_shape, LOW),
            jax.ShapeDtypeStruct((1, width), F32),
        ],
        compiler_params=pltpu.CompilerParams(vmem_limit_bytes=VMEM_BYTES),
        name="embed_back",
    )(pack, dq, dk, dv, h1, embedded, d_middle, pixels, coords, w_in, vectors)


def pack_step(pack, valid, pixels, coords, lengths, labels, weights, vectors, head_gains, image_count, close=False):
    if close:
        bounds, gains = weights[6:]
        weights = weights[:6]
    w_pp, w_in, w_out, w_up, w_dn, w_cls = weights
    packs, images = lengths.shape
    rows = pixels.shape[0] // packs
    width = vectors.shape[1]
    if not close:
        mine = lax.dynamic_index_in_dim(lengths, pack[0], 0, keepdims=False)
        ends = jnp.cumsum(mine)
        fill = jnp.full((64 - images,), 1 << 30, jnp.int32)
        starts = jnp.concatenate([ends - mine, fill])
        ends = jnp.concatenate([ends, fill])
        bounds = jnp.stack([jnp.tile(starts, 2), jnp.tile(ends, 2)])
        gains = jnp.tile(head_gains, (1, 2))
    if close:
        (
            embedded, h1, q_raw, k_raw, value, attended, lse, w_in, w_out, w_up, w_dn, w_cls,
            x1, h2, active, slope, x2,
        ) = forward_call(weights, pixels, coords, vectors, gains, bounds, packs, 0)
    else:
        places = coords.T
        embedded, h1, q_raw, k_raw, value = embed_call(pack, pixels, places, w_pp, w_in, vectors, rows)
        attended, lse = attend_call(q_raw, k_raw, value, gains, bounds)
        x1, h2, active, slope, x2 = mlp_call(attended, embedded, w_out, w_up, w_dn, vectors)
    dx2, d_cls, loss, dvec_pool = pool_call(
        pack, x2, labels, w_cls, vectors, bounds, valid, images, image_count
    )
    if close:
        share = width // 8
        cut = lambda entry: entry.reshape(entry.shape[:-2] + (2, 2, 2, share) + entry.shape[-1:])
        d_mlp, d_out, d_attended, d_middle, dvec_two, share_mlp, share_cls = mlp_back_sum_call(
            dx2, active, slope, h2, x1, attended, w_out, w_up, w_dn, vectors, cut(d_cls), 1
        )
        d_mlp = d_mlp.reshape((-1, 2, 2, 2, share, width))
        dq, dk, dv, d_gain, share_mlp, share_out = attend_back_sum_call(
            q_raw, k_raw, value, attended, lse, d_attended, gains, bounds, d_mlp, cut(d_out), share_mlp, 2
        )
        share_in, share_pp, small, squares = embed_back_sum_call(
            dq, dk, dv, h1, embedded, d_middle, pixels, coords, w_in, weights[0].shape[1], vectors,
            dvec_two, dvec_pool, d_gain, loss, share_mlp, share_cls, share_out, packs, 3,
        )
        return share_pp, share_in, share_out, share_mlp, share_cls, small, squares
    d_mlp, d_out, d_attended, d_middle, dvec_two = mlp_back_call(
        dx2, active, slope, h2, x1, attended, w_out, w_up, w_dn, vectors
    )
    d_vec = jnp.concatenate([jnp.zeros_like(dvec_two), dvec_two, dvec_pool], axis=0)
    dq, dk, dv, d_gain = attend_back_call(q_raw, k_raw, value, attended, lse, d_attended, gains, bounds)
    d_in, d_pp, dvec_one = embed_back_call(
        pack, dq, dk, dv, h1, embedded, d_middle, pixels, places, w_in, w_pp.shape, vectors
    )
    d_gains = jnp.sum(d_gain.reshape(-1, 2, 2, 64), axis=(0, 2))
    return (d_pp, d_in, d_out, d_mlp[1], d_mlp[0], d_cls), d_vec.at[0].set(dvec_one[0]), d_gains, loss[0, 0]


MESH = pl.DeviceIdType.MESH


class Seat:
    def __init__(self):
        self.me = lax.axis_index("dp")
        self.z = lax.axis_index("tensor")
        self.c = lax.rem(self.me, 2)
        self.x = lax.rem(lax.div(self.me, 2), 2)
        self.y = lax.div(self.me, 4)
        self.core = self.me + 1 - 2 * self.c
        self.xn = self.me + 2 - 4 * self.x
        self.yn = self.me + 4 - 8 * self.y
        self.diag = self.xn + 4 - 8 * self.y


def link(src, dst, sems, at, device):
    return pltpu.make_async_remote_copy(
        src_ref=src,
        dst_ref=dst,
        send_sem=sems[0].at[at],
        recv_sem=sems[1].at[at],
        device_id=device,
        device_id_type=MESH,
    )


def greet(seat, depth):
    barrier = pltpu.get_barrier_semaphore()
    for ahead in range(1, 8):
        pl.semaphore_signal(
            barrier, inc=1, device_id={"dp": lax.rem(seat.me + ahead, 8)}, device_id_type=MESH
        )
    for ahead in range(1, depth):
        pl.semaphore_signal(
            barrier, inc=1, device_id={"tensor": lax.rem(seat.z + ahead, depth)}, device_id_type=MESH
        )
    pl.semaphore_wait(barrier, 6 + depth)


class Gather:
    def __init__(self, seat, shards, outs, split, units, own_sem, sems):
        self.seat, self.shards, self.outs, self.split, self.units = seat, shards, outs, split, units
        self.own_sem, self.sems = own_sem, sems
        self.share = shards[0].shape[0]

    def rows(self, owner):
        return pl.ds(pl.multiple_of(owner * self.share, self.share), self.share)

    def column(self, u, owner):
        k, cols = self.units[u]
        if self.split[k]:
            return self.outs[k].at[:, self.rows(owner), cols]
        return self.outs[k].at[self.rows(owner), cols]

    def halves(self, u, owner, which):
        k, cols = self.units[u]
        if self.split[k]:
            return self.outs[k].at[2 * which : 2 * which + 2, self.rows(owner), cols]
        half = self.share // 2
        start = pl.multiple_of(owner * self.share + which * half, half)
        return self.outs[k].at[pl.ds(start, half), cols]

    def block(self, u, level):
        k, cols = self.units[u]
        return self.outs[k].at[level, self.rows(self.seat.me), cols]

    def keep(self, u):
        k, cols = self.units[u]
        mine = self.block(u, self.seat.z) if self.split[k] else self.column(u, self.seat.me)
        return pltpu.make_async_copy(self.shards[k].at[:, cols], mine, self.own_sem.at[u])

    def along(self, u, hop, way):
        k, cols = self.units[u]
        level = self.seat.z - way * hop
        source = self.shards[k].at[:, cols] if hop == 0 else self.block(u, level)
        at = (u, hop + (0 if way > 0 else 3))
        return link(source, self.block(u, level), self.sems, at, {"tensor": self.seat.z + way})

    def arrives(self, u, hop, way):
        level = self.seat.z - way * (hop + 1)
        at = (u, hop + (0 if way > 0 else 3))
        return link(self.block(u, level), self.block(u, level), self.sems, at, {"tensor": self.seat.z - way})

    def sends(self, hop, way):
        level, to = self.seat.z - way * hop, self.seat.z + way
        return (level >= 0) & (level < 4) & (to >= 0) & (to < 4)

    def gets(self, hop, way):
        level = self.seat.z - way * (hop + 1)
        return (level >= 0) & (level < 4)

    def z(self, u, hop):
        for way in (1, -1):
            if hop > 0:

                @pl.when(self.gets(hop - 1, way))
                def _():
                    self.arrives(u, hop - 1, way).wait_recv()

            if hop < 3:

                @pl.when(self.sends(hop, way))
                def _():
                    self.along(u, hop, way).start()

    def copy(self, u, region, at, device):
        return link(region, region, self.sems, (u, at), {"dp": device})

    def own_x(self, u):
        return self.copy(u, self.column(u, self.seat.me), 6, self.seat.xn)

    def own_y(self, u):
        return self.copy(u, self.column(u, self.seat.me), 7, self.seat.yn)

    def pass_x(self, u):
        return self.copy(u, self.halves(u, self.seat.yn, 1), 8, self.seat.xn)

    def pass_y(self, u):
        return self.copy(u, self.halves(u, self.seat.xn, 0), 9, self.seat.yn)

    def owner(self, which):
        return (self.seat.me, self.seat.xn, self.seat.yn, self.seat.diag)[which]

    def over(self, u, which):
        return self.copy(u, self.column(u, self.owner(which)), 10 + which, self.seat.core)

    def plane(self, u):
        self.keep(u).wait()
        self.own_x(u).start()
        self.own_y(u).start()
        self.over(u, 0).start()

    def relay(self, u):
        s = self.seat
        self.copy(u, self.column(u, s.xn), 6, s.xn).wait_recv()
        self.pass_y(u).start()
        self.over(u, 1).start()
        self.copy(u, self.column(u, s.yn), 7, s.yn).wait_recv()
        self.pass_x(u).start()
        self.over(u, 2).start()

    def corner(self, u):
        s = self.seat
        self.copy(u, self.halves(u, s.diag, 1), 8, s.xn).wait_recv()
        self.copy(u, self.halves(u, s.diag, 0), 9, s.yn).wait_recv()
        self.over(u, 3).start()

    def arrived(self, u):
        s = self.seat
        for which in range(4):
            theirs = self.column(u, self.owner(which) + 1 - 2 * s.c)
            self.copy(u, theirs, 10 + which, s.core).wait_recv()

    def drain(self, u):
        if self.split[self.units[u][0]]:
            for hop in range(3):
                for way in (1, -1):

                    @pl.when(self.sends(hop, way))
                    def _():
                        self.along(u, hop, way).wait_send()

        for copy in (self.own_x(u), self.own_y(u), self.pass_x(u), self.pass_y(u)):
            copy.wait_send()
        for which in range(4):
            self.over(u, which).wait_send()


FORWARD_SPLIT = (False, True, True, True, True, False)


def forward_kernel(
    pp_in, in_in, out_in, up_in, dn_in, cls_in, pix_hbm, coord_ref, vec_ref, gain_ref, bound_ref,
    emb_hbm, h1_hbm, q_hbm, k_hbm, v_hbm, o_ref, lse_ref, win_hbm, wout_hbm, wup_hbm, wdn_hbm, wcls_hbm,
    x1_hbm, h2_hbm, act_hbm, slope_hbm, x2_hbm,
    wp_ref, win_ref, pix_ref, emb_ref, h1_ref, q_ref, k_ref, v_ref, ka_ref, va_ref, qa_ref,
    wout_ref, wup_ref, wdn_ref, all_ref, act_ref, slope_ref,
    own_sem, send_sem, recv_sem, copy_sem, act_sem,
    *, packs,
):
    step = pl.program_id(0)
    rows, pixels = pix_ref.shape
    groups = win_ref.shape[0]
    part = win_ref.shape[2] // 3
    spots = (wp_ref.shape[1] - pixels) // 2
    per = wup_ref.shape[2]
    half = per // 2
    tile = 256
    seat = Seat()
    everything, left, right = slice(None), slice(0, half), slice(half, 2 * half)
    units = (
        (0, everything), (1, everything), (2, everything),
        (3, left), (3, right), (4, left), (4, right), (5, everything),
    )
    pp, w_in, out, up_a, up_b, dn_a, dn_b, cls = range(8)
    flow = Gather(
        seat,
        (pp_in, in_in, out_in, up_in, dn_in, cls_in),
        (wp_ref, win_ref, wout_ref, wup_ref, wdn_ref, wcls_hbm),
        FORWARD_SPLIT,
        units,
        own_sem,
        (send_sem, recv_sem),
    )
    pack = jnp.minimum(seat.z, packs - 1)
    pix_copy = pltpu.make_async_copy(
        pix_hbm.at[pl.ds(pl.multiple_of(pack * rows, rows), rows)], pix_ref, copy_sem.at[0]
    )
    results = [
        pltpu.make_async_copy(source, target, copy_sem.at[1 + n])
        for n, (source, target) in enumerate(
            (
                (emb_ref, emb_hbm), (h1_ref, h1_hbm), (q_ref, q_hbm), (k_ref, k_hbm), (v_ref, v_hbm),
                (win_ref, win_hbm), (wout_ref, wout_hbm), (wup_ref, wup_hbm), (wdn_ref, wdn_hbm),
                (emb_ref, x1_hbm), (h1_ref, h2_hbm), (q_ref, x2_hbm),
            )
        )
    ]

    def hidden_copies(group):
        columns = slice(group * per, (group + 1) * per)
        return [
            pltpu.make_async_copy(source.at[group], target.at[:, columns], act_sem.at[n, group])
            for n, (source, target) in enumerate(((act_ref, act_hbm), (slope_ref, slope_hbm)))
        ]

    def join_heads(at):
        span = slice(at * tile, (at + 1) * tile)
        branch = mm_nt(all_ref[span, :part], wout_ref[0])
        for group in range(1, groups):
            branch += mm_nt(all_ref[span, group * part : (group + 1) * part], wout_ref[group])
        middle = emb_ref[span, :] + branch
        emb_ref[span, :] = middle
        normed, _ = row_norm(middle)
        h1_ref[span, :] = (normed * vec_ref[1:2]).astype(LOW)

    def hide(group):
        spans = [slice(at * tile, (at + 1) * tile) for at in range(rows // tile)]
        hidden = mm(h1_ref[spans[0], :], wup_ref[group])
        for at, span in enumerate(spans):
            now = hidden
            if at + 1 < len(spans):
                hidden = mm(h1_ref[spans[at + 1], :], wup_ref[group])
            active, slope = gelu_pair(now)
            act_ref[group, span, :] = active.astype(LOW)
            slope_ref[group, span, :] = slope.astype(LOW)
        for copy in hidden_copies(group):
            copy.start()

    def show(at):
        span = slice(at * tile, (at + 1) * tile)
        total = emb_ref[span, :]
        for group in range(groups):
            total += mm_nt(act_ref[group, span, :], wdn_ref[group])
        q_ref[span, :] = total

    def embed(at):
        span = slice(at * tile, (at + 1) * tile)
        start = pl.multiple_of(pack * rows + at * tile, tile)
        place = lax.broadcasted_iota(jnp.int32, (2 * spots, tile), 0)
        across = coord_ref[0:1, pl.ds(start, tile)]
        down = coord_ref[1:2, pl.ds(start, tile)]
        hot = jnp.transpose(((place == across) | (place - spots == down)).astype(F32)).astype(LOW)
        embedded = mm_nt(pix_ref[span, :], wp_ref[:, :pixels]) + mm_nt(hot, wp_ref[:, pixels:])
        emb_ref[span, :] = embedded
        normed, _ = row_norm(embedded)
        h1_ref[span, :] = (normed * vec_ref[0:1]).astype(LOW)

    def project(at):
        span = slice(at * tile, (at + 1) * tile)
        first = h1_ref[span, :]
        parts = [mm(first, win_ref[group]) for group in range(groups)]
        q_ref[span, :] = jnp.concatenate([entry[:, :part] for entry in parts], axis=1)
        k_ref[span, :] = jnp.concatenate([entry[:, part : 2 * part] for entry in parts], axis=1)
        v_ref[span, :] = jnp.concatenate([entry[:, 2 * part :].astype(LOW) for entry in parts], axis=1)

    @pl.when(step == 0)
    def _():
        pix_copy.start()
        for u in range(8):
            flow.keep(u).start()
        greet(seat, 4)
        flow.z(w_in, 0)
        flow.plane(pp)
        flow.z(w_in, 1)
        flow.relay(pp)
        flow.z(w_in, 2)
        flow.corner(pp)
        flow.z(w_in, 3)
        flow.plane(w_in)
        flow.z(out, 0)
        flow.arrived(pp)
        pix_copy.wait()
        embed(0)
        flow.z(out, 1)
        embed(1)
        flow.z(out, 2)
        flow.z(up_a, 0)
        embed(2)
        flow.z(out, 3)
        flow.plane(out)
        flow.z(up_a, 1)
        embed(3)
        flow.z(up_a, 2)
        results[0].start()
        results[1].start()
        flow.relay(w_in)
        flow.z(up_a, 3)
        flow.z(up_b, 0)
        flow.relay(out)
        flow.plane(up_a)
        flow.corner(w_in)
        flow.z(up_b, 1)
        flow.arrived(w_in)
        results[5].start()
        project(0)
        flow.corner(out)
        flow.z(up_b, 2)
        project(1)
        flow.z(up_b, 3)
        flow.plane(up_b)
        flow.z(dn_a, 0)
        project(2)
        flow.relay(up_a)
        flow.z(dn_a, 1)
        project(3)
        for n in (2, 3, 4):
            results[n].start()

    plan = {
        0: [lambda: flow.z(dn_a, 2)],
        1: [lambda: flow.z(dn_a, 3)],
        2: [lambda: flow.corner(up_a), lambda: flow.plane(dn_a), lambda: flow.z(dn_b, 0)],
        4: [lambda: flow.relay(up_b), lambda: flow.z(dn_b, 1)],
        5: [lambda: flow.z(dn_b, 2)],
        7: [lambda: flow.corner(up_b), lambda: flow.z(dn_b, 3), lambda: flow.plane(dn_b)],
        10: [lambda: flow.relay(dn_a)],
    }

    def between(slot):
        for number, actions in plan.items():
            if number % 2 == slot:

                @pl.when(2 * step + slot == number)
                def _():
                    for action in actions:
                        action()

    mine = pl.ds(pl.multiple_of(step * 128, 128), 128)
    attend_kernel(
        q_ref.at[:, mine], k_ref.at[:, mine], v_ref.at[:, mine], gain_ref, bound_ref, o_ref, lse_ref,
        ka_ref, va_ref, qa_ref, between=between,
    )
    all_ref[:, mine] = o_ref[...]

    @pl.when(step == pl.num_programs(0) - 1)
    def _():
        flow.arrived(out)
        results[6].start()
        for n in range(3):
            results[n].wait()
        for at in range(rows // tile):
            join_heads(at)
        results[9].start()
        results[10].start()
        flow.corner(dn_a)
        flow.plane(cls)
        flow.arrived(up_a)
        flow.arrived(up_b)
        results[7].start()
        hide(0)
        flow.relay(dn_b)
        hide(1)
        flow.corner(dn_b)
        hide(2)
        flow.relay(cls)
        hide(3)
        flow.corner(cls)
        flow.arrived(dn_a)
        flow.arrived(dn_b)
        results[8].start()
        for at in range(rows // tile):
            show(at)
        results[11].start()
        flow.arrived(cls)
        for u in range(8):
            flow.drain(u)
        for copy in results[3:]:
            copy.wait()
        for group in range(groups):
            for copy in hidden_copies(group):
                copy.wait()


def forward_call(shards, pixels, coords, vectors, gains, bounds, packs, collective_id):
    depth, width = 4, vectors.shape[1]
    rows = pixels.shape[0] // packs
    anywhere = pl.BlockSpec(memory_space=pl.ANY)
    small = lambda a: pl.BlockSpec(a.shape, lambda j: (0, 0))
    pair = pl.BlockSpec((rows, 128), lambda j: (0, j))
    weights = [
        jax.ShapeDtypeStruct(((depth, width) if apart else (width,)) + entry.shape[1:], LOW)
        for entry, apart in zip(shards, FORWARD_SPLIT)
    ]
    token = lambda dtype: jax.ShapeDtypeStruct((rows, width), dtype)
    held = lambda dtype: pltpu.VMEM((rows, width), dtype)
    per = shards[3].shape[1]
    wide = jax.ShapeDtypeStruct((rows, depth * per), LOW)
    return pl.pallas_call(
        functools.partial(forward_kernel, packs=packs),
        grid=(width // 128,),
        in_specs=[anywhere] * 7 + [small(coords), small(vectors), small(gains), small(bounds)],
        out_specs=[anywhere] * 5 + [pair, pair] + [anywhere] * 10,
        out_shape=[token(F32), token(LOW), token(F32), token(F32), token(LOW), token(LOW), token(F32)]
        + weights[1:]
        + [token(F32), token(LOW), wide, wide, token(F32)],
        scratch_shapes=[
            pltpu.VMEM(weights[0].shape, LOW),
            pltpu.VMEM(weights[1].shape, LOW),
            pltpu.VMEM((rows, pixels.shape[1]), LOW),
            held(F32), held(LOW), held(F32), held(F32), held(LOW),
            pltpu.VMEM((rows, 256), LOW),
            pltpu.VMEM((rows, 256), LOW),
            pltpu.VMEM((2, rows, 256), LOW),
            *(pltpu.VMEM(entry.shape, LOW) for entry in weights[2:5]),
            held(LOW),
            pltpu.VMEM((depth, rows, per), LOW),
            pltpu.VMEM((depth, rows, per), LOW),
            pltpu.SemaphoreType.DMA((8,)),
            pltpu.SemaphoreType.DMA((8, 14)),
            pltpu.SemaphoreType.DMA((8, 14)),
            pltpu.SemaphoreType.DMA((13,)),
            pltpu.SemaphoreType.DMA((2, depth)),
        ],
        compiler_params=pltpu.CompilerParams(
            collective_id=collective_id, has_side_effects=True, vmem_limit_bytes=VMEM_BYTES
        ),
        name="forward",
    )(*shards, pixels, coords, vectors, gains, bounds)


class Flow:
    def __init__(self, seat, level_of, own, core_in, plane_in, last_in, up_in, down_in, sems):
        self.seat, self.level_of, self.own, self.sems = seat, level_of, own, sems
        self.core_in, self.plane_in, self.last_in = core_in, plane_in, last_in
        self.up_in, self.down_in = up_in, down_in

    def to_core(self, i, source):
        return link(source, self.core_in.at[i], self.sems, (i, 0), {"dp": self.seat.core})

    def first(self, i, along_x):
        s = self.seat
        source = self.own(i).at[:, 1 - s.x] if along_x else self.own(i).at[1 - s.y]
        return link(source, self.plane_in.at[i], self.sems, (i, 1), {"dp": s.xn if along_x else s.yn})

    def second(self, i, along_x):
        s = self.seat
        source = self.own(i).at[s.y, 1 - s.x] if along_x else self.own(i).at[1 - s.y, s.x]
        return link(source, self.last_in.at[i], self.sems, (i, 2), {"dp": s.xn if along_x else s.yn})

    def along(self, i, way):
        s = self.seat
        buffer = self.up_in if way > 0 else self.down_in
        at = (i, 3 if way > 0 else 4)
        return link(self.own(i).at[s.y, s.x], buffer.at[i], self.sems, at, {"tensor": s.z + way})

    def x_first(self, i, then, other):
        pl.when(lax.rem(i, 2) == 0)(then)
        pl.when(lax.rem(i, 2) == 1)(other)

    def one(self, i):
        mine = self.own(i)
        mine[...] = mine[...] + self.core_in[i]
        self.x_first(i, lambda: self.first(i, True).start(), lambda: self.first(i, False).start())

    def two(self, i):
        s, mine = self.seat, self.own(i)

        def from_x():
            self.first(i, True).wait_recv()
            mine[:, s.x] = mine[:, s.x] + self.plane_in[i]
            self.second(i, False).start()

        def from_y():
            self.first(i, False).wait_recv()
            mine[s.y] = mine[s.y] + self.plane_in[i]
            self.second(i, True).start()

        self.x_first(i, from_x, from_y)

    def three(self, i):
        s, mine = self.seat, self.own(i)
        self.second(i, False).wait_recv()
        mine[s.y, s.x] = mine[s.y, s.x] + self.last_in[i]

        @pl.when((s.z == 0) & (self.level_of(i) > 0))
        def _():
            self.along(i, 1).start()

        @pl.when((s.z == 3) & (self.level_of(i) < 3))
        def _():
            self.along(i, -1).start()

    def hop(self, i, reach):
        s, mine = self.seat, self.own(i)

        @pl.when((s.z == reach) & (self.level_of(i) > reach))
        def _():
            self.along(i, 1).wait_recv()
            mine[s.y, s.x] = mine[s.y, s.x] + self.up_in[i]
            self.along(i, 1).start()

        @pl.when((s.z == 3 - reach) & (self.level_of(i) < 3 - reach))
        def _():
            self.along(i, -1).wait_recv()
            mine[s.y, s.x] = mine[s.y, s.x] + self.down_in[i]
            self.along(i, -1).start()

    def total(self, i):
        s = self.seat
        values = self.own(i)[s.y, s.x].astype(F32)

        @pl.when(s.z > 0)
        def _():
            self.along(i, 1).wait_recv()

        @pl.when(s.z < 3)
        def _():
            self.along(i, -1).wait_recv()

        @pl.when(s.z == 0)
        def _():
            self.up_in[i] = jnp.zeros(self.up_in.shape[1:], LOW)

        @pl.when(s.z == 3)
        def _():
            self.down_in[i] = jnp.zeros(self.down_in.shape[1:], LOW)

        return values + self.up_in[i].astype(F32) + self.down_in[i].astype(F32)

    def drain(self, i):
        s = self.seat
        self.first(i, True).wait_send()
        self.second(i, True).wait_send()

        @pl.when(s.z < self.level_of(i))
        def _():
            self.along(i, 1).wait_send()

        @pl.when(s.z > self.level_of(i))
        def _():
            self.along(i, -1).wait_send()


class Whole:
    def __init__(self, seat, own, core_in, plane_in, last_in, level_in, sems):
        self.seat, self.own, self.sems = seat, own, sems
        self.core_in, self.plane_in, self.last_in, self.level_in = core_in, plane_in, last_in, level_in
        self.half = core_in.shape[2] // 2

    def to_core(self, source):
        return link(source, self.core_in, self.sems, 0, {"dp": self.seat.core})

    def rows(self, which):
        return slice(which * self.half, (which + 1) * self.half)

    def first(self, which):
        s = self.seat
        rows = self.rows(which)
        source = self.own.at[1 - s.y, :, rows] if which else self.own.at[:, 1 - s.x, rows]
        return link(source, self.plane_in.at[which], self.sems, 1 + which, {"dp": s.yn if which else s.xn})

    def second(self, which):
        s = self.seat
        rows = self.rows(which)
        source = self.own.at[s.y, 1 - s.x, rows] if which else self.own.at[1 - s.y, s.x, rows]
        return link(source, self.last_in.at[which], self.sems, 3 + which, {"dp": s.xn if which else s.yn})

    def lift(self):
        s = self.seat
        return link(self.own.at[s.y, s.x], self.level_in.at[0], self.sems, 5, {"tensor": s.z + 1 - 2 * (s.z % 2)})

    def cross(self):
        s = self.seat
        return link(self.own.at[s.y, s.x], self.level_in.at[1], self.sems, 6, {"tensor": 3 - s.z})

    def give(self):
        s = self.seat
        return link(self.own.at[s.y, s.x], self.level_in.at[1], self.sems, 7, {"tensor": s.z + 1 - 2 * (s.z % 2)})

    def middle(self):
        return (self.seat.z == 1) | (self.seat.z == 2)

    def ends(self):
        return (self.seat.z == 0) | (self.seat.z == 3)

    def one(self):
        for a in range(2):
            for b in range(2):
                self.own[a, b] = self.own[a, b] + self.core_in[a, b]
        self.first(0).start()
        self.first(1).start()

    def two(self):
        s, own = self.seat, self.own
        for which in range(2):
            rows = self.rows(which)
            self.first(which).wait_recv()
            for a in range(2):
                if which:
                    own[s.y, a, rows] = own[s.y, a, rows] + self.plane_in[which, a]
                else:
                    own[a, s.x, rows] = own[a, s.x, rows] + self.plane_in[which, a]
            self.second(which).start()

    def three(self):
        s, own = self.seat, self.own
        for which in range(2):
            rows = self.rows(which)
            self.second(which).wait_recv()
            own[s.y, s.x, rows] = own[s.y, s.x, rows] + self.last_in[which]
        pl.when(self.ends())(lambda: self.lift().start())

    def four(self):
        s, own = self.seat, self.own

        @pl.when(self.middle())
        def _():
            self.lift().wait_recv()
            own[s.y, s.x] = own[s.y, s.x] + self.level_in[0]
            self.cross().start()

    def five(self):
        s, own = self.seat, self.own

        @pl.when(self.middle())
        def _():
            self.cross().wait_recv()
            self.cross().wait_send()
            own[s.y, s.x] = own[s.y, s.x] + self.level_in[1]
            self.give().start()

    def total(self):
        s = self.seat

        @pl.when(self.ends())
        def _():
            self.give().wait_recv()

        @pl.when(self.middle())
        def _():
            self.level_in[1] = self.own[s.y, s.x]

        return self.level_in[1].astype(F32)

    def drain(self):
        for which in range(2):
            self.first(which).wait_send()
            self.second(which).wait_send()
        pl.when(self.ends())(lambda: self.lift().wait_send())
        pl.when(self.middle())(lambda: self.give().wait_send())


class Tiny:
    def __init__(self, seat, value, came, sems):
        self.seat, self.value, self.came, self.sems = seat, value, came, sems

    def near(self, ahead, own):
        s = self.seat
        other = lax.rem(s.me + (ahead if own else 8 - ahead), 8)
        place = self.came.at[s.me if own else other]
        return link(self.value.at[0], place, self.sems, ahead - 1, {"dp": other})

    def far(self, ahead, own):
        s = self.seat
        other = lax.rem(s.z + (ahead if own else 4 - ahead), 4)
        place = self.came.at[8 + (s.z if own else other)]
        return link(self.value.at[1], place, self.sems, 6 + ahead, {"tensor": other})

    def start_plane(self):
        for ahead in range(1, 8):
            self.near(ahead, True).start()

    def total(self, first, count):
        total = self.came[first]
        for n in range(1, count):
            total = total + self.came[first + n]
        return total

    def turn_levels(self):
        for ahead in range(1, 8):
            self.near(ahead, False).wait_recv()
        self.came[self.seat.me] = self.value[0]
        self.value[1] = self.total(0, 8)
        for ahead in range(1, 4):
            self.far(ahead, True).start()

    def finish(self):
        for ahead in range(1, 4):
            self.far(ahead, False).wait_recv()
        self.came[8 + self.seat.z] = self.value[1]
        return self.total(8, 4)

    def drain(self):
        for ahead in range(1, 8):
            self.near(ahead, True).wait_send()
        for ahead in range(1, 4):
            self.far(ahead, True).wait_send()


def flow_scratch(chunks, share, cols):
    low = lambda *shape: pltpu.VMEM(shape, LOW)
    sems = lambda: pltpu.SemaphoreType.DMA((chunks, 5))
    return [
        low(chunks, 2, 2, share, cols),
        low(chunks, 2, share, cols),
        low(chunks, share, cols),
        low(chunks, share, cols),
        low(chunks, share, cols),
        sems(),
        sems(),
    ]


def whole_scratch(share, cols):
    low = lambda *shape: pltpu.VMEM(shape, LOW)
    return [
        low(2, 2, share, cols),
        low(2, 2, share // 2, cols),
        low(2, share // 2, cols),
        low(2, share, cols),
        pltpu.SemaphoreType.DMA((8,)),
        pltpu.SemaphoreType.DMA((8,)),
    ]


def tiny_scratch(shape):
    sems = lambda: pltpu.SemaphoreType.DMA((10,))
    return [pltpu.VMEM((2,) + shape, F32), pltpu.VMEM((12,) + shape, F32), sems(), sems()]


MLP_BACK_IO = (10, 5)
MLP_BACK_SCRATCH = 5


def mlp_back_sum_kernel(*refs):
    ins, outs = MLP_BACK_IO
    inputs, dcls_ref = refs[:ins], refs[ins]
    outputs = refs[ins + 1 : ins + 1 + outs]
    share_ref, cls_ref = refs[ins + 1 + outs : ins + 3 + outs]
    rest = refs[ins + 3 + outs :]
    scratch, rest = rest[:MLP_BACK_SCRATCH], rest[MLP_BACK_SCRATCH:]
    full, flow_refs = rest[0], rest[1:8]
    cls_own, cls_load, cls_refs = rest[8], rest[9], rest[10:16]
    step = pl.program_id(0)
    seat = Seat()
    c = seat.c
    share = full.shape[-2]
    flow = Flow(
        seat, lambda i: 1, lambda i: full.at[i, :, :, c], *flow_refs[:5], flow_refs[5:]
    )
    cls = Whole(seat, cls_own, *cls_refs[:4], cls_refs[4:])
    loading = pltpu.make_async_copy(dcls_ref.at[:, :, c], cls_own, cls_load)
    cls_to_core = cls.to_core(dcls_ref.at[:, :, 1 - c])

    def to_core(i):
        return flow.to_core(i, full.at[i, :, :, 1 - c])

    def one(i):
        to_core(i).wait_recv()
        flow.one(i)

    def last(i):
        @pl.when(seat.z == flow.level_of(i))
        def _():
            share_ref[i] = flow.total(i)

    @pl.when(step == 0)
    def _():
        loading.start()
        greet(seat, 4)
        cls_to_core.start()
        share_ref[...] = jnp.zeros(share_ref.shape, F32)

    def keep(kind, at, value):
        full[kind, at // 2, at % 2] = value.reshape(2, share, value.shape[1])

    def cls_total():
        cls_ref[...] = cls.total()

    def cls_one():
        loading.wait()
        cls_to_core.wait_recv()
        cls.one()

    plan = {
        0: [cls_one],
        1: [lambda: to_core(0).start(), lambda: to_core(1).start(), cls.two],
        2: [lambda: one(0), lambda: one(1), cls.three],
        4: [lambda: flow.two(0), lambda: flow.two(1), cls.four],
        5: [lambda: flow.three(0), lambda: flow.three(1)],
        6: [cls.five],
        7: [lambda: flow.hop(0, 1), lambda: flow.hop(1, 1)],
    }

    def between(now, odd):
        for number, actions in plan.items():
            if number % 2 != odd:
                continue

            @pl.when(now == number)
            def _():
                for action in actions:
                    action()

    mlp_back_kernel(*inputs, *outputs, *scratch, keep=keep, between=between)

    @pl.when(step == pl.num_programs(0) - 1)
    def _():
        cls_total()
        for i in range(2):
            last(i)
        for i in range(2):
            to_core(i).wait_send()
            flow.drain(i)
        cls_to_core.wait_send()
        cls.drain()


def mlp_back_sum_call(dx2, active, slope, h2, x1, attended, w_out, w_up, w_dn, vectors, d_cls, collective_id):
    rows, width = dx2.shape
    groups, _, per = w_up.shape
    chunk = per
    hidden = groups * per
    share, classes = d_cls.shape[-2:]
    turned = lambda j: j + 1 - 2 * (j % 2)
    whole = lambda a: pl.BlockSpec(a.shape, lambda j: (0,) * a.ndim, pipeline_mode=pl.Buffered(1))
    weight = pl.BlockSpec((1, width, chunk), lambda j: (turned(j), 0, 0))
    piece = pl.BlockSpec((rows, chunk), lambda j: (0, turned(j)))
    full = lambda *shape: pl.BlockSpec(shape, lambda j: (0,) * len(shape))
    late = lambda j: jnp.maximum(j - 1, 0)
    return pl.pallas_call(
        mlp_back_sum_kernel,
        grid=(hidden // chunk,),
        in_specs=[
            whole(dx2), piece, piece, whole(h2), whole(x1), whole(attended), whole(w_out),
            weight, weight, whole(vectors), pl.BlockSpec(memory_space=pl.ANY),
        ],
        out_specs=[
            pl.BlockSpec((2, 1, width, chunk), lambda j: (0, late(j), 0, 0)),
            full(*w_out.shape),
            full(rows, width),
            full(rows, width),
            full(1, width),
            full(2, share, width),
            full(share, classes),
        ],
        out_shape=[
            jax.ShapeDtypeStruct((2, groups - 1) + w_up.shape[1:], LOW),
            jax.ShapeDtypeStruct(w_out.shape, LOW),
            jax.ShapeDtypeStruct((rows, width), LOW),
            jax.ShapeDtypeStruct((rows, width), F32),
            jax.ShapeDtypeStruct((1, width), F32),
            jax.ShapeDtypeStruct((2, share, width), F32),
            jax.ShapeDtypeStruct((share, classes), F32),
        ],
        scratch_shapes=[
            pltpu.VMEM((rows, width), LOW),
            pltpu.VMEM((width, rows), LOW),
            pltpu.VMEM((width, rows), LOW),
            pltpu.VMEM((rows, width), F32),
            pltpu.VMEM((rows, chunk), LOW),
            pltpu.VMEM((2, 2, 2, 2, share, width), LOW),
        ]
        + flow_scratch(2, share, width)
        + [pltpu.VMEM((2, 2, share, classes), LOW), pltpu.SemaphoreType.DMA]
        + whole_scratch(share, classes),
        compiler_params=pltpu.CompilerParams(
            collective_id=collective_id, has_side_effects=True, vmem_limit_bytes=VMEM_BYTES
        ),
        name="mlp_back_sum",
    )(dx2, active, slope, h2, x1, attended, w_out, w_up, w_dn, vectors, d_cls)


def embed_back_sum_kernel(
    dq_hbm, dk_hbm, dv_hbm, h1_hbm, emb_hbm, dmid_hbm, pix_hbm, coord_ref, win_hbm, vec_ref,
    two_ref, pool_ref, gains_ref, loss_ref, mlp_ref, cls_ref, out_ref,
    in_ref, pp_ref, small_out, square_out,
    dq_ref, dk_ref, dv_ref, h1_ref, emb_ref, dmid_ref, pix_ref, win_ref, tile_sem, load_sem,
    h1t_ref, embt_ref, join_ref, hot_ref, in_full, pp_full,
    *rest, packs,
):
    rows, width = h1_ref.shape
    groups = 4
    part = win_ref.shape[2] // 3
    tile = 256
    seat = Seat()
    c = seat.c
    share = in_full.shape[-2]
    flow = Flow(
        seat, lambda i: (3 * i) % 4, lambda i: in_full.at[i, :, :, c], *rest[:5], rest[5:7]
    )
    pp = Whole(seat, pp_full.at[:, :, c], *rest[7:11], rest[11:13])
    small = Tiny(seat, rest[13], rest[14], rest[15:17])
    square = Tiny(seat, rest[17], rest[18], rest[19:21])
    small_value, square_value = rest[13], rest[17]
    pp_to_core = pp.to_core(pp_full.at[:, :, 1 - c])
    leader = jnp.where(seat.z == 0, 1.0, 0.0)

    def in_to_core(i):
        return flow.to_core(i, in_full.at[i, :, :, 1 - c])

    def one(i):
        in_to_core(i).wait_recv()
        flow.one(i)

    def last(i):
        @pl.when(flow.level_of(i) == seat.z)
        def _():
            in_ref[...] = flow.total(i)

    tiled = (
        (dq_hbm, dq_ref), (dk_hbm, dk_ref), (dv_hbm, dv_ref), (h1_hbm, h1_ref),
        (emb_hbm, emb_ref), (dmid_hbm, dmid_ref),
    )

    def tile_copies(at, numbers):
        span = pl.ds(at * tile, tile)
        return [
            pltpu.make_async_copy(tiled[n][0].at[span], tiled[n][1].at[span], tile_sem.at[n, at])
            for n in numbers
        ]

    win_copy = pltpu.make_async_copy(win_hbm, win_ref, load_sem.at[0])
    pack = jnp.minimum(seat.z, packs - 1)
    pix_copy = pltpu.make_async_copy(
        pix_hbm.at[pl.ds(pl.multiple_of(pack * rows, rows), rows)], pix_ref, load_sem.at[1]
    )
    for at in range(rows // tile):
        for copy in tile_copies(at, range(4)):
            copy.start()
    win_copy.start()
    for at in range(rows // tile):
        for copy in tile_copies(at, range(4, 6)):
            copy.start()
    pix_copy.start()
    greet(seat, 4)
    gain = vec_ref[0:1]
    pixels = pix_ref.shape[1]
    spots = (pp_ref.shape[1] - pixels) // 2
    gain_sum = jnp.zeros((1, width), F32)
    for at in range(rows // tile):
        for copy in tile_copies(at, range(4)):
            copy.wait()
        span = slice(at * tile, (at + 1) * tile)
        for group in range(groups):
            mine = slice(group * part, (group + 1) * part)
            join_ref[group, span, :] = jnp.concatenate(
                [dq_ref[span, mine], dk_ref[span, mine], dv_ref[span, mine]], axis=1
            )
        h1t_ref[:, span] = jnp.transpose(h1_ref[span, :].astype(F32)).astype(LOW)

    def project(i):
        group = flow.level_of(i)
        for at in range(4):
            span = slice(at * 2 * share, (at + 1) * 2 * share)
            value = mm(h1t_ref[span, :], join_ref[group]).astype(LOW)
            in_full[i, at // 2, at % 2] = value.reshape(2, share, value.shape[1])
        in_to_core(i).start()

    project(0)
    project(1)
    win_copy.wait()
    for at in range(rows // tile):
        for copy in tile_copies(at, range(4, 6)):
            copy.wait()
        span = slice(at * tile, (at + 1) * tile)
        d_first = jnp.zeros((tile, width), F32)
        for group in range(groups):
            d_first += mm_nt(join_ref[group, span, :], win_ref[group])
        normed, inverse = row_norm(emb_ref[span, :])
        gain_sum += jnp.sum(d_first * normed, axis=0, keepdims=True)
        d_embed = dmid_ref[span, :] + row_norm_back(d_first, gain, normed, inverse)
        embt_ref[:, span] = jnp.transpose(d_embed).astype(LOW)
        if at < 2:
            one(at)
    flow.two(0)
    small_value[0] = jnp.zeros(small_out.shape, F32)
    small_value[0, 0:1] = gain_sum
    small_value[0, 1:2] = two_ref[...]
    small_value[0, 2:4] = pool_ref[...]
    heads = jnp.sum(gains_ref[...], axis=0)
    small_value[0, 4:5, :128] = heads[0:1]
    small_value[0, 4:5, 128:256] = heads[1:2]
    small_value[0, 5:6, :128] = loss_ref[0:1, :]
    small.start_plane()
    place = lax.broadcasted_iota(jnp.int32, (2 * spots, rows), 0)
    mine = pl.ds(pl.multiple_of(pack * rows, rows), rows)
    hot = (place == coord_ref[0:1, mine]) | (place - spots == coord_ref[1:2, mine])
    hot_ref[...] = hot.astype(F32).astype(LOW)
    pix_copy.wait()
    for at in range(4):
        span = slice(at * 2 * share, (at + 1) * 2 * share)
        picture = mm(embt_ref[span, :], pix_ref[...]).astype(LOW)
        pp_full[at // 2, at % 2, :, :, :pixels] = picture.reshape(2, share, pixels)
        place = mm_nt(embt_ref[span, :], hot_ref[...]).astype(LOW)
        pp_full[at // 2, at % 2, :, :, pixels:] = place.reshape(2, share, 2 * spots)
    pp_to_core.start()
    flow.two(1)
    project(2)
    pp_to_core.wait_recv()
    pp.one()
    flow.three(0)
    small.turn_levels()
    project(3)
    one(2)
    flow.three(1)
    flow.hop(0, 1)
    pp.two()
    one(3)
    flow.hop(1, 1)
    flow.hop(0, 2)
    small_out[...] = small.finish()
    mlp_sum = mlp_ref[...]
    out_sum = out_ref[...]
    squares = jnp.sum(mlp_sum[0] * mlp_sum[0] + mlp_sum[1] * mlp_sum[1], axis=0, keepdims=True)
    total = jnp.sum(squares, axis=1, keepdims=True)
    total = total + jnp.sum(jnp.sum(out_sum * out_sum, axis=0, keepdims=True), axis=1, keepdims=True)
    cls_sum = cls_ref[...]
    shared = jnp.sum(jnp.sum(cls_sum * cls_sum, axis=0, keepdims=True), axis=1, keepdims=True)
    pp.three()
    flow.two(2)
    flow.hop(1, 2)
    flow.two(3)
    pp.four()
    flow.three(2)
    flow.three(3)
    pp.five()
    flow.hop(2, 1)
    flow.hop(3, 1)
    pp_sum = pp.total()
    pp_ref[...] = pp_sum
    shared += jnp.sum(jnp.sum(pp_sum * pp_sum, axis=0, keepdims=True), axis=1, keepdims=True)
    for i in range(groups):
        last(i)
    in_sum = in_ref[...]
    total = total + jnp.sum(jnp.sum(in_sum * in_sum, axis=0, keepdims=True), axis=1, keepdims=True)
    square_value[0] = jnp.broadcast_to(total + leader * shared, (8, 128))
    square.start_plane()
    square.turn_levels()
    square_out[...] = square.finish()
    pp_to_core.wait_send()
    for entry in (pp, small, square):
        entry.drain()
    for i in range(groups):
        in_to_core(i).wait_send()
        flow.drain(i)


def embed_back_sum_call(
    dq, dk, dv, h1, embedded, d_middle, pixels, coords, w_in, pp_cols, vectors,
    d_two, d_pool, d_gain, loss, share_mlp, share_cls, share_out, packs, collective_id,
):
    rows, width = h1.shape
    groups, share = w_in.shape[0], width // 8
    cols = w_in.shape[2]
    low = lambda *shape: pltpu.VMEM(shape, LOW)
    inside = pl.BlockSpec(memory_space=pltpu.VMEM)
    anywhere = pl.BlockSpec(memory_space=pl.ANY)
    loaded = (dq, dk, dv, h1, embedded, d_middle, pixels, w_in)
    return pl.pallas_call(
        functools.partial(embed_back_sum_kernel, packs=packs),
        in_specs=[anywhere] * 7 + [inside, anywhere] + [inside] * 8,
        out_specs=[inside] * 4,
        out_shape=[
            jax.ShapeDtypeStruct((share, cols), F32),
            jax.ShapeDtypeStruct((share, pp_cols), F32),
            jax.ShapeDtypeStruct((8, width), F32),
            jax.ShapeDtypeStruct((8, 128), F32),
        ],
        scratch_shapes=[pltpu.VMEM((rows,) + a.shape[1:] if a is pixels else a.shape, a.dtype) for a in loaded]
        + [pltpu.SemaphoreType.DMA((6, rows // 256)), pltpu.SemaphoreType.DMA((2,))]
        + [
            low(width, rows),
            low(width, rows),
            low(groups, rows, cols),
            low(pp_cols - pixels.shape[1], rows),
            low(groups, 2, 2, 2, share, cols),
            low(2, 2, 2, share, pp_cols),
        ]
        + flow_scratch(groups, share, cols)
        + whole_scratch(share, pp_cols)
        + tiny_scratch((8, width))
        + tiny_scratch((8, 128)),
        compiler_params=pltpu.CompilerParams(
            collective_id=collective_id, has_side_effects=True, vmem_limit_bytes=VMEM_BYTES
        ),
        name="embed_back_sum",
    )(
        dq, dk, dv, h1, embedded, d_middle, pixels, coords, w_in, vectors,
        d_two, d_pool, d_gain, loss, share_mlp, share_cls, share_out,
    )


def prepare_kernel(
    length_ref, patch_ref, pos_ref, in_ref, out_ref, up_ref, dn_ref, cls_ref, gain_ref,
    pp_low, in_low, out_low, up_low, dn_low, cls_low, bound_out, gain_out,
):
    packs, images = length_ref.shape
    pixels = patch_ref.shape[1]
    kinds, spots, share = pos_ref.shape
    pp_low[:, :pixels] = patch_ref[...].astype(LOW)
    pp_low[:, pixels:] = jnp.transpose(pos_ref[...].reshape(kinds * spots, share)).astype(LOW)
    in_low[...] = jnp.concatenate([in_ref[n] for n in range(in_ref.shape[0])], axis=1).astype(LOW)
    out_low[...] = jnp.transpose(out_ref[...]).astype(LOW)
    up_low[...] = up_ref[...].astype(LOW)
    dn_low[...] = dn_ref[...].astype(LOW)
    cls_low[...] = cls_ref[...].astype(LOW)
    gain_out[...] = jnp.concatenate([gain_ref[...], gain_ref[...]], axis=1)
    pack = jnp.minimum(lax.axis_index("tensor"), packs - 1)
    lane = lax.broadcasted_iota(jnp.int32, (1, 128), 1)
    slot = jnp.where(lane >= 64, lane - 64, lane)
    starts = jnp.full((1, 128), 1 << 30, jnp.int32)
    ends = starts
    place = jnp.int32(0)
    for n in range(images):
        after = place + length_ref[pack, n]
        starts = jnp.where(slot == n, place, starts)
        ends = jnp.where(slot == n, after, ends)
        place = after
    bound_out[0:1, :] = starts
    bound_out[1:2, :] = ends


def prepare_call(lengths, patch, pos, w_in, w_out, up, dn, cls, gains):
    share, width = up.shape
    low = lambda cols: jax.ShapeDtypeStruct((share, cols), LOW)
    inside = pl.BlockSpec(memory_space=pltpu.VMEM)
    return pl.pallas_call(
        prepare_kernel,
        in_specs=[pl.BlockSpec(memory_space=pltpu.SMEM)] + [inside] * 8,
        out_specs=[inside] * 8,
        out_shape=[
            low(patch.shape[1] + pos.shape[0] * pos.shape[1]),
            low(w_in.shape[0] * w_in.shape[2]),
            low(w_out.shape[0]),
            low(width),
            low(width),
            low(cls.shape[1]),
            jax.ShapeDtypeStruct((2, 128), jnp.int32),
            jax.ShapeDtypeStruct((2, 128), F32),
        ],
        compiler_params=pltpu.CompilerParams(vmem_limit_bytes=VMEM_BYTES),
        name="prepare",
    )(lengths, patch, pos, w_in, w_out, up, dn, cls, gains)


RATES = (RATE_BASE, RATE_POSITION, RATE_BASE, RATE_MIDDLE, RATE_BASE, RATE_BASE, RATE_MIDDLE, RATE_VECTOR, RATE_VECTOR)


def update_kernel(*refs):
    states, shares, outs = refs[:27], refs[27:34], refs[34:61]
    loss_ref, norm_ref = refs[61:]
    pp_ref, in_ref, out_ref, mlp_ref, cls_ref, small_ref, square_ref = shares
    pixels = states[0].shape[1]
    kinds, spots, share = states[3].shape
    part = states[6].shape[2]
    vectors = small_ref[0:4, :]
    row = small_ref[4:5, :]
    head = states[24].shape[1]
    gains = jnp.concatenate(
        [row[:, :head] + row[:, head : 2 * head], row[:, 2 * head : 3 * head] + row[:, 3 * head : 4 * head]],
        axis=0,
    )

    def square_sum(entry):
        return jnp.sum(jnp.sum(entry * entry, axis=0, keepdims=True), axis=1, keepdims=True)

    norm = jnp.sqrt(square_ref[0:1, 0:1] + square_sum(vectors) + square_sum(gains))
    clip = CLIP / jnp.maximum(norm, CLIP)
    grads = (
        pp_ref[:, :pixels],
        jnp.transpose(pp_ref[:, pixels:]).reshape(kinds, spots, share),
        None,
        jnp.transpose(out_ref[...]),
        mlp_ref[1],
        mlp_ref[0],
        cls_ref[...],
        vectors,
        gains,
    )
    for n, grad in enumerate(grads):
        decay = DECAY if n < 7 else 0.0
        if n == 2:
            for kind in range(states[6].shape[0]):
                results = adam(
                    *(state[kind] for state in states[6:9]),
                    in_ref[:, kind * part : (kind + 1) * part], clip, RATES[n], decay,
                )
                for result, out in zip(results, outs[6:9]):
                    out[kind] = result
        else:
            mine = clip.reshape(1, 1, 1) if grad.ndim == 3 else clip
            results = adam(*(state[...] for state in states[3 * n : 3 * n + 3]), grad, mine, RATES[n], decay)
            for result, out in zip(results, outs[3 * n : 3 * n + 3]):
                out[...] = result
    loss_ref[...] = small_ref[5:6, 0:1]
    norm_ref[...] = norm


def update_call(states, shares):
    inside = pl.BlockSpec(memory_space=pltpu.VMEM)
    scalar = jax.ShapeDtypeStruct((1, 1), F32)
    return pl.pallas_call(
        update_kernel,
        in_specs=[inside] * (len(states) + len(shares)),
        out_specs=[inside] * (len(states) + 2),
        out_shape=[jax.ShapeDtypeStruct(a.shape, F32) for a in states] + [scalar, scalar],
        compiler_params=pltpu.CompilerParams(vmem_limit_bytes=VMEM_BYTES),
        name="update",
    )(*states, *shares)


def adam(master, first_moment, second_moment, gradient, clip_scale, rate, decay_rate):
    gradient = gradient * clip_scale
    first_new = BETA_ONE * first_moment + (1 - BETA_ONE) * gradient
    second_new = BETA_TWO * second_moment + (1 - BETA_TWO) * gradient * gradient
    update = (
        first_new / (1 - BETA_ONE**STEP) / (jnp.sqrt(second_new / (1 - BETA_TWO**STEP)) + ADAM_EPS)
    )
    return (master - rate * (update + decay_rate * master), first_new, second_new)


def squared(entry):
    return jnp.sum(entry * entry)


def per_device(
    pixels, coords, lengths, labels,
    patch_table, patch_first, patch_second,
    position_table, position_first, position_second,
    attend_in, attend_in_first, attend_in_second,
    attend_out, attend_out_first, attend_out_second,
    expand, expand_first, expand_second,
    shrink, shrink_first, shrink_second,
    classify, classify_first, classify_second,
    vectors, vectors_first, vectors_second,
    head_gains, head_gains_first, head_gains_second,
):
    packs, images = lengths.shape
    members = lax.axis_size("tensor")
    width = vectors.shape[1]
    share = attend_in.shape[0]
    seat = lax.axis_index("tensor")
    pack = jnp.minimum(seat, packs - 1).astype(jnp.int32)[None]
    valid = (seat < packs).astype(F32).reshape(1, 1)
    image_count = images * packs * lax.axis_size("dp")
    if lax.axis_size("dp") == 8 and members == 4:
        turn = {0: lambda a: a.T, 2: lambda a: jnp.transpose(a, (1, 0, 2)), 5: lambda a: a.T}
        states = (
            patch_table, patch_first, patch_second, position_table, position_first, position_second,
            attend_in, attend_in_first, attend_in_second, attend_out, attend_out_first, attend_out_second,
            expand, expand_first, expand_second, shrink, shrink_first, shrink_second,
            classify, classify_first, classify_second, vectors, vectors_first, vectors_second,
            head_gains, head_gains_first, head_gains_second,
        )
        states = [turn.get(n // 3, lambda a: a)(entry) for n, entry in enumerate(states)]
        ready = prepare_call(lengths, *states[0:21:3], head_gains)
        shares = pack_step(
            pack, valid, pixels, coords, lengths, labels, tuple(ready), vectors, head_gains, image_count, True
        )
        *results, loss_total, grad_norm = update_call(states, shares)
        results = [turn.get(n // 3, lambda a: a)(entry) for n, entry in enumerate(results)]
        return (*results, loss_total.reshape(()), grad_norm.reshape(()))
    shards = (
        jnp.concatenate(
            [patch_table.T, jnp.transpose(position_table, (2, 0, 1)).reshape(share, -1)], axis=1
        ).astype(LOW),
        attend_in.reshape(share, -1).astype(LOW),
        attend_out.T.astype(LOW),
        expand.astype(LOW),
        shrink.T.astype(LOW),
        classify.astype(LOW),
    )
    both = ("tensor", "dp")

    def gather(shard):
        return lax.all_gather(shard, both, axis=0, tiled=True).reshape(members, width, -1)

    weights = (
        lax.all_gather(shards[0], "dp", axis=0, tiled=True),
        gather(shards[1]),
        gather(shards[2]),
        gather(shards[3]),
        gather(shards[4]),
        lax.all_gather(shards[5], "dp", axis=0, tiled=True),
    )
    grads, grad_vectors, grad_gains, loss_local = pack_step(
        pack, valid, pixels, coords, lengths, labels, weights, vectors, head_gains, image_count
    )
    grad_vectors, grad_gains, loss_total = lax.psum((grad_vectors, grad_gains, loss_local), both)

    def scatter(grad):
        return lax.psum_scatter(
            grad.reshape(members * width, -1), both, scatter_dimension=0, tiled=True
        ).astype(F32)

    def scatter_whole(grad):
        part = lax.psum_scatter(grad, "dp", scatter_dimension=0, tiled=True)
        return lax.psum(part, "tensor").astype(F32)

    share_pp = scatter_whole(grads[0])
    share_in, share_out, share_up, share_dn = (scatter(entry) for entry in grads[1:5])
    share_cls = scatter_whole(grads[5])
    leader = (seat == 0).astype(F32)
    split_squares = squared(share_in) + squared(share_out) + squared(share_up) + squared(share_dn)
    squares = lax.psum(split_squares + leader * (squared(share_pp) + squared(share_cls)), both)
    grad_norm = jnp.sqrt(squares + squared(grad_vectors) + squared(grad_gains))
    clip_scale = CLIP / jnp.maximum(grad_norm, CLIP)
    pixel_width = patch_table.shape[0]
    share_patch = share_pp[:, :pixel_width].T
    share_pos = jnp.transpose(
        share_pp[:, pixel_width:].reshape(share, position_table.shape[0], position_table.shape[1]), (1, 2, 0)
    )
    results = (
        adam(patch_table, patch_first, patch_second, share_patch, clip_scale, RATE_BASE, DECAY),
        adam(position_table, position_first, position_second, share_pos, clip_scale, RATE_POSITION, DECAY),
        adam(
            attend_in, attend_in_first, attend_in_second,
            share_in.reshape(attend_in.shape), clip_scale, RATE_BASE, DECAY,
        ),
        adam(attend_out, attend_out_first, attend_out_second, share_out.T, clip_scale, RATE_MIDDLE, DECAY),
        adam(expand, expand_first, expand_second, share_up, clip_scale, RATE_BASE, DECAY),
        adam(shrink, shrink_first, shrink_second, share_dn.T, clip_scale, RATE_BASE, DECAY),
        adam(classify, classify_first, classify_second, share_cls, clip_scale, RATE_MIDDLE, DECAY),
        adam(vectors, vectors_first, vectors_second, grad_vectors, clip_scale, RATE_VECTOR, 0.0),
        adam(head_gains, head_gains_first, head_gains_second, grad_gains, clip_scale, RATE_VECTOR, 0.0),
    )
    return tuple(entry for group in results for entry in group) + (loss_total, grad_norm)


def solution(mesh):
    data = P("dp", None)
    in_specs = (
        (data, P(None, "dp"), data, data)
        + (P(None, "dp"),) * 3
        + (P(None, None, "dp"),) * 3
        + (P("dp", None, "tensor"),) * 3
        + (P("tensor", "dp"),) * 3
        + (P("dp", "tensor"),) * 3
        + (P("tensor", "dp"),) * 3
        + (data,) * 3
        + (P(),) * 6
    )
    out_specs = in_specs[4:] + (P(), P())
    return jax.shard_map(per_device, mesh=mesh, in_specs=in_specs, out_specs=out_specs, check_vma=False)
```
